32 devices in a mesh: pipe: 2 (over x), seq: 4 (over z), dp: 4 (over y, core).
Axes of the slice: x: 2, y: 2, z: 4, core: 2. Of those that a mesh axis runs over, the one named last changes fastest.
Arguments:
- queries: bfloat16 [2, 4, 4, 384, 1536], P('pipe', 'dp', 'seq'), may hold values from -18 to 18
- keys: bfloat16 [2, 4, 4, 384, 1536], P('pipe', 'dp', 'seq'), may hold values from -18 to 18
- values: bfloat16 [2, 4, 4, 384, 1536], P('pipe', 'dp', 'seq'), may hold values from -6 to 6
- grad_out: bfloat16 [2, 4, 4, 384, 1536], P('pipe', 'dp', 'seq'), may hold values from -20 to 20
- norm_gains: float32 [2, 2, 128], P('pipe'), may hold values from 0.5 to 1.5
- kv_tiles: int32 [2, 4, 4, 3], P('pipe', 'dp', 'seq'), may hold values from -1 to 3, as said below
Outputs:
- qkv_grad: bfloat16 [2, 3, 4, 4, 384, 1536], P('pipe', None, 'dp', 'seq')
- gain_grads: float32 [2, 2, 128], P('pipe')
The draws below stay inside these ranges and needn't reach their ends.
Inputs may be any that keep to these rules, and one draw needn't show every extreme that they name: `kv_tiles`: tile t covers frame tile t // 1 and spatial tile t % 1. The row of tile t names tile t itself and some of the other tiles of frame tiles t - 1, t // 1 and t + 1 inside the sample, each at most once, in some order; its other entries are -1.
All inputs are finite; a program needn't handle non-finite values.
Results may differ from the reference program's by a relative error of at most 0.007.
Values may be sent and summed in bfloat16 or wider, within the bound.
No kernel may reach another device: no remote copies, remote signals or barrier semaphores. Data moves between devices by JAX's collectives and lax.ppermute only.
A program may use at most 256 MiB of HBM per device.

```python
import math
import jax
import jax.numpy as jnp
from jax import lax

TPD = 1
TILE = 384
HEADS = 12
HEAD_DIM = 128
SLOTS = 3
HD = 1536
FRAME_TILES = 4
TILES = 4
BATCH = 4
SEGMENTS = 2


def draw_kv_tiles(key, part):
    tile_ids = jnp.arange(TILES, dtype=jnp.int32)
    frame_ids = tile_ids // TPD
    slot_ids = jnp.arange(SLOTS, dtype=jnp.int32)
    frame_step = slot_ids // TPD - 1
    spot_ids = slot_ids % TPD
    cand_frame = frame_ids[:, None] + frame_step[None, :]
    usable = (cand_frame >= 0) & (cand_frame < FRAME_TILES)
    cand_tile = jnp.where(usable, cand_frame * TPD + spot_ids[None, :], -1)
    cand_full = jnp.broadcast_to(cand_tile, (SEGMENTS, BATCH, TILES, SLOTS))
    own_slot = cand_full == tile_ids[None, None, :, None]
    keep_bits = jax.random.randint(jax.random.fold_in(key, 5), (SEGMENTS, BATCH, TILES, SLOTS), 0, 2)
    kept = own_slot | (keep_bits == 1)
    cand_full = jnp.where(kept, cand_full, -1)
    random_rank = jax.random.randint(jax.random.fold_in(key, 7), (SEGMENTS, BATCH, TILES, SLOTS), 0, 1 << 20)
    ranking = random_rank * 64 + slot_ids
    order = jnp.argsort(ranking, axis=-1, stable=True)
    return jnp.take_along_axis(cand_full, order, axis=-1).astype(jnp.int32)


def token_scales(key, lowest, highest):
    full_shape = (SEGMENTS, BATCH, TILES, TILE, HEADS, 1)
    return jnp.exp(jax.random.uniform(key, full_shape, jnp.float32, jnp.log(lowest), jnp.log(highest)))


def headed(key):
    noise_key = jax.random.fold_in(key, 1)
    scale_key = jax.random.fold_in(key, 2)
    full_shape = (SEGMENTS, BATCH, TILES, TILE, HEADS, HEAD_DIM)
    noise_part = jnp.clip(jax.random.normal(noise_key, full_shape, jnp.float32), -4.0, 4.0)
    noise_part = noise_part * token_scales(scale_key, 0.3, 3.0)
    return noise_part.reshape(SEGMENTS, BATCH, TILES, TILE, HEADS * HEAD_DIM)


def draw_queries(key, part):
    return headed(jax.random.fold_in(key, 11)).astype(jnp.bfloat16)


def draw_keys(key, part):
    return headed(jax.random.fold_in(key, 23)).astype(jnp.bfloat16)


def draw_grad_out(key, part):
    noise_key = jax.random.fold_in(key, 31)
    full_shape = (SEGMENTS, BATCH, TILES, TILE, HEADS * HEAD_DIM)
    frame_pos = (jnp.arange(TILES, dtype=jnp.int32) // TPD).astype(jnp.float32)
    frame_ramp = (1.0 + 2.0 * frame_pos / (FRAME_TILES - 1)).reshape(1, 1, TILES, 1, 1)
    noise_part = jnp.clip(jax.random.normal(noise_key, full_shape, jnp.float32), -4.0, 4.0)
    return (noise_part * frame_ramp).astype(jnp.bfloat16)


def block_scale(rng, shape, split, least, high):
    gain, own = 1.0, jax.random.fold_in(rng, 6)
    for position, parts in split:
        steps = jnp.exp(jax.random.uniform(jax.random.fold_in(own, position), (parts,), jnp.float32, least / len(split), high / len(split)))
        gain = gain * jnp.repeat(steps, shape[position] // parts).reshape([-1 if axis == position else 1 for axis in range(len(shape))])
    return gain


def noise(own_key, shape, deviation, reach, pieces=(), kind=jnp.bfloat16):
    result = deviation * jax.random.normal(own_key, shape, jnp.float32)
    if pieces:
        result = result * block_scale(own_key, shape, pieces, -0.22, 0.18)
    return jnp.clip(result, -reach, reach).astype(kind)


def setup_inputs(seed: int = 0) -> dict:
    key_list = jax.random.split(jax.random.key(seed), 7)
    queries = draw_queries(jax.random.fold_in(key_list[6], 71), 0)
    keys = draw_keys(jax.random.fold_in(key_list[6], 71), 0)
    values = noise(key_list[2], (SEGMENTS, BATCH, TILES, TILE, HD), 1.0, 6.0, ((0, 2), (1, 4), (2, 4)))
    grad_out = draw_grad_out(jax.random.fold_in(key_list[6], 71), 0)
    norm_gains = jnp.clip(1.0 + 0.1 * jax.random.normal(key_list[4], (SEGMENTS, 2, HEAD_DIM), jnp.float32), 0.5, 1.5)
    kv_tiles = draw_kv_tiles(jax.random.fold_in(key_list[6], 71), 0)
    return dict(queries=queries, keys=keys, values=values, grad_out=grad_out, norm_gains=norm_gains, kv_tiles=kv_tiles)


epsilon = 1e-06

def normalize(source, gain_row):
    floats = source.astype(jnp.float32).reshape(source.shape[:-1] + (HEADS, HEAD_DIM))
    scaled = lax.rsqrt(lax.optimization_barrier(jnp.mean(floats * floats, axis=-1, keepdims=True)) + epsilon)
    normed = (floats * scaled * gain_row).astype(jnp.bfloat16)
    return (normed, floats, scaled)

def norm_back(grad_hat, floats, scaled, gain_row):
    projected = lax.optimization_barrier(jnp.sum(gain_row * grad_hat * floats, axis=-1, keepdims=True))
    gradient = scaled * gain_row * grad_hat - scaled ** 3 * floats * projected / HEAD_DIM
    gain_part = lax.optimization_barrier(jnp.sum((grad_hat * floats * scaled).reshape(-1, HEAD_DIM), axis=0))
    return (gradient.reshape(gradient.shape[:-2] + (HEADS * HEAD_DIM,)), gain_part)

def rounded(source):
    return lax.optimization_barrier(source.astype(jnp.bfloat16)).astype(jnp.float32)

def one_sample(query_in, key_in, value_in, grad_in, gain_rows, tile_lists):
    query_hat, query_floats, query_scale = normalize(query_in, gain_rows[0])
    key_hat, key_floats, key_scale = normalize(key_in, gain_rows[1])
    value_head = value_in.astype(jnp.float32).reshape(TILES, TILE, HEADS, HEAD_DIM)
    grad_head = grad_in.astype(jnp.float32).reshape(TILES, TILE, HEADS, HEAD_DIM)
    root_scale = HEAD_DIM ** (-0.5)

    def visit(carry, tile_index):
        key_acc, value_acc = carry
        listed = tile_lists[tile_index].astype(jnp.int32)
        live = (listed >= 0).astype(jnp.float32)
        chosen = jnp.maximum(listed, 0).astype(jnp.int32)
        key_mask = jnp.repeat(live, TILE)
        keys_here = key_hat[chosen].astype(jnp.float32).reshape(SLOTS * TILE, HEADS, HEAD_DIM)
        values_here = value_head[chosen].reshape(SLOTS * TILE, HEADS, HEAD_DIM)
        query_tile = query_hat[tile_index].astype(jnp.float32)
        grad_tile = grad_head[tile_index]
        scores = jnp.einsum('qhd,khd->hqk', query_tile, keys_here) * root_scale
        exp_scores = jnp.exp(scores) * key_mask
        attention = exp_scores / lax.optimization_barrier(jnp.sum(exp_scores, axis=-1, keepdims=True))
        grad_attn = jnp.einsum('qhd,khd->hqk', grad_tile, values_here)
        deltas = lax.optimization_barrier(jnp.sum(attention * grad_attn, axis=-1, keepdims=True))
        dscore = rounded(attention * (grad_attn - deltas))
        attn_low = rounded(attention)
        query_grad = jnp.einsum('hqk,khd->qhd', dscore, keys_here) * root_scale
        key_part = jnp.einsum('hqk,qhd->khd', dscore, query_tile) * root_scale
        value_part = jnp.einsum('hqk,qhd->khd', attn_low, grad_tile)
        slot_mask = live[:, None, None, None]
        key_acc = key_acc.at[chosen].add(key_part.reshape(SLOTS, TILE, HEADS, HEAD_DIM) * slot_mask)
        value_acc = value_acc.at[chosen].add(value_part.reshape(SLOTS, TILE, HEADS, HEAD_DIM) * slot_mask)
        return ((key_acc, value_acc), query_grad)
    zero_acc = jnp.zeros((TILES, TILE, HEADS, HEAD_DIM), jnp.float32)
    (key_acc, value_acc), query_grads = lax.scan(visit, (zero_acc, zero_acc), jnp.arange(TILES, dtype=jnp.int32))
    query_grad, query_gain = norm_back(query_grads, query_floats, query_scale, gain_rows[0])
    key_grad, key_gain = norm_back(key_acc, key_floats, key_scale, gain_rows[1])
    value_grad = value_acc.reshape(TILES, TILE, HEADS * HEAD_DIM)
    stacked = jnp.stack([query_grad, key_grad, value_grad]).astype(jnp.bfloat16)
    return (stacked, jnp.stack([query_gain, key_gain]))

def reference(queries, keys, values, grad_out, norm_gains, kv_tiles):
    segment_grads = []
    segment_gains = []
    for segment_index in range(SEGMENTS):
        sample_grads = []
        gain_total = jnp.zeros((2, HEAD_DIM), jnp.float32)
        for sample_index in range(BATCH):
            grads, gain_terms = one_sample(queries[segment_index, sample_index], keys[segment_index, sample_index], values[segment_index, sample_index], grad_out[segment_index, sample_index], norm_gains[segment_index], kv_tiles[segment_index, sample_index])
            sample_grads.append(grads)
            gain_total = gain_total + gain_terms
        segment_grads.append(jnp.stack(sample_grads, axis=1))
        segment_gains.append(gain_total / math.sqrt(BATCH * TILES * TILE * HEADS))
    grads_all = jnp.stack(segment_grads)
    return (jnp.roll(grads_all, -1, axis=0), jnp.stack(segment_gains))
```

```python
import functools
import math

import jax
import jax.numpy as jnp
from jax import lax
from jax.experimental import pallas as pl
from jax.experimental.pallas import tpu as pltpu
from jax.sharding import PartitionSpec as P

HEADS = 12
HEAD_DIM = 128
EPSILON = 1e-06
ROOT_SCALE = HEAD_DIM ** (-0.5)
EXP2_SCALE = ROOT_SCALE * math.log2(math.e)
GROUPS = ((0, 4, False), (4, 4, False), (8, 4, True))
VMEM_LIMIT = 48 * 1024 * 1024


def dot_nt(left, right):
    return lax.dot_general(
        left, right, (((1,), (1,)), ((), ())), preferred_element_type=jnp.float32
    )


def dot_nn(left, right):
    return lax.dot_general(
        left, right, (((1,), (0,)), ((), ())), preferred_element_type=jnp.float32
    )


def dot_tn(left, right):
    return lax.dot_general(
        left, right, (((0,), (0,)), ((), ())), preferred_element_type=jnp.float32
    )


def normalize(source, gain):
    floats = source.astype(jnp.float32)
    scaled = lax.rsqrt(jnp.mean(floats * floats, axis=-1, keepdims=True) + EPSILON)
    normed = floats * scaled
    return floats, scaled, normed, (normed * gain).astype(jnp.bfloat16)


def norm_back(grad_hat, floats, scaled, gain):
    scaled_grad = gain * grad_hat
    projected = jnp.sum(scaled_grad * floats, axis=-1, keepdims=True)
    return scaled * scaled_grad - (scaled**3 * projected * (1.0 / HEAD_DIM)) * floats


def main_kernel(
    info, query, grad, key, value, pair_prev, pair_next,
    query_out, own_out, prev_out, next_out, gain_out,
):
    query_gain = info[0:1, :HEAD_DIM]
    key_gain = info[1:2, :HEAD_DIM]
    query_floats, query_scale, query_normed, query_hat = normalize(query[...], query_gain)
    grad_in = grad[...]
    sides = (
        (key[...], value[...], None),
        (pair_prev[0], pair_prev[1], info[2:3, :]),
        (pair_next[0], pair_next[1], info[3:4, :]),
    )
    parts = []
    totals = None
    for key_in, value_in, live in sides:
        _, _, key_normed, key_hat = normalize(key_in, key_gain)
        weights = jnp.exp2(dot_nt(key_hat, query_hat) * EXP2_SCALE)
        grad_probs = dot_nt(value_in, grad_in)
        weight_sum = jnp.sum(weights, axis=0, keepdims=True)
        cross_sum = jnp.sum(weights * grad_probs, axis=0, keepdims=True)
        if live is not None:
            weight_sum = weight_sum * live
            cross_sum = cross_sum * live
        totals = weight_sum if totals is None else totals + weight_sum
        crosses = cross_sum if live is None else crosses + cross_sum
        parts.append((key_normed, key_hat, weights, grad_probs, live))
    inverse = 1.0 / totals
    deltas = crosses * inverse
    query_grad_t = None
    key_gain_sum = None
    for (key_normed, key_hat, weights, grad_probs, live), out in zip(
        parts, (own_out, prev_out, next_out)
    ):
        probs = weights * (inverse if live is None else inverse * live)
        dscores = (probs * (grad_probs - deltas)).astype(jnp.bfloat16)
        key_part = dot_nn(dscores, query_hat) * ROOT_SCALE
        value_part = dot_nn(probs.astype(jnp.bfloat16), grad_in)
        out[0] = key_part.astype(out.dtype)
        out[1] = value_part.astype(out.dtype)
        gain_part = jnp.sum(key_part * key_normed, axis=0, keepdims=True)
        key_gain_sum = gain_part if key_gain_sum is None else key_gain_sum + gain_part
        query_part = dot_tn(key_hat, dscores)
        query_grad_t = query_part if query_grad_t is None else query_grad_t + query_part
    query_grad = query_grad_t.T * ROOT_SCALE
    query_out[...] = norm_back(query_grad, query_floats, query_scale, query_gain).astype(
        query_out.dtype
    )
    query_gain_sum = jnp.sum(query_grad * query_normed, axis=0, keepdims=True)

    @pl.when(pl.program_id(0) == 0)
    def _():
        gain_out[...] = jnp.zeros_like(gain_out)

    gain_out[0:1, :] += query_gain_sum
    gain_out[1:2, :] += key_gain_sum


def finish_kernel(info, key, own, from_prev, from_next, out):
    key_gain = info[1:2, :HEAD_DIM]
    key_floats, key_scale, _, _ = normalize(key[...], key_gain)
    key_grad = own[0] + from_prev[0].astype(jnp.float32) + from_next[0].astype(jnp.float32)
    out[0] = norm_back(key_grad, key_floats, key_scale, key_gain).astype(out.dtype)
    value_grad = own[1] + from_prev[1].astype(jnp.float32) + from_next[1].astype(jnp.float32)
    out[1] = value_grad.astype(out.dtype)


def head_block(rows, first):
    return pl.BlockSpec((rows, HEAD_DIM), lambda head: (0, first + head))


def pair_block(rows):
    return pl.BlockSpec((2, rows, HEAD_DIM), lambda head: (0, 0, head))


def whole_block(shape):
    return pl.BlockSpec(shape, lambda head: (0,) * len(shape))


def main_call(info, query, grad, key, value, pair_prev, pair_next, first, count):
    rows = query.shape[0]
    lanes = count * HEAD_DIM
    return pl.pallas_call(
        main_kernel,
        grid=(count,),
        in_specs=[whole_block(info.shape)]
        + [head_block(rows, first)] * 4
        + [pair_block(rows)] * 2,
        out_specs=[head_block(rows, 0)] + [pair_block(rows)] * 3 + [whole_block((8, HEAD_DIM))],
        out_shape=[
            jax.ShapeDtypeStruct((rows, lanes), jnp.bfloat16),
            jax.ShapeDtypeStruct((2, rows, lanes), jnp.float32),
            jax.ShapeDtypeStruct((2, rows, lanes), jnp.bfloat16),
            jax.ShapeDtypeStruct((2, rows, lanes), jnp.bfloat16),
            jax.ShapeDtypeStruct((8, HEAD_DIM), jnp.float32),
        ],
        compiler_params=pltpu.CompilerParams(vmem_limit_bytes=VMEM_LIMIT),
        cost_estimate=pl.CostEstimate(
            flops=count * 30 * rows * rows * HEAD_DIM,
            bytes_accessed=count * 14 * rows * HEAD_DIM * 2,
            transcendentals=count * 3 * rows * rows,
        ),
    )(info, query, grad, key, value, pair_prev, pair_next)


def finish_call(info, key, own, from_prev, from_next, first, count):
    rows = key.shape[0]
    lanes = count * HEAD_DIM
    return pl.pallas_call(
        finish_kernel,
        grid=(count,),
        in_specs=[whole_block(info.shape), head_block(rows, first)] + [pair_block(rows)] * 3,
        out_specs=pair_block(rows),
        out_shape=jax.ShapeDtypeStruct((2, rows, lanes), jnp.bfloat16),
        compiler_params=pltpu.CompilerParams(vmem_limit_bytes=VMEM_LIMIT),
        cost_estimate=pl.CostEstimate(
            flops=count * 20 * rows * HEAD_DIM,
            bytes_accessed=count * 12 * rows * HEAD_DIM * 2,
            transcendentals=0,
        ),
    )(info, key, own, from_prev, from_next)


def shifted(value, axis, step):
    count = lax.axis_size(axis)
    pairs = [(i, i + step) for i in range(count) if 0 <= i + step < count]
    return lax.ppermute(value, axis, pairs)


def swapped(value):
    count = lax.axis_size("pipe")
    return lax.ppermute(value, "pipe", [(i, (i - 1) % count) for i in range(count)])


def local(queries, keys, values, grad_out, norm_gains, kv_tiles):
    query, key, value, grad = (a[0, 0, 0] for a in (queries, keys, values, grad_out))
    rows = query.shape[0]
    tile = lax.axis_index("seq")
    listed = kv_tiles[0, 0, 0]
    has_prev = (jnp.any(listed == tile - 1) & (tile > 0)).astype(jnp.float32)
    has_next = jnp.any(listed == tile + 1).astype(jnp.float32)
    info = jnp.concatenate(
        [
            jnp.pad(norm_gains[0], ((0, 0), (0, rows - HEAD_DIM))),
            jnp.full((1, rows), has_prev),
            jnp.full((1, rows), has_next),
            jnp.zeros((4, rows), jnp.float32),
        ],
        axis=0,
    )

    def lanes(array, first, count):
        return array[:, first * HEAD_DIM : (first + count) * HEAD_DIM]

    sources = []
    for first, count, away in GROUPS:
        if away:
            moved = swapped(
                jnp.stack([lanes(a, first, count) for a in (query, grad, key, value)])
            )
            sources.append((swapped(info), tuple(moved[i] for i in range(4)), 0, moved[2:]))
        else:
            pair = jnp.stack([lanes(key, first, count), lanes(value, first, count)])
            sources.append((info, (query, grad, key, value), first, pair))
    gathered = [
        (shifted(pair, "seq", 1), shifted(pair, "seq", -1)) for _, _, _, pair in sources
    ]
    gain_sums = [jnp.zeros((2, HEAD_DIM), jnp.float32)] * 2
    query_parts, pair_parts = [], []
    for (first, count, away), (group_info, arrays, offset, _), (prev, following) in zip(
        GROUPS, sources, gathered
    ):
        query_low, own, to_prev, to_next, gain = main_call(
            group_info, *arrays, prev, following, offset, count
        )
        gain_sums[away] = gain_sums[away] + gain[:2]
        from_next = shifted(to_prev, "seq", -1)
        from_prev = shifted(to_next, "seq", 1)
        pair_low = finish_call(group_info, arrays[2], own, from_prev, from_next, offset, count)
        query_parts.append(query_low if away else swapped(query_low))
        pair_parts.append(pair_low if away else swapped(pair_low))
    mine = lax.axis_index("pipe")
    segments = lax.axis_size("pipe")
    here = jnp.arange(segments)[:, None, None] == mine
    contribution = jnp.where(here, gain_sums[0][None], gain_sums[1][None])
    summed = lax.psum(contribution, ("pipe", "seq", "dp"))
    tokens = lax.axis_size("dp") * lax.axis_size("seq") * rows * HEADS
    gain_grads = lax.dynamic_index_in_dim(summed, mine, 0, keepdims=True) / math.sqrt(tokens)
    out = jnp.concatenate(
        [jnp.concatenate(query_parts, axis=-1)[None], jnp.concatenate(pair_parts, axis=-1)], axis=0
    )
    return (out[None, :, None, None], gain_grads)


def solution(mesh):
    placed = (
        P("pipe", "dp", "seq", None, None),
        P("pipe", "dp", "seq", None, None),
        P("pipe", "dp", "seq", None, None),
        P("pipe", "dp", "seq", None, None),
        P("pipe", None, None),
        P("pipe", "dp", "seq", None),
    )
    return jax.shard_map(
        local,
        mesh=mesh,
        in_specs=placed,
        out_specs=(P("pipe", None, "dp", "seq", None, None), P("pipe", None, None)),
        check_vma=False,
    )
```

```python
import functools
import math

import jax
import jax.numpy as jnp
from jax import lax
from jax.experimental import pallas as pl
from jax.experimental.pallas import tpu as pltpu
from jax.sharding import PartitionSpec as P

HEADS = 12
HEAD_DIM = 128
EPSILON = 1e-06
ROOT_SCALE = HEAD_DIM ** (-0.5)
EXP2_SCALE = ROOT_SCALE * math.log2(math.e)
GROUPS = ((0, 4, False), (4, 4, False), (8, 4, True))
VMEM_LIMIT = 48 * 1024 * 1024
COST = pl.CostEstimate(flops=1, bytes_accessed=1, transcendentals=0)


def dot_nt(left, right):
    return lax.dot_general(
        left, right, (((1,), (1,)), ((), ())), preferred_element_type=jnp.float32
    )


def dot_nn(left, right):
    return lax.dot_general(
        left, right, (((1,), (0,)), ((), ())), preferred_element_type=jnp.float32
    )


def dot_tn(left, right):
    return lax.dot_general(
        left, right, (((0,), (0,)), ((), ())), preferred_element_type=jnp.float32
    )


def normalize(source, gain):
    floats = source.astype(jnp.float32)
    scaled = lax.rsqrt(jnp.mean(floats * floats, axis=-1, keepdims=True) + EPSILON)
    normed = floats * scaled
    return floats, scaled, normed, (normed * gain).astype(jnp.bfloat16)


def norm_back(grad_hat, floats, scaled, gain):
    scaled_grad = gain * grad_hat
    projected = jnp.sum(scaled_grad * floats, axis=-1, keepdims=True)
    return scaled * scaled_grad - (scaled**3 * projected * (1.0 / HEAD_DIM)) * floats


def pack_kernel(first_in, second_in, out):
    out[0] = first_in[...]
    out[1] = second_in[...]


def main_kernel(
    info, query, grad, key, value, pair_even, pair_odd,
    query_out, own_out, even_out, odd_out, gain_out,
):
    query_gain = info[0:1, :HEAD_DIM]
    key_gain = info[1:2, :HEAD_DIM]
    query_floats, query_scale, query_normed, query_hat = normalize(query[...], query_gain)
    grad_in = grad[...]
    sides = (
        (key[...], value[...], None),
        (pair_even[0], pair_even[1], info[2:3, :]),
        (pair_odd[0], pair_odd[1], info[3:4, :]),
    )
    parts = []
    totals = None
    for key_in, value_in, live in sides:
        _, _, key_normed, key_hat = normalize(key_in, key_gain)
        weights = jnp.exp2(dot_nt(key_hat, query_hat) * EXP2_SCALE)
        grad_probs = dot_nt(value_in, grad_in)
        weight_sum = jnp.sum(weights, axis=0, keepdims=True)
        cross_sum = jnp.sum(weights * grad_probs, axis=0, keepdims=True)
        if live is not None:
            weight_sum = weight_sum * live
            cross_sum = cross_sum * live
        totals = weight_sum if totals is None else totals + weight_sum
        crosses = cross_sum if live is None else crosses + cross_sum
        parts.append((key_normed, key_hat, weights, grad_probs, live))
    inverse = 1.0 / totals
    deltas = crosses * inverse
    query_grad_t = None
    key_gain_sum = None
    for (key_normed, key_hat, weights, grad_probs, live), out in zip(
        parts, (own_out, even_out, odd_out)
    ):
        probs = weights * (inverse if live is None else inverse * live)
        dscores = (probs * (grad_probs - deltas)).astype(jnp.bfloat16)
        key_part = dot_nn(dscores, query_hat) * ROOT_SCALE
        value_part = dot_nn(probs.astype(jnp.bfloat16), grad_in)
        out[0] = key_part.astype(out.dtype)
        out[1] = value_part.astype(out.dtype)
        gain_part = jnp.sum(key_part * key_normed, axis=0, keepdims=True)
        key_gain_sum = gain_part if key_gain_sum is None else key_gain_sum + gain_part
        query_part = dot_tn(key_hat, dscores)
        query_grad_t = query_part if query_grad_t is None else query_grad_t + query_part
    query_grad = query_grad_t.T * ROOT_SCALE
    query_out[...] = norm_back(query_grad, query_floats, query_scale, query_gain).astype(
        query_out.dtype
    )
    query_gain_sum = jnp.sum(query_grad * query_normed, axis=0, keepdims=True)

    @pl.when(pl.program_id(0) == 0)
    def _():
        gain_out[...] = jnp.zeros_like(gain_out)

    gain_out[0:1, :] += query_gain_sum
    gain_out[1:2, :] += key_gain_sum


def finished(info, key, own, from_even, from_odd):
    key_gain = info[1:2, :HEAD_DIM]
    key_floats, key_scale, _, _ = normalize(key[...], key_gain)
    key_grad = own[0] + from_even[0].astype(jnp.float32) + from_odd[0].astype(jnp.float32)
    value_grad = own[1] + from_even[1].astype(jnp.float32) + from_odd[1].astype(jnp.float32)
    return norm_back(key_grad, key_floats, key_scale, key_gain), value_grad


def finish_kernel(info, key, own, from_even, from_odd, out):
    key_grad, value_grad = finished(info, key, own, from_even, from_odd)
    out[0] = key_grad.astype(out.dtype)
    out[1] = value_grad.astype(out.dtype)


def last_kernel(info, key, own, from_even, from_odd, *rest, places, first, count):
    pieces, (out, held, sems) = rest[: len(places)], rest[len(places) :]
    head = pl.program_id(0)
    copies = [
        pltpu.make_async_copy(
            piece, out.at[planes, :, start : start + piece.shape[-1]], sems.at[slot]
        )
        for slot, (piece, (planes, start)) in enumerate(zip(pieces, places))
    ]

    def head_copy(index):
        start = pl.multiple_of((first + index) * HEAD_DIM, HEAD_DIM)
        return pltpu.make_async_copy(
            held.at[index],
            out.at[pl.ds(1, 2), :, pl.ds(start, HEAD_DIM)],
            sems.at[len(places) + index],
        )

    @pl.when(head == 0)
    def _():
        for copy in copies:
            copy.start()

    key_grad, value_grad = finished(info, key, own, from_even, from_odd)
    held[head, 0] = key_grad.astype(held.dtype)
    held[head, 1] = value_grad.astype(held.dtype)
    head_copy(head).start()

    @pl.when(head == count - 1)
    def _():
        for copy in copies:
            copy.wait()
        for index in range(count):
            head_copy(index).wait()


def head_block(rows, first, slot=None):
    if slot is None:
        return pl.BlockSpec((rows, HEAD_DIM), lambda head: (0, first + head))
    return pl.BlockSpec((None, rows, HEAD_DIM), lambda head: (slot, 0, first + head))


def pair_block(rows):
    return pl.BlockSpec((2, rows, HEAD_DIM), lambda head: (0, 0, head))


def whole_block(shape):
    return pl.BlockSpec(shape, lambda head: (0,) * len(shape))


def pack_call(first_in, second_in, first, count):
    rows = first_in.shape[0]
    return pl.pallas_call(
        pack_kernel,
        grid=(count,),
        in_specs=[head_block(rows, first)] * 2,
        out_specs=pair_block(rows),
        out_shape=jax.ShapeDtypeStruct((2, rows, count * HEAD_DIM), jnp.bfloat16),
        cost_estimate=COST,
    )(first_in, second_in)


def main_call(info, operands, pair_even, pair_odd, count):
    rows = pair_even.shape[1]
    lanes = count * HEAD_DIM
    return pl.pallas_call(
        main_kernel,
        grid=(count,),
        in_specs=[whole_block(info.shape)]
        + [head_block(rows, first, slot) for _, first, slot in operands]
        + [pair_block(rows)] * 2,
        out_specs=[head_block(rows, 0)] + [pair_block(rows)] * 3 + [whole_block((8, HEAD_DIM))],
        out_shape=[
            jax.ShapeDtypeStruct((rows, lanes), jnp.bfloat16),
            jax.ShapeDtypeStruct((2, rows, lanes), jnp.float32),
            jax.ShapeDtypeStruct((2, rows, lanes), jnp.bfloat16),
            jax.ShapeDtypeStruct((2, rows, lanes), jnp.bfloat16),
            jax.ShapeDtypeStruct((8, HEAD_DIM), jnp.float32),
        ],
        compiler_params=pltpu.CompilerParams(vmem_limit_bytes=VMEM_LIMIT),
        cost_estimate=COST,
    )(info, *[array for array, _, _ in operands], pair_even, pair_odd)


def finish_call(info, key, own, from_even, from_odd, count):
    array, first, slot = key
    rows = own.shape[1]
    return pl.pallas_call(
        finish_kernel,
        grid=(count,),
        in_specs=[whole_block(info.shape), head_block(rows, first, slot)] + [pair_block(rows)] * 3,
        out_specs=pair_block(rows),
        out_shape=jax.ShapeDtypeStruct((2, rows, count * HEAD_DIM), jnp.bfloat16),
        compiler_params=pltpu.CompilerParams(vmem_limit_bytes=VMEM_LIMIT),
        cost_estimate=COST,
    )(info, array, own, from_even, from_odd)


def last_call(info, key, own, from_even, from_odd, pieces, places, first, count):
    array, offset, slot = key
    rows = own.shape[1]
    anywhere = pl.BlockSpec(memory_space=pl.ANY)
    return pl.pallas_call(
        functools.partial(last_kernel, places=places, first=first, count=count),
        grid=(count,),
        in_specs=[whole_block(info.shape), head_block(rows, offset, slot)]
        + [pair_block(rows)] * 3
        + [anywhere] * len(pieces),
        out_specs=anywhere,
        out_shape=jax.ShapeDtypeStruct((3, rows, HEADS * HEAD_DIM), jnp.bfloat16),
        scratch_shapes=[
            pltpu.VMEM((count, 2, rows, HEAD_DIM), jnp.bfloat16),
            pltpu.SemaphoreType.DMA((len(pieces) + count,)),
        ],
        compiler_params=pltpu.CompilerParams(vmem_limit_bytes=VMEM_LIMIT),
        cost_estimate=COST,
    )(info, array, own, from_even, from_odd, *pieces)


def partner(tile, parity, count):
    other = tile + 1 if tile % 2 == parity else tile - 1
    return other if 0 <= other < count else tile


def exchanged(value, parity):
    count, width = lax.axis_size("seq"), lax.axis_size("dp")
    pairs = []
    for tile in range(count):
        other = partner(tile, parity, count)
        for sample in range(width):
            moved = sample ^ 1 if other == tile and width % 2 == 0 else sample
            pairs.append((tile * width + sample, other * width + moved))
    return lax.ppermute(value, ("seq", "dp"), pairs)


def total_over(value, axis):
    count = lax.axis_size(axis)
    step = 1
    while step < count:
        value = value + lax.ppermute(value, axis, [(i, i ^ step) for i in range(count)])
        step *= 2
    return value


def turned(value, step):
    count = lax.axis_size("pipe")
    return lax.ppermute(value, "pipe", [(i, (i + step) % count) for i in range(count)])


def listing(listed, tile, seq_count, parity):
    step = jnp.where(tile % 2 == parity, 1, -1)
    other = tile + step
    inside = (other >= 0) & (other < seq_count)
    return (inside & jnp.any(listed == other)).astype(jnp.float32)


def local(queries, keys, values, grad_out, norm_gains, kv_tiles):
    query, key, value, grad = (a[0, 0, 0] for a in (queries, keys, values, grad_out))
    rows = query.shape[0]
    tile = lax.axis_index("seq")
    seq_count = lax.axis_size("seq")
    listed = kv_tiles[0, 0, 0]
    info = jnp.concatenate(
        [
            jnp.pad(norm_gains[0], ((0, 0), (0, rows - HEAD_DIM))),
            jnp.full((1, rows), listing(listed, tile, seq_count, 0)),
            jnp.full((1, rows), listing(listed, tile, seq_count, 1)),
            jnp.zeros((4, rows), jnp.float32),
        ],
        axis=0,
    )
    sources = []
    for first, count, away in GROUPS:
        pair = pack_call(key, value, first, count)
        if away:
            pair = turned(pair, -1)
            asked = turned(pack_call(query, grad, first, count), -1)
            operands = ((asked, 0, 0), (asked, 0, 1), (pair, 0, 0), (pair, 0, 1))
            sources.append((turned(info, -1), operands, pair))
        else:
            operands = tuple((a, first, None) for a in (query, grad, key, value))
            sources.append((info, operands, pair))
    gathered = [(exchanged(pair, 0), exchanged(pair, 1)) for _, _, pair in sources]
    gain_sums = [jnp.zeros((2, HEAD_DIM), jnp.float32)] * 2
    pieces, places = [], []
    out = None
    for (first, count, away), (group_info, operands, _), (even, odd) in zip(
        GROUPS, sources, gathered
    ):
        query_low, own, to_even, to_odd, gain = main_call(
            group_info, operands, even, odd, count
        )
        gain_sums[away] = gain_sums[away] + gain[:2]
        from_even = exchanged(to_even, 0)
        from_odd = exchanged(to_odd, 1)
        last = (first, count, away) == GROUPS[-1]
        pieces.append(query_low if away else turned(query_low, -1))
        places.append((0, first * HEAD_DIM))
        if last:
            out = last_call(
                group_info, operands[2], own, from_even, from_odd, pieces, tuple(places), first, count
            )
        else:
            pair_low = finish_call(group_info, operands[2], own, from_even, from_odd, count)
            pieces.append(pair_low if away else turned(pair_low, -1))
            places.append((slice(1, 3), first * HEAD_DIM))
    summed = gain_sums[0] + turned(gain_sums[1], 1)
    for axis in ("seq", "dp"):
        summed = total_over(summed, axis)
    tokens = lax.axis_size("dp") * seq_count * rows * HEADS
    return (out[None, :, None, None], (summed / math.sqrt(tokens))[None])


def solution(mesh):
    placed = (
        P("pipe", "dp", "seq", None, None),
        P("pipe", "dp", "seq", None, None),
        P("pipe", "dp", "seq", None, None),
        P("pipe", "dp", "seq", None, None),
        P("pipe", None, None),
        P("pipe", "dp", "seq", None),
    )
    return jax.shard_map(
        local,
        mesh=mesh,
        in_specs=placed,
        out_specs=(P("pipe", None, "dp", "seq", None, None), P("pipe", None, None)),
        check_vma=False,
    )
```

```python
import functools
import math

import jax
import jax.numpy as jnp
from jax import lax
from jax.experimental import pallas as pl
from jax.experimental.pallas import tpu as pltpu
from jax.sharding import PartitionSpec as P

HEADS = 12
HEAD_DIM = 128
EPSILON = 1e-06
ROOT_SCALE = HEAD_DIM ** (-0.5)
EXP2_SCALE = ROOT_SCALE * math.log2(math.e)
GROUPS = ((0, 4, False), (4, 4, False), (8, 4, True))
MAIN_VMEM = 20 * 1024 * 1024
SMALL_VMEM = 12 * 1024 * 1024
PACK_VMEM = 4 * 1024 * 1024
COST = pl.CostEstimate(flops=1, bytes_accessed=1, transcendentals=0)
MAIN_COST = pl.CostEstimate(flops=6 * 10**9, bytes_accessed=1, transcendentals=0)


def dot_nt(left, right):
    return lax.dot_general(
        left, right, (((1,), (1,)), ((), ())), preferred_element_type=jnp.float32
    )


def dot_nn(left, right):
    return lax.dot_general(
        left, right, (((1,), (0,)), ((), ())), preferred_element_type=jnp.float32
    )


def dot_tn(left, right):
    return lax.dot_general(
        left, right, (((0,), (0,)), ((), ())), preferred_element_type=jnp.float32
    )


def normalize(source, gain):
    floats = source.astype(jnp.float32)
    scaled = lax.rsqrt(jnp.mean(floats * floats, axis=-1, keepdims=True) + EPSILON)
    normed = floats * scaled
    return floats, scaled, normed, (normed * gain).astype(jnp.bfloat16)


def norm_back(grad_hat, floats, scaled, gain):
    scaled_grad = gain * grad_hat
    projected = jnp.sum(scaled_grad * floats, axis=-1, keepdims=True)
    return scaled * scaled_grad - (scaled**3 * projected * (1.0 / HEAD_DIM)) * floats


def pack_kernel(first_in, second_in, out, sems, *, start, width):
    rows = first_in.shape[0]
    copies = [
        pltpu.make_async_copy(
            source.at[:, start : start + width], out.at[slot, :rows], sems.at[slot]
        )
        for slot, source in enumerate((first_in, second_in))
    ]
    for copy in copies:
        copy.start()
    for copy in copies:
        copy.wait()


def info_kernel(listed, gains, info):
    tile = lax.axis_index("seq")
    last = lax.axis_size("seq") - 1
    info[...] = jnp.zeros_like(info)
    info[0:2, :] = gains[...]
    for parity in range(2):
        other = jnp.where(lax.rem(tile, 2) == parity, tile + 1, tile - 1)
        found = listed[0] == other
        for slot in range(1, listed.shape[0]):
            found = found | (listed[slot] == other)
        found = found & (other >= 0) & (other <= last)
        live = jnp.where(found, 1.0, 0.0)
        info[2 + parity : 3 + parity, :] = jnp.full((1, HEAD_DIM), live, jnp.float32)


def ask_kernel(info, query, grad, out, sems, *, start, width):
    rows = query.shape[0]
    value = info[...]
    planes = []
    for _ in range(3):
        low = value.astype(jnp.bfloat16)
        planes.append(low)
        value = value - low.astype(jnp.float32)
    planes.append(jnp.zeros_like(planes[0]))
    out[0, rows : rows + 16, :HEAD_DIM] = jnp.concatenate(planes[:2], axis=0)
    out[1, rows : rows + 16, :HEAD_DIM] = jnp.concatenate(planes[2:], axis=0)
    pack_kernel(query, grad, out, sems, start=start, width=width)


def told_info(told):
    floats = told[...].astype(jnp.float32)
    return floats[0, 0:8] + floats[0, 8:16] + floats[1, 0:8]


def main_kernel(
    info, query, grad, key, value, pair_even, pair_odd, *rest
):
    query_out, own_out, even_out, odd_out, gain_out = rest[-5:]
    told = told_info(info) if len(info.shape) == 3 else info[...]
    query_gain = told[0:1]
    key_gain = told[1:2]
    rows = query.shape[0]
    lives = [jnp.concatenate([told[row : row + 1]] * (rows // HEAD_DIM), axis=1) for row in (2, 3)]
    query_floats, query_scale, query_normed, query_hat = normalize(query[...], query_gain)
    grad_in = grad[...]
    sides = (
        (key[...], value[...], None),
        (pair_even[0], pair_even[1], lives[0]),
        (pair_odd[0], pair_odd[1], lives[1]),
    )
    parts = []
    totals = None
    for key_in, value_in, live in sides:
        _, _, key_normed, key_hat = normalize(key_in, key_gain)
        weights = jnp.exp2(dot_nt(key_hat, query_hat) * EXP2_SCALE)
        grad_probs = dot_nt(value_in, grad_in)
        weight_sum = jnp.sum(weights, axis=0, keepdims=True)
        cross_sum = jnp.sum(weights * grad_probs, axis=0, keepdims=True)
        if live is not None:
            weight_sum = weight_sum * live
            cross_sum = cross_sum * live
        totals = weight_sum if totals is None else totals + weight_sum
        crosses = cross_sum if live is None else crosses + cross_sum
        parts.append((key_normed, key_hat, weights, grad_probs, live))
    inverse = 1.0 / totals
    deltas = crosses * inverse
    query_grad_t = None
    key_gain_sum = None
    for (key_normed, key_hat, weights, grad_probs, live), out in zip(
        parts, (own_out, even_out, odd_out)
    ):
        probs = weights * (inverse if live is None else inverse * live)
        dscores = (probs * (grad_probs - deltas)).astype(jnp.bfloat16)
        key_part = dot_nn(dscores, query_hat) * ROOT_SCALE
        value_part = dot_nn(probs.astype(jnp.bfloat16), grad_in)
        out[0] = key_part.astype(out.dtype)
        out[1] = value_part.astype(out.dtype)
        gain_part = jnp.sum(key_part * key_normed, axis=0, keepdims=True)
        key_gain_sum = gain_part if key_gain_sum is None else key_gain_sum + gain_part
        query_part = dot_tn(key_hat, dscores)
        query_grad_t = query_part if query_grad_t is None else query_grad_t + query_part
    query_grad = query_grad_t.T * ROOT_SCALE
    query_out[...] = norm_back(query_grad, query_floats, query_scale, query_gain).astype(
        query_out.dtype
    )
    query_gain_sum = jnp.sum(query_grad * query_normed, axis=0, keepdims=True)

    @pl.when(pl.program_id(0) == 0)
    def _():
        gain_out[...] = jnp.zeros_like(gain_out)

    gain_out[0:1, :] += query_gain_sum
    gain_out[1:2, :] += key_gain_sum


def finished(info, key, own, from_even, from_odd):
    told = told_info(info) if len(info.shape) == 3 else info[...]
    key_gain = told[1:2]
    key_floats, key_scale, _, _ = normalize(key[...], key_gain)
    key_grad = own[0] + from_even[0].astype(jnp.float32) + from_odd[0].astype(jnp.float32)
    value_grad = own[1] + from_even[1].astype(jnp.float32) + from_odd[1].astype(jnp.float32)
    return norm_back(key_grad, key_floats, key_scale, key_gain), value_grad


def finish_kernel(info, key, own, from_even, from_odd, out):
    key_grad, value_grad = finished(info, key, own, from_even, from_odd)
    out[0] = key_grad.astype(out.dtype)
    out[1] = value_grad.astype(out.dtype)


def last_kernel(info, key, own, from_even, from_odd, *rest, places, first, count):
    amount = len(places)
    pieces, (out, held) = rest[:amount], rest[amount : amount + 2]
    staged, (load_sems, store_sems) = rest[amount + 2 : -2], rest[-2:]
    head = pl.program_id(0)
    loads = [
        pltpu.make_async_copy(piece, stage, load_sems.at[slot])
        for slot, (piece, stage) in enumerate(zip(pieces, staged))
    ]
    stores = [
        pltpu.make_async_copy(
            stage, out.at[planes, :, start : start + stage.shape[-1]], store_sems.at[slot]
        )
        for slot, (stage, (planes, start)) in enumerate(zip(staged, places))
    ]

    def head_copy(index):
        start = pl.multiple_of((first + index) * HEAD_DIM, HEAD_DIM)
        return pltpu.make_async_copy(
            held.at[index],
            out.at[pl.ds(1, 2), :, pl.ds(start, HEAD_DIM)],
            store_sems.at[amount + index],
        )

    @pl.when(head == 0)
    def _():
        for load in loads:
            load.start()

    @pl.when(head == min(1, count - 1))
    def _():
        for load, store in zip(loads, stores):
            load.wait()
            store.start()

    key_grad, value_grad = finished(info, key, own, from_even, from_odd)
    held[head, 0] = key_grad.astype(held.dtype)
    held[head, 1] = value_grad.astype(held.dtype)
    head_copy(head).start()

    @pl.when(head == count - 1)
    def _():
        for store in stores:
            store.wait()
        for index in range(count):
            head_copy(index).wait()


def head_block(rows, first, slot=None):
    if slot is None:
        return pl.BlockSpec((rows, HEAD_DIM), lambda head: (0, first + head))
    return pl.BlockSpec((None, rows, HEAD_DIM), lambda head: (slot, 0, first + head))


def pair_block(rows, first=0):
    return pl.BlockSpec((2, rows, HEAD_DIM), lambda head: (0, 0, first + head))


def whole_block(shape):
    return pl.BlockSpec(shape, lambda head: (0,) * len(shape))


def pack_params():
    return dict(
        scratch_shapes=[pltpu.SemaphoreType.DMA((2,))],
        compiler_params=pltpu.CompilerParams(vmem_limit_bytes=PACK_VMEM),
        cost_estimate=COST,
    )


def pack_call(first_in, second_in, first, count):
    rows = first_in.shape[0]
    width = count * HEAD_DIM
    return pl.pallas_call(
        functools.partial(pack_kernel, start=first * HEAD_DIM, width=width),
        grid=(1,),
        in_specs=[pl.BlockSpec(memory_space=pl.ANY)] * 2,
        out_specs=whole_block((2, rows, width)),
        out_shape=jax.ShapeDtypeStruct((2, rows, width), jnp.bfloat16),
        **pack_params(),
    )(first_in, second_in)


def ask_call(info, query, grad, first, count):
    rows = query.shape[0]
    width = count * HEAD_DIM
    return pl.pallas_call(
        functools.partial(ask_kernel, start=first * HEAD_DIM, width=width),
        grid=(1,),
        in_specs=[whole_block(info.shape)] + [pl.BlockSpec(memory_space=pl.ANY)] * 2,
        out_specs=whole_block((2, rows + 16, width)),
        out_shape=jax.ShapeDtypeStruct((2, rows + 16, width), jnp.bfloat16),
        **pack_params(),
    )(info, query, grad)


def info_call(listed, gains):
    return pl.pallas_call(
        info_kernel,
        in_specs=[pl.BlockSpec(memory_space=pltpu.SMEM), pl.BlockSpec(memory_space=pltpu.VMEM)],
        out_specs=pl.BlockSpec(memory_space=pltpu.VMEM),
        out_shape=jax.ShapeDtypeStruct((8, HEAD_DIM), jnp.float32),
        compiler_params=pltpu.CompilerParams(vmem_limit_bytes=PACK_VMEM),
        cost_estimate=COST,
    )(listed, gains)


def info_block(info):
    if info.ndim == 2:
        return whole_block(info.shape)
    below = info.shape[1] // 16 - 1
    return pl.BlockSpec((2, 16, HEAD_DIM), lambda head: (0, below, 0))


def main_call(
    info, operands, pair_even, pair_odd, pair_first, count, query_grads, query_heads, query_first
):
    rows = pair_even.shape[1]
    lanes = count * HEAD_DIM
    earlier = [] if query_grads is None else [query_grads]
    return pl.pallas_call(
        main_kernel,
        grid=(count,),
        in_specs=[info_block(info)]
        + [head_block(rows, first, slot) for _, first, slot in operands]
        + [pair_block(rows, pair_first)] * 2
        + [pl.BlockSpec(memory_space=pl.ANY)] * len(earlier),
        out_specs=[head_block(rows, query_first)]
        + [pair_block(rows)] * 3
        + [whole_block((8, HEAD_DIM))],
        out_shape=[
            jax.ShapeDtypeStruct((rows, query_heads * HEAD_DIM), jnp.bfloat16),
            jax.ShapeDtypeStruct((2, rows, lanes), jnp.float32),
            jax.ShapeDtypeStruct((2, rows, lanes), jnp.bfloat16),
            jax.ShapeDtypeStruct((2, rows, lanes), jnp.bfloat16),
            jax.ShapeDtypeStruct((8, HEAD_DIM), jnp.float32),
        ],
        input_output_aliases={7: 0} if earlier else {},
        compiler_params=pltpu.CompilerParams(vmem_limit_bytes=MAIN_VMEM),
        cost_estimate=MAIN_COST,
    )(info, *[array for array, _, _ in operands], pair_even, pair_odd, *earlier)


def finish_call(info, key, own, from_even, from_odd, count):
    array, first, slot = key
    rows = own.shape[1]
    return pl.pallas_call(
        finish_kernel,
        grid=(count,),
        in_specs=[info_block(info), head_block(rows, first, slot)] + [pair_block(rows)] * 3,
        out_specs=pair_block(rows),
        out_shape=jax.ShapeDtypeStruct((2, rows, count * HEAD_DIM), jnp.bfloat16),
        compiler_params=pltpu.CompilerParams(vmem_limit_bytes=SMALL_VMEM),
        cost_estimate=COST,
    )(info, array, own, from_even, from_odd)


def last_call(info, key, own, from_even, from_odd, pieces, places, first, count):
    array, offset, slot = key
    rows = own.shape[1]
    anywhere = pl.BlockSpec(memory_space=pl.ANY)
    return pl.pallas_call(
        functools.partial(last_kernel, places=places, first=first, count=count),
        grid=(count,),
        in_specs=[info_block(info), head_block(rows, offset, slot)]
        + [pair_block(rows)] * 3
        + [anywhere] * len(pieces),
        out_specs=anywhere,
        out_shape=jax.ShapeDtypeStruct((3, rows, HEADS * HEAD_DIM), jnp.bfloat16),
        scratch_shapes=[
            pltpu.VMEM((count, 2, rows, HEAD_DIM), jnp.bfloat16),
            *[pltpu.VMEM(piece.shape, piece.dtype) for piece in pieces],
            pltpu.SemaphoreType.DMA((len(pieces),)),
            pltpu.SemaphoreType.DMA((len(pieces) + count,)),
        ],
        compiler_params=pltpu.CompilerParams(vmem_limit_bytes=SMALL_VMEM),
        cost_estimate=COST,
    )(info, array, own, from_even, from_odd, *pieces)


def partner(tile, parity, count):
    other = tile + 1 if tile % 2 == parity else tile - 1
    return other if 0 <= other < count else tile


def exchanged(value, parity):
    count, width = lax.axis_size("seq"), lax.axis_size("dp")
    pairs = []
    for tile in range(count):
        other = partner(tile, parity, count)
        for sample in range(width):
            moved = sample ^ 1 if other == tile and width % 2 == 0 else sample
            pairs.append((tile * width + sample, other * width + moved))
    return lax.ppermute(value, ("seq", "dp"), pairs)


def after(value, *others):
    return lax.optimization_barrier((value, *others))[0]


def turned(value, step):
    count = lax.axis_size("pipe")
    return lax.ppermute(value, "pipe", [(i, (i + step) % count) for i in range(count)])


def total_over(value, axis):
    count = lax.axis_size(axis)
    step = 1
    while step < count:
        value = value + lax.ppermute(value, axis, [(i, i ^ step) for i in range(count)])
        step *= 2
    return value


def local(queries, keys, values, grad_out, norm_gains, kv_tiles):
    query, key, value, grad = (a[0, 0, 0] for a in (queries, keys, values, grad_out))
    rows = query.shape[0]
    seq_count = lax.axis_size("seq")
    home_heads = sum(count for _, count, away in GROUPS if not away)
    home_pair = pack_call(key, value, 0, home_heads)
    away_pair = pack_call(after(key, home_pair), value, home_heads, HEADS - home_heads)
    home_gathered = (exchanged(home_pair, 0), exchanged(home_pair, 1))
    info = info_call(kv_tiles[0, 0, 0], after(norm_gains[0], away_pair))
    away_pair = turned(away_pair, -1)
    asked = ask_call(info, after(query, away_pair), grad, home_heads, HEADS - home_heads)
    asked = turned(asked, -1)
    away_gathered = (exchanged(away_pair, 0), exchanged(away_pair, 1))
    sources, parts, sums = [], [], []
    query_grads = None
    for first, count, away in GROUPS:
        if away:
            asked = after(asked, query_grads)
            operands = [(asked, 0, 0), (asked, 0, 1), (away_pair, 0, 0), (away_pair, 0, 1)]
            sources.append((asked, operands))
            query_low, own, to_even, to_odd, gain = main_call(
                *sources[-1], *away_gathered, 0, count, None, count, 0
            )
            sums.append(turned(gain[:2], 1))
        else:
            sources.append((info, [(a, first, None) for a in (query, grad, key, value)]))
            query_grads, own, to_even, to_odd, gain = main_call(
                *sources[-1], *home_gathered, first, count, query_grads, home_heads, first
            )
            sums.append(gain[:2])
        parts.append((own, exchanged(to_even, 0), exchanged(to_odd, 1)))
    query_grads = turned(query_grads, -1)
    pieces = [query_grads, query_low]
    places = [(0, 0), (0, home_heads * HEAD_DIM)]
    for index, ((first, count, away), (group_info, operands), part) in enumerate(
        zip(GROUPS, sources, parts)
    ):
        own, from_even, from_odd = part
        if away:
            out = last_call(
                group_info, operands[2], own, from_even, from_odd, pieces, tuple(places), first, count
            )
        else:
            own = after(own, query_grads, *(sums[-1:] if index == 0 else ()))
            pair_low = finish_call(group_info, operands[2], own, from_even, from_odd, count)
            pieces.append(turned(pair_low, -1))
            places.append((slice(1, 3), first * HEAD_DIM))
    summed = total_over(total_over(sum(sums), "dp"), "seq")
    tokens = lax.axis_size("dp") * seq_count * rows * HEADS
    return (out[None, :, None, None], (summed / math.sqrt(tokens))[None])


def solution(mesh):
    placed = (
        P("pipe", "dp", "seq", None, None),
        P("pipe", "dp", "seq", None, None),
        P("pipe", "dp", "seq", None, None),
        P("pipe", "dp", "seq", None, None),
        P("pipe", None, None),
        P("pipe", "dp", "seq", None),
    )
    return jax.shard_map(
        local,
        mesh=mesh,
        in_specs=placed,
        out_specs=(P("pipe", None, "dp", "seq", None, None), P("pipe", None, None)),
        check_vma=False,
    )
```

```python
import functools
import math

import jax
import jax.numpy as jnp
from jax import lax
from jax.experimental import pallas as pl
from jax.experimental.pallas import tpu as pltpu
from jax.sharding import PartitionSpec as P

HEADS = 12
HEAD_DIM = 128
EPSILON = 1e-06
ROOT_SCALE = HEAD_DIM ** (-0.5)
EXP2_SCALE = ROOT_SCALE * math.log2(math.e)
GROUPS = ((0, 4, False), (4, 3, False), (7, 5, True))
MAIN_VMEM = 20 * 1024 * 1024
SMALL_VMEM = 12 * 1024 * 1024
PACK_VMEM = 4 * 1024 * 1024
COST = pl.CostEstimate(flops=1, bytes_accessed=1, transcendentals=0)
MAIN_COST = pl.CostEstimate(flops=6 * 10**9, bytes_accessed=1, transcendentals=0)


def dot_nt(left, right):
    return lax.dot_general(
        left, right, (((1,), (1,)), ((), ())), preferred_element_type=jnp.float32
    )


def dot_nn(left, right):
    return lax.dot_general(
        left, right, (((1,), (0,)), ((), ())), preferred_element_type=jnp.float32
    )


def dot_tn(left, right):
    return lax.dot_general(
        left, right, (((0,), (0,)), ((), ())), preferred_element_type=jnp.float32
    )


def normalize(source, gain):
    floats = source.astype(jnp.float32)
    scaled = lax.rsqrt(jnp.mean(floats * floats, axis=-1, keepdims=True) + EPSILON)
    normed = floats * scaled
    return floats, scaled, normed, (normed * gain).astype(jnp.bfloat16)


def norm_back(grad_hat, floats, scaled, gain):
    scaled_grad = gain * grad_hat
    projected = jnp.sum(scaled_grad * floats, axis=-1, keepdims=True)
    return scaled * scaled_grad - (scaled**3 * projected * (1.0 / HEAD_DIM)) * floats


def pack_kernel(first_in, second_in, out, sems, *, start, width):
    rows = first_in.shape[0]
    copies = [
        pltpu.make_async_copy(
            source.at[:, start : start + width], out.at[slot, :rows], sems.at[slot]
        )
        for slot, source in enumerate((first_in, second_in))
    ]
    for copy in copies:
        copy.start()
    for copy in copies:
        copy.wait()


def info_kernel(listed, gains, info):
    tile = lax.axis_index("seq")
    last = lax.axis_size("seq") - 1
    info[...] = jnp.zeros_like(info)
    info[0:2, :] = gains[...]
    for parity in range(2):
        other = jnp.where(lax.rem(tile, 2) == parity, tile + 1, tile - 1)
        found = listed[0] == other
        for slot in range(1, listed.shape[0]):
            found = found | (listed[slot] == other)
        found = found & (other >= 0) & (other <= last)
        live = jnp.where(found, 1.0, 0.0)
        info[2 + parity : 3 + parity, :] = jnp.full((1, HEAD_DIM), live, jnp.float32)


def ask_kernel(info, query, grad, out, sems, *, start, width):
    rows = query.shape[0]
    value = info[...]
    planes = []
    for _ in range(3):
        low = value.astype(jnp.bfloat16)
        planes.append(low)
        value = value - low.astype(jnp.float32)
    planes.append(jnp.zeros_like(planes[0]))
    out[0, rows : rows + 16, :HEAD_DIM] = jnp.concatenate(planes[:2], axis=0)
    out[1, rows : rows + 16, :HEAD_DIM] = jnp.concatenate(planes[2:], axis=0)
    pack_kernel(query, grad, out, sems, start=start, width=width)


def told_info(told):
    floats = told[...].astype(jnp.float32)
    return floats[0, 0:8] + floats[0, 8:16] + floats[1, 0:8]


def main_kernel(
    info, query, grad, key, value, pair_even, pair_odd, *rest
):
    query_out, own_out, even_out, odd_out, gain_out = rest[-5:]
    told = told_info(info) if len(info.shape) == 3 else info[...]
    query_gain = told[0:1]
    key_gain = told[1:2]
    rows = query.shape[0]
    lives = [jnp.concatenate([told[row : row + 1]] * (rows // HEAD_DIM), axis=1) for row in (2, 3)]
    query_floats, query_scale, query_normed, query_hat = normalize(query[...], query_gain)
    grad_in = grad[...]
    sides = (
        (key[...], value[...], None),
        (pair_even[0], pair_even[1], lives[0]),
        (pair_odd[0], pair_odd[1], lives[1]),
    )
    parts = []
    totals = None
    for key_in, value_in, live in sides:
        _, _, key_normed, key_hat = normalize(key_in, key_gain)
        weights = jnp.exp2(dot_nt(key_hat, query_hat) * EXP2_SCALE)
        grad_probs = dot_nt(value_in, grad_in)
        weight_sum = jnp.sum(weights, axis=0, keepdims=True)
        cross_sum = jnp.sum(weights * grad_probs, axis=0, keepdims=True)
        if live is not None:
            weight_sum = weight_sum * live
            cross_sum = cross_sum * live
        totals = weight_sum if totals is None else totals + weight_sum
        crosses = cross_sum if live is None else crosses + cross_sum
        parts.append((key_normed, key_hat, weights, grad_probs, live))
    inverse = 1.0 / totals
    deltas = crosses * inverse
    query_grad_t = None
    key_gain_sum = None
    for (key_normed, key_hat, weights, grad_probs, live), out in zip(
        parts, (own_out, even_out, odd_out)
    ):
        probs = weights * (inverse if live is None else inverse * live)
        dscores = (probs * (grad_probs - deltas)).astype(jnp.bfloat16)
        key_part = dot_nn(dscores, query_hat) * ROOT_SCALE
        value_part = dot_nn(probs.astype(jnp.bfloat16), grad_in)
        out[0] = key_part.astype(out.dtype)
        out[1] = value_part.astype(out.dtype)
        gain_part = jnp.sum(key_part * key_normed, axis=0, keepdims=True)
        key_gain_sum = gain_part if key_gain_sum is None else key_gain_sum + gain_part
        query_part = dot_tn(key_hat, dscores)
        query_grad_t = query_part if query_grad_t is None else query_grad_t + query_part
    query_grad = query_grad_t.T * ROOT_SCALE
    query_out[...] = norm_back(query_grad, query_floats, query_scale, query_gain).astype(
        query_out.dtype
    )
    query_gain_sum = jnp.sum(query_grad * query_normed, axis=0, keepdims=True)

    @pl.when(pl.program_id(0) == 0)
    def _():
        gain_out[...] = jnp.zeros_like(gain_out)

    gain_out[0:1, :] += query_gain_sum
    gain_out[1:2, :] += key_gain_sum


def finished(info, key, own, from_even, from_odd):
    told = told_info(info) if len(info.shape) == 3 else info[...]
    key_gain = told[1:2]
    key_floats, key_scale, _, _ = normalize(key[...], key_gain)
    key_grad = own[0] + from_even[0].astype(jnp.float32) + from_odd[0].astype(jnp.float32)
    value_grad = own[1] + from_even[1].astype(jnp.float32) + from_odd[1].astype(jnp.float32)
    return norm_back(key_grad, key_floats, key_scale, key_gain), value_grad


def finish_kernel(info, key, own, from_even, from_odd, out):
    key_grad, value_grad = finished(info, key, own, from_even, from_odd)
    out[0] = key_grad.astype(out.dtype)
    out[1] = value_grad.astype(out.dtype)


def last_kernel(info, key, own, from_even, from_odd, *rest, places, first, count):
    amount = len(places)
    pieces, (out, held) = rest[:amount], rest[amount : amount + 2]
    staged, (load_sems, store_sems) = rest[amount + 2 : -2], rest[-2:]
    head = pl.program_id(0)
    loads = [
        pltpu.make_async_copy(piece, stage, load_sems.at[slot])
        for slot, (piece, stage) in enumerate(zip(pieces, staged))
    ]
    stores = [
        pltpu.make_async_copy(
            stage, out.at[planes, :, start : start + stage.shape[-1]], store_sems.at[slot]
        )
        for slot, (stage, (planes, start)) in enumerate(zip(staged, places))
    ]

    def head_copy(index):
        start = pl.multiple_of((first + index) * HEAD_DIM, HEAD_DIM)
        return pltpu.make_async_copy(
            held.at[index],
            out.at[pl.ds(1, 2), :, pl.ds(start, HEAD_DIM)],
            store_sems.at[amount + index],
        )

    @pl.when(head == 0)
    def _():
        for load in loads:
            load.start()

    @pl.when(head == min(1, count - 1))
    def _():
        for load, store in zip(loads, stores):
            load.wait()
            store.start()

    key_grad, value_grad = finished(info, key, own, from_even, from_odd)
    held[head, 0] = key_grad.astype(held.dtype)
    held[head, 1] = value_grad.astype(held.dtype)
    head_copy(head).start()

    @pl.when(head == count - 1)
    def _():
        for store in stores:
            store.wait()
        for index in range(count):
            head_copy(index).wait()


def head_block(rows, first, slot=None):
    if slot is None:
        return pl.BlockSpec((rows, HEAD_DIM), lambda head: (0, first + head))
    return pl.BlockSpec((None, rows, HEAD_DIM), lambda head: (slot, 0, first + head))


def pair_block(rows, first=0):
    return pl.BlockSpec((2, rows, HEAD_DIM), lambda head: (0, 0, first + head))


def whole_block(shape):
    return pl.BlockSpec(shape, lambda head: (0,) * len(shape))


def pack_params():
    return dict(
        scratch_shapes=[pltpu.SemaphoreType.DMA((2,))],
        compiler_params=pltpu.CompilerParams(vmem_limit_bytes=PACK_VMEM),
        cost_estimate=COST,
    )


def pack_call(first_in, second_in, first, count):
    rows = first_in.shape[0]
    width = count * HEAD_DIM
    return pl.pallas_call(
        functools.partial(pack_kernel, start=first * HEAD_DIM, width=width),
        grid=(1,),
        in_specs=[pl.BlockSpec(memory_space=pl.ANY)] * 2,
        out_specs=whole_block((2, rows, width)),
        out_shape=jax.ShapeDtypeStruct((2, rows, width), jnp.bfloat16),
        **pack_params(),
    )(first_in, second_in)


def ask_call(info, query, grad, first, count):
    rows = query.shape[0]
    width = count * HEAD_DIM
    return pl.pallas_call(
        functools.partial(ask_kernel, start=first * HEAD_DIM, width=width),
        grid=(1,),
        in_specs=[whole_block(info.shape)] + [pl.BlockSpec(memory_space=pl.ANY)] * 2,
        out_specs=whole_block((2, rows + 16, width)),
        out_shape=jax.ShapeDtypeStruct((2, rows + 16, width), jnp.bfloat16),
        **pack_params(),
    )(info, query, grad)


def info_call(listed, gains):
    return pl.pallas_call(
        info_kernel,
        in_specs=[pl.BlockSpec(memory_space=pltpu.SMEM), pl.BlockSpec(memory_space=pltpu.VMEM)],
        out_specs=pl.BlockSpec(memory_space=pltpu.VMEM),
        out_shape=jax.ShapeDtypeStruct((8, HEAD_DIM), jnp.float32),
        compiler_params=pltpu.CompilerParams(vmem_limit_bytes=PACK_VMEM),
        cost_estimate=COST,
    )(listed, gains)


def info_block(info):
    if info.ndim == 2:
        return whole_block(info.shape)
    below = info.shape[1] // 16 - 1
    return pl.BlockSpec((2, 16, HEAD_DIM), lambda head: (0, below, 0))


def main_call(
    info, operands, pair_even, pair_odd, pair_first, count, query_grads, query_heads, query_first
):
    rows = pair_even.shape[1]
    lanes = count * HEAD_DIM
    earlier = [] if query_grads is None else [query_grads]
    return pl.pallas_call(
        main_kernel,
        grid=(count,),
        in_specs=[info_block(info)]
        + [head_block(rows, first, slot) for _, first, slot in operands]
        + [pair_block(rows, pair_first)] * 2
        + [pl.BlockSpec(memory_space=pl.ANY)] * len(earlier),
        out_specs=[head_block(rows, query_first)]
        + [pair_block(rows)] * 3
        + [whole_block((8, HEAD_DIM))],
        out_shape=[
            jax.ShapeDtypeStruct((rows, query_heads * HEAD_DIM), jnp.bfloat16),
            jax.ShapeDtypeStruct((2, rows, lanes), jnp.float32),
            jax.ShapeDtypeStruct((2, rows, lanes), jnp.bfloat16),
            jax.ShapeDtypeStruct((2, rows, lanes), jnp.bfloat16),
            jax.ShapeDtypeStruct((8, HEAD_DIM), jnp.float32),
        ],
        input_output_aliases={7: 0} if earlier else {},
        compiler_params=pltpu.CompilerParams(vmem_limit_bytes=MAIN_VMEM),
        cost_estimate=MAIN_COST,
    )(info, *[array for array, _, _ in operands], pair_even, pair_odd, *earlier)


def finish_call(info, key, own, from_even, from_odd, count):
    array, first, slot = key
    rows = own.shape[1]
    return pl.pallas_call(
        finish_kernel,
        grid=(count,),
        in_specs=[info_block(info), head_block(rows, first, slot)] + [pair_block(rows)] * 3,
        out_specs=pair_block(rows),
        out_shape=jax.ShapeDtypeStruct((2, rows, count * HEAD_DIM), jnp.bfloat16),
        compiler_params=pltpu.CompilerParams(vmem_limit_bytes=SMALL_VMEM),
        cost_estimate=COST,
    )(info, array, own, from_even, from_odd)


def last_call(info, key, own, from_even, from_odd, pieces, places, first, count):
    array, offset, slot = key
    rows = own.shape[1]
    anywhere = pl.BlockSpec(memory_space=pl.ANY)
    return pl.pallas_call(
        functools.partial(last_kernel, places=places, first=first, count=count),
        grid=(count,),
        in_specs=[info_block(info), head_block(rows, offset, slot)]
        + [pair_block(rows)] * 3
        + [anywhere] * len(pieces),
        out_specs=anywhere,
        out_shape=jax.ShapeDtypeStruct((3, rows, HEADS * HEAD_DIM), jnp.bfloat16),
        scratch_shapes=[
            pltpu.VMEM((count, 2, rows, HEAD_DIM), jnp.bfloat16),
            *[pltpu.VMEM(piece.shape, piece.dtype) for piece in pieces],
            pltpu.SemaphoreType.DMA((len(pieces),)),
            pltpu.SemaphoreType.DMA((len(pieces) + count,)),
        ],
        compiler_params=pltpu.CompilerParams(vmem_limit_bytes=SMALL_VMEM),
        cost_estimate=COST,
    )(info, array, own, from_even, from_odd, *pieces)


def partner(tile, parity, count):
    other = tile + 1 if tile % 2 == parity else tile - 1
    return other if 0 <= other < count else tile


def exchanged(value, parity):
    count, width = lax.axis_size("seq"), lax.axis_size("dp")
    pairs = []
    for tile in range(count):
        other = partner(tile, parity, count)
        for sample in range(width):
            moved = sample ^ 1 if other == tile and width % 2 == 0 else sample
            pairs.append((tile * width + sample, other * width + moved))
    return lax.ppermute(value, ("seq", "dp"), pairs)


def after(value, *others):
    return lax.optimization_barrier((value, *others))[0]


def turned(value, step):
    count = lax.axis_size("pipe")
    return lax.ppermute(value, "pipe", [(i, (i + step) % count) for i in range(count)])


def total_over(value, axis):
    count = lax.axis_size(axis)
    step = 1
    while step < count:
        value = value + lax.ppermute(value, axis, [(i, i ^ step) for i in range(count)])
        step *= 2
    return value


def local(queries, keys, values, grad_out, norm_gains, kv_tiles):
    query, key, value, grad = (a[0, 0, 0] for a in (queries, keys, values, grad_out))
    rows = query.shape[0]
    seq_count = lax.axis_size("seq")
    home_heads = sum(count for _, count, away in GROUPS if not away)
    home_pair = pack_call(key, value, 0, home_heads)
    away_pair = pack_call(after(key, home_pair), value, home_heads, HEADS - home_heads)
    home_gathered = (exchanged(home_pair, 0), exchanged(home_pair, 1))
    info = info_call(kv_tiles[0, 0, 0], after(norm_gains[0], away_pair))
    away_pair = turned(away_pair, -1)
    asked = ask_call(info, after(query, away_pair), grad, home_heads, HEADS - home_heads)
    asked = turned(asked, -1)
    away_gathered = (exchanged(away_pair, 0), exchanged(away_pair, 1))
    sources, parts, sums = [], [], []
    query_grads = None
    for first, count, away in GROUPS:
        if away:
            asked = after(asked, query_grads)
            operands = [(asked, 0, 0), (asked, 0, 1), (away_pair, 0, 0), (away_pair, 0, 1)]
            sources.append((asked, operands))
            query_low, own, to_even, to_odd, gain = main_call(
                *sources[-1], *away_gathered, 0, count, None, count, 0
            )
            sums.append(turned(gain[:2], 1))
        else:
            group_info = after(info, asked) if first else info
            sources.append((group_info, [(a, first, None) for a in (query, grad, key, value)]))
            query_grads, own, to_even, to_odd, gain = main_call(
                *sources[-1], *home_gathered, first, count, query_grads, home_heads, first
            )
            sums.append(gain[:2])
        parts.append((own, exchanged(to_even, 0), exchanged(to_odd, 1)))
    query_grads = turned(query_grads, -1)
    pieces = [query_grads, query_low]
    places = [(0, 0), (0, home_heads * HEAD_DIM)]
    for index, ((first, count, away), (group_info, operands), part) in enumerate(
        zip(GROUPS, sources, parts)
    ):
        own, from_even, from_odd = part
        if away:
            out = last_call(
                group_info, operands[2], own, from_even, from_odd, pieces, tuple(places), first, count
            )
        else:
            own = after(own, query_grads, *(sums[-1:] if index == 0 else ()))
            pair_low = finish_call(group_info, operands[2], own, from_even, from_odd, count)
            pieces.append(turned(pair_low, -1))
            places.append((slice(1, 3), first * HEAD_DIM))
    summed = total_over(total_over(sum(sums), "dp"), "seq")
    tokens = lax.axis_size("dp") * seq_count * rows * HEADS
    return (out[None, :, None, None], (summed / math.sqrt(tokens))[None])


def solution(mesh):
    placed = (
        P("pipe", "dp", "seq", None, None),
        P("pipe", "dp", "seq", None, None),
        P("pipe", "dp", "seq", None, None),
        P("pipe", "dp", "seq", None, None),
        P("pipe", None, None),
        P("pipe", "dp", "seq", None),
    )
    return jax.shard_map(
        local,
        mesh=mesh,
        in_specs=placed,
        out_specs=(P("pipe", None, "dp", "seq", None, None), P("pipe", None, None)),
        check_vma=False,
    )
```

```python
import functools
import math

import jax
import jax.numpy as jnp
from jax import lax
from jax.experimental import pallas as pl
from jax.experimental.pallas import tpu as pltpu
from jax.sharding import PartitionSpec as P

HEADS = 12
HEAD_DIM = 128
EPSILON = 1e-06
ROOT_SCALE = HEAD_DIM ** (-0.5)
EXP2_SCALE = ROOT_SCALE * math.log2(math.e)
GROUPS = ((0, 4, False), (4, 3, False), (7, 5, True))
MAIN_VMEM = 20 * 1024 * 1024
SMALL_VMEM = 12 * 1024 * 1024
PACK_VMEM = 4 * 1024 * 1024
COST = pl.CostEstimate(flops=1, bytes_accessed=1, transcendentals=0)
LONG_COST = pl.CostEstimate(flops=2 * 10**10, bytes_accessed=1, transcendentals=0)
MAIN_COST = pl.CostEstimate(flops=6 * 10**9, bytes_accessed=1, transcendentals=0)


def dot_nt(left, right):
    return lax.dot_general(
        left, right, (((1,), (1,)), ((), ())), preferred_element_type=jnp.float32
    )


def dot_nn(left, right):
    return lax.dot_general(
        left, right, (((1,), (0,)), ((), ())), preferred_element_type=jnp.float32
    )


def dot_tn(left, right):
    return lax.dot_general(
        left, right, (((0,), (0,)), ((), ())), preferred_element_type=jnp.float32
    )


def normalize(source, gain):
    floats = source.astype(jnp.float32)
    scaled = lax.rsqrt(jnp.mean(floats * floats, axis=-1, keepdims=True) + EPSILON)
    normed = floats * scaled
    return floats, scaled, normed, (normed * gain).astype(jnp.bfloat16)


def norm_back(grad_hat, floats, scaled, gain):
    scaled_grad = gain * grad_hat
    projected = jnp.sum(scaled_grad * floats, axis=-1, keepdims=True)
    return scaled * scaled_grad - (scaled**3 * projected * (1.0 / HEAD_DIM)) * floats


def pack_kernel(first_in, second_in, out, sems, *, start, width):
    rows = first_in.shape[0]
    copies = [
        pltpu.make_async_copy(
            source.at[:, start : start + width], out.at[slot, :rows], sems.at[slot]
        )
        for slot, source in enumerate((first_in, second_in))
    ]
    for copy in copies:
        copy.start()
    for copy in copies:
        copy.wait()


def info_kernel(listed, gains, info):
    tile = lax.axis_index("seq")
    last = lax.axis_size("seq") - 1
    info[...] = jnp.zeros_like(info)
    info[0:2, :] = gains[...]
    for parity in range(2):
        other = jnp.where(lax.rem(tile, 2) == parity, tile + 1, tile - 1)
        found = listed[0] == other
        for slot in range(1, listed.shape[0]):
            found = found | (listed[slot] == other)
        found = found & (other >= 0) & (other <= last)
        live = jnp.where(found, 1.0, 0.0)
        info[2 + parity : 3 + parity, :] = jnp.full((1, HEAD_DIM), live, jnp.float32)


def ask_kernel(info, query, grad, out, sems, *, start, width):
    rows = query.shape[0]
    value = info[...]
    planes = []
    for _ in range(3):
        low = value.astype(jnp.bfloat16)
        planes.append(low)
        value = value - low.astype(jnp.float32)
    planes.append(jnp.zeros_like(planes[0]))
    out[0, rows : rows + 16, :HEAD_DIM] = jnp.concatenate(planes[:2], axis=0)
    out[1, rows : rows + 16, :HEAD_DIM] = jnp.concatenate(planes[2:], axis=0)
    pack_kernel(query, grad, out, sems, start=start, width=width)


def told_info(told):
    floats = told[...].astype(jnp.float32)
    return floats[0, 0:8] + floats[0, 8:16] + floats[1, 0:8]


def main_kernel(
    info, query, grad, key, value, pair_even, pair_odd, *rest
):
    query_out, own_out, even_out, odd_out, gain_out = rest[-5:]
    told = told_info(info) if len(info.shape) == 3 else info[...]
    query_gain = told[0:1]
    key_gain = told[1:2]
    rows = query.shape[0]
    lives = [jnp.concatenate([told[row : row + 1]] * (rows // HEAD_DIM), axis=1) for row in (2, 3)]
    query_floats, query_scale, query_normed, query_hat = normalize(query[...], query_gain)
    grad_in = grad[...]
    sides = (
        (key[...], value[...], None),
        (pair_even[0], pair_even[1], lives[0]),
        (pair_odd[0], pair_odd[1], lives[1]),
    )
    parts = []
    totals = None
    for key_in, value_in, live in sides:
        _, _, key_normed, key_hat = normalize(key_in, key_gain)
        weights = jnp.exp2(dot_nt(key_hat, query_hat) * EXP2_SCALE)
        grad_probs = dot_nt(value_in, grad_in)
        weight_sum = jnp.sum(weights, axis=0, keepdims=True)
        cross_sum = jnp.sum(weights * grad_probs, axis=0, keepdims=True)
        if live is not None:
            weight_sum = weight_sum * live
            cross_sum = cross_sum * live
        totals = weight_sum if totals is None else totals + weight_sum
        crosses = cross_sum if live is None else crosses + cross_sum
        parts.append((key_normed, key_hat, weights, grad_probs, live))
    inverse = 1.0 / totals
    deltas = crosses * inverse
    query_grad_t = None
    key_gain_sum = None
    for (key_normed, key_hat, weights, grad_probs, live), out in zip(
        parts, (own_out, even_out, odd_out)
    ):
        probs = weights * (inverse if live is None else inverse * live)
        dscores = (probs * (grad_probs - deltas)).astype(jnp.bfloat16)
        key_part = dot_nn(dscores, query_hat) * ROOT_SCALE
        value_part = dot_nn(probs.astype(jnp.bfloat16), grad_in)
        out[0] = key_part.astype(out.dtype)
        out[1] = value_part.astype(out.dtype)
        gain_part = jnp.sum(key_part * key_normed, axis=0, keepdims=True)
        key_gain_sum = gain_part if key_gain_sum is None else key_gain_sum + gain_part
        query_part = dot_tn(key_hat, dscores)
        query_grad_t = query_part if query_grad_t is None else query_grad_t + query_part
    query_grad = query_grad_t.T * ROOT_SCALE
    query_out[...] = norm_back(query_grad, query_floats, query_scale, query_gain).astype(
        query_out.dtype
    )
    query_gain_sum = jnp.sum(query_grad * query_normed, axis=0, keepdims=True)

    @pl.when(pl.program_id(0) == 0)
    def _():
        gain_out[...] = jnp.zeros_like(gain_out)

    gain_out[0:1, :] += query_gain_sum
    gain_out[1:2, :] += key_gain_sum


def finished(info, key, own, from_even, from_odd):
    told = told_info(info) if len(info.shape) == 3 else info[...]
    key_gain = told[1:2]
    key_floats, key_scale, _, _ = normalize(key[...], key_gain)
    key_grad = own[0] + from_even[0].astype(jnp.float32) + from_odd[0].astype(jnp.float32)
    value_grad = own[1] + from_even[1].astype(jnp.float32) + from_odd[1].astype(jnp.float32)
    return norm_back(key_grad, key_floats, key_scale, key_gain), value_grad


def finish_kernel(info, key, own, from_even, from_odd, out):
    key_grad, value_grad = finished(info, key, own, from_even, from_odd)
    out[0] = key_grad.astype(out.dtype)
    out[1] = value_grad.astype(out.dtype)


def last_kernel(info, key, own, from_even, from_odd, *rest, places, first, count):
    amount = len(places)
    pieces, (out, held) = rest[:amount], rest[amount : amount + 2]
    staged, (load_sems, store_sems) = rest[amount + 2 : -2], rest[-2:]
    head = pl.program_id(0)
    loads = [
        pltpu.make_async_copy(piece, stage, load_sems.at[slot])
        for slot, (piece, stage) in enumerate(zip(pieces, staged))
    ]
    stores = [
        pltpu.make_async_copy(
            stage, out.at[planes, :, start : start + stage.shape[-1]], store_sems.at[slot]
        )
        for slot, (stage, (planes, start)) in enumerate(zip(staged, places))
    ]

    def head_copy(index):
        start = pl.multiple_of((first + index) * HEAD_DIM, HEAD_DIM)
        return pltpu.make_async_copy(
            held.at[index],
            out.at[pl.ds(1, 2), :, pl.ds(start, HEAD_DIM)],
            store_sems.at[amount + index],
        )

    @pl.when(head == 0)
    def _():
        for load in loads:
            load.start()

    @pl.when(head == min(1, count - 1))
    def _():
        for load, store in zip(loads, stores):
            load.wait()
            store.start()

    key_grad, value_grad = finished(info, key, own, from_even, from_odd)
    held[head, 0] = key_grad.astype(held.dtype)
    held[head, 1] = value_grad.astype(held.dtype)
    head_copy(head).start()

    @pl.when(head == count - 1)
    def _():
        for store in stores:
            store.wait()
        for index in range(count):
            head_copy(index).wait()


def head_block(rows, first, slot=None):
    if slot is None:
        return pl.BlockSpec((rows, HEAD_DIM), lambda head: (0, first + head))
    return pl.BlockSpec((None, rows, HEAD_DIM), lambda head: (slot, 0, first + head))


def pair_block(rows, first=0):
    return pl.BlockSpec((2, rows, HEAD_DIM), lambda head: (0, 0, first + head))


def whole_block(shape):
    return pl.BlockSpec(shape, lambda head: (0,) * len(shape))


def pack_params():
    return dict(
        scratch_shapes=[pltpu.SemaphoreType.DMA((2,))],
        compiler_params=pltpu.CompilerParams(vmem_limit_bytes=PACK_VMEM),
        cost_estimate=COST,
    )


def pack_call(first_in, second_in, first, count):
    rows = first_in.shape[0]
    width = count * HEAD_DIM
    return pl.pallas_call(
        functools.partial(pack_kernel, start=first * HEAD_DIM, width=width),
        grid=(1,),
        in_specs=[pl.BlockSpec(memory_space=pl.ANY)] * 2,
        out_specs=whole_block((2, rows, width)),
        out_shape=jax.ShapeDtypeStruct((2, rows, width), jnp.bfloat16),
        **pack_params(),
    )(first_in, second_in)


def ask_call(info, query, grad, first, count):
    rows = query.shape[0]
    width = count * HEAD_DIM
    return pl.pallas_call(
        functools.partial(ask_kernel, start=first * HEAD_DIM, width=width),
        grid=(1,),
        in_specs=[whole_block(info.shape)] + [pl.BlockSpec(memory_space=pl.ANY)] * 2,
        out_specs=whole_block((2, rows + 16, width)),
        out_shape=jax.ShapeDtypeStruct((2, rows + 16, width), jnp.bfloat16),
        **pack_params(),
    )(info, query, grad)


def info_call(listed, gains):
    return pl.pallas_call(
        info_kernel,
        in_specs=[pl.BlockSpec(memory_space=pltpu.SMEM), pl.BlockSpec(memory_space=pltpu.VMEM)],
        out_specs=pl.BlockSpec(memory_space=pltpu.VMEM),
        out_shape=jax.ShapeDtypeStruct((8, HEAD_DIM), jnp.float32),
        compiler_params=pltpu.CompilerParams(vmem_limit_bytes=PACK_VMEM),
        cost_estimate=LONG_COST,
    )(listed, gains)


def info_block(info):
    if info.ndim == 2:
        return whole_block(info.shape)
    below = info.shape[1] // 16 - 1
    return pl.BlockSpec((2, 16, HEAD_DIM), lambda head: (0, below, 0))


def main_call(
    info, operands, pair_even, pair_odd, pair_first, count, query_grads, query_heads, query_first
):
    rows = pair_even.shape[1]
    lanes = count * HEAD_DIM
    earlier = [] if query_grads is None else [query_grads]
    return pl.pallas_call(
        main_kernel,
        grid=(count,),
        in_specs=[info_block(info)]
        + [head_block(rows, first, slot) for _, first, slot in operands]
        + [pair_block(rows, pair_first)] * 2
        + [pl.BlockSpec(memory_space=pl.ANY)] * len(earlier),
        out_specs=[head_block(rows, query_first)]
        + [pair_block(rows)] * 3
        + [whole_block((8, HEAD_DIM))],
        out_shape=[
            jax.ShapeDtypeStruct((rows, query_heads * HEAD_DIM), jnp.bfloat16),
            jax.ShapeDtypeStruct((2, rows, lanes), jnp.float32),
            jax.ShapeDtypeStruct((2, rows, lanes), jnp.bfloat16),
            jax.ShapeDtypeStruct((2, rows, lanes), jnp.bfloat16),
            jax.ShapeDtypeStruct((8, HEAD_DIM), jnp.float32),
        ],
        input_output_aliases={7: 0} if earlier else {},
        compiler_params=pltpu.CompilerParams(vmem_limit_bytes=MAIN_VMEM),
        cost_estimate=MAIN_COST,
    )(info, *[array for array, _, _ in operands], pair_even, pair_odd, *earlier)


def finish_call(info, key, own, from_even, from_odd, count):
    array, first, slot = key
    rows = own.shape[1]
    return pl.pallas_call(
        finish_kernel,
        grid=(count,),
        in_specs=[info_block(info), head_block(rows, first, slot)] + [pair_block(rows)] * 3,
        out_specs=pair_block(rows),
        out_shape=jax.ShapeDtypeStruct((2, rows, count * HEAD_DIM), jnp.bfloat16),
        compiler_params=pltpu.CompilerParams(vmem_limit_bytes=SMALL_VMEM),
        cost_estimate=LONG_COST,
    )(info, array, own, from_even, from_odd)


def last_call(info, key, own, from_even, from_odd, pieces, places, first, count):
    array, offset, slot = key
    rows = own.shape[1]
    anywhere = pl.BlockSpec(memory_space=pl.ANY)
    return pl.pallas_call(
        functools.partial(last_kernel, places=places, first=first, count=count),
        grid=(count,),
        in_specs=[info_block(info), head_block(rows, offset, slot)]
        + [pair_block(rows)] * 3
        + [anywhere] * len(pieces),
        out_specs=anywhere,
        out_shape=jax.ShapeDtypeStruct((3, rows, HEADS * HEAD_DIM), jnp.bfloat16),
        scratch_shapes=[
            pltpu.VMEM((count, 2, rows, HEAD_DIM), jnp.bfloat16),
            *[pltpu.VMEM(piece.shape, piece.dtype) for piece in pieces],
            pltpu.SemaphoreType.DMA((len(pieces),)),
            pltpu.SemaphoreType.DMA((len(pieces) + count,)),
        ],
        compiler_params=pltpu.CompilerParams(vmem_limit_bytes=SMALL_VMEM),
        cost_estimate=COST,
    )(info, array, own, from_even, from_odd, *pieces)


def partner(tile, parity, count):
    other = tile + 1 if tile % 2 == parity else tile - 1
    return other if 0 <= other < count else tile


def exchanged(value, parity):
    count, width = lax.axis_size("seq"), lax.axis_size("dp")
    pairs = []
    for tile in range(count):
        other = partner(tile, parity, count)
        for sample in range(width):
            moved = sample ^ 1 if other == tile and width % 2 == 0 else sample
            pairs.append((tile * width + sample, other * width + moved))
    return lax.ppermute(value, ("seq", "dp"), pairs)


def after(value, *others):
    return lax.optimization_barrier((value, *others))[0]


def turned(value, step):
    count = lax.axis_size("pipe")
    return lax.ppermute(value, "pipe", [(i, (i + step) % count) for i in range(count)])


def total_over(value, axis, *late):
    count = lax.axis_size(axis)
    step = 1
    while step < count:
        other = lax.ppermute(value, axis, [(i, i ^ step) for i in range(count)])
        step *= 2
        value = value + (other if step < count else after(other, *late))
    return value


def local(queries, keys, values, grad_out, norm_gains, kv_tiles):
    query, key, value, grad = (a[0, 0, 0] for a in (queries, keys, values, grad_out))
    rows = query.shape[0]
    seq_count = lax.axis_size("seq")
    home_heads = sum(count for _, count, away in GROUPS if not away)
    home_pair = pack_call(key, value, 0, home_heads)
    away_pair = pack_call(after(key, home_pair), value, home_heads, HEADS - home_heads)
    home_gathered = (exchanged(home_pair, 0), exchanged(home_pair, 1))
    info = info_call(kv_tiles[0, 0, 0], after(norm_gains[0], away_pair))
    away_pair = turned(away_pair, -1)
    asked = ask_call(info, after(query, away_pair), grad, home_heads, HEADS - home_heads)
    asked = turned(asked, -1)
    away_gathered = (exchanged(away_pair, 0), exchanged(away_pair, 1))
    sources, parts, sums = [], [], []
    query_grads = None
    for first, count, away in GROUPS:
        if away:
            asked = after(asked, query_grads)
            operands = [(asked, 0, 0), (asked, 0, 1), (away_pair, 0, 0), (away_pair, 0, 1)]
            sources.append((asked, operands))
            query_low, own, to_even, to_odd, gain = main_call(
                *sources[-1], *away_gathered, 0, count, None, count, 0
            )
            sums.append(turned(gain[:2], 1))
        else:
            group_info = after(info, asked) if first else info
            sources.append((group_info, [(a, first, None) for a in (query, grad, key, value)]))
            query_grads, own, to_even, to_odd, gain = main_call(
                *sources[-1], *home_gathered, first, count, query_grads, home_heads, first
            )
            sums.append(gain[:2])
        parts.append((own, exchanged(to_even, 0), exchanged(to_odd, 1)))
    query_grads = turned(query_grads, -1)
    pieces = [query_grads, query_low]
    places = [(0, 0), (0, home_heads * HEAD_DIM)]
    for index, ((first, count, away), (group_info, operands), part) in enumerate(
        zip(GROUPS, sources, parts)
    ):
        own, from_even, from_odd = part
        if away:
            out = last_call(
                group_info, operands[2], own, from_even, from_odd, pieces, tuple(places), first, count
            )
        else:
            own = after(own, query_grads, *(sums[-1:] if index == 0 else ()))
            pair_low = finish_call(group_info, operands[2], own, from_even, from_odd, count)
            pieces.append(turned(pair_low, -1))
            places.append((slice(1, 3), first * HEAD_DIM))
    summed = total_over(total_over(sum(sums), "dp"), "seq", out)
    tokens = lax.axis_size("dp") * seq_count * rows * HEADS
    return (out[None, :, None, None], (summed / math.sqrt(tokens))[None])


def solution(mesh):
    placed = (
        P("pipe", "dp", "seq", None, None),
        P("pipe", "dp", "seq", None, None),
        P("pipe", "dp", "seq", None, None),
        P("pipe", "dp", "seq", None, None),
        P("pipe", None, None),
        P("pipe", "dp", "seq", None),
    )
    return jax.shard_map(
        local,
        mesh=mesh,
        in_specs=placed,
        out_specs=(P("pipe", None, "dp", "seq", None, None), P("pipe", None, None)),
        check_vma=False,
    )
```

```python
import functools
import math

import jax
import jax.numpy as jnp
from jax import lax
from jax.experimental import pallas as pl
from jax.experimental.pallas import tpu as pltpu
from jax.sharding import PartitionSpec as P

HEADS = 12
HEAD_DIM = 128
EPSILON = 1e-06
ROOT_SCALE = HEAD_DIM ** (-0.5)
EXP2_SCALE = ROOT_SCALE * math.log2(math.e)
GROUPS = ((0, 3, False), (3, 4, False), (7, 5, True))
MAIN_VMEM = 20 * 1024 * 1024
SMALL_VMEM = 12 * 1024 * 1024
PACK_VMEM = 4 * 1024 * 1024
COST = pl.CostEstimate(flops=1, bytes_accessed=1, transcendentals=0)
LONG_COST = pl.CostEstimate(flops=2 * 10**10, bytes_accessed=1, transcendentals=0)
MAIN_COST = pl.CostEstimate(flops=6 * 10**9, bytes_accessed=1, transcendentals=0)


def dot_nt(left, right):
    return lax.dot_general(
        left, right, (((1,), (1,)), ((), ())), preferred_element_type=jnp.float32
    )


def dot_nn(left, right):
    return lax.dot_general(
        left, right, (((1,), (0,)), ((), ())), preferred_element_type=jnp.float32
    )


def dot_tn(left, right):
    return lax.dot_general(
        left, right, (((0,), (0,)), ((), ())), preferred_element_type=jnp.float32
    )


def normalize(source, gain):
    floats = source.astype(jnp.float32)
    scaled = lax.rsqrt(jnp.mean(floats * floats, axis=-1, keepdims=True) + EPSILON)
    normed = floats * scaled
    return floats, scaled, normed, (normed * gain).astype(jnp.bfloat16)


def norm_back(grad_hat, floats, scaled, gain):
    scaled_grad = gain * grad_hat
    projected = jnp.sum(scaled_grad * floats, axis=-1, keepdims=True)
    return scaled * scaled_grad - (scaled**3 * projected * (1.0 / HEAD_DIM)) * floats


def pack_kernel(first_in, second_in, out, sems, *, start, width):
    rows = first_in.shape[0]
    copies = [
        pltpu.make_async_copy(
            source.at[:, start : start + width], out.at[slot, :rows], sems.at[slot]
        )
        for slot, source in enumerate((first_in, second_in))
    ]
    for copy in copies:
        copy.start()
    for copy in copies:
        copy.wait()


def info_kernel(listed, gains, info):
    tile = lax.axis_index("seq")
    last = lax.axis_size("seq") - 1
    info[...] = jnp.zeros_like(info)
    info[0:2, :] = gains[...]
    for parity in range(2):
        other = jnp.where(lax.rem(tile, 2) == parity, tile + 1, tile - 1)
        found = listed[0] == other
        for slot in range(1, listed.shape[0]):
            found = found | (listed[slot] == other)
        found = found & (other >= 0) & (other <= last)
        live = jnp.where(found, 1.0, 0.0)
        info[2 + parity : 3 + parity, :] = jnp.full((1, HEAD_DIM), live, jnp.float32)


def ask_kernel(info, query, grad, out, sems, *, start, width):
    rows = query.shape[0]
    value = info[...]
    planes = []
    for _ in range(3):
        low = value.astype(jnp.bfloat16)
        planes.append(low)
        value = value - low.astype(jnp.float32)
    planes.append(jnp.zeros_like(planes[0]))
    out[0, rows : rows + 16, :HEAD_DIM] = jnp.concatenate(planes[:2], axis=0)
    out[1, rows : rows + 16, :HEAD_DIM] = jnp.concatenate(planes[2:], axis=0)
    pack_kernel(query, grad, out, sems, start=start, width=width)


def told_info(told):
    floats = told[...].astype(jnp.float32)
    return floats[0, 0:8] + floats[0, 8:16] + floats[1, 0:8]


def main_kernel(
    info, query, grad, key, value, pair_even, pair_odd, *rest
):
    query_out, own_out, even_out, odd_out, gain_out = rest[-5:]
    told = told_info(info) if len(info.shape) == 3 else info[...]
    query_gain = told[0:1]
    key_gain = told[1:2]
    rows = query.shape[0]
    lives = [jnp.concatenate([told[row : row + 1]] * (rows // HEAD_DIM), axis=1) for row in (2, 3)]
    query_floats, query_scale, query_normed, query_hat = normalize(query[...], query_gain)
    grad_in = grad[...]
    sides = (
        (key[...], value[...], None),
        (pair_even[0], pair_even[1], lives[0]),
        (pair_odd[0], pair_odd[1], lives[1]),
    )
    parts = []
    totals = None
    for key_in, value_in, live in sides:
        _, _, key_normed, key_hat = normalize(key_in, key_gain)
        weights = jnp.exp2(dot_nt(key_hat, query_hat) * EXP2_SCALE)
        grad_probs = dot_nt(value_in, grad_in)
        weight_sum = jnp.sum(weights, axis=0, keepdims=True)
        cross_sum = jnp.sum(weights * grad_probs, axis=0, keepdims=True)
        if live is not None:
            weight_sum = weight_sum * live
            cross_sum = cross_sum * live
        totals = weight_sum if totals is None else totals + weight_sum
        crosses = cross_sum if live is None else crosses + cross_sum
        parts.append((key_normed, key_hat, weights, grad_probs, live))
    inverse = 1.0 / totals
    deltas = crosses * inverse
    query_grad_t = None
    key_gain_sum = None
    for (key_normed, key_hat, weights, grad_probs, live), out in zip(
        parts, (own_out, even_out, odd_out)
    ):
        probs = weights * (inverse if live is None else inverse * live)
        dscores = (probs * (grad_probs - deltas)).astype(jnp.bfloat16)
        key_part = dot_nn(dscores, query_hat) * ROOT_SCALE
        value_part = dot_nn(probs.astype(jnp.bfloat16), grad_in)
        out[0] = key_part.astype(out.dtype)
        out[1] = value_part.astype(out.dtype)
        gain_part = jnp.sum(key_part * key_normed, axis=0, keepdims=True)
        key_gain_sum = gain_part if key_gain_sum is None else key_gain_sum + gain_part
        query_part = dot_tn(key_hat, dscores)
        query_grad_t = query_part if query_grad_t is None else query_grad_t + query_part
    query_grad = query_grad_t.T * ROOT_SCALE
    query_out[...] = norm_back(query_grad, query_floats, query_scale, query_gain).astype(
        query_out.dtype
    )
    query_gain_sum = jnp.sum(query_grad * query_normed, axis=0, keepdims=True)

    @pl.when(pl.program_id(0) == 0)
    def _():
        gain_out[...] = jnp.zeros_like(gain_out)

    gain_out[0:1, :] += query_gain_sum
    gain_out[1:2, :] += key_gain_sum


def tile_sums(key_hat, value_in, query_hat, grad_in):
    weights = jnp.exp2(dot_nt(key_hat, query_hat) * EXP2_SCALE)
    grad_probs = dot_nt(value_in, grad_in)
    return weights, grad_probs


def wide_lives(told, rows):
    return [jnp.concatenate([told[row : row + 1]] * (rows // HEAD_DIM), axis=1) for row in (2, 3)]


def near_is_even():
    place = lax.rem(lax.axis_index("seq"), 4)
    return (place == 0) | (place == 3)


def sums_kernel(info, query, grad, key, value, pair_even, pair_odd, *rest, far_count):
    outs = rest[-2 - far_count :]
    told = info[...]
    _, _, _, key_hat = normalize(key[...], told[1:2])
    value_in = value[...]
    rows = []
    for query_in, grad_in in (
        (query[...], grad[...]), (pair_even[0], pair_even[1]), (pair_odd[0], pair_odd[1])
    ):
        _, _, _, query_hat = normalize(query_in, told[0:1])
        weights, grad_probs = tile_sums(key_hat, value_in, query_hat, grad_in)
        rows.append(
            [
                jnp.sum(weights, axis=0, keepdims=True),
                jnp.sum(weights * grad_probs, axis=0, keepdims=True),
            ]
        )
    own, even, odd = rows
    tail = wide_lives(told, query.shape[0])
    blank = jnp.zeros_like(tail[0])
    outs[0][...] = jnp.concatenate([*own, *even, *tail, blank, blank], axis=0)
    outs[1][...] = jnp.concatenate([*own, *odd, *tail, blank, blank], axis=0)
    near = near_is_even()
    for index, out in enumerate(outs[2:]):
        first, second = (even, odd) if index == 0 else (odd, even)
        chosen = [jnp.where(near, one, two) for one, two in zip(first, second)]
        out[...] = jnp.concatenate([*chosen, *[blank] * 6], axis=0)


def grads_kernel(
    info, query, grad, key, value, pair_even, pair_odd,
    sent_even, sent_odd, from_even, from_odd, *rest, far_count,
):
    fars = [far[0:2, :] for far in rest[:far_count]]
    pair_out, own_out, even_out, odd_out, gain_out = rest[-5:]
    told = info[...]
    near = near_is_even()
    if far_count == 2:
        far_even = jnp.where(near, fars[0], fars[1])
        far_odd = jnp.where(near, fars[1], fars[0])
    elif far_count == 1:
        far_even = jnp.where(near, fars[0], jnp.zeros_like(fars[0]))
        far_odd = jnp.where(near, jnp.zeros_like(fars[0]), fars[0])
    else:
        far_even = far_odd = jnp.zeros_like(from_even[0:2, :])
    own_sums = (
        sent_even[0:2, :]
        + sent_even[4:5, :] * from_even[2:4, :]
        + sent_even[5:6, :] * from_odd[2:4, :]
    )
    even_sums = (
        from_even[0:2, :] + from_even[4:5, :] * sent_even[2:4, :] + from_even[5:6, :] * far_even
    )
    odd_sums = (
        from_odd[0:2, :] + from_odd[5:6, :] * sent_odd[2:4, :] + from_odd[4:5, :] * far_odd
    )
    key_floats, key_scale, key_normed, key_hat = normalize(key[...], told[1:2])
    value_in = value[...]
    key_grad = value_grad = query_gain_sum = None
    for query_in, grad_in, sums, live, out in (
        (query[...], grad[...], own_sums, None, own_out),
        (pair_even[0], pair_even[1], even_sums, from_even[4:5, :], even_out),
        (pair_odd[0], pair_odd[1], odd_sums, from_odd[5:6, :], odd_out),
    ):
        _, _, query_normed, query_hat = normalize(query_in, told[0:1])
        weights, grad_probs = tile_sums(key_hat, value_in, query_hat, grad_in)
        inverse = 1.0 / sums[0:1]
        deltas = sums[1:2] * inverse
        probs = weights * (inverse if live is None else inverse * live)
        dscores = (probs * (grad_probs - deltas)).astype(jnp.bfloat16)
        key_part = dot_nn(dscores, query_hat)
        value_part = dot_nn(probs.astype(jnp.bfloat16), grad_in)
        query_part = dot_tn(key_hat, dscores).T * ROOT_SCALE
        out[...] = query_part.astype(out.dtype)
        gain_part = jnp.sum(query_part * query_normed, axis=0, keepdims=True)
        key_grad = key_part if key_grad is None else key_grad + key_part
        value_grad = value_part if value_grad is None else value_grad + value_part
        query_gain_sum = gain_part if query_gain_sum is None else query_gain_sum + gain_part
    key_grad = key_grad * ROOT_SCALE
    key_back = norm_back(key_grad, key_floats, key_scale, told[1:2])
    pair_out[0] = key_back.astype(pair_out.dtype)
    pair_out[1] = value_grad.astype(pair_out.dtype)

    @pl.when(pl.program_id(0) == 0)
    def _():
        gain_out[...] = jnp.zeros_like(gain_out)

    gain_out[0:1, :] += query_gain_sum
    gain_out[1:2, :] += jnp.sum(key_grad * key_normed, axis=0, keepdims=True)


def answer_kernel(info, query, own, from_even, from_odd, out):
    gain = info[0:1, :]
    floats, scaled, _, _ = normalize(query[...], gain)
    total = own[...] + from_even[...].astype(jnp.float32) + from_odd[...].astype(jnp.float32)
    out[...] = norm_back(total, floats, scaled, gain).astype(out.dtype)


def finished(info, key, own, from_even, from_odd):
    told = told_info(info) if len(info.shape) == 3 else info[...]
    key_gain = told[1:2]
    key_floats, key_scale, _, _ = normalize(key[...], key_gain)
    key_grad = own[0] + from_even[0].astype(jnp.float32) + from_odd[0].astype(jnp.float32)
    value_grad = own[1] + from_even[1].astype(jnp.float32) + from_odd[1].astype(jnp.float32)
    return norm_back(key_grad, key_floats, key_scale, key_gain), value_grad


def last_kernel(info, key, own, from_even, from_odd, *rest, places, first, count):
    amount = len(places)
    pieces, (out, held) = rest[:amount], rest[amount : amount + 2]
    staged, (load_sems, store_sems) = rest[amount + 2 : -2], rest[-2:]
    head = pl.program_id(0)
    loads = [
        pltpu.make_async_copy(piece, stage, load_sems.at[slot])
        for slot, (piece, stage) in enumerate(zip(pieces, staged))
    ]
    stores = [
        pltpu.make_async_copy(
            stage, out.at[planes, :, start : start + stage.shape[-1]], store_sems.at[slot]
        )
        for slot, (stage, (planes, start)) in enumerate(zip(staged, places))
    ]

    def head_copy(index):
        start = pl.multiple_of((first + index) * HEAD_DIM, HEAD_DIM)
        return pltpu.make_async_copy(
            held.at[index],
            out.at[pl.ds(1, 2), :, pl.ds(start, HEAD_DIM)],
            store_sems.at[amount + index],
        )

    @pl.when(head == 0)
    def _():
        for load in loads:
            load.start()

    @pl.when(head == min(1, count - 1))
    def _():
        for load, store in zip(loads, stores):
            load.wait()
            store.start()

    key_grad, value_grad = finished(info, key, own, from_even, from_odd)
    held[head, 0] = key_grad.astype(held.dtype)
    held[head, 1] = value_grad.astype(held.dtype)
    head_copy(head).start()

    @pl.when(head == count - 1)
    def _():
        for store in stores:
            store.wait()
        for index in range(count):
            head_copy(index).wait()


def head_block(rows, first, slot=None):
    if slot is None:
        return pl.BlockSpec((rows, HEAD_DIM), lambda head: (0, first + head))
    return pl.BlockSpec((None, rows, HEAD_DIM), lambda head: (slot, 0, first + head))


def pair_block(rows, first=0):
    return pl.BlockSpec((2, rows, HEAD_DIM), lambda head: (0, 0, first + head))


def whole_block(shape):
    return pl.BlockSpec(shape, lambda head: (0,) * len(shape))


def pack_params():
    return dict(
        scratch_shapes=[pltpu.SemaphoreType.DMA((2,))],
        compiler_params=pltpu.CompilerParams(vmem_limit_bytes=PACK_VMEM),
        cost_estimate=COST,
    )


def pack_call(first_in, second_in, first, count):
    rows = first_in.shape[0]
    width = count * HEAD_DIM
    return pl.pallas_call(
        functools.partial(pack_kernel, start=first * HEAD_DIM, width=width),
        grid=(1,),
        in_specs=[pl.BlockSpec(memory_space=pl.ANY)] * 2,
        out_specs=whole_block((2, rows, width)),
        out_shape=jax.ShapeDtypeStruct((2, rows, width), jnp.bfloat16),
        **pack_params(),
    )(first_in, second_in)


def ask_call(info, query, grad, first, count):
    rows = query.shape[0]
    width = count * HEAD_DIM
    return pl.pallas_call(
        functools.partial(ask_kernel, start=first * HEAD_DIM, width=width),
        grid=(1,),
        in_specs=[whole_block(info.shape)] + [pl.BlockSpec(memory_space=pl.ANY)] * 2,
        out_specs=whole_block((2, rows + 16, width)),
        out_shape=jax.ShapeDtypeStruct((2, rows + 16, width), jnp.bfloat16),
        **pack_params(),
    )(info, query, grad)


def info_call(listed, gains):
    return pl.pallas_call(
        info_kernel,
        in_specs=[pl.BlockSpec(memory_space=pltpu.SMEM), pl.BlockSpec(memory_space=pltpu.VMEM)],
        out_specs=pl.BlockSpec(memory_space=pltpu.VMEM),
        out_shape=jax.ShapeDtypeStruct((8, HEAD_DIM), jnp.float32),
        compiler_params=pltpu.CompilerParams(vmem_limit_bytes=PACK_VMEM),
        cost_estimate=LONG_COST,
    )(listed, gains)


def info_block(info):
    if info.ndim == 2:
        return whole_block(info.shape)
    below = info.shape[1] // 16 - 1
    return pl.BlockSpec((2, 16, HEAD_DIM), lambda head: (0, below, 0))


def main_call(info, operands, pair_even, pair_odd, count):
    rows = pair_even.shape[1]
    lanes = count * HEAD_DIM
    return pl.pallas_call(
        main_kernel,
        grid=(count,),
        in_specs=[info_block(info)]
        + [head_block(rows, first, slot) for _, first, slot in operands]
        + [pair_block(rows)] * 2,
        out_specs=[head_block(rows, 0)] + [pair_block(rows)] * 3 + [whole_block((8, HEAD_DIM))],
        out_shape=[
            jax.ShapeDtypeStruct((rows, lanes), jnp.bfloat16),
            jax.ShapeDtypeStruct((2, rows, lanes), jnp.float32),
            jax.ShapeDtypeStruct((2, rows, lanes), jnp.bfloat16),
            jax.ShapeDtypeStruct((2, rows, lanes), jnp.bfloat16),
            jax.ShapeDtypeStruct((8, HEAD_DIM), jnp.float32),
        ],
        compiler_params=pltpu.CompilerParams(vmem_limit_bytes=MAIN_VMEM),
        cost_estimate=MAIN_COST,
    )(info, *[array for array, _, _ in operands], pair_even, pair_odd)


def row_block(rows, first):
    return pl.BlockSpec((8, rows), lambda head: (first + head, 0))


def sums_call(info, arrays, pair_even, pair_odd, first, count, heads, earlier, far_count):
    rows = pair_even.shape[1]
    amount = 2 + far_count
    earlier = [] if earlier is None else earlier
    return pl.pallas_call(
        functools.partial(sums_kernel, far_count=far_count),
        grid=(count,),
        in_specs=[info_block(info)]
        + [head_block(rows, first)] * 4
        + [pair_block(rows)] * 2
        + [pl.BlockSpec(memory_space=pl.ANY)] * len(earlier),
        out_specs=[row_block(rows, first)] * amount,
        out_shape=[jax.ShapeDtypeStruct((8 * heads, rows), jnp.float32)] * amount,
        input_output_aliases={7 + index: index for index in range(len(earlier))},
        compiler_params=pltpu.CompilerParams(vmem_limit_bytes=MAIN_VMEM),
        cost_estimate=MAIN_COST,
    )(info, *arrays, pair_even, pair_odd, *earlier)


def grads_call(info, arrays, pair_even, pair_odd, sums, first, count, heads, earlier, far_count):
    rows = pair_even.shape[1]
    lanes = heads * HEAD_DIM
    earlier = [] if earlier is None else earlier
    place = 7 + len(sums)
    return pl.pallas_call(
        functools.partial(grads_kernel, far_count=far_count),
        grid=(count,),
        in_specs=[info_block(info)]
        + [head_block(rows, first)] * 4
        + [pair_block(rows)] * 2
        + [row_block(rows, first)] * len(sums)
        + [pl.BlockSpec(memory_space=pl.ANY)] * len(earlier),
        out_specs=[pair_block(rows)] + [head_block(rows, first)] * 3 + [whole_block((8, HEAD_DIM))],
        out_shape=[
            jax.ShapeDtypeStruct((2, rows, count * HEAD_DIM), jnp.bfloat16),
            jax.ShapeDtypeStruct((rows, lanes), jnp.float32),
            jax.ShapeDtypeStruct((rows, lanes), jnp.bfloat16),
            jax.ShapeDtypeStruct((rows, lanes), jnp.bfloat16),
            jax.ShapeDtypeStruct((8, HEAD_DIM), jnp.float32),
        ],
        input_output_aliases={place + index: 1 + index for index in range(len(earlier))},
        compiler_params=pltpu.CompilerParams(vmem_limit_bytes=MAIN_VMEM),
        cost_estimate=MAIN_COST,
    )(info, *arrays, pair_even, pair_odd, *sums, *earlier)


def answer_call(info, query, own, from_even, from_odd, first, count):
    rows = own.shape[0]
    return pl.pallas_call(
        answer_kernel,
        grid=(count,),
        in_specs=[info_block(info), head_block(rows, first)] + [head_block(rows, 0)] * 3,
        out_specs=head_block(rows, 0),
        out_shape=jax.ShapeDtypeStruct((rows, count * HEAD_DIM), jnp.bfloat16),
        compiler_params=pltpu.CompilerParams(vmem_limit_bytes=SMALL_VMEM),
        cost_estimate=LONG_COST,
    )(info, query, own, from_even, from_odd)


def last_call(info, key, own, from_even, from_odd, pieces, places, first, count):
    array, offset, slot = key
    rows = own.shape[1]
    anywhere = pl.BlockSpec(memory_space=pl.ANY)
    return pl.pallas_call(
        functools.partial(last_kernel, places=places, first=first, count=count),
        grid=(count,),
        in_specs=[info_block(info), head_block(rows, offset, slot)]
        + [pair_block(rows)] * 3
        + [anywhere] * len(pieces),
        out_specs=anywhere,
        out_shape=jax.ShapeDtypeStruct((3, rows, HEADS * HEAD_DIM), jnp.bfloat16),
        scratch_shapes=[
            pltpu.VMEM((count, 2, rows, HEAD_DIM), jnp.bfloat16),
            *[pltpu.VMEM(piece.shape, piece.dtype) for piece in pieces],
            pltpu.SemaphoreType.DMA((len(pieces),)),
            pltpu.SemaphoreType.DMA((len(pieces) + count,)),
        ],
        compiler_params=pltpu.CompilerParams(vmem_limit_bytes=SMALL_VMEM),
        cost_estimate=COST,
    )(info, array, own, from_even, from_odd, *pieces)


def partner(tile, parity, count):
    other = tile + 1 if tile % 2 == parity else tile - 1
    return other if 0 <= other < count else tile


def far_partner(tile, base, count):
    other = ((tile - base) ^ 2) + base if tile >= base else tile
    return other if 0 <= other < count else tile


def paired(value, partners):
    width = lax.axis_size("dp")
    pairs = []
    for tile, other in enumerate(partners):
        for sample in range(width):
            moved = sample ^ 1 if other == tile and width % 2 == 0 else sample
            pairs.append((tile * width + sample, other * width + moved))
    return lax.ppermute(value, ("seq", "dp"), pairs)


def exchanged(value, parity):
    count = lax.axis_size("seq")
    return paired(value, [partner(tile, parity, count) for tile in range(count)])


def far_partners(count):
    both = [[far_partner(tile, base, count) for tile in range(count)] for base in (0, 2)]
    return [partners for partners in both if partners != list(range(count))]


def after(value, *others):
    return lax.optimization_barrier((value, *others))[0]


def turned(value, step):
    count = lax.axis_size("pipe")
    return lax.ppermute(value, "pipe", [(i, (i + step) % count) for i in range(count)])


def total_over(value, axis, *late):
    count = lax.axis_size(axis)
    step = 1
    while step < count:
        other = lax.ppermute(value, axis, [(i, i ^ step) for i in range(count)])
        step *= 2
        value = value + (other if step < count else after(other, *late))
    return value


def local(queries, keys, values, grad_out, norm_gains, kv_tiles):
    query, key, value, grad = (a[0, 0, 0] for a in (queries, keys, values, grad_out))
    rows = query.shape[0]
    seq_count = lax.axis_size("seq")
    *home, (away_first, away_count, _) = GROUPS
    home_heads = sum(count for _, count, _ in home)
    fars = far_partners(seq_count)
    asks = [pack_call(query, grad, *home[0][:2])]
    away_pair = pack_call(after(key, asks[0]), value, away_first, away_count)
    for first, count, _ in home[1:]:
        asks.append(pack_call(after(query, away_pair), grad, first, count))
    asked_home = [(exchanged(ask, 0), exchanged(ask, 1)) for ask in asks]
    info = info_call(kv_tiles[0, 0, 0], after(norm_gains[0], asks[-1]))
    away_pair = turned(away_pair, -1)
    arrays = (query, grad, key, value)
    asked = ask_call(info, after(query, away_pair), grad, away_first, away_count)
    sums = None
    for (first, count, _), ask in zip(home, asked_home):
        told = info if sums is None else after(info, asked)
        sums = sums_call(told, arrays, *ask, first, count, home_heads, sums, len(fars))
    asked = turned(asked, -1)
    received = [exchanged(sums[0], 0), exchanged(sums[1], 1)]
    received += [paired(value, partners) for value, partners in zip(sums[2:], fars)]
    all_sums = (*sums[:2], *received)
    away_pair = after(away_pair, *received)
    away_gathered = (exchanged(away_pair, 0), exchanged(away_pair, 1))
    gains, pieces, places = [], [], []
    parts = None
    for (first, count, _), ask in zip(home, asked_home):
        told = after(info, asked) if gains else info
        pair_low, *parts, gain = grads_call(
            told, arrays, *ask, all_sums, first, count, home_heads, parts, len(fars)
        )
        if gains:
            pair_low = after(pair_low, *away_gathered)
        gains.append(gain[:2])
        pieces.append(turned(pair_low, -1))
        places.append((slice(1, 3), first * HEAD_DIM))
    to_even, to_odd = (after(part, *away_gathered) for part in parts[1:])
    answer = (after(parts[0], pieces[0]), exchanged(to_even, 0), exchanged(to_odd, 1))
    asked = after(asked, pair_low)
    operands = [(asked, 0, 0), (asked, 0, 1), (away_pair, 0, 0), (away_pair, 0, 1)]
    query_low, own, to_even, to_odd, gain = main_call(
        asked, operands, *away_gathered, away_count
    )
    gains.append(turned(after(gain[:2], pieces[len(home) - 1]), 1))
    returned = (exchanged(to_even, 0), exchanged(to_odd, 1))
    pieces.append(query_low)
    places.append((0, away_first * HEAD_DIM))
    answer = answer_call(info, query, *answer, 0, home_heads)
    pieces.append(turned(answer, -1))
    places.append((0, 0))
    out = last_call(
        asked, operands[2], own, *returned, pieces, tuple(places), away_first, away_count
    )
    summed = total_over(total_over(sum(gains), "dp"), "seq", out)
    tokens = lax.axis_size("dp") * seq_count * rows * HEADS
    return (out[None, :, None, None], (summed / math.sqrt(tokens))[None])


def solution(mesh):
    placed = (
        P("pipe", "dp", "seq", None, None),
        P("pipe", "dp", "seq", None, None),
        P("pipe", "dp", "seq", None, None),
        P("pipe", "dp", "seq", None, None),
        P("pipe", None, None),
        P("pipe", "dp", "seq", None),
    )
    return jax.shard_map(
        local,
        mesh=mesh,
        in_specs=placed,
        out_specs=(P("pipe", None, "dp", "seq", None, None), P("pipe", None, None)),
        check_vma=False,
    )
```

```python
import functools
import math

import jax
import jax.numpy as jnp
from jax import lax
from jax.experimental import pallas as pl
from jax.experimental.pallas import tpu as pltpu
from jax.sharding import PartitionSpec as P

HEADS = 12
HEAD_DIM = 128
EPSILON = 1e-06
ROOT_SCALE = HEAD_DIM ** (-0.5)
EXP2_SCALE = ROOT_SCALE * math.log2(math.e)
GROUPS = ((0, 3, False), (3, 3, False), (6, 6, True))
MAIN_VMEM = 20 * 1024 * 1024
SMALL_VMEM = 12 * 1024 * 1024
PACK_VMEM = 4 * 1024 * 1024
COST = pl.CostEstimate(flops=1, bytes_accessed=1, transcendentals=0)
LONG_COST = pl.CostEstimate(flops=2 * 10**10, bytes_accessed=1, transcendentals=0)
MAIN_COST = pl.CostEstimate(flops=6 * 10**9, bytes_accessed=1, transcendentals=0)


def dot_nt(left, right):
    return lax.dot_general(
        left, right, (((1,), (1,)), ((), ())), preferred_element_type=jnp.float32
    )


def dot_nn(left, right):
    return lax.dot_general(
        left, right, (((1,), (0,)), ((), ())), preferred_element_type=jnp.float32
    )


def dot_tn(left, right):
    return lax.dot_general(
        left, right, (((0,), (0,)), ((), ())), preferred_element_type=jnp.float32
    )


def normalize(source, gain):
    floats = source.astype(jnp.float32)
    scaled = lax.rsqrt(jnp.mean(floats * floats, axis=-1, keepdims=True) + EPSILON)
    normed = floats * scaled
    return floats, scaled, normed, (normed * gain).astype(jnp.bfloat16)


def norm_back(grad_hat, floats, scaled, gain):
    scaled_grad = gain * grad_hat
    projected = jnp.sum(scaled_grad * floats, axis=-1, keepdims=True)
    return scaled * scaled_grad - (scaled**3 * projected * (1.0 / HEAD_DIM)) * floats


def pack_kernel(first_in, second_in, out, sems, *, start, width):
    rows = first_in.shape[0]
    copies = [
        pltpu.make_async_copy(
            source.at[:, start : start + width], out.at[slot, :rows], sems.at[slot]
        )
        for slot, source in enumerate((first_in, second_in))
    ]
    for copy in copies:
        copy.start()
    for copy in copies:
        copy.wait()


def info_kernel(listed, gains, info):
    tile = lax.axis_index("seq")
    last = lax.axis_size("seq") - 1
    info[...] = jnp.zeros_like(info)
    info[0:2, :] = gains[...]
    for parity in range(2):
        other = jnp.where(lax.rem(tile, 2) == parity, tile + 1, tile - 1)
        found = listed[0] == other
        for slot in range(1, listed.shape[0]):
            found = found | (listed[slot] == other)
        found = found & (other >= 0) & (other <= last)
        live = jnp.where(found, 1.0, 0.0)
        info[2 + parity : 3 + parity, :] = jnp.full((1, HEAD_DIM), live, jnp.float32)


def ask_kernel(info, query, grad, out, sems, *, start, width):
    rows = query.shape[0]
    value = info[...]
    planes = []
    for _ in range(3):
        low = value.astype(jnp.bfloat16)
        planes.append(low)
        value = value - low.astype(jnp.float32)
    planes.append(jnp.zeros_like(planes[0]))
    out[0, rows : rows + 16, :HEAD_DIM] = jnp.concatenate(planes[:2], axis=0)
    out[1, rows : rows + 16, :HEAD_DIM] = jnp.concatenate(planes[2:], axis=0)
    pack_kernel(query, grad, out, sems, start=start, width=width)


def told_info(told):
    floats = told[...].astype(jnp.float32)
    return floats[0, 0:8] + floats[0, 8:16] + floats[1, 0:8]


def main_kernel(
    info, query, grad, key, value, pair_even, pair_odd, *rest
):
    query_out, own_out, even_out, odd_out, gain_out = rest[-5:]
    told = told_info(info) if len(info.shape) == 3 else info[...]
    query_gain = told[0:1]
    key_gain = told[1:2]
    rows = query.shape[0]
    lives = [jnp.concatenate([told[row : row + 1]] * (rows // HEAD_DIM), axis=1) for row in (2, 3)]
    query_floats, query_scale, query_normed, query_hat = normalize(query[...], query_gain)
    grad_in = grad[...]
    sides = (
        (key[...], value[...], None),
        (pair_even[0], pair_even[1], lives[0]),
        (pair_odd[0], pair_odd[1], lives[1]),
    )
    parts = []
    totals = None
    for key_in, value_in, live in sides:
        _, _, key_normed, key_hat = normalize(key_in, key_gain)
        weights = jnp.exp2(dot_nt(key_hat, query_hat) * EXP2_SCALE)
        grad_probs = dot_nt(value_in, grad_in)
        weight_sum = jnp.sum(weights, axis=0, keepdims=True)
        cross_sum = jnp.sum(weights * grad_probs, axis=0, keepdims=True)
        if live is not None:
            weight_sum = weight_sum * live
            cross_sum = cross_sum * live
        totals = weight_sum if totals is None else totals + weight_sum
        crosses = cross_sum if live is None else crosses + cross_sum
        parts.append((key_normed, key_hat, weights, grad_probs, live))
    inverse = 1.0 / totals
    deltas = crosses * inverse
    query_grad_t = None
    key_gain_sum = None
    for (key_normed, key_hat, weights, grad_probs, live), out in zip(
        parts, (own_out, even_out, odd_out)
    ):
        probs = weights * (inverse if live is None else inverse * live)
        dscores = (probs * (grad_probs - deltas)).astype(jnp.bfloat16)
        key_part = dot_nn(dscores, query_hat) * ROOT_SCALE
        value_part = dot_nn(probs.astype(jnp.bfloat16), grad_in)
        out[0] = key_part.astype(out.dtype)
        out[1] = value_part.astype(out.dtype)
        gain_part = jnp.sum(key_part * key_normed, axis=0, keepdims=True)
        key_gain_sum = gain_part if key_gain_sum is None else key_gain_sum + gain_part
        query_part = dot_tn(key_hat, dscores)
        query_grad_t = query_part if query_grad_t is None else query_grad_t + query_part
    query_grad = query_grad_t.T * ROOT_SCALE
    query_out[...] = norm_back(query_grad, query_floats, query_scale, query_gain).astype(
        query_out.dtype
    )
    query_gain_sum = jnp.sum(query_grad * query_normed, axis=0, keepdims=True)

    @pl.when(pl.program_id(0) == 0)
    def _():
        gain_out[...] = jnp.zeros_like(gain_out)

    gain_out[0:1, :] += query_gain_sum
    gain_out[1:2, :] += key_gain_sum


def tile_sums(key_hat, value_in, query_hat, grad_in):
    weights = jnp.exp2(dot_nt(key_hat, query_hat) * EXP2_SCALE)
    grad_probs = dot_nt(value_in, grad_in)
    return weights, grad_probs


def wide_lives(told, rows):
    return [jnp.concatenate([told[row : row + 1]] * (rows // HEAD_DIM), axis=1) for row in (2, 3)]


def near_is_even():
    place = lax.rem(lax.axis_index("seq"), 4)
    return (place == 0) | (place == 3)


def sums_kernel(info, query, grad, key, value, pair_even, pair_odd, *rest, far_count):
    outs = rest[-2 - far_count :]
    told = info[...]
    _, _, _, key_hat = normalize(key[...], told[1:2])
    value_in = value[...]
    rows = []
    for query_in, grad_in in (
        (query[...], grad[...]), (pair_even[0], pair_even[1]), (pair_odd[0], pair_odd[1])
    ):
        _, _, _, query_hat = normalize(query_in, told[0:1])
        weights, grad_probs = tile_sums(key_hat, value_in, query_hat, grad_in)
        rows.append(
            [
                jnp.sum(weights, axis=0, keepdims=True),
                jnp.sum(weights * grad_probs, axis=0, keepdims=True),
            ]
        )
    own, even, odd = rows
    tail = wide_lives(told, query.shape[0])
    blank = jnp.zeros_like(tail[0])
    outs[0][...] = jnp.concatenate([*own, *even, *tail, blank, blank], axis=0)
    outs[1][...] = jnp.concatenate([*own, *odd, *tail, blank, blank], axis=0)
    near = near_is_even()
    for index, out in enumerate(outs[2:]):
        first, second = (even, odd) if index == 0 else (odd, even)
        chosen = [jnp.where(near, one, two) for one, two in zip(first, second)]
        out[...] = jnp.concatenate([*chosen, *[blank] * 6], axis=0)


def grads_kernel(
    info, query, grad, key, value, pair_even, pair_odd,
    sent_even, sent_odd, from_even, from_odd, *rest, far_count,
):
    fars = [far[0:2, :] for far in rest[:far_count]]
    pair_out, own_out, even_out, odd_out, gain_out = rest[-5:]
    told = info[...]
    near = near_is_even()
    if far_count == 2:
        far_even = jnp.where(near, fars[0], fars[1])
        far_odd = jnp.where(near, fars[1], fars[0])
    elif far_count == 1:
        far_even = jnp.where(near, fars[0], jnp.zeros_like(fars[0]))
        far_odd = jnp.where(near, jnp.zeros_like(fars[0]), fars[0])
    else:
        far_even = far_odd = jnp.zeros_like(from_even[0:2, :])
    own_sums = (
        sent_even[0:2, :]
        + sent_even[4:5, :] * from_even[2:4, :]
        + sent_even[5:6, :] * from_odd[2:4, :]
    )
    even_sums = (
        from_even[0:2, :] + from_even[4:5, :] * sent_even[2:4, :] + from_even[5:6, :] * far_even
    )
    odd_sums = (
        from_odd[0:2, :] + from_odd[5:6, :] * sent_odd[2:4, :] + from_odd[4:5, :] * far_odd
    )
    key_floats, key_scale, key_normed, key_hat = normalize(key[...], told[1:2])
    value_in = value[...]
    key_grad = value_grad = query_gain_sum = None
    for query_in, grad_in, sums, live, out in (
        (query[...], grad[...], own_sums, None, own_out),
        (pair_even[0], pair_even[1], even_sums, from_even[4:5, :], even_out),
        (pair_odd[0], pair_odd[1], odd_sums, from_odd[5:6, :], odd_out),
    ):
        _, _, query_normed, query_hat = normalize(query_in, told[0:1])
        weights, grad_probs = tile_sums(key_hat, value_in, query_hat, grad_in)
        inverse = 1.0 / sums[0:1]
        deltas = sums[1:2] * inverse
        probs = weights * (inverse if live is None else inverse * live)
        dscores = (probs * (grad_probs - deltas)).astype(jnp.bfloat16)
        key_part = dot_nn(dscores, query_hat)
        value_part = dot_nn(probs.astype(jnp.bfloat16), grad_in)
        query_part = dot_tn(key_hat, dscores).T * ROOT_SCALE
        out[...] = query_part.astype(out.dtype)
        gain_part = jnp.sum(query_part * query_normed, axis=0, keepdims=True)
        key_grad = key_part if key_grad is None else key_grad + key_part
        value_grad = value_part if value_grad is None else value_grad + value_part
        query_gain_sum = gain_part if query_gain_sum is None else query_gain_sum + gain_part
    key_grad = key_grad * ROOT_SCALE
    key_back = norm_back(key_grad, key_floats, key_scale, told[1:2])
    pair_out[0] = key_back.astype(pair_out.dtype)
    pair_out[1] = value_grad.astype(pair_out.dtype)

    @pl.when(pl.program_id(0) == 0)
    def _():
        gain_out[...] = jnp.zeros_like(gain_out)

    gain_out[0:1, :] += query_gain_sum
    gain_out[1:2, :] += jnp.sum(key_grad * key_normed, axis=0, keepdims=True)


def answer_kernel(info, query, own, from_even, from_odd, out):
    gain = info[0:1, :]
    floats, scaled, _, _ = normalize(query[...], gain)
    total = own[...] + from_even[...].astype(jnp.float32) + from_odd[...].astype(jnp.float32)
    out[...] = norm_back(total, floats, scaled, gain).astype(out.dtype)


def finished(info, key, own, from_even, from_odd):
    told = told_info(info) if len(info.shape) == 3 else info[...]
    key_gain = told[1:2]
    key_floats, key_scale, _, _ = normalize(key[...], key_gain)
    key_grad = own[0] + from_even[0].astype(jnp.float32) + from_odd[0].astype(jnp.float32)
    value_grad = own[1] + from_even[1].astype(jnp.float32) + from_odd[1].astype(jnp.float32)
    return norm_back(key_grad, key_floats, key_scale, key_gain), value_grad


def last_kernel(info, key, own, from_even, from_odd, *rest, places, first, count):
    amount = len(places)
    pieces, (out, held) = rest[:amount], rest[amount : amount + 2]
    staged, (load_sems, store_sems) = rest[amount + 2 : -2], rest[-2:]
    head = pl.program_id(0)
    loads = [
        pltpu.make_async_copy(piece, stage, load_sems.at[slot])
        for slot, (piece, stage) in enumerate(zip(pieces, staged))
    ]
    stores = [
        pltpu.make_async_copy(
            stage, out.at[planes, :, start : start + stage.shape[-1]], store_sems.at[slot]
        )
        for slot, (stage, (planes, start)) in enumerate(zip(staged, places))
    ]

    def head_copy(index):
        start = pl.multiple_of((first + index) * HEAD_DIM, HEAD_DIM)
        return pltpu.make_async_copy(
            held.at[index],
            out.at[pl.ds(1, 2), :, pl.ds(start, HEAD_DIM)],
            store_sems.at[amount + index],
        )

    @pl.when(head == 0)
    def _():
        for load in loads:
            load.start()

    @pl.when(head == min(1, count - 1))
    def _():
        for load, store in zip(loads, stores):
            load.wait()
            store.start()

    key_grad, value_grad = finished(info, key, own, from_even, from_odd)
    held[head, 0] = key_grad.astype(held.dtype)
    held[head, 1] = value_grad.astype(held.dtype)
    head_copy(head).start()

    @pl.when(head == count - 1)
    def _():
        for store in stores:
            store.wait()
        for index in range(count):
            head_copy(index).wait()


def head_block(rows, first, slot=None):
    if slot is None:
        return pl.BlockSpec((rows, HEAD_DIM), lambda head: (0, first + head))
    return pl.BlockSpec((None, rows, HEAD_DIM), lambda head: (slot, 0, first + head))


def pair_block(rows, first=0):
    return pl.BlockSpec((2, rows, HEAD_DIM), lambda head: (0, 0, first + head))


def whole_block(shape):
    return pl.BlockSpec(shape, lambda head: (0,) * len(shape))


def pack_params(limit):
    return dict(
        scratch_shapes=[pltpu.SemaphoreType.DMA((2,))],
        compiler_params=pltpu.CompilerParams(vmem_limit_bytes=limit),
        cost_estimate=COST,
    )


def pack_call(first_in, second_in, first, count, limit=PACK_VMEM):
    rows = first_in.shape[0]
    width = count * HEAD_DIM
    return pl.pallas_call(
        functools.partial(pack_kernel, start=first * HEAD_DIM, width=width),
        grid=(1,),
        in_specs=[pl.BlockSpec(memory_space=pl.ANY)] * 2,
        out_specs=whole_block((2, rows, width)),
        out_shape=jax.ShapeDtypeStruct((2, rows, width), jnp.bfloat16),
        **pack_params(limit),
    )(first_in, second_in)


def ask_call(info, query, grad, first, count):
    rows = query.shape[0]
    width = count * HEAD_DIM
    return pl.pallas_call(
        functools.partial(ask_kernel, start=first * HEAD_DIM, width=width),
        grid=(1,),
        in_specs=[whole_block(info.shape)] + [pl.BlockSpec(memory_space=pl.ANY)] * 2,
        out_specs=whole_block((2, rows + 16, width)),
        out_shape=jax.ShapeDtypeStruct((2, rows + 16, width), jnp.bfloat16),
        **pack_params(PACK_VMEM),
    )(info, query, grad)


def info_call(listed, gains):
    return pl.pallas_call(
        info_kernel,
        in_specs=[pl.BlockSpec(memory_space=pltpu.SMEM), pl.BlockSpec(memory_space=pltpu.VMEM)],
        out_specs=pl.BlockSpec(memory_space=pltpu.VMEM),
        out_shape=jax.ShapeDtypeStruct((8, HEAD_DIM), jnp.float32),
        compiler_params=pltpu.CompilerParams(vmem_limit_bytes=PACK_VMEM),
        cost_estimate=LONG_COST,
    )(listed, gains)


def info_block(info):
    if info.ndim == 2:
        return whole_block(info.shape)
    below = info.shape[1] // 16 - 1
    return pl.BlockSpec((2, 16, HEAD_DIM), lambda head: (0, below, 0))


def main_call(info, operands, pair_even, pair_odd, count):
    rows = pair_even.shape[1]
    lanes = count * HEAD_DIM
    return pl.pallas_call(
        main_kernel,
        grid=(count,),
        in_specs=[info_block(info)]
        + [head_block(rows, first, slot) for _, first, slot in operands]
        + [pair_block(rows)] * 2,
        out_specs=[head_block(rows, 0)] + [pair_block(rows)] * 3 + [whole_block((8, HEAD_DIM))],
        out_shape=[
            jax.ShapeDtypeStruct((rows, lanes), jnp.bfloat16),
            jax.ShapeDtypeStruct((2, rows, lanes), jnp.float32),
            jax.ShapeDtypeStruct((2, rows, lanes), jnp.bfloat16),
            jax.ShapeDtypeStruct((2, rows, lanes), jnp.bfloat16),
            jax.ShapeDtypeStruct((8, HEAD_DIM), jnp.float32),
        ],
        compiler_params=pltpu.CompilerParams(vmem_limit_bytes=MAIN_VMEM),
        cost_estimate=MAIN_COST,
    )(info, *[array for array, _, _ in operands], pair_even, pair_odd)


def row_block(rows, first):
    return pl.BlockSpec((8, rows), lambda head: (first + head, 0))


def sums_call(info, arrays, pair_even, pair_odd, first, count, heads, earlier, far_count):
    rows = pair_even.shape[1]
    amount = 2 + far_count
    earlier = [] if earlier is None else earlier
    return pl.pallas_call(
        functools.partial(sums_kernel, far_count=far_count),
        grid=(count,),
        in_specs=[info_block(info)]
        + [head_block(rows, first)] * 4
        + [pair_block(rows)] * 2
        + [pl.BlockSpec(memory_space=pl.ANY)] * len(earlier),
        out_specs=[row_block(rows, first)] * amount,
        out_shape=[jax.ShapeDtypeStruct((8 * heads, rows), jnp.float32)] * amount,
        input_output_aliases={7 + index: index for index in range(len(earlier))},
        compiler_params=pltpu.CompilerParams(vmem_limit_bytes=MAIN_VMEM),
        cost_estimate=MAIN_COST,
    )(info, *arrays, pair_even, pair_odd, *earlier)


def grads_call(info, arrays, pair_even, pair_odd, sums, first, count, heads, earlier, far_count):
    rows = pair_even.shape[1]
    lanes = heads * HEAD_DIM
    earlier = [] if earlier is None else earlier
    place = 7 + len(sums)
    return pl.pallas_call(
        functools.partial(grads_kernel, far_count=far_count),
        grid=(count,),
        in_specs=[info_block(info)]
        + [head_block(rows, first)] * 4
        + [pair_block(rows)] * 2
        + [row_block(rows, first)] * len(sums)
        + [pl.BlockSpec(memory_space=pl.ANY)] * len(earlier),
        out_specs=[pair_block(rows)] + [head_block(rows, first)] * 3 + [whole_block((8, HEAD_DIM))],
        out_shape=[
            jax.ShapeDtypeStruct((2, rows, count * HEAD_DIM), jnp.bfloat16),
            jax.ShapeDtypeStruct((rows, lanes), jnp.float32),
            jax.ShapeDtypeStruct((rows, lanes), jnp.bfloat16),
            jax.ShapeDtypeStruct((rows, lanes), jnp.bfloat16),
            jax.ShapeDtypeStruct((8, HEAD_DIM), jnp.float32),
        ],
        input_output_aliases={place + index: 1 + index for index in range(len(earlier))},
        compiler_params=pltpu.CompilerParams(vmem_limit_bytes=MAIN_VMEM),
        cost_estimate=MAIN_COST,
    )(info, *arrays, pair_even, pair_odd, *sums, *earlier)


def answer_call(info, query, own, from_even, from_odd, first, count):
    rows = own.shape[0]
    return pl.pallas_call(
        answer_kernel,
        grid=(count,),
        in_specs=[info_block(info), head_block(rows, first)] + [head_block(rows, 0)] * 3,
        out_specs=head_block(rows, 0),
        out_shape=jax.ShapeDtypeStruct((rows, count * HEAD_DIM), jnp.bfloat16),
        compiler_params=pltpu.CompilerParams(vmem_limit_bytes=SMALL_VMEM),
        cost_estimate=LONG_COST,
    )(info, query, own, from_even, from_odd)


def last_call(info, key, own, from_even, from_odd, pieces, places, first, count):
    array, offset, slot = key
    rows = own.shape[1]
    anywhere = pl.BlockSpec(memory_space=pl.ANY)
    return pl.pallas_call(
        functools.partial(last_kernel, places=places, first=first, count=count),
        grid=(count,),
        in_specs=[info_block(info), head_block(rows, offset, slot)]
        + [pair_block(rows)] * 3
        + [anywhere] * len(pieces),
        out_specs=anywhere,
        out_shape=jax.ShapeDtypeStruct((3, rows, HEADS * HEAD_DIM), jnp.bfloat16),
        scratch_shapes=[
            pltpu.VMEM((count, 2, rows, HEAD_DIM), jnp.bfloat16),
            *[pltpu.VMEM(piece.shape, piece.dtype) for piece in pieces],
            pltpu.SemaphoreType.DMA((len(pieces),)),
            pltpu.SemaphoreType.DMA((len(pieces) + count,)),
        ],
        compiler_params=pltpu.CompilerParams(vmem_limit_bytes=SMALL_VMEM),
        cost_estimate=COST,
    )(info, array, own, from_even, from_odd, *pieces)


def partner(tile, parity, count):
    other = tile + 1 if tile % 2 == parity else tile - 1
    return other if 0 <= other < count else tile


def far_partner(tile, base, count):
    other = ((tile - base) ^ 2) + base if tile >= base else tile
    return other if 0 <= other < count else tile


def paired(value, partners):
    width = lax.axis_size("dp")
    pairs = []
    for tile, other in enumerate(partners):
        for sample in range(width):
            moved = sample ^ 1 if other == tile and width % 2 == 0 else sample
            pairs.append((tile * width + sample, other * width + moved))
    return lax.ppermute(value, ("seq", "dp"), pairs)


def exchanged(value, parity):
    count = lax.axis_size("seq")
    return paired(value, [partner(tile, parity, count) for tile in range(count)])


def far_partners(count):
    both = [[far_partner(tile, base, count) for tile in range(count)] for base in (0, 2)]
    return [partners for partners in both if partners != list(range(count))]


def after(value, *others):
    return lax.optimization_barrier((value, *others))[0]


def turned(value, step):
    count = lax.axis_size("pipe")
    return lax.ppermute(value, "pipe", [(i, (i + step) % count) for i in range(count)])


def total_over(value, axis, *late):
    count = lax.axis_size(axis)
    step = 1
    while step < count:
        other = lax.ppermute(value, axis, [(i, i ^ step) for i in range(count)])
        step *= 2
        value = value + (other if step < count else after(other, *late))
    return value


def local(queries, keys, values, grad_out, norm_gains, kv_tiles):
    query, key, value, grad = (a[0, 0, 0] for a in (queries, keys, values, grad_out))
    rows = query.shape[0]
    seq_count = lax.axis_size("seq")
    *home, (away_first, away_count, _) = GROUPS
    home_heads = sum(count for _, count, _ in home)
    fars = far_partners(seq_count)
    asks = [pack_call(query, grad, *home[0][:2])]
    away_pair = pack_call(after(key, asks[0]), value, away_first, away_count)
    for first, count, _ in home[1:]:
        asks.append(pack_call(after(query, away_pair), grad, first, count))
    asked_home = [(exchanged(ask, 0), exchanged(ask, 1)) for ask in asks]
    info = info_call(kv_tiles[0, 0, 0], after(norm_gains[0], asks[-1]))
    away_pair = turned(away_pair, -1)
    arrays = (query, grad, key, value)
    sums = None
    for (first, count, _), ask in zip(home, asked_home):
        sums = sums_call(info, arrays, *ask, first, count, home_heads, sums, len(fars))
    asked = ask_call(info, after(query, away_pair, sums[0]), grad, away_first, away_count)
    asked = turned(asked, -1)
    received = [exchanged(sums[0], 0), exchanged(sums[1], 1)]
    received += [paired(value, partners) for value, partners in zip(sums[2:], fars)]
    all_sums = (*sums[:2], *received)
    away_pair = after(away_pair, *received)
    away_gathered = (exchanged(away_pair, 0), exchanged(away_pair, 1))
    gains, pieces, places = [], [], []
    parts = None
    for (first, count, _), ask in zip(home[::-1], asked_home[::-1]):
        pair_low, *parts, gain = grads_call(
            info, arrays, *ask, all_sums, first, count, home_heads, parts, len(fars)
        )
        gains.append(gain[:2])
        pieces.append(turned(pair_low, -1))
        places.append((slice(1, 3), first * HEAD_DIM))
    answer = (parts[0], exchanged(parts[1], 0), exchanged(parts[2], 1))
    asked = after(asked, pair_low)
    operands = [(asked, 0, 0), (asked, 0, 1), (away_pair, 0, 0), (away_pair, 0, 1)]
    query_low, own, to_even, to_odd, gain = main_call(
        asked, operands, *away_gathered, away_count
    )
    gains.append(turned(after(gain[:2], *answer[1:]), 1))
    returned = (exchanged(to_even, 0), exchanged(to_odd, 1))
    pieces.append(query_low)
    places.append((0, away_first * HEAD_DIM))
    answer = answer_call(info, query, *answer, 0, home_heads)
    pieces.append(turned(after(answer, gains[-1], pieces[0]), -1))
    places.append((0, 0))
    out = last_call(
        asked, operands[2], own, *returned, pieces, tuple(places), away_first, away_count
    )
    summed = total_over(total_over(sum(gains), "dp"), "seq", out)
    tokens = lax.axis_size("dp") * seq_count * rows * HEADS
    return (out[None, :, None, None], (summed / math.sqrt(tokens))[None])


def solution(mesh):
    placed = (
        P("pipe", "dp", "seq", None, None),
        P("pipe", "dp", "seq", None, None),
        P("pipe", "dp", "seq", None, None),
        P("pipe", "dp", "seq", None, None),
        P("pipe", None, None),
        P("pipe", "dp", "seq", None),
    )
    return jax.shard_map(
        local,
        mesh=mesh,
        in_specs=placed,
        out_specs=(P("pipe", None, "dp", "seq", None, None), P("pipe", None, None)),
        check_vma=False,
    )
```

```python
import functools
import math

import jax
import jax.numpy as jnp
from jax import lax
from jax.experimental import pallas as pl
from jax.experimental.pallas import tpu as pltpu
from jax.sharding import PartitionSpec as P

HEADS = 12
HEAD_DIM = 128
EPSILON = 1e-06
ROOT_SCALE = HEAD_DIM ** (-0.5)
EXP2_SCALE = ROOT_SCALE * math.log2(math.e)
QUERY_GROUPS = ((0, 3), (3, 2))
KEY_GROUP = (5, 2)
AWAY_GROUP = (7, 5)
MAIN_VMEM = 20 * 1024 * 1024
SMALL_VMEM = 12 * 1024 * 1024
PACK_VMEM = 4 * 1024 * 1024
COST = pl.CostEstimate(flops=1, bytes_accessed=1, transcendentals=0)
LONG_COST = pl.CostEstimate(flops=2 * 10**10, bytes_accessed=1, transcendentals=0)
MAIN_COST = pl.CostEstimate(flops=6 * 10**9, bytes_accessed=1, transcendentals=0)


def dot_nt(left, right):
    return lax.dot_general(
        left, right, (((1,), (1,)), ((), ())), preferred_element_type=jnp.float32
    )


def dot_nn(left, right):
    return lax.dot_general(
        left, right, (((1,), (0,)), ((), ())), preferred_element_type=jnp.float32
    )


def dot_tn(left, right):
    return lax.dot_general(
        left, right, (((0,), (0,)), ((), ())), preferred_element_type=jnp.float32
    )


def normalize(source, gain):
    floats = source.astype(jnp.float32)
    scaled = lax.rsqrt(jnp.mean(floats * floats, axis=-1, keepdims=True) + EPSILON)
    normed = floats * scaled
    return floats, scaled, normed, (normed * gain).astype(jnp.bfloat16)


def norm_back(grad_hat, floats, scaled, gain):
    scaled_grad = gain * grad_hat
    projected = jnp.sum(scaled_grad * floats, axis=-1, keepdims=True)
    return scaled * scaled_grad - (scaled**3 * projected * (1.0 / HEAD_DIM)) * floats


def pack_kernel(first_in, second_in, out, sems, *, start, width):
    rows = first_in.shape[0]
    copies = [
        pltpu.make_async_copy(
            source.at[:, start : start + width], out.at[slot, :rows], sems.at[slot]
        )
        for slot, source in enumerate((first_in, second_in))
    ]
    for copy in copies:
        copy.start()
    for copy in copies:
        copy.wait()


def info_kernel(listed, gains, info):
    tile = lax.axis_index("seq")
    last = lax.axis_size("seq") - 1
    info[...] = jnp.zeros_like(info)
    info[0:2, :] = gains[...]
    for parity in range(2):
        other = jnp.where(lax.rem(tile, 2) == parity, tile + 1, tile - 1)
        found = listed[0] == other
        for slot in range(1, listed.shape[0]):
            found = found | (listed[slot] == other)
        found = found & (other >= 0) & (other <= last)
        live = jnp.where(found, 1.0, 0.0)
        info[2 + parity : 3 + parity, :] = jnp.full((1, HEAD_DIM), live, jnp.float32)


def ask_kernel(info, query, grad, out, sems, *, start, width):
    rows = query.shape[0]
    value = info[...]
    planes = []
    for _ in range(3):
        low = value.astype(jnp.bfloat16)
        planes.append(low)
        value = value - low.astype(jnp.float32)
    planes.append(jnp.zeros_like(planes[0]))
    out[0, rows : rows + 16, :HEAD_DIM] = jnp.concatenate(planes[:2], axis=0)
    out[1, rows : rows + 16, :HEAD_DIM] = jnp.concatenate(planes[2:], axis=0)
    pack_kernel(query, grad, out, sems, start=start, width=width)


def told_info(told):
    floats = told[...].astype(jnp.float32)
    return floats[0, 0:8] + floats[0, 8:16] + floats[1, 0:8]


def main_kernel(
    info, query, grad, key, value, pair_even, pair_odd, *rest
):
    query_out, own_out, even_out, odd_out, gain_out = rest[-5:]
    told = told_info(info) if len(info.shape) == 3 else info[...]
    query_gain = told[0:1]
    key_gain = told[1:2]
    rows = query.shape[0]
    lives = [jnp.concatenate([told[row : row + 1]] * (rows // HEAD_DIM), axis=1) for row in (2, 3)]
    query_floats, query_scale, query_normed, query_hat = normalize(query[...], query_gain)
    grad_in = grad[...]
    sides = (
        (key[...], value[...], None),
        (pair_even[0], pair_even[1], lives[0]),
        (pair_odd[0], pair_odd[1], lives[1]),
    )
    parts = []
    totals = None
    for key_in, value_in, live in sides:
        _, _, key_normed, key_hat = normalize(key_in, key_gain)
        weights = jnp.exp2(dot_nt(key_hat, query_hat) * EXP2_SCALE)
        grad_probs = dot_nt(value_in, grad_in)
        weight_sum = jnp.sum(weights, axis=0, keepdims=True)
        cross_sum = jnp.sum(weights * grad_probs, axis=0, keepdims=True)
        if live is not None:
            weight_sum = weight_sum * live
            cross_sum = cross_sum * live
        totals = weight_sum if totals is None else totals + weight_sum
        crosses = cross_sum if live is None else crosses + cross_sum
        parts.append((key_normed, key_hat, weights, grad_probs, live))
    inverse = 1.0 / totals
    deltas = crosses * inverse
    query_grad_t = None
    key_gain_sum = None
    for (key_normed, key_hat, weights, grad_probs, live), out in zip(
        parts, (own_out, even_out, odd_out)
    ):
        probs = weights * (inverse if live is None else inverse * live)
        dscores = (probs * (grad_probs - deltas)).astype(jnp.bfloat16)
        key_part = dot_nn(dscores, query_hat) * ROOT_SCALE
        value_part = dot_nn(probs.astype(jnp.bfloat16), grad_in)
        out[0] = key_part.astype(out.dtype)
        out[1] = value_part.astype(out.dtype)
        gain_part = jnp.sum(key_part * key_normed, axis=0, keepdims=True)
        key_gain_sum = gain_part if key_gain_sum is None else key_gain_sum + gain_part
        query_part = dot_tn(key_hat, dscores)
        query_grad_t = query_part if query_grad_t is None else query_grad_t + query_part
    query_grad = query_grad_t.T * ROOT_SCALE
    query_out[...] = norm_back(query_grad, query_floats, query_scale, query_gain).astype(
        query_out.dtype
    )
    query_gain_sum = jnp.sum(query_grad * query_normed, axis=0, keepdims=True)

    @pl.when(pl.program_id(0) == 0)
    def _():
        gain_out[...] = jnp.zeros_like(gain_out)

    gain_out[0:1, :] += query_gain_sum
    gain_out[1:2, :] += key_gain_sum


def tile_sums(key_hat, value_in, query_hat, grad_in):
    weights = jnp.exp2(dot_nt(key_hat, query_hat) * EXP2_SCALE)
    grad_probs = dot_nt(value_in, grad_in)
    return weights, grad_probs


def wide_lives(told, rows):
    return [jnp.concatenate([told[row : row + 1]] * (rows // HEAD_DIM), axis=1) for row in (2, 3)]


def near_is_even():
    place = lax.rem(lax.axis_index("seq"), 4)
    return (place == 0) | (place == 3)


def sums_kernel(info, query, grad, key, value, pair_even, pair_odd, *rest, far_count):
    outs = rest[-2 - far_count :]
    told = info[...]
    _, _, _, key_hat = normalize(key[...], told[1:2])
    value_in = value[...]
    rows = []
    for query_in, grad_in in (
        (query[...], grad[...]), (pair_even[0], pair_even[1]), (pair_odd[0], pair_odd[1])
    ):
        _, _, _, query_hat = normalize(query_in, told[0:1])
        weights, grad_probs = tile_sums(key_hat, value_in, query_hat, grad_in)
        rows.append(
            [
                jnp.sum(weights, axis=0, keepdims=True),
                jnp.sum(weights * grad_probs, axis=0, keepdims=True),
            ]
        )
    own, even, odd = rows
    tail = wide_lives(told, query.shape[0])
    blank = jnp.zeros_like(tail[0])
    outs[0][...] = jnp.concatenate([*own, *even, *tail, blank, blank], axis=0)
    outs[1][...] = jnp.concatenate([*own, *odd, *tail, blank, blank], axis=0)
    near = near_is_even()
    for index, out in enumerate(outs[2:]):
        first, second = (even, odd) if index == 0 else (odd, even)
        chosen = [jnp.where(near, one, two) for one, two in zip(first, second)]
        out[...] = jnp.concatenate([*chosen, *[blank] * 6], axis=0)


def grads_kernel(
    info, query, grad, key, value, pair_even, pair_odd,
    sent_even, sent_odd, from_even, from_odd, *rest, far_count,
):
    fars = [far[0:2, :] for far in rest[:far_count]]
    pair_out, own_out, even_out, odd_out, gain_out = rest[-5:]
    told = info[...]
    near = near_is_even()
    if far_count == 2:
        far_even = jnp.where(near, fars[0], fars[1])
        far_odd = jnp.where(near, fars[1], fars[0])
    elif far_count == 1:
        far_even = jnp.where(near, fars[0], jnp.zeros_like(fars[0]))
        far_odd = jnp.where(near, jnp.zeros_like(fars[0]), fars[0])
    else:
        far_even = far_odd = jnp.zeros_like(from_even[0:2, :])
    own_sums = (
        sent_even[0:2, :]
        + sent_even[4:5, :] * from_even[2:4, :]
        + sent_even[5:6, :] * from_odd[2:4, :]
    )
    even_sums = (
        from_even[0:2, :] + from_even[4:5, :] * sent_even[2:4, :] + from_even[5:6, :] * far_even
    )
    odd_sums = (
        from_odd[0:2, :] + from_odd[5:6, :] * sent_odd[2:4, :] + from_odd[4:5, :] * far_odd
    )
    key_floats, key_scale, key_normed, key_hat = normalize(key[...], told[1:2])
    value_in = value[...]
    key_grad = value_grad = query_gain_sum = None
    for query_in, grad_in, sums, live, out in (
        (query[...], grad[...], own_sums, None, own_out),
        (pair_even[0], pair_even[1], even_sums, from_even[4:5, :], even_out),
        (pair_odd[0], pair_odd[1], odd_sums, from_odd[5:6, :], odd_out),
    ):
        _, _, query_normed, query_hat = normalize(query_in, told[0:1])
        weights, grad_probs = tile_sums(key_hat, value_in, query_hat, grad_in)
        inverse = 1.0 / sums[0:1]
        deltas = sums[1:2] * inverse
        probs = weights * (inverse if live is None else inverse * live)
        dscores = (probs * (grad_probs - deltas)).astype(jnp.bfloat16)
        key_part = dot_nn(dscores, query_hat)
        value_part = dot_nn(probs.astype(jnp.bfloat16), grad_in)
        query_part = dot_tn(key_hat, dscores).T * ROOT_SCALE
        out[...] = query_part.astype(out.dtype)
        gain_part = jnp.sum(query_part * query_normed, axis=0, keepdims=True)
        key_grad = key_part if key_grad is None else key_grad + key_part
        value_grad = value_part if value_grad is None else value_grad + value_part
        query_gain_sum = gain_part if query_gain_sum is None else query_gain_sum + gain_part
    key_grad = key_grad * ROOT_SCALE
    key_back = norm_back(key_grad, key_floats, key_scale, told[1:2])
    pair_out[0] = key_back.astype(pair_out.dtype)
    pair_out[1] = value_grad.astype(pair_out.dtype)

    @pl.when(pl.program_id(0) == 0)
    def _():
        gain_out[...] = jnp.zeros_like(gain_out)

    gain_out[0:1, :] += query_gain_sum
    gain_out[1:2, :] += jnp.sum(key_grad * key_normed, axis=0, keepdims=True)


def answer_kernel(info, query, own, from_even, from_odd, _, out):
    gain = info[0:1, :]
    floats, scaled, _, _ = normalize(query[...], gain)
    total = own[...] + from_even[...].astype(jnp.float32) + from_odd[...].astype(jnp.float32)
    out[...] = norm_back(total, floats, scaled, gain).astype(out.dtype)


def finished(info, key, own, from_even, from_odd):
    told = told_info(info) if len(info.shape) == 3 else info[...]
    key_gain = told[1:2]
    key_floats, key_scale, _, _ = normalize(key[...], key_gain)
    key_grad = own[0] + from_even[0].astype(jnp.float32) + from_odd[0].astype(jnp.float32)
    value_grad = own[1] + from_even[1].astype(jnp.float32) + from_odd[1].astype(jnp.float32)
    return norm_back(key_grad, key_floats, key_scale, key_gain), value_grad


def finish_kernel(info, key, own, from_even, from_odd, out):
    key_grad, value_grad = finished(info, key, own, from_even, from_odd)
    out[0] = key_grad.astype(out.dtype)
    out[1] = value_grad.astype(out.dtype)


def last_kernel(info, key, own, from_even, from_odd, *rest, places, first, count):
    amount = len(places)
    pieces, (out, held) = rest[:amount], rest[amount : amount + 2]
    staged, (load_sems, store_sems) = rest[amount + 2 : -2], rest[-2:]
    head = pl.program_id(0)
    loads = [
        pltpu.make_async_copy(piece, stage, load_sems.at[slot])
        for slot, (piece, stage) in enumerate(zip(pieces, staged))
    ]
    stores = [
        pltpu.make_async_copy(
            stage, out.at[planes, :, start : start + stage.shape[-1]], store_sems.at[slot]
        )
        for slot, (stage, (planes, start)) in enumerate(zip(staged, places))
    ]

    def head_copy(index):
        start = pl.multiple_of((first + index) * HEAD_DIM, HEAD_DIM)
        return pltpu.make_async_copy(
            held.at[index],
            out.at[pl.ds(1, 2), :, pl.ds(start, HEAD_DIM)],
            store_sems.at[amount + index],
        )

    @pl.when(head == 0)
    def _():
        for load in loads:
            load.start()

    @pl.when(head == min(1, count - 1))
    def _():
        for load, store in zip(loads, stores):
            load.wait()
            store.start()

    key_grad, value_grad = finished(info, key, own, from_even, from_odd)
    held[head, 0] = key_grad.astype(held.dtype)
    held[head, 1] = value_grad.astype(held.dtype)
    head_copy(head).start()

    @pl.when(head == count - 1)
    def _():
        for store in stores:
            store.wait()
        for index in range(count):
            head_copy(index).wait()


def head_block(rows, first, slot=None):
    if slot is None:
        return pl.BlockSpec((rows, HEAD_DIM), lambda head: (0, first + head))
    return pl.BlockSpec((None, rows, HEAD_DIM), lambda head: (slot, 0, first + head))


def pair_block(rows, first=0):
    return pl.BlockSpec((2, rows, HEAD_DIM), lambda head: (0, 0, first + head))


def whole_block(shape):
    return pl.BlockSpec(shape, lambda head: (0,) * len(shape))


def pack_params(limit):
    return dict(
        scratch_shapes=[pltpu.SemaphoreType.DMA((2,))],
        compiler_params=pltpu.CompilerParams(vmem_limit_bytes=limit),
        cost_estimate=COST,
    )


def pack_call(first_in, second_in, first, count, limit=PACK_VMEM):
    rows = first_in.shape[0]
    width = count * HEAD_DIM
    return pl.pallas_call(
        functools.partial(pack_kernel, start=first * HEAD_DIM, width=width),
        grid=(1,),
        in_specs=[pl.BlockSpec(memory_space=pl.ANY)] * 2,
        out_specs=whole_block((2, rows, width)),
        out_shape=jax.ShapeDtypeStruct((2, rows, width), jnp.bfloat16),
        **pack_params(limit),
    )(first_in, second_in)


def ask_call(info, query, grad, first, count):
    rows = query.shape[0]
    width = count * HEAD_DIM
    return pl.pallas_call(
        functools.partial(ask_kernel, start=first * HEAD_DIM, width=width),
        grid=(1,),
        in_specs=[whole_block(info.shape)] + [pl.BlockSpec(memory_space=pl.ANY)] * 2,
        out_specs=whole_block((2, rows + 16, width)),
        out_shape=jax.ShapeDtypeStruct((2, rows + 16, width), jnp.bfloat16),
        **pack_params(PACK_VMEM),
    )(info, query, grad)


def info_call(listed, gains):
    return pl.pallas_call(
        info_kernel,
        in_specs=[pl.BlockSpec(memory_space=pltpu.SMEM), pl.BlockSpec(memory_space=pltpu.VMEM)],
        out_specs=pl.BlockSpec(memory_space=pltpu.VMEM),
        out_shape=jax.ShapeDtypeStruct((8, HEAD_DIM), jnp.float32),
        compiler_params=pltpu.CompilerParams(vmem_limit_bytes=PACK_VMEM),
        cost_estimate=LONG_COST,
    )(listed, gains)


def info_block(info):
    if info.ndim == 2:
        return whole_block(info.shape)
    below = info.shape[1] // 16 - 1
    return pl.BlockSpec((2, 16, HEAD_DIM), lambda head: (0, below, 0))


def main_call(info, operands, pair_even, pair_odd, count, heads, place):
    rows = pair_even.shape[1]
    lanes = count * HEAD_DIM
    return pl.pallas_call(
        main_kernel,
        grid=(count,),
        in_specs=[info_block(info)]
        + [head_block(rows, first, slot) for _, first, slot in operands]
        + [pair_block(rows)] * 2,
        out_specs=[head_block(rows, place)] + [pair_block(rows)] * 3 + [whole_block((8, HEAD_DIM))],
        out_shape=[
            jax.ShapeDtypeStruct((rows, heads * HEAD_DIM), jnp.bfloat16),
            jax.ShapeDtypeStruct((2, rows, lanes), jnp.float32),
            jax.ShapeDtypeStruct((2, rows, lanes), jnp.bfloat16),
            jax.ShapeDtypeStruct((2, rows, lanes), jnp.bfloat16),
            jax.ShapeDtypeStruct((8, HEAD_DIM), jnp.float32),
        ],
        compiler_params=pltpu.CompilerParams(vmem_limit_bytes=MAIN_VMEM),
        cost_estimate=MAIN_COST,
    )(info, *[array for array, _, _ in operands], pair_even, pair_odd)


def finish_call(info, key, own, from_even, from_odd, count):
    array, first, slot = key
    rows = own.shape[1]
    return pl.pallas_call(
        finish_kernel,
        grid=(count,),
        in_specs=[info_block(info), head_block(rows, first, slot)] + [pair_block(rows)] * 3,
        out_specs=pair_block(rows),
        out_shape=jax.ShapeDtypeStruct((2, rows, count * HEAD_DIM), jnp.bfloat16),
        compiler_params=pltpu.CompilerParams(vmem_limit_bytes=SMALL_VMEM),
        cost_estimate=COST,
    )(info, array, own, from_even, from_odd)


def row_block(rows, first):
    return pl.BlockSpec((8, rows), lambda head: (first + head, 0))


def sums_call(info, arrays, pair_even, pair_odd, first, count, heads, earlier, far_count):
    rows = pair_even.shape[1]
    amount = 2 + far_count
    earlier = [] if earlier is None else earlier
    return pl.pallas_call(
        functools.partial(sums_kernel, far_count=far_count),
        grid=(count,),
        in_specs=[info_block(info)]
        + [head_block(rows, first)] * 4
        + [pair_block(rows)] * 2
        + [pl.BlockSpec(memory_space=pl.ANY)] * len(earlier),
        out_specs=[row_block(rows, first)] * amount,
        out_shape=[jax.ShapeDtypeStruct((8 * heads, rows), jnp.float32)] * amount,
        input_output_aliases={7 + index: index for index in range(len(earlier))},
        compiler_params=pltpu.CompilerParams(vmem_limit_bytes=MAIN_VMEM),
        cost_estimate=MAIN_COST,
    )(info, *arrays, pair_even, pair_odd, *earlier)


def grads_call(info, arrays, pair_even, pair_odd, sums, first, count, heads, earlier, far_count):
    rows = pair_even.shape[1]
    lanes = heads * HEAD_DIM
    earlier = [] if earlier is None else earlier
    place = 7 + len(sums)
    return pl.pallas_call(
        functools.partial(grads_kernel, far_count=far_count),
        grid=(count,),
        in_specs=[info_block(info)]
        + [head_block(rows, first)] * 4
        + [pair_block(rows)] * 2
        + [row_block(rows, first)] * len(sums)
        + [pl.BlockSpec(memory_space=pl.ANY)] * len(earlier),
        out_specs=[pair_block(rows, first)]
        + [head_block(rows, first)] * 3
        + [whole_block((8, HEAD_DIM))],
        out_shape=[
            jax.ShapeDtypeStruct((2, rows, lanes), jnp.bfloat16),
            jax.ShapeDtypeStruct((rows, lanes), jnp.float32),
            jax.ShapeDtypeStruct((rows, lanes), jnp.bfloat16),
            jax.ShapeDtypeStruct((rows, lanes), jnp.bfloat16),
            jax.ShapeDtypeStruct((8, HEAD_DIM), jnp.float32),
        ],
        input_output_aliases={place + index: index for index in range(len(earlier))},
        compiler_params=pltpu.CompilerParams(vmem_limit_bytes=MAIN_VMEM),
        cost_estimate=MAIN_COST,
    )(info, *arrays, pair_even, pair_odd, *sums, *earlier)


def answer_call(info, query, own, from_even, from_odd, low):
    rows, lanes = own.shape
    return pl.pallas_call(
        answer_kernel,
        grid=(lanes // HEAD_DIM,),
        in_specs=[info_block(info)]
        + [head_block(rows, 0)] * 4
        + [pl.BlockSpec(memory_space=pl.ANY)],
        out_specs=head_block(rows, 0),
        out_shape=jax.ShapeDtypeStruct(low.shape, low.dtype),
        input_output_aliases={5: 0},
        compiler_params=pltpu.CompilerParams(vmem_limit_bytes=SMALL_VMEM),
        cost_estimate=LONG_COST,
    )(info, query, own, from_even, from_odd, low)


def last_call(info, key, own, from_even, from_odd, pieces, places, first, count):
    array, offset, slot = key
    rows = own.shape[1]
    anywhere = pl.BlockSpec(memory_space=pl.ANY)
    return pl.pallas_call(
        functools.partial(last_kernel, places=places, first=first, count=count),
        grid=(count,),
        in_specs=[info_block(info), head_block(rows, offset, slot)]
        + [pair_block(rows)] * 3
        + [anywhere] * len(pieces),
        out_specs=anywhere,
        out_shape=jax.ShapeDtypeStruct((3, rows, HEADS * HEAD_DIM), jnp.bfloat16),
        scratch_shapes=[
            pltpu.VMEM((count, 2, rows, HEAD_DIM), jnp.bfloat16),
            *[pltpu.VMEM(piece.shape, piece.dtype) for piece in pieces],
            pltpu.SemaphoreType.DMA((len(pieces),)),
            pltpu.SemaphoreType.DMA((len(pieces) + count,)),
        ],
        compiler_params=pltpu.CompilerParams(vmem_limit_bytes=SMALL_VMEM),
        cost_estimate=COST,
    )(info, array, own, from_even, from_odd, *pieces)


def partner(tile, parity, count):
    other = tile + 1 if tile % 2 == parity else tile - 1
    return other if 0 <= other < count else tile


def far_partner(tile, base, count):
    other = ((tile - base) ^ 2) + base if tile >= base else tile
    return other if 0 <= other < count else tile


def paired(value, partners):
    width = lax.axis_size("dp")
    pairs = []
    for tile, other in enumerate(partners):
        for sample in range(width):
            moved = sample ^ 1 if other == tile and width % 2 == 0 else sample
            pairs.append((tile * width + sample, other * width + moved))
    return lax.ppermute(value, ("seq", "dp"), pairs)


def exchanged(value, parity):
    count = lax.axis_size("seq")
    return paired(value, [partner(tile, parity, count) for tile in range(count)])


def far_partners(count):
    both = [[far_partner(tile, base, count) for tile in range(count)] for base in (0, 2)]
    return [partners for partners in both if partners != list(range(count))]


def after(value, *others):
    return lax.optimization_barrier((value, *others))[0]


def turned(value, step):
    count = lax.axis_size("pipe")
    return lax.ppermute(value, "pipe", [(i, (i + step) % count) for i in range(count)])


def total_over(value, axis, *late):
    count = lax.axis_size(axis)
    step = 1
    while step < count:
        other = lax.ppermute(value, axis, [(i, i ^ step) for i in range(count)])
        step *= 2
        value = value + (other if step < count else after(other, *late))
    return value


def local(queries, keys, values, grad_out, norm_gains, kv_tiles):
    query, key, value, grad = (a[0, 0, 0] for a in (queries, keys, values, grad_out))
    rows = query.shape[0]
    seq_count = lax.axis_size("seq")
    key_first, key_count = KEY_GROUP
    away_first, away_count = AWAY_GROUP
    fars = far_partners(seq_count)
    arrays = (query, grad, key, value)
    asks = [pack_call(query, grad, *QUERY_GROUPS[0])]
    away_pair = pack_call(after(key, asks[0]), value, away_first, away_count)
    for first, count in QUERY_GROUPS[1:]:
        asks.append(pack_call(after(query, away_pair), grad, first, count))
    told_pairs = [(exchanged(ask, 0), exchanged(ask, 1)) for ask in asks]
    key_pair = pack_call(after(key, asks[-1]), value, key_first, key_count)
    key_pair = after(key_pair, *told_pairs[0])
    key_pairs = (exchanged(key_pair, 0), exchanged(key_pair, 1))
    info = info_call(kv_tiles[0, 0, 0], after(norm_gains[0], asks[-1]))
    away_pair = turned(away_pair, -1)
    sums = None
    for (first, count), told in zip(QUERY_GROUPS, told_pairs):
        sums = sums_call(info, arrays, *told, first, count, key_first, sums, len(fars))
    received = [exchanged(sums[0], 0), exchanged(sums[1], 1)]
    received += [
        paired(after(value, away_pair), partners) for value, partners in zip(sums[2:], fars)
    ]
    all_sums = (*sums[:2], *received)
    asked = ask_call(info, after(query, away_pair, sums[0]), grad, away_first, away_count)
    asked = turned(asked, -1)
    away_sent = after(away_pair, *key_pairs)
    away_pairs = (exchanged(away_sent, 0), exchanged(away_sent, 1))
    gains, parts = [], None
    for (first, count), told in zip(QUERY_GROUPS, told_pairs):
        *parts, gain = grads_call(
            info, arrays, *told, all_sums, first, count, key_first, parts, len(fars)
        )
        gains.append(gain[:2])
    pair_low, own, to_even, to_odd = parts
    pieces = [turned(pair_low, -1)]
    places = [(slice(1, 3), 0)]
    answer = (own, exchanged(to_even, 0), exchanged(to_odd, 1))
    operands = [(array, key_first, None) for array in arrays]
    low, own, to_even, to_odd, gain = main_call(
        after(info, pair_low), operands, *key_pairs, key_count, away_first, key_first
    )
    gains.append(gain[:2])
    key_answer = (own, exchanged(to_even, 0), exchanged(to_odd, 1))
    operands = [(asked, 0, 0), (asked, 0, 1), (away_pair, 0, 0), (away_pair, 0, 1)]
    query_low, own, to_even, to_odd, gain = main_call(
        after(asked, low), operands, *away_pairs, away_count, away_count, 0
    )
    gains.append(turned(after(gain[:2], *answer[1:], pieces[0]), 1))
    returned = (exchanged(to_even, 0), exchanged(to_odd, 1))
    pieces.append(query_low)
    places.append((0, away_first * HEAD_DIM))
    low = answer_call(info, query, *answer, low)
    pieces.append(turned(after(low, gains[-1], pieces[0]), -1))
    places.append((0, 0))
    low = finish_call(after(info, pieces[0]), (key, key_first, None), *key_answer, key_count)
    pieces.append(turned(low, -1))
    places.append((slice(1, 3), key_first * HEAD_DIM))
    out = last_call(
        asked, operands[2], own, *returned, pieces, tuple(places), away_first, away_count
    )
    summed = total_over(total_over(sum(gains), "dp"), "seq", out)
    tokens = lax.axis_size("dp") * seq_count * rows * HEADS
    return (out[None, :, None, None], (summed / math.sqrt(tokens))[None])


def solution(mesh):
    placed = (
        P("pipe", "dp", "seq", None, None),
        P("pipe", "dp", "seq", None, None),
        P("pipe", "dp", "seq", None, None),
        P("pipe", "dp", "seq", None, None),
        P("pipe", None, None),
        P("pipe", "dp", "seq", None),
    )
    return jax.shard_map(
        local,
        mesh=mesh,
        in_specs=placed,
        out_specs=(P("pipe", None, "dp", "seq", None, None), P("pipe", None, None)),
        check_vma=False,
    )
```

```python
import functools
import math

import jax
import jax.numpy as jnp
from jax import lax
from jax.experimental import pallas as pl
from jax.experimental.pallas import tpu as pltpu
from jax.sharding import PartitionSpec as P

HEADS = 12
HEAD_DIM = 128
EPSILON = 1e-06
ROOT_SCALE = HEAD_DIM ** (-0.5)
EXP2_SCALE = ROOT_SCALE * math.log2(math.e)
QUERY_GROUPS = ((0, 3), (3, 2))
KEY_GROUP = (5, 2)
AWAY_GROUP = (7, 5)
MAIN_VMEM = 20 * 1024 * 1024
SMALL_VMEM = 12 * 1024 * 1024
PACK_VMEM = 4 * 1024 * 1024
COST = pl.CostEstimate(flops=1, bytes_accessed=1, transcendentals=0)
LONG_COST = pl.CostEstimate(flops=2 * 10**10, bytes_accessed=1, transcendentals=0)
MAIN_COST = pl.CostEstimate(flops=6 * 10**9, bytes_accessed=1, transcendentals=0)


def dot_nt(left, right):
    return lax.dot_general(
        left, right, (((1,), (1,)), ((), ())), preferred_element_type=jnp.float32
    )


def dot_nn(left, right):
    return lax.dot_general(
        left, right, (((1,), (0,)), ((), ())), preferred_element_type=jnp.float32
    )


def dot_tn(left, right):
    return lax.dot_general(
        left, right, (((0,), (0,)), ((), ())), preferred_element_type=jnp.float32
    )


def normalize(source, gain):
    floats = source.astype(jnp.float32)
    scaled = lax.rsqrt(jnp.mean(floats * floats, axis=-1, keepdims=True) + EPSILON)
    normed = floats * scaled
    return floats, scaled, normed, (normed * gain).astype(jnp.bfloat16)


def norm_back(grad_hat, floats, scaled, gain):
    scaled_grad = gain * grad_hat
    projected = jnp.sum(scaled_grad * floats, axis=-1, keepdims=True)
    return scaled * scaled_grad - (scaled**3 * projected * (1.0 / HEAD_DIM)) * floats


def pack_kernel(first_in, second_in, out, sems, *, start, width):
    rows = first_in.shape[0]
    copies = [
        pltpu.make_async_copy(
            source.at[:, start : start + width], out.at[slot, :rows], sems.at[slot]
        )
        for slot, source in enumerate((first_in, second_in))
    ]
    for copy in copies:
        copy.start()
    for copy in copies:
        copy.wait()


def info_kernel(listed, gains, info):
    tile = lax.axis_index("seq")
    last = lax.axis_size("seq") - 1
    info[...] = jnp.zeros_like(info)
    info[0:2, :] = gains[...]
    for parity in range(2):
        other = jnp.where(lax.rem(tile, 2) == parity, tile + 1, tile - 1)
        found = listed[0] == other
        for slot in range(1, listed.shape[0]):
            found = found | (listed[slot] == other)
        found = found & (other >= 0) & (other <= last)
        live = jnp.where(found, 1.0, 0.0)
        info[2 + parity : 3 + parity, :] = jnp.full((1, HEAD_DIM), live, jnp.float32)


def ask_kernel(info, query, grad, out, sems, *, start, width):
    rows = query.shape[0]
    value = info[...]
    planes = []
    for _ in range(3):
        low = value.astype(jnp.bfloat16)
        planes.append(low)
        value = value - low.astype(jnp.float32)
    planes.append(jnp.zeros_like(planes[0]))
    out[0, rows : rows + 16, :HEAD_DIM] = jnp.concatenate(planes[:2], axis=0)
    out[1, rows : rows + 16, :HEAD_DIM] = jnp.concatenate(planes[2:], axis=0)
    pack_kernel(query, grad, out, sems, start=start, width=width)


def told_info(told):
    floats = told[...].astype(jnp.float32)
    return floats[0, 0:8] + floats[0, 8:16] + floats[1, 0:8]


def main_kernel(
    info, query, grad, key, value, pair_even, pair_odd, *rest
):
    query_out, own_out, even_out, odd_out, gain_out = rest[-5:]
    told = told_info(info) if len(info.shape) == 3 else info[...]
    query_gain = told[0:1]
    key_gain = told[1:2]
    rows = query.shape[0]
    lives = [jnp.concatenate([told[row : row + 1]] * (rows // HEAD_DIM), axis=1) for row in (2, 3)]
    query_floats, query_scale, query_normed, query_hat = normalize(query[...], query_gain)
    grad_in = grad[...]
    sides = (
        (key[...], value[...], None),
        (pair_even[0], pair_even[1], lives[0]),
        (pair_odd[0], pair_odd[1], lives[1]),
    )
    parts = []
    totals = None
    for key_in, value_in, live in sides:
        _, _, key_normed, key_hat = normalize(key_in, key_gain)
        weights = jnp.exp2(dot_nt(key_hat, query_hat) * EXP2_SCALE)
        grad_probs = dot_nt(value_in, grad_in)
        weight_sum = jnp.sum(weights, axis=0, keepdims=True)
        cross_sum = jnp.sum(weights * grad_probs, axis=0, keepdims=True)
        if live is not None:
            weight_sum = weight_sum * live
            cross_sum = cross_sum * live
        totals = weight_sum if totals is None else totals + weight_sum
        crosses = cross_sum if live is None else crosses + cross_sum
        parts.append((key_normed, key_hat, weights, grad_probs, live))
    inverse = 1.0 / totals
    deltas = crosses * inverse
    query_grad_t = None
    key_gain_sum = None
    for (key_normed, key_hat, weights, grad_probs, live), out in zip(
        parts, (own_out, even_out, odd_out)
    ):
        probs = weights * (inverse if live is None else inverse * live)
        dscores = (probs * (grad_probs - deltas)).astype(jnp.bfloat16)
        key_part = dot_nn(dscores, query_hat) * ROOT_SCALE
        value_part = dot_nn(probs.astype(jnp.bfloat16), grad_in)
        out[0] = key_part.astype(out.dtype)
        out[1] = value_part.astype(out.dtype)
        gain_part = jnp.sum(key_part * key_normed, axis=0, keepdims=True)
        key_gain_sum = gain_part if key_gain_sum is None else key_gain_sum + gain_part
        query_part = dot_tn(key_hat, dscores)
        query_grad_t = query_part if query_grad_t is None else query_grad_t + query_part
    query_grad = query_grad_t.T * ROOT_SCALE
    query_out[...] = norm_back(query_grad, query_floats, query_scale, query_gain).astype(
        query_out.dtype
    )
    query_gain_sum = jnp.sum(query_grad * query_normed, axis=0, keepdims=True)

    @pl.when(pl.program_id(0) == 0)
    def _():
        gain_out[...] = jnp.zeros_like(gain_out)

    gain_out[0:1, :] += query_gain_sum
    gain_out[1:2, :] += key_gain_sum


def tile_sums(key_hat, value_in, query_hat, grad_in):
    weights = jnp.exp2(dot_nt(key_hat, query_hat) * EXP2_SCALE)
    grad_probs = dot_nt(value_in, grad_in)
    return weights, grad_probs


def wide_lives(told, rows):
    return [jnp.concatenate([told[row : row + 1]] * (rows // HEAD_DIM), axis=1) for row in (2, 3)]


def near_is_even():
    place = lax.rem(lax.axis_index("seq"), 4)
    return (place == 0) | (place == 3)


def sums_kernel(info, query, grad, key, value, pair_even, pair_odd, *rest, far_count):
    outs = rest[-2 - far_count :]
    told = info[...]
    _, _, _, key_hat = normalize(key[...], told[1:2])
    value_in = value[...]
    rows = []
    for query_in, grad_in in (
        (query[...], grad[...]), (pair_even[0], pair_even[1]), (pair_odd[0], pair_odd[1])
    ):
        _, _, _, query_hat = normalize(query_in, told[0:1])
        weights, grad_probs = tile_sums(key_hat, value_in, query_hat, grad_in)
        rows.append(
            [
                jnp.sum(weights, axis=0, keepdims=True),
                jnp.sum(weights * grad_probs, axis=0, keepdims=True),
            ]
        )
    own, even, odd = rows
    tail = wide_lives(told, query.shape[0])
    blank = jnp.zeros_like(tail[0])
    outs[0][...] = jnp.concatenate([*own, *even, *tail, blank, blank], axis=0)
    outs[1][...] = jnp.concatenate([*own, *odd, *tail, blank, blank], axis=0)
    near = near_is_even()
    for index, out in enumerate(outs[2:]):
        first, second = (even, odd) if index == 0 else (odd, even)
        chosen = [jnp.where(near, one, two) for one, two in zip(first, second)]
        out[...] = jnp.concatenate([*chosen, *[blank] * 6], axis=0)


def grads_kernel(
    info, query, grad, key, value, pair_even, pair_odd,
    sent_even, sent_odd, from_even, from_odd, *rest, far_count,
):
    fars = [far[0:2, :] for far in rest[:far_count]]
    pair_out, own_out, even_out, odd_out, gain_out = rest[-5:]
    told = info[...]
    near = near_is_even()
    if far_count == 2:
        far_even = jnp.where(near, fars[0], fars[1])
        far_odd = jnp.where(near, fars[1], fars[0])
    elif far_count == 1:
        far_even = jnp.where(near, fars[0], jnp.zeros_like(fars[0]))
        far_odd = jnp.where(near, jnp.zeros_like(fars[0]), fars[0])
    else:
        far_even = far_odd = jnp.zeros_like(from_even[0:2, :])
    own_sums = (
        sent_even[0:2, :]
        + sent_even[4:5, :] * from_even[2:4, :]
        + sent_even[5:6, :] * from_odd[2:4, :]
    )
    even_sums = (
        from_even[0:2, :] + from_even[4:5, :] * sent_even[2:4, :] + from_even[5:6, :] * far_even
    )
    odd_sums = (
        from_odd[0:2, :] + from_odd[5:6, :] * sent_odd[2:4, :] + from_odd[4:5, :] * far_odd
    )
    key_floats, key_scale, key_normed, key_hat = normalize(key[...], told[1:2])
    value_in = value[...]
    key_grad = value_grad = query_gain_sum = None
    for query_in, grad_in, sums, live, out in (
        (query[...], grad[...], own_sums, None, own_out),
        (pair_even[0], pair_even[1], even_sums, from_even[4:5, :], even_out),
        (pair_odd[0], pair_odd[1], odd_sums, from_odd[5:6, :], odd_out),
    ):
        _, _, query_normed, query_hat = normalize(query_in, told[0:1])
        weights, grad_probs = tile_sums(key_hat, value_in, query_hat, grad_in)
        inverse = 1.0 / sums[0:1]
        deltas = sums[1:2] * inverse
        probs = weights * (inverse if live is None else inverse * live)
        dscores = (probs * (grad_probs - deltas)).astype(jnp.bfloat16)
        key_part = dot_nn(dscores, query_hat)
        value_part = dot_nn(probs.astype(jnp.bfloat16), grad_in)
        query_part = dot_tn(key_hat, dscores).T * ROOT_SCALE
        out[...] = query_part.astype(out.dtype)
        gain_part = jnp.sum(query_part * query_normed, axis=0, keepdims=True)
        key_grad = key_part if key_grad is None else key_grad + key_part
        value_grad = value_part if value_grad is None else value_grad + value_part
        query_gain_sum = gain_part if query_gain_sum is None else query_gain_sum + gain_part
    key_grad = key_grad * ROOT_SCALE
    key_back = norm_back(key_grad, key_floats, key_scale, told[1:2])
    pair_out[0] = key_back.astype(pair_out.dtype)
    pair_out[1] = value_grad.astype(pair_out.dtype)

    @pl.when(pl.program_id(0) == 0)
    def _():
        gain_out[...] = jnp.zeros_like(gain_out)

    gain_out[0:1, :] += query_gain_sum
    gain_out[1:2, :] += jnp.sum(key_grad * key_normed, axis=0, keepdims=True)


def answer_kernel(info, query, own, from_even, from_odd, _, out):
    gain = info[0:1, :]
    floats, scaled, _, _ = normalize(query[...], gain)
    total = own[...] + from_even[...].astype(jnp.float32) + from_odd[...].astype(jnp.float32)
    out[...] = norm_back(total, floats, scaled, gain).astype(out.dtype)


def finished(info, key, own, from_even, from_odd):
    told = told_info(info) if len(info.shape) == 3 else info[...]
    key_gain = told[1:2]
    key_floats, key_scale, _, _ = normalize(key[...], key_gain)
    key_grad = own[0] + from_even[0].astype(jnp.float32) + from_odd[0].astype(jnp.float32)
    value_grad = own[1] + from_even[1].astype(jnp.float32) + from_odd[1].astype(jnp.float32)
    return norm_back(key_grad, key_floats, key_scale, key_gain), value_grad


def finish_kernel(info, key, own, from_even, from_odd, out):
    key_grad, value_grad = finished(info, key, own, from_even, from_odd)
    out[0] = key_grad.astype(out.dtype)
    out[1] = value_grad.astype(out.dtype)


def last_kernel(info, key, own, from_even, from_odd, *rest, places, first, count):
    amount = len(places)
    pieces, (out, held) = rest[:amount], rest[amount : amount + 2]
    staged, (load_sems, store_sems) = rest[amount + 2 : -2], rest[-2:]
    head = pl.program_id(0)
    loads = [
        pltpu.make_async_copy(piece, stage, load_sems.at[slot])
        for slot, (piece, stage) in enumerate(zip(pieces, staged))
    ]
    stores = [
        pltpu.make_async_copy(
            stage, out.at[planes, :, start : start + stage.shape[-1]], store_sems.at[slot]
        )
        for slot, (stage, (planes, start)) in enumerate(zip(staged, places))
    ]

    def head_copy(index):
        start = pl.multiple_of((first + index) * HEAD_DIM, HEAD_DIM)
        return pltpu.make_async_copy(
            held.at[index],
            out.at[pl.ds(1, 2), :, pl.ds(start, HEAD_DIM)],
            store_sems.at[amount + index],
        )

    @pl.when(head == 0)
    def _():
        for load in loads:
            load.start()

    @pl.when(head == min(1, count - 1))
    def _():
        for load, store in zip(loads, stores):
            load.wait()
            store.start()

    key_grad, value_grad = finished(info, key, own, from_even, from_odd)
    held[head, 0] = key_grad.astype(held.dtype)
    held[head, 1] = value_grad.astype(held.dtype)
    head_copy(head).start()

    @pl.when(head == count - 1)
    def _():
        for store in stores:
            store.wait()
        for index in range(count):
            head_copy(index).wait()


def head_block(rows, first, slot=None):
    if slot is None:
        return pl.BlockSpec((rows, HEAD_DIM), lambda head: (0, first + head))
    return pl.BlockSpec((None, rows, HEAD_DIM), lambda head: (slot, 0, first + head))


def pair_block(rows, first=0):
    return pl.BlockSpec((2, rows, HEAD_DIM), lambda head: (0, 0, first + head))


def whole_block(shape):
    return pl.BlockSpec(shape, lambda head: (0,) * len(shape))


def pack_params(limit):
    return dict(
        scratch_shapes=[pltpu.SemaphoreType.DMA((2,))],
        compiler_params=pltpu.CompilerParams(vmem_limit_bytes=limit),
        cost_estimate=COST,
    )


def pack_call(first_in, second_in, first, count, limit=PACK_VMEM):
    rows = first_in.shape[0]
    width = count * HEAD_DIM
    return pl.pallas_call(
        functools.partial(pack_kernel, start=first * HEAD_DIM, width=width),
        grid=(1,),
        in_specs=[pl.BlockSpec(memory_space=pl.ANY)] * 2,
        out_specs=whole_block((2, rows, width)),
        out_shape=jax.ShapeDtypeStruct((2, rows, width), jnp.bfloat16),
        **pack_params(limit),
    )(first_in, second_in)


def ask_call(info, query, grad, first, count):
    rows = query.shape[0]
    width = count * HEAD_DIM
    return pl.pallas_call(
        functools.partial(ask_kernel, start=first * HEAD_DIM, width=width),
        grid=(1,),
        in_specs=[whole_block(info.shape)] + [pl.BlockSpec(memory_space=pl.ANY)] * 2,
        out_specs=whole_block((2, rows + 16, width)),
        out_shape=jax.ShapeDtypeStruct((2, rows + 16, width), jnp.bfloat16),
        **pack_params(PACK_VMEM),
    )(info, query, grad)


def info_call(listed, gains):
    return pl.pallas_call(
        info_kernel,
        in_specs=[pl.BlockSpec(memory_space=pltpu.SMEM), pl.BlockSpec(memory_space=pltpu.VMEM)],
        out_specs=pl.BlockSpec(memory_space=pltpu.VMEM),
        out_shape=jax.ShapeDtypeStruct((8, HEAD_DIM), jnp.float32),
        compiler_params=pltpu.CompilerParams(vmem_limit_bytes=PACK_VMEM),
        cost_estimate=LONG_COST,
    )(listed, gains)


def info_block(info):
    if info.ndim == 2:
        return whole_block(info.shape)
    below = info.shape[1] // 16 - 1
    return pl.BlockSpec((2, 16, HEAD_DIM), lambda head: (0, below, 0))


def main_call(info, operands, pair_even, pair_odd, count, heads, place):
    rows = pair_even.shape[1]
    lanes = count * HEAD_DIM
    return pl.pallas_call(
        main_kernel,
        grid=(count,),
        in_specs=[info_block(info)]
        + [head_block(rows, first, slot) for _, first, slot in operands]
        + [pair_block(rows)] * 2,
        out_specs=[head_block(rows, place)] + [pair_block(rows)] * 3 + [whole_block((8, HEAD_DIM))],
        out_shape=[
            jax.ShapeDtypeStruct((rows, heads * HEAD_DIM), jnp.bfloat16),
            jax.ShapeDtypeStruct((2, rows, lanes), jnp.float32),
            jax.ShapeDtypeStruct((2, rows, lanes), jnp.bfloat16),
            jax.ShapeDtypeStruct((2, rows, lanes), jnp.bfloat16),
            jax.ShapeDtypeStruct((8, HEAD_DIM), jnp.float32),
        ],
        compiler_params=pltpu.CompilerParams(vmem_limit_bytes=MAIN_VMEM),
        cost_estimate=MAIN_COST,
    )(info, *[array for array, _, _ in operands], pair_even, pair_odd)


def finish_call(info, key, own, from_even, from_odd, count):
    array, first, slot = key
    rows = own.shape[1]
    return pl.pallas_call(
        finish_kernel,
        grid=(count,),
        in_specs=[info_block(info), head_block(rows, first, slot)] + [pair_block(rows)] * 3,
        out_specs=pair_block(rows),
        out_shape=jax.ShapeDtypeStruct((2, rows, count * HEAD_DIM), jnp.bfloat16),
        compiler_params=pltpu.CompilerParams(vmem_limit_bytes=SMALL_VMEM),
        cost_estimate=COST,
    )(info, array, own, from_even, from_odd)


def row_block(rows, first):
    return pl.BlockSpec((8, rows), lambda head: (first + head, 0))


def sums_call(info, arrays, pair_even, pair_odd, first, count, heads, earlier, far_count):
    rows = pair_even.shape[1]
    amount = 2 + far_count
    earlier = [] if earlier is None else earlier
    return pl.pallas_call(
        functools.partial(sums_kernel, far_count=far_count),
        grid=(count,),
        in_specs=[info_block(info)]
        + [head_block(rows, first)] * 4
        + [pair_block(rows)] * 2
        + [pl.BlockSpec(memory_space=pl.ANY)] * len(earlier),
        out_specs=[row_block(rows, first)] * amount,
        out_shape=[jax.ShapeDtypeStruct((8 * heads, rows), jnp.float32)] * amount,
        input_output_aliases={7 + index: index for index in range(len(earlier))},
        compiler_params=pltpu.CompilerParams(vmem_limit_bytes=MAIN_VMEM),
        cost_estimate=MAIN_COST,
    )(info, *arrays, pair_even, pair_odd, *earlier)


def grads_call(info, arrays, pair_even, pair_odd, sums, first, count, heads, earlier, far_count):
    rows = pair_even.shape[1]
    lanes = heads * HEAD_DIM
    earlier = [] if earlier is None else earlier
    place = 7 + len(sums)
    return pl.pallas_call(
        functools.partial(grads_kernel, far_count=far_count),
        grid=(count,),
        in_specs=[info_block(info)]
        + [head_block(rows, first)] * 4
        + [pair_block(rows)] * 2
        + [row_block(rows, first)] * len(sums)
        + [pl.BlockSpec(memory_space=pl.ANY)] * len(earlier),
        out_specs=[pair_block(rows, first)]
        + [head_block(rows, first)] * 3
        + [whole_block((8, HEAD_DIM))],
        out_shape=[
            jax.ShapeDtypeStruct((2, rows, lanes), jnp.bfloat16),
            jax.ShapeDtypeStruct((rows, lanes), jnp.float32),
            jax.ShapeDtypeStruct((rows, lanes), jnp.bfloat16),
            jax.ShapeDtypeStruct((rows, lanes), jnp.bfloat16),
            jax.ShapeDtypeStruct((8, HEAD_DIM), jnp.float32),
        ],
        input_output_aliases={place + index: index for index in range(len(earlier))},
        compiler_params=pltpu.CompilerParams(vmem_limit_bytes=MAIN_VMEM),
        cost_estimate=MAIN_COST,
    )(info, *arrays, pair_even, pair_odd, *sums, *earlier)


def answer_call(info, query, own, from_even, from_odd, low):
    rows, lanes = own.shape
    return pl.pallas_call(
        answer_kernel,
        grid=(lanes // HEAD_DIM,),
        in_specs=[info_block(info)]
        + [head_block(rows, 0)] * 4
        + [pl.BlockSpec(memory_space=pl.ANY)],
        out_specs=head_block(rows, 0),
        out_shape=jax.ShapeDtypeStruct(low.shape, low.dtype),
        input_output_aliases={5: 0},
        compiler_params=pltpu.CompilerParams(vmem_limit_bytes=SMALL_VMEM),
        cost_estimate=LONG_COST,
    )(info, query, own, from_even, from_odd, low)


def last_call(info, key, own, from_even, from_odd, pieces, places, first, count):
    array, offset, slot = key
    rows = own.shape[1]
    anywhere = pl.BlockSpec(memory_space=pl.ANY)
    return pl.pallas_call(
        functools.partial(last_kernel, places=places, first=first, count=count),
        grid=(count,),
        in_specs=[info_block(info), head_block(rows, offset, slot)]
        + [pair_block(rows)] * 3
        + [anywhere] * len(pieces),
        out_specs=anywhere,
        out_shape=jax.ShapeDtypeStruct((3, rows, HEADS * HEAD_DIM), jnp.bfloat16),
        scratch_shapes=[
            pltpu.VMEM((count, 2, rows, HEAD_DIM), jnp.bfloat16),
            *[pltpu.VMEM(piece.shape, piece.dtype) for piece in pieces],
            pltpu.SemaphoreType.DMA((len(pieces),)),
            pltpu.SemaphoreType.DMA((len(pieces) + count,)),
        ],
        compiler_params=pltpu.CompilerParams(vmem_limit_bytes=SMALL_VMEM),
        cost_estimate=COST,
    )(info, array, own, from_even, from_odd, *pieces)


def partner(tile, parity, count):
    other = tile + 1 if tile % 2 == parity else tile - 1
    return other if 0 <= other < count else tile


def far_partner(tile, base, count):
    other = ((tile - base) ^ 2) + base if tile >= base else tile
    return other if 0 <= other < count else tile


def paired(value, partners):
    width = lax.axis_size("dp")
    pairs = []
    for tile, other in enumerate(partners):
        for sample in range(width):
            moved = sample ^ 1 if other == tile and width % 2 == 0 else sample
            pairs.append((tile * width + sample, other * width + moved))
    return lax.ppermute(value, ("seq", "dp"), pairs)


def exchanged(value, parity):
    count = lax.axis_size("seq")
    return paired(value, [partner(tile, parity, count) for tile in range(count)])


def far_partners(count):
    both = [[far_partner(tile, base, count) for tile in range(count)] for base in (0, 2)]
    return [partners for partners in both if partners != list(range(count))]


def after(value, *others):
    return lax.optimization_barrier((value, *others))[0]


def turned(value, step):
    count = lax.axis_size("pipe")
    return lax.ppermute(value, "pipe", [(i, (i + step) % count) for i in range(count)])


def total_over(value, axis, *late):
    count = lax.axis_size(axis)
    step = 1
    while step < count:
        other = lax.ppermute(value, axis, [(i, i ^ step) for i in range(count)])
        step *= 2
        value = value + (other if step < count else after(other, *late))
    return value


def local(queries, keys, values, grad_out, norm_gains, kv_tiles):
    query, key, value, grad = (a[0, 0, 0] for a in (queries, keys, values, grad_out))
    rows = query.shape[0]
    seq_count = lax.axis_size("seq")
    key_first, key_count = KEY_GROUP
    away_first, away_count = AWAY_GROUP
    fars = far_partners(seq_count)
    arrays = (query, grad, key, value)
    asks = [pack_call(query, grad, *QUERY_GROUPS[0])]
    away_pair = pack_call(after(key, asks[0]), value, away_first, away_count)
    for first, count in QUERY_GROUPS[1:]:
        asks.append(pack_call(after(query, away_pair), grad, first, count))
    told_pairs = [(exchanged(ask, 0), exchanged(ask, 1)) for ask in asks]
    key_pair = pack_call(after(key, asks[-1]), value, key_first, key_count)
    key_pair = after(key_pair, *told_pairs[0])
    key_pairs = (exchanged(key_pair, 0), exchanged(key_pair, 1))
    info = info_call(kv_tiles[0, 0, 0], after(norm_gains[0], asks[-1]))
    away_pair = turned(away_pair, -1)
    ask_low = ask_call(info, after(query, *told_pairs[-1]), grad, away_first, away_count)
    sums = None
    for (first, count), told in zip(QUERY_GROUPS, told_pairs):
        info_then = info if sums is None else after(info, ask_low)
        sums = sums_call(info_then, arrays, *told, first, count, key_first, sums, len(fars))
    received = [exchanged(sums[0], 0), exchanged(sums[1], 1)]
    received += [
        paired(after(value, *key_pairs), partners)
        for value, partners in zip(sums[2:], fars)
    ]
    all_sums = (*sums[:2], *received)
    asked = turned(ask_low, -1)
    away_sent = after(away_pair, *key_pairs)
    away_pairs = (exchanged(away_sent, 0), exchanged(away_sent, 1))
    gains, parts = [], None
    for (first, count), told in zip(QUERY_GROUPS, told_pairs):
        *parts, gain = grads_call(
            info, arrays, *told, all_sums, first, count, key_first, parts, len(fars)
        )
        gains.append(gain[:2])
    pair_low, own, to_even, to_odd = parts
    pieces = [turned(pair_low, -1)]
    places = [(slice(1, 3), 0)]
    answer = (own, exchanged(to_even, 0), exchanged(to_odd, 1))
    operands = [(array, key_first, None) for array in arrays]
    low, own, to_even, to_odd, gain = main_call(
        after(info, pair_low, asked), operands, *key_pairs, key_count, away_first, key_first
    )
    gains.append(gain[:2])
    key_answer = (own, exchanged(to_even, 0), exchanged(to_odd, 1))
    operands = [(asked, 0, 0), (asked, 0, 1), (away_pair, 0, 0), (away_pair, 0, 1)]
    query_low, own, to_even, to_odd, gain = main_call(
        after(asked, low), operands, *away_pairs, away_count, away_count, 0
    )
    gains.append(turned(after(gain[:2], pieces[0]), 1))
    returned = (exchanged(to_even, 0), exchanged(to_odd, 1))
    pieces.append(query_low)
    places.append((0, away_first * HEAD_DIM))
    low = answer_call(info, query, *answer, low)
    pieces.append(turned(after(low, gains[-1]), -1))
    places.append((0, 0))
    low = finish_call(after(info, pieces[0]), (key, key_first, None), *key_answer, key_count)
    pieces.append(turned(low, -1))
    places.append((slice(1, 3), key_first * HEAD_DIM))
    out = last_call(
        asked, operands[2], own, *returned, pieces, tuple(places), away_first, away_count
    )
    summed = total_over(total_over(sum(gains), "dp"), "seq", out)
    tokens = lax.axis_size("dp") * seq_count * rows * HEADS
    return (out[None, :, None, None], (summed / math.sqrt(tokens))[None])


def solution(mesh):
    placed = (
        P("pipe", "dp", "seq", None, None),
        P("pipe", "dp", "seq", None, None),
        P("pipe", "dp", "seq", None, None),
        P("pipe", "dp", "seq", None, None),
        P("pipe", None, None),
        P("pipe", "dp", "seq", None),
    )
    return jax.shard_map(
        local,
        mesh=mesh,
        in_specs=placed,
        out_specs=(P("pipe", None, "dp", "seq", None, None), P("pipe", None, None)),
        check_vma=False,
    )
```

```python
import functools
import math

import jax
import jax.numpy as jnp
from jax import lax
from jax.experimental import pallas as pl
from jax.experimental.pallas import tpu as pltpu
from jax.sharding import PartitionSpec as P

HEADS = 12
HEAD_DIM = 128
EPSILON = 1e-06
ROOT_SCALE = HEAD_DIM ** (-0.5)
EXP2_SCALE = ROOT_SCALE * math.log2(math.e)
QUERY_GROUPS = ((0, 3), (3, 2))
KEY_GROUP = (5, 2)
AWAY_GROUP = (7, 5)
MAIN_VMEM = 20 * 1024 * 1024
SMALL_VMEM = 12 * 1024 * 1024
PACK_VMEM = 4 * 1024 * 1024
COST = pl.CostEstimate(flops=1, bytes_accessed=1, transcendentals=0)
LONG_COST = pl.CostEstimate(flops=2 * 10**10, bytes_accessed=1, transcendentals=0)
MAIN_COST = pl.CostEstimate(flops=6 * 10**9, bytes_accessed=1, transcendentals=0)


def dot_nt(left, right):
    return lax.dot_general(
        left, right, (((1,), (1,)), ((), ())), preferred_element_type=jnp.float32
    )


def dot_nn(left, right):
    return lax.dot_general(
        left, right, (((1,), (0,)), ((), ())), preferred_element_type=jnp.float32
    )


def dot_tn(left, right):
    return lax.dot_general(
        left, right, (((0,), (0,)), ((), ())), preferred_element_type=jnp.float32
    )


def normalize(source, gain):
    floats = source.astype(jnp.float32)
    scaled = lax.rsqrt(jnp.mean(floats * floats, axis=-1, keepdims=True) + EPSILON)
    normed = floats * scaled
    return floats, scaled, normed, (normed * gain).astype(jnp.bfloat16)


def norm_back(grad_hat, floats, scaled, gain):
    scaled_grad = gain * grad_hat
    projected = jnp.sum(scaled_grad * floats, axis=-1, keepdims=True)
    return scaled * scaled_grad - (scaled**3 * projected * (1.0 / HEAD_DIM)) * floats


def pack_kernel(first_in, second_in, out, sems, *, start, width):
    rows = first_in.shape[0]
    copies = [
        pltpu.make_async_copy(
            source.at[:, start : start + width], out.at[slot, :rows], sems.at[slot]
        )
        for slot, source in enumerate((first_in, second_in))
    ]
    for copy in copies:
        copy.start()
    for copy in copies:
        copy.wait()


def info_kernel(listed, gains, info):
    tile = lax.axis_index("seq")
    last = lax.axis_size("seq") - 1
    info[...] = jnp.zeros_like(info)
    info[0:2, :] = gains[...]
    for parity in range(2):
        other = jnp.where(lax.rem(tile, 2) == parity, tile + 1, tile - 1)
        found = listed[0] == other
        for slot in range(1, listed.shape[0]):
            found = found | (listed[slot] == other)
        found = found & (other >= 0) & (other <= last)
        live = jnp.where(found, 1.0, 0.0)
        info[2 + parity : 3 + parity, :] = jnp.full((1, HEAD_DIM), live, jnp.float32)


def ask_kernel(info, query, grad, out, sems, *, start, width):
    rows = query.shape[0]
    value = info[...]
    planes = []
    for _ in range(3):
        low = value.astype(jnp.bfloat16)
        planes.append(low)
        value = value - low.astype(jnp.float32)
    planes.append(jnp.zeros_like(planes[0]))
    out[0, rows : rows + 16, :HEAD_DIM] = jnp.concatenate(planes[:2], axis=0)
    out[1, rows : rows + 16, :HEAD_DIM] = jnp.concatenate(planes[2:], axis=0)
    pack_kernel(query, grad, out, sems, start=start, width=width)


def told_info(told):
    floats = told[...].astype(jnp.float32)
    return floats[0, 0:8] + floats[0, 8:16] + floats[1, 0:8]


def main_kernel(
    info, query, grad, key, value, pair_even, pair_odd, *rest
):
    query_out, own_out, even_out, odd_out, gain_out = rest[-5:]
    told = told_info(info) if len(info.shape) == 3 else info[...]
    query_gain = told[0:1]
    key_gain = told[1:2]
    rows = query.shape[0]
    lives = [jnp.concatenate([told[row : row + 1]] * (rows // HEAD_DIM), axis=1) for row in (2, 3)]
    query_floats, query_scale, query_normed, query_hat = normalize(query[...], query_gain)
    grad_in = grad[...]
    sides = (
        (key[...], value[...], None),
        (pair_even[0], pair_even[1], lives[0]),
        (pair_odd[0], pair_odd[1], lives[1]),
    )
    parts = []
    totals = None
    for key_in, value_in, live in sides:
        _, _, key_normed, key_hat = normalize(key_in, key_gain)
        weights = jnp.exp2(dot_nt(key_hat, query_hat) * EXP2_SCALE)
        grad_probs = dot_nt(value_in, grad_in)
        weight_sum = jnp.sum(weights, axis=0, keepdims=True)
        cross_sum = jnp.sum(weights * grad_probs, axis=0, keepdims=True)
        if live is not None:
            weight_sum = weight_sum * live
            cross_sum = cross_sum * live
        totals = weight_sum if totals is None else totals + weight_sum
        crosses = cross_sum if live is None else crosses + cross_sum
        parts.append((key_normed, key_hat, weights, grad_probs, live))
    inverse = 1.0 / totals
    deltas = crosses * inverse
    query_grad_t = None
    key_gain_sum = None
    for (key_normed, key_hat, weights, grad_probs, live), out in zip(
        parts, (own_out, even_out, odd_out)
    ):
        probs = weights * (inverse if live is None else inverse * live)
        dscores = (probs * (grad_probs - deltas)).astype(jnp.bfloat16)
        key_part = dot_nn(dscores, query_hat) * ROOT_SCALE
        value_part = dot_nn(probs.astype(jnp.bfloat16), grad_in)
        out[0] = key_part.astype(out.dtype)
        out[1] = value_part.astype(out.dtype)
        gain_part = jnp.sum(key_part * key_normed, axis=0, keepdims=True)
        key_gain_sum = gain_part if key_gain_sum is None else key_gain_sum + gain_part
        query_part = dot_tn(key_hat, dscores)
        query_grad_t = query_part if query_grad_t is None else query_grad_t + query_part
    query_grad = query_grad_t.T * ROOT_SCALE
    query_out[...] = norm_back(query_grad, query_floats, query_scale, query_gain).astype(
        query_out.dtype
    )
    query_gain_sum = jnp.sum(query_grad * query_normed, axis=0, keepdims=True)

    @pl.when(pl.program_id(0) == 0)
    def _():
        gain_out[...] = jnp.zeros_like(gain_out)

    gain_out[0:1, :] += query_gain_sum
    gain_out[1:2, :] += key_gain_sum


def tile_sums(key_hat, value_in, query_hat, grad_in):
    weights = jnp.exp2(dot_nt(key_hat, query_hat) * EXP2_SCALE)
    grad_probs = dot_nt(value_in, grad_in)
    return weights, grad_probs


def wide_lives(told, rows):
    return [jnp.concatenate([told[row : row + 1]] * (rows // HEAD_DIM), axis=1) for row in (2, 3)]


def near_is_even():
    place = lax.rem(lax.axis_index("seq"), 4)
    return (place == 0) | (place == 3)


def sums_kernel(info, query, grad, key, value, pair_even, pair_odd, *rest, far_count):
    outs = rest[-2 - far_count :]
    told = info[...]
    _, _, _, key_hat = normalize(key[...], told[1:2])
    value_in = value[...]
    rows = []
    for query_in, grad_in in (
        (query[...], grad[...]), (pair_even[0], pair_even[1]), (pair_odd[0], pair_odd[1])
    ):
        _, _, _, query_hat = normalize(query_in, told[0:1])
        weights, grad_probs = tile_sums(key_hat, value_in, query_hat, grad_in)
        rows.append(
            [
                jnp.sum(weights, axis=0, keepdims=True),
                jnp.sum(weights * grad_probs, axis=0, keepdims=True),
            ]
        )
    own, even, odd = rows
    tail = wide_lives(told, query.shape[0])
    blank = jnp.zeros_like(tail[0])
    outs[0][...] = jnp.concatenate([*own, *even, *tail, blank, blank], axis=0)
    outs[1][...] = jnp.concatenate([*own, *odd, *tail, blank, blank], axis=0)
    near = near_is_even()
    for index, out in enumerate(outs[2:]):
        first, second = (even, odd) if index == 0 else (odd, even)
        chosen = [jnp.where(near, one, two) for one, two in zip(first, second)]
        out[...] = jnp.concatenate([*chosen, *[blank] * 6], axis=0)


def grads_kernel(
    info, query, grad, key, value, pair_even, pair_odd,
    sent_even, sent_odd, from_even, from_odd, *rest, far_count,
):
    fars = [far[0:2, :] for far in rest[:far_count]]
    pair_out, own_out, even_out, odd_out, gain_out = rest[-5:]
    told = info[...]
    near = near_is_even()
    if far_count == 2:
        far_even = jnp.where(near, fars[0], fars[1])
        far_odd = jnp.where(near, fars[1], fars[0])
    elif far_count == 1:
        far_even = jnp.where(near, fars[0], jnp.zeros_like(fars[0]))
        far_odd = jnp.where(near, jnp.zeros_like(fars[0]), fars[0])
    else:
        far_even = far_odd = jnp.zeros_like(from_even[0:2, :])
    own_sums = (
        sent_even[0:2, :]
        + sent_even[4:5, :] * from_even[2:4, :]
        + sent_even[5:6, :] * from_odd[2:4, :]
    )
    even_sums = (
        from_even[0:2, :] + from_even[4:5, :] * sent_even[2:4, :] + from_even[5:6, :] * far_even
    )
    odd_sums = (
        from_odd[0:2, :] + from_odd[5:6, :] * sent_odd[2:4, :] + from_odd[4:5, :] * far_odd
    )
    key_floats, key_scale, key_normed, key_hat = normalize(key[...], told[1:2])
    value_in = value[...]
    key_grad = value_grad = query_gain_sum = None
    for query_in, grad_in, sums, live, out in (
        (query[...], grad[...], own_sums, None, own_out),
        (pair_even[0], pair_even[1], even_sums, from_even[4:5, :], even_out),
        (pair_odd[0], pair_odd[1], odd_sums, from_odd[5:6, :], odd_out),
    ):
        _, _, query_normed, query_hat = normalize(query_in, told[0:1])
        weights, grad_probs = tile_sums(key_hat, value_in, query_hat, grad_in)
        inverse = 1.0 / sums[0:1]
        deltas = sums[1:2] * inverse
        probs = weights * (inverse if live is None else inverse * live)
        dscores = (probs * (grad_probs - deltas)).astype(jnp.bfloat16)
        key_part = dot_nn(dscores, query_hat)
        value_part = dot_nn(probs.astype(jnp.bfloat16), grad_in)
        query_part = dot_tn(key_hat, dscores).T * ROOT_SCALE
        out[...] = query_part.astype(out.dtype)
        gain_part = jnp.sum(query_part * query_normed, axis=0, keepdims=True)
        key_grad = key_part if key_grad is None else key_grad + key_part
        value_grad = value_part if value_grad is None else value_grad + value_part
        query_gain_sum = gain_part if query_gain_sum is None else query_gain_sum + gain_part
    key_grad = key_grad * ROOT_SCALE
    key_back = norm_back(key_grad, key_floats, key_scale, told[1:2])
    pair_out[0] = key_back.astype(pair_out.dtype)
    pair_out[1] = value_grad.astype(pair_out.dtype)

    @pl.when(pl.program_id(0) == 0)
    def _():
        gain_out[...] = jnp.zeros_like(gain_out)

    gain_out[0:1, :] += query_gain_sum
    gain_out[1:2, :] += jnp.sum(key_grad * key_normed, axis=0, keepdims=True)


def answer_kernel(info, query, own, from_even, from_odd, _, out):
    gain = info[0:1, :]
    floats, scaled, _, _ = normalize(query[...], gain)
    total = own[...] + from_even[...].astype(jnp.float32) + from_odd[...].astype(jnp.float32)
    out[...] = norm_back(total, floats, scaled, gain).astype(out.dtype)


def finished(info, key, own, from_even, from_odd):
    told = told_info(info) if len(info.shape) == 3 else info[...]
    key_gain = told[1:2]
    key_floats, key_scale, _, _ = normalize(key[...], key_gain)
    key_grad = own[0] + from_even[0].astype(jnp.float32) + from_odd[0].astype(jnp.float32)
    value_grad = own[1] + from_even[1].astype(jnp.float32) + from_odd[1].astype(jnp.float32)
    return norm_back(key_grad, key_floats, key_scale, key_gain), value_grad


def finish_kernel(info, key, own, from_even, from_odd, out):
    key_grad, value_grad = finished(info, key, own, from_even, from_odd)
    out[0] = key_grad.astype(out.dtype)
    out[1] = value_grad.astype(out.dtype)


def last_kernel(info, key, own, from_even, from_odd, *rest, places, first, count):
    amount = len(places)
    pieces, (out, held) = rest[:amount], rest[amount : amount + 2]
    staged, (load_sems, store_sems) = rest[amount + 2 : -2], rest[-2:]
    head = pl.program_id(0)
    loads = [
        pltpu.make_async_copy(piece, stage, load_sems.at[slot])
        for slot, (piece, stage) in enumerate(zip(pieces, staged))
    ]
    stores = [
        pltpu.make_async_copy(
            stage, out.at[planes, :, start : start + stage.shape[-1]], store_sems.at[slot]
        )
        for slot, (stage, (planes, start)) in enumerate(zip(staged, places))
    ]

    def head_copy(index):
        start = pl.multiple_of((first + index) * HEAD_DIM, HEAD_DIM)
        return pltpu.make_async_copy(
            held.at[index],
            out.at[pl.ds(1, 2), :, pl.ds(start, HEAD_DIM)],
            store_sems.at[amount + index],
        )

    @pl.when(head == 0)
    def _():
        for load in loads:
            load.start()

    @pl.when(head == min(1, count - 1))
    def _():
        for load, store in zip(loads, stores):
            load.wait()
            store.start()

    key_grad, value_grad = finished(info, key, own, from_even, from_odd)
    held[head, 0] = key_grad.astype(held.dtype)
    held[head, 1] = value_grad.astype(held.dtype)
    head_copy(head).start()

    @pl.when(head == count - 1)
    def _():
        for store in stores:
            store.wait()
        for index in range(count):
            head_copy(index).wait()


def head_block(rows, first, slot=None):
    if slot is None:
        return pl.BlockSpec((rows, HEAD_DIM), lambda head: (0, first + head))
    return pl.BlockSpec((None, rows, HEAD_DIM), lambda head: (slot, 0, first + head))


def pair_block(rows, first=0):
    return pl.BlockSpec((2, rows, HEAD_DIM), lambda head: (0, 0, first + head))


def whole_block(shape):
    return pl.BlockSpec(shape, lambda head: (0,) * len(shape))


def pack_params(limit):
    return dict(
        scratch_shapes=[pltpu.SemaphoreType.DMA((2,))],
        compiler_params=pltpu.CompilerParams(vmem_limit_bytes=limit),
        cost_estimate=COST,
    )


def pack_call(first_in, second_in, first, count, limit=PACK_VMEM):
    rows = first_in.shape[0]
    width = count * HEAD_DIM
    return pl.pallas_call(
        functools.partial(pack_kernel, start=first * HEAD_DIM, width=width),
        grid=(1,),
        in_specs=[pl.BlockSpec(memory_space=pl.ANY)] * 2,
        out_specs=whole_block((2, rows, width)),
        out_shape=jax.ShapeDtypeStruct((2, rows, width), jnp.bfloat16),
        **pack_params(limit),
    )(first_in, second_in)


def ask_call(info, query, grad, first, count):
    rows = query.shape[0]
    width = count * HEAD_DIM
    return pl.pallas_call(
        functools.partial(ask_kernel, start=first * HEAD_DIM, width=width),
        grid=(1,),
        in_specs=[whole_block(info.shape)] + [pl.BlockSpec(memory_space=pl.ANY)] * 2,
        out_specs=whole_block((2, rows + 16, width)),
        out_shape=jax.ShapeDtypeStruct((2, rows + 16, width), jnp.bfloat16),
        **pack_params(PACK_VMEM),
    )(info, query, grad)


def info_call(listed, gains):
    return pl.pallas_call(
        info_kernel,
        in_specs=[pl.BlockSpec(memory_space=pltpu.SMEM), pl.BlockSpec(memory_space=pltpu.VMEM)],
        out_specs=pl.BlockSpec(memory_space=pltpu.VMEM),
        out_shape=jax.ShapeDtypeStruct((8, HEAD_DIM), jnp.float32),
        compiler_params=pltpu.CompilerParams(vmem_limit_bytes=PACK_VMEM),
        cost_estimate=LONG_COST,
    )(listed, gains)


def info_block(info):
    if info.ndim == 2:
        return whole_block(info.shape)
    below = info.shape[1] // 16 - 1
    return pl.BlockSpec((2, 16, HEAD_DIM), lambda head: (0, below, 0))


def main_call(info, operands, pair_even, pair_odd, count, heads, place):
    rows = pair_even.shape[1]
    lanes = count * HEAD_DIM
    return pl.pallas_call(
        main_kernel,
        grid=(count,),
        in_specs=[info_block(info)]
        + [head_block(rows, first, slot) for _, first, slot in operands]
        + [pair_block(rows)] * 2,
        out_specs=[head_block(rows, place)] + [pair_block(rows)] * 3 + [whole_block((8, HEAD_DIM))],
        out_shape=[
            jax.ShapeDtypeStruct((rows, heads * HEAD_DIM), jnp.bfloat16),
            jax.ShapeDtypeStruct((2, rows, lanes), jnp.float32),
            jax.ShapeDtypeStruct((2, rows, lanes), jnp.bfloat16),
            jax.ShapeDtypeStruct((2, rows, lanes), jnp.bfloat16),
            jax.ShapeDtypeStruct((8, HEAD_DIM), jnp.float32),
        ],
        compiler_params=pltpu.CompilerParams(vmem_limit_bytes=MAIN_VMEM),
        cost_estimate=MAIN_COST,
    )(info, *[array for array, _, _ in operands], pair_even, pair_odd)


def finish_call(info, key, own, from_even, from_odd, count):
    array, first, slot = key
    rows = own.shape[1]
    return pl.pallas_call(
        finish_kernel,
        grid=(count,),
        in_specs=[info_block(info), head_block(rows, first, slot)] + [pair_block(rows)] * 3,
        out_specs=pair_block(rows),
        out_shape=jax.ShapeDtypeStruct((2, rows, count * HEAD_DIM), jnp.bfloat16),
        compiler_params=pltpu.CompilerParams(vmem_limit_bytes=SMALL_VMEM),
        cost_estimate=COST,
    )(info, array, own, from_even, from_odd)


def row_block(rows, first):
    return pl.BlockSpec((8, rows), lambda head: (first + head, 0))


def sums_call(info, arrays, pair_even, pair_odd, first, count, heads, earlier, far_count):
    rows = pair_even.shape[1]
    amount = 2 + far_count
    earlier = [] if earlier is None else earlier
    return pl.pallas_call(
        functools.partial(sums_kernel, far_count=far_count),
        grid=(count,),
        in_specs=[info_block(info)]
        + [head_block(rows, first)] * 4
        + [pair_block(rows)] * 2
        + [pl.BlockSpec(memory_space=pl.ANY)] * len(earlier),
        out_specs=[row_block(rows, first)] * amount,
        out_shape=[jax.ShapeDtypeStruct((8 * heads, rows), jnp.float32)] * amount,
        input_output_aliases={7 + index: index for index in range(len(earlier))},
        compiler_params=pltpu.CompilerParams(vmem_limit_bytes=MAIN_VMEM),
        cost_estimate=MAIN_COST,
    )(info, *arrays, pair_even, pair_odd, *earlier)


def grads_call(info, arrays, pair_even, pair_odd, sums, first, count, heads, earlier, far_count):
    rows = pair_even.shape[1]
    lanes = heads * HEAD_DIM
    earlier = [] if earlier is None else earlier
    place = 7 + len(sums)
    return pl.pallas_call(
        functools.partial(grads_kernel, far_count=far_count),
        grid=(count,),
        in_specs=[info_block(info)]
        + [head_block(rows, first)] * 4
        + [pair_block(rows)] * 2
        + [row_block(rows, first)] * len(sums)
        + [pl.BlockSpec(memory_space=pl.ANY)] * len(earlier),
        out_specs=[pair_block(rows, first)]
        + [head_block(rows, first)] * 3
        + [whole_block((8, HEAD_DIM))],
        out_shape=[
            jax.ShapeDtypeStruct((2, rows, lanes), jnp.bfloat16),
            jax.ShapeDtypeStruct((rows, lanes), jnp.float32),
            jax.ShapeDtypeStruct((rows, lanes), jnp.bfloat16),
            jax.ShapeDtypeStruct((rows, lanes), jnp.bfloat16),
            jax.ShapeDtypeStruct((8, HEAD_DIM), jnp.float32),
        ],
        input_output_aliases={place + index: index for index in range(len(earlier))},
        compiler_params=pltpu.CompilerParams(vmem_limit_bytes=MAIN_VMEM),
        cost_estimate=COST,
    )(info, *arrays, pair_even, pair_odd, *sums, *earlier)


def answer_call(info, query, own, from_even, from_odd, low):
    rows, lanes = own.shape
    return pl.pallas_call(
        answer_kernel,
        grid=(lanes // HEAD_DIM,),
        in_specs=[info_block(info)]
        + [head_block(rows, 0)] * 4
        + [pl.BlockSpec(memory_space=pl.ANY)],
        out_specs=head_block(rows, 0),
        out_shape=jax.ShapeDtypeStruct(low.shape, low.dtype),
        input_output_aliases={5: 0},
        compiler_params=pltpu.CompilerParams(vmem_limit_bytes=SMALL_VMEM),
        cost_estimate=LONG_COST,
    )(info, query, own, from_even, from_odd, low)


def last_call(info, key, own, from_even, from_odd, pieces, places, first, count):
    array, offset, slot = key
    rows = own.shape[1]
    anywhere = pl.BlockSpec(memory_space=pl.ANY)
    return pl.pallas_call(
        functools.partial(last_kernel, places=places, first=first, count=count),
        grid=(count,),
        in_specs=[info_block(info), head_block(rows, offset, slot)]
        + [pair_block(rows)] * 3
        + [anywhere] * len(pieces),
        out_specs=anywhere,
        out_shape=jax.ShapeDtypeStruct((3, rows, HEADS * HEAD_DIM), jnp.bfloat16),
        scratch_shapes=[
            pltpu.VMEM((count, 2, rows, HEAD_DIM), jnp.bfloat16),
            *[pltpu.VMEM(piece.shape, piece.dtype) for piece in pieces],
            pltpu.SemaphoreType.DMA((len(pieces),)),
            pltpu.SemaphoreType.DMA((len(pieces) + count,)),
        ],
        compiler_params=pltpu.CompilerParams(vmem_limit_bytes=SMALL_VMEM),
        cost_estimate=COST,
    )(info, array, own, from_even, from_odd, *pieces)


def partner(tile, parity, count):
    other = tile + 1 if tile % 2 == parity else tile - 1
    return other if 0 <= other < count else tile


def far_partner(tile, base, count):
    other = ((tile - base) ^ 2) + base if tile >= base else tile
    return other if 0 <= other < count else tile


def paired(value, partners):
    width = lax.axis_size("dp")
    pairs = []
    for tile, other in enumerate(partners):
        for sample in range(width):
            moved = sample ^ 1 if other == tile and width % 2 == 0 else sample
            pairs.append((tile * width + sample, other * width + moved))
    return lax.ppermute(value, ("seq", "dp"), pairs)


def exchanged(value, parity):
    count = lax.axis_size("seq")
    return paired(value, [partner(tile, parity, count) for tile in range(count)])


def far_partners(count):
    both = [[far_partner(tile, base, count) for tile in range(count)] for base in (0, 2)]
    return [partners for partners in both if partners != list(range(count))]


def after(value, *others):
    return lax.optimization_barrier((value, *others))[0]


def turned(value, step):
    count = lax.axis_size("pipe")
    return lax.ppermute(value, "pipe", [(i, (i + step) % count) for i in range(count)])


def total_over(value, axis, *late):
    count = lax.axis_size(axis)
    step = 1
    while step < count:
        other = lax.ppermute(value, axis, [(i, i ^ step) for i in range(count)])
        step *= 2
        value = value + (other if step < count else after(other, *late))
    return value


def local(queries, keys, values, grad_out, norm_gains, kv_tiles):
    query, key, value, grad = (a[0, 0, 0] for a in (queries, keys, values, grad_out))
    rows = query.shape[0]
    seq_count = lax.axis_size("seq")
    key_first, key_count = KEY_GROUP
    away_first, away_count = AWAY_GROUP
    fars = far_partners(seq_count)
    arrays = (query, grad, key, value)
    asks = [pack_call(query, grad, *QUERY_GROUPS[0])]
    away_pair = pack_call(after(key, asks[0]), value, away_first, away_count)
    for first, count in QUERY_GROUPS[1:]:
        asks.append(pack_call(after(query, away_pair), grad, first, count))
    told_pairs = [(exchanged(ask, 0), exchanged(ask, 1)) for ask in asks]
    key_pair = pack_call(after(key, asks[-1]), value, key_first, key_count)
    key_pair = after(key_pair, *told_pairs[0])
    key_pairs = (exchanged(key_pair, 0), exchanged(key_pair, 1))
    info = info_call(kv_tiles[0, 0, 0], after(norm_gains[0], asks[-1]))
    away_pair = turned(away_pair, -1)
    sums = None
    for (first, count), told in zip(QUERY_GROUPS, told_pairs):
        sums = sums_call(info, arrays, *told, first, count, key_first, sums, len(fars))
    received = [exchanged(sums[0], 0), exchanged(sums[1], 1)]
    received += [
        paired(value, partners) for value, partners in zip(sums[2:], fars)
    ]
    all_sums = (*sums[:2], *received)
    asked = ask_call(info, after(query, away_pair, sums[0]), grad, away_first, away_count)
    asked = turned(asked, -1)
    away_sent = after(away_pair, *key_pairs, *received)
    away_pairs = (exchanged(away_sent, 0), exchanged(away_sent, 1))
    gains, parts = [], None
    for (first, count), told in zip(QUERY_GROUPS, told_pairs):
        *parts, gain = grads_call(
            info, arrays, *told, all_sums, first, count, key_first, parts, len(fars)
        )
        gains.append(gain[:2])
    pair_low, own, to_even, to_odd = parts
    pieces = [turned(pair_low, -1)]
    places = [(slice(1, 3), 0)]
    answer = (own, exchanged(to_even, 0), exchanged(to_odd, 1))
    operands = [(array, key_first, None) for array in arrays]
    low, own, to_even, to_odd, gain = main_call(
        after(info, pair_low), operands, *key_pairs, key_count, away_first, key_first
    )
    gains.append(gain[:2])
    key_answer = (own, exchanged(to_even, 0), exchanged(to_odd, 1))
    operands = [(asked, 0, 0), (asked, 0, 1), (away_pair, 0, 0), (away_pair, 0, 1)]
    query_low, own, to_even, to_odd, gain = main_call(
        after(asked, low), operands, *away_pairs, away_count, away_count, 0
    )
    returned = (exchanged(to_even, 0), exchanged(to_odd, 1))
    pieces.append(query_low)
    places.append((0, away_first * HEAD_DIM))
    low = answer_call(info, query, *answer, low)
    gains.append(turned(after(gain[:2], low, pieces[0]), 1))
    pieces.append(turned(after(low, gains[-1]), -1))
    places.append((0, 0))
    low = finish_call(after(info, pieces[0]), (key, key_first, None), *key_answer, key_count)
    pieces.append(turned(low, -1))
    places.append((slice(1, 3), key_first * HEAD_DIM))
    out = last_call(
        asked, operands[2], own, *returned, pieces, tuple(places), away_first, away_count
    )
    summed = total_over(total_over(sum(gains), "dp"), "seq", out)
    tokens = lax.axis_size("dp") * seq_count * rows * HEADS
    return (out[None, :, None, None], (summed / math.sqrt(tokens))[None])


def solution(mesh):
    placed = (
        P("pipe", "dp", "seq", None, None),
        P("pipe", "dp", "seq", None, None),
        P("pipe", "dp", "seq", None, None),
        P("pipe", "dp", "seq", None, None),
        P("pipe", None, None),
        P("pipe", "dp", "seq", None),
    )
    return jax.shard_map(
        local,
        mesh=mesh,
        in_specs=placed,
        out_specs=(P("pipe", None, "dp", "seq", None, None), P("pipe", None, None)),
        check_vma=False,
    )
```

```python
import functools
import math

import jax
import jax.numpy as jnp
from jax import lax
from jax.experimental import pallas as pl
from jax.experimental.pallas import tpu as pltpu
from jax.sharding import PartitionSpec as P

HEADS = 12
HEAD_DIM = 128
EPSILON = 1e-06
ROOT_SCALE = HEAD_DIM ** (-0.5)
EXP2_SCALE = ROOT_SCALE * math.log2(math.e)
QUERY_GROUPS = ((0, 3), (3, 2))
KEY_GROUP = (5, 2)
AWAY_GROUP = (7, 5)
MAIN_VMEM = 20 * 1024 * 1024
SMALL_VMEM = 12 * 1024 * 1024
PACK_VMEM = 4 * 1024 * 1024
COST = pl.CostEstimate(flops=1, bytes_accessed=1, transcendentals=0)
LONG_COST = pl.CostEstimate(flops=2 * 10**10, bytes_accessed=1, transcendentals=0)
GRAD_COST = pl.CostEstimate(flops=4000000000, bytes_accessed=1, transcendentals=0)
MAIN_COST = pl.CostEstimate(flops=6 * 10**9, bytes_accessed=1, transcendentals=0)


def dot_nt(left, right):
    return lax.dot_general(
        left, right, (((1,), (1,)), ((), ())), preferred_element_type=jnp.float32
    )


def dot_nn(left, right):
    return lax.dot_general(
        left, right, (((1,), (0,)), ((), ())), preferred_element_type=jnp.float32
    )


def dot_tn(left, right):
    return lax.dot_general(
        left, right, (((0,), (0,)), ((), ())), preferred_element_type=jnp.float32
    )


def normalize(source, gain):
    floats = source.astype(jnp.float32)
    scaled = lax.rsqrt(jnp.mean(floats * floats, axis=-1, keepdims=True) + EPSILON)
    normed = floats * scaled
    return floats, scaled, normed, (normed * gain).astype(jnp.bfloat16)


def norm_back(grad_hat, floats, scaled, gain):
    scaled_grad = gain * grad_hat
    projected = jnp.sum(scaled_grad * floats, axis=-1, keepdims=True)
    return scaled * scaled_grad - (scaled**3 * projected * (1.0 / HEAD_DIM)) * floats


def pack_kernel(first_in, second_in, out, sems, *, start, width):
    rows = first_in.shape[0]
    copies = [
        pltpu.make_async_copy(
            source.at[:, start : start + width], out.at[slot, :rows], sems.at[slot]
        )
        for slot, source in enumerate((first_in, second_in))
    ]
    for copy in copies:
        copy.start()
    for copy in copies:
        copy.wait()


def info_kernel(listed, gains, info):
    tile = lax.axis_index("seq")
    last = lax.axis_size("seq") - 1
    info[...] = jnp.zeros_like(info)
    info[0:2, :] = gains[...]
    for parity in range(2):
        other = jnp.where(lax.rem(tile, 2) == parity, tile + 1, tile - 1)
        found = listed[0] == other
        for slot in range(1, listed.shape[0]):
            found = found | (listed[slot] == other)
        found = found & (other >= 0) & (other <= last)
        live = jnp.where(found, 1.0, 0.0)
        info[2 + parity : 3 + parity, :] = jnp.full((1, HEAD_DIM), live, jnp.float32)


def ask_kernel(info, query, grad, out, sems, *, start, width):
    rows = query.shape[0]
    value = info[...]
    planes = []
    for _ in range(3):
        low = value.astype(jnp.bfloat16)
        planes.append(low)
        value = value - low.astype(jnp.float32)
    planes.append(jnp.zeros_like(planes[0]))
    out[0, rows : rows + 16, :HEAD_DIM] = jnp.concatenate(planes[:2], axis=0)
    out[1, rows : rows + 16, :HEAD_DIM] = jnp.concatenate(planes[2:], axis=0)
    pack_kernel(query, grad, out, sems, start=start, width=width)


def told_info(told):
    floats = told[...].astype(jnp.float32)
    return floats[0, 0:8] + floats[0, 8:16] + floats[1, 0:8]


def main_kernel(
    info, query, grad, key, value, pair_even, pair_odd, *rest
):
    query_out, own_out, even_out, odd_out, gain_out = rest[-5:]
    told = told_info(info) if len(info.shape) == 3 else info[...]
    query_gain = told[0:1]
    key_gain = told[1:2]
    rows = query.shape[0]
    lives = [jnp.concatenate([told[row : row + 1]] * (rows // HEAD_DIM), axis=1) for row in (2, 3)]
    query_floats, query_scale, query_normed, query_hat = normalize(query[...], query_gain)
    grad_in = grad[...]
    sides = (
        (key[...], value[...], None),
        (pair_even[0], pair_even[1], lives[0]),
        (pair_odd[0], pair_odd[1], lives[1]),
    )
    parts = []
    totals = None
    for key_in, value_in, live in sides:
        _, _, key_normed, key_hat = normalize(key_in, key_gain)
        weights = jnp.exp2(dot_nt(key_hat, query_hat) * EXP2_SCALE)
        grad_probs = dot_nt(value_in, grad_in)
        weight_sum = jnp.sum(weights, axis=0, keepdims=True)
        cross_sum = jnp.sum(weights * grad_probs, axis=0, keepdims=True)
        if live is not None:
            weight_sum = weight_sum * live
            cross_sum = cross_sum * live
        totals = weight_sum if totals is None else totals + weight_sum
        crosses = cross_sum if live is None else crosses + cross_sum
        parts.append((key_normed, key_hat, weights, grad_probs, live))
    inverse = 1.0 / totals
    deltas = crosses * inverse
    query_grad_t = None
    key_gain_sum = None
    for (key_normed, key_hat, weights, grad_probs, live), out in zip(
        parts, (own_out, even_out, odd_out)
    ):
        probs = weights * (inverse if live is None else inverse * live)
        dscores = (probs * (grad_probs - deltas)).astype(jnp.bfloat16)
        key_part = dot_nn(dscores, query_hat) * ROOT_SCALE
        value_part = dot_nn(probs.astype(jnp.bfloat16), grad_in)
        out[0] = key_part.astype(out.dtype)
        out[1] = value_part.astype(out.dtype)
        gain_part = jnp.sum(key_part * key_normed, axis=0, keepdims=True)
        key_gain_sum = gain_part if key_gain_sum is None else key_gain_sum + gain_part
        query_part = dot_tn(key_hat, dscores)
        query_grad_t = query_part if query_grad_t is None else query_grad_t + query_part
    query_grad = query_grad_t.T * ROOT_SCALE
    query_out[...] = norm_back(query_grad, query_floats, query_scale, query_gain).astype(
        query_out.dtype
    )
    query_gain_sum = jnp.sum(query_grad * query_normed, axis=0, keepdims=True)

    @pl.when(pl.program_id(0) == 0)
    def _():
        gain_out[...] = jnp.zeros_like(gain_out)

    gain_out[0:1, :] += query_gain_sum
    gain_out[1:2, :] += key_gain_sum


def tile_sums(key_hat, value_in, query_hat, grad_in):
    weights = jnp.exp2(dot_nt(key_hat, query_hat) * EXP2_SCALE)
    grad_probs = dot_nt(value_in, grad_in)
    return weights, grad_probs


def wide_lives(told, rows):
    return [jnp.concatenate([told[row : row + 1]] * (rows // HEAD_DIM), axis=1) for row in (2, 3)]


def near_is_even():
    place = lax.rem(lax.axis_index("seq"), 4)
    return (place == 0) | (place == 3)


def sums_kernel(info, query, grad, key, value, pair_even, pair_odd, *rest, far_count):
    outs = rest[-2 - far_count :]
    told = info[...]
    _, _, _, key_hat = normalize(key[...], told[1:2])
    value_in = value[...]
    rows = []
    for query_in, grad_in in (
        (query[...], grad[...]), (pair_even[0], pair_even[1]), (pair_odd[0], pair_odd[1])
    ):
        _, _, _, query_hat = normalize(query_in, told[0:1])
        weights, grad_probs = tile_sums(key_hat, value_in, query_hat, grad_in)
        rows.append(
            [
                jnp.sum(weights, axis=0, keepdims=True),
                jnp.sum(weights * grad_probs, axis=0, keepdims=True),
            ]
        )
    own, even, odd = rows
    tail = wide_lives(told, query.shape[0])
    blank = jnp.zeros_like(tail[0])
    outs[0][...] = jnp.concatenate([*own, *even, *tail, blank, blank], axis=0)
    outs[1][...] = jnp.concatenate([*own, *odd, *tail, blank, blank], axis=0)
    near = near_is_even()
    for index, out in enumerate(outs[2:]):
        first, second = (even, odd) if index == 0 else (odd, even)
        chosen = [jnp.where(near, one, two) for one, two in zip(first, second)]
        out[...] = jnp.concatenate([*chosen, *[blank] * 6], axis=0)


def grads_kernel(
    info, query, grad, key, value, pair_even, pair_odd,
    sent_even, sent_odd, from_even, from_odd, *rest, far_count,
):
    fars = [far[0:2, :] for far in rest[:far_count]]
    pair_out, own_out, even_out, odd_out, gain_out = rest[-5:]
    told = info[...]
    near = near_is_even()
    if far_count == 2:
        far_even = jnp.where(near, fars[0], fars[1])
        far_odd = jnp.where(near, fars[1], fars[0])
    elif far_count == 1:
        far_even = jnp.where(near, fars[0], jnp.zeros_like(fars[0]))
        far_odd = jnp.where(near, jnp.zeros_like(fars[0]), fars[0])
    else:
        far_even = far_odd = jnp.zeros_like(from_even[0:2, :])
    own_sums = (
        sent_even[0:2, :]
        + sent_even[4:5, :] * from_even[2:4, :]
        + sent_even[5:6, :] * from_odd[2:4, :]
    )
    even_sums = (
        from_even[0:2, :] + from_even[4:5, :] * sent_even[2:4, :] + from_even[5:6, :] * far_even
    )
    odd_sums = (
        from_odd[0:2, :] + from_odd[5:6, :] * sent_odd[2:4, :] + from_odd[4:5, :] * far_odd
    )
    key_floats, key_scale, key_normed, key_hat = normalize(key[...], told[1:2])
    value_in = value[...]
    key_grad = value_grad = query_gain_sum = None
    for query_in, grad_in, sums, live, out in (
        (query[...], grad[...], own_sums, None, own_out),
        (pair_even[0], pair_even[1], even_sums, from_even[4:5, :], even_out),
        (pair_odd[0], pair_odd[1], odd_sums, from_odd[5:6, :], odd_out),
    ):
        _, _, query_normed, query_hat = normalize(query_in, told[0:1])
        weights, grad_probs = tile_sums(key_hat, value_in, query_hat, grad_in)
        inverse = 1.0 / sums[0:1]
        deltas = sums[1:2] * inverse
        probs = weights * (inverse if live is None else inverse * live)
        dscores = (probs * (grad_probs - deltas)).astype(jnp.bfloat16)
        key_part = dot_nn(dscores, query_hat)
        value_part = dot_nn(probs.astype(jnp.bfloat16), grad_in)
        query_part = dot_tn(key_hat, dscores).T * ROOT_SCALE
        out[...] = query_part.astype(out.dtype)
        gain_part = jnp.sum(query_part * query_normed, axis=0, keepdims=True)
        key_grad = key_part if key_grad is None else key_grad + key_part
        value_grad = value_part if value_grad is None else value_grad + value_part
        query_gain_sum = gain_part if query_gain_sum is None else query_gain_sum + gain_part
    key_grad = key_grad * ROOT_SCALE
    key_back = norm_back(key_grad, key_floats, key_scale, told[1:2])
    pair_out[0] = key_back.astype(pair_out.dtype)
    pair_out[1] = value_grad.astype(pair_out.dtype)

    @pl.when(pl.program_id(0) == 0)
    def _():
        gain_out[...] = jnp.zeros_like(gain_out)

    gain_out[0:1, :] += query_gain_sum
    gain_out[1:2, :] += jnp.sum(key_grad * key_normed, axis=0, keepdims=True)


def answer_kernel(info, query, own, from_even, from_odd, _, out):
    gain = info[0:1, :]
    floats, scaled, _, _ = normalize(query[...], gain)
    total = own[...] + from_even[...].astype(jnp.float32) + from_odd[...].astype(jnp.float32)
    out[...] = norm_back(total, floats, scaled, gain).astype(out.dtype)


def finished(info, key, own, from_even, from_odd):
    told = told_info(info) if len(info.shape) == 3 else info[...]
    key_gain = told[1:2]
    key_floats, key_scale, _, _ = normalize(key[...], key_gain)
    key_grad = own[0] + from_even[0].astype(jnp.float32) + from_odd[0].astype(jnp.float32)
    value_grad = own[1] + from_even[1].astype(jnp.float32) + from_odd[1].astype(jnp.float32)
    return norm_back(key_grad, key_floats, key_scale, key_gain), value_grad


def finish_kernel(info, key, own, from_even, from_odd, out):
    key_grad, value_grad = finished(info, key, own, from_even, from_odd)
    out[0] = key_grad.astype(out.dtype)
    out[1] = value_grad.astype(out.dtype)


def last_kernel(info, key, own, from_even, from_odd, *rest, places, first, count):
    amount = len(places)
    pieces, (out, held) = rest[:amount], rest[amount : amount + 2]
    staged, (load_sems, store_sems) = rest[amount + 2 : -2], rest[-2:]
    head = pl.program_id(0)
    loads = [
        pltpu.make_async_copy(piece, stage, load_sems.at[slot])
        for slot, (piece, stage) in enumerate(zip(pieces, staged))
    ]
    stores = [
        pltpu.make_async_copy(
            stage, out.at[planes, :, start : start + stage.shape[-1]], store_sems.at[slot]
        )
        for slot, (stage, (planes, start)) in enumerate(zip(staged, places))
    ]

    def head_copy(index):
        start = pl.multiple_of((first + index) * HEAD_DIM, HEAD_DIM)
        return pltpu.make_async_copy(
            held.at[index],
            out.at[pl.ds(1, 2), :, pl.ds(start, HEAD_DIM)],
            store_sems.at[amount + index],
        )

    @pl.when(head == 0)
    def _():
        for load in loads:
            load.start()

    @pl.when(head == min(1, count - 1))
    def _():
        for load, store in zip(loads, stores):
            load.wait()
            store.start()

    key_grad, value_grad = finished(info, key, own, from_even, from_odd)
    held[head, 0] = key_grad.astype(held.dtype)
    held[head, 1] = value_grad.astype(held.dtype)
    head_copy(head).start()

    @pl.when(head == count - 1)
    def _():
        for store in stores:
            store.wait()
        for index in range(count):
            head_copy(index).wait()


def head_block(rows, first, slot=None):
    if slot is None:
        return pl.BlockSpec((rows, HEAD_DIM), lambda head: (0, first + head))
    return pl.BlockSpec((None, rows, HEAD_DIM), lambda head: (slot, 0, first + head))


def pair_block(rows, first=0):
    return pl.BlockSpec((2, rows, HEAD_DIM), lambda head: (0, 0, first + head))


def whole_block(shape):
    return pl.BlockSpec(shape, lambda head: (0,) * len(shape))


def pack_params(limit):
    return dict(
        scratch_shapes=[pltpu.SemaphoreType.DMA((2,))],
        compiler_params=pltpu.CompilerParams(vmem_limit_bytes=limit),
        cost_estimate=COST,
    )


def pack_call(first_in, second_in, first, count, limit=PACK_VMEM):
    rows = first_in.shape[0]
    width = count * HEAD_DIM
    return pl.pallas_call(
        functools.partial(pack_kernel, start=first * HEAD_DIM, width=width),
        grid=(1,),
        in_specs=[pl.BlockSpec(memory_space=pl.ANY)] * 2,
        out_specs=whole_block((2, rows, width)),
        out_shape=jax.ShapeDtypeStruct((2, rows, width), jnp.bfloat16),
        **pack_params(limit),
    )(first_in, second_in)


def ask_call(info, query, grad, first, count):
    rows = query.shape[0]
    width = count * HEAD_DIM
    return pl.pallas_call(
        functools.partial(ask_kernel, start=first * HEAD_DIM, width=width),
        grid=(1,),
        in_specs=[whole_block(info.shape)] + [pl.BlockSpec(memory_space=pl.ANY)] * 2,
        out_specs=whole_block((2, rows + 16, width)),
        out_shape=jax.ShapeDtypeStruct((2, rows + 16, width), jnp.bfloat16),
        **pack_params(PACK_VMEM),
    )(info, query, grad)


def info_call(listed, gains):
    return pl.pallas_call(
        info_kernel,
        in_specs=[pl.BlockSpec(memory_space=pltpu.SMEM), pl.BlockSpec(memory_space=pltpu.VMEM)],
        out_specs=pl.BlockSpec(memory_space=pltpu.VMEM),
        out_shape=jax.ShapeDtypeStruct((8, HEAD_DIM), jnp.float32),
        compiler_params=pltpu.CompilerParams(vmem_limit_bytes=PACK_VMEM),
        cost_estimate=LONG_COST,
    )(listed, gains)


def info_block(info):
    if info.ndim == 2:
        return whole_block(info.shape)
    below = info.shape[1] // 16 - 1
    return pl.BlockSpec((2, 16, HEAD_DIM), lambda head: (0, below, 0))


def main_call(info, operands, pair_even, pair_odd, count, heads, place):
    rows = pair_even.shape[1]
    lanes = count * HEAD_DIM
    return pl.pallas_call(
        main_kernel,
        grid=(count,),
        in_specs=[info_block(info)]
        + [head_block(rows, first, slot) for _, first, slot in operands]
        + [pair_block(rows)] * 2,
        out_specs=[head_block(rows, place)] + [pair_block(rows)] * 3 + [whole_block((8, HEAD_DIM))],
        out_shape=[
            jax.ShapeDtypeStruct((rows, heads * HEAD_DIM), jnp.bfloat16),
            jax.ShapeDtypeStruct((2, rows, lanes), jnp.float32),
            jax.ShapeDtypeStruct((2, rows, lanes), jnp.bfloat16),
            jax.ShapeDtypeStruct((2, rows, lanes), jnp.bfloat16),
            jax.ShapeDtypeStruct((8, HEAD_DIM), jnp.float32),
        ],
        compiler_params=pltpu.CompilerParams(vmem_limit_bytes=MAIN_VMEM),
        cost_estimate=MAIN_COST,
    )(info, *[array for array, _, _ in operands], pair_even, pair_odd)


def finish_call(info, key, own, from_even, from_odd, count):
    array, first, slot = key
    rows = own.shape[1]
    return pl.pallas_call(
        finish_kernel,
        grid=(count,),
        in_specs=[info_block(info), head_block(rows, first, slot)] + [pair_block(rows)] * 3,
        out_specs=pair_block(rows),
        out_shape=jax.ShapeDtypeStruct((2, rows, count * HEAD_DIM), jnp.bfloat16),
        compiler_params=pltpu.CompilerParams(vmem_limit_bytes=SMALL_VMEM),
        cost_estimate=COST,
    )(info, array, own, from_even, from_odd)


def row_block(rows, first):
    return pl.BlockSpec((8, rows), lambda head: (first + head, 0))


def sums_call(info, arrays, pair_even, pair_odd, first, count, heads, earlier, far_count):
    rows = pair_even.shape[1]
    amount = 2 + far_count
    earlier = [] if earlier is None else earlier
    return pl.pallas_call(
        functools.partial(sums_kernel, far_count=far_count),
        grid=(count,),
        in_specs=[info_block(info)]
        + [head_block(rows, first)] * 4
        + [pair_block(rows)] * 2
        + [pl.BlockSpec(memory_space=pl.ANY)] * len(earlier),
        out_specs=[row_block(rows, first)] * amount,
        out_shape=[jax.ShapeDtypeStruct((8 * heads, rows), jnp.float32)] * amount,
        input_output_aliases={7 + index: index for index in range(len(earlier))},
        compiler_params=pltpu.CompilerParams(vmem_limit_bytes=MAIN_VMEM),
        cost_estimate=MAIN_COST,
    )(info, *arrays, pair_even, pair_odd, *earlier)


def grads_call(info, arrays, pair_even, pair_odd, sums, first, count, heads, earlier, far_count):
    rows = pair_even.shape[1]
    lanes = heads * HEAD_DIM
    earlier = [] if earlier is None else earlier
    place = 7 + len(sums)
    return pl.pallas_call(
        functools.partial(grads_kernel, far_count=far_count),
        grid=(count,),
        in_specs=[info_block(info)]
        + [head_block(rows, first)] * 4
        + [pair_block(rows)] * 2
        + [row_block(rows, first)] * len(sums)
        + [pl.BlockSpec(memory_space=pl.ANY)] * len(earlier),
        out_specs=[pair_block(rows, first)]
        + [head_block(rows, first)] * 3
        + [whole_block((8, HEAD_DIM))],
        out_shape=[
            jax.ShapeDtypeStruct((2, rows, lanes), jnp.bfloat16),
            jax.ShapeDtypeStruct((rows, lanes), jnp.float32),
            jax.ShapeDtypeStruct((rows, lanes), jnp.bfloat16),
            jax.ShapeDtypeStruct((rows, lanes), jnp.bfloat16),
            jax.ShapeDtypeStruct((8, HEAD_DIM), jnp.float32),
        ],
        input_output_aliases={place + index: index for index in range(len(earlier))},
        compiler_params=pltpu.CompilerParams(vmem_limit_bytes=MAIN_VMEM),
        cost_estimate=GRAD_COST,
    )(info, *arrays, pair_even, pair_odd, *sums, *earlier)


def answer_call(info, query, own, from_even, from_odd, low):
    rows, lanes = own.shape
    return pl.pallas_call(
        answer_kernel,
        grid=(lanes // HEAD_DIM,),
        in_specs=[info_block(info)]
        + [head_block(rows, 0)] * 4
        + [pl.BlockSpec(memory_space=pl.ANY)],
        out_specs=head_block(rows, 0),
        out_shape=jax.ShapeDtypeStruct(low.shape, low.dtype),
        input_output_aliases={5: 0},
        compiler_params=pltpu.CompilerParams(vmem_limit_bytes=SMALL_VMEM),
        cost_estimate=LONG_COST,
    )(info, query, own, from_even, from_odd, low)


def last_call(info, key, own, from_even, from_odd, pieces, places, first, count):
    array, offset, slot = key
    rows = own.shape[1]
    anywhere = pl.BlockSpec(memory_space=pl.ANY)
    return pl.pallas_call(
        functools.partial(last_kernel, places=places, first=first, count=count),
        grid=(count,),
        in_specs=[info_block(info), head_block(rows, offset, slot)]
        + [pair_block(rows)] * 3
        + [anywhere] * len(pieces),
        out_specs=anywhere,
        out_shape=jax.ShapeDtypeStruct((3, rows, HEADS * HEAD_DIM), jnp.bfloat16),
        scratch_shapes=[
            pltpu.VMEM((count, 2, rows, HEAD_DIM), jnp.bfloat16),
            *[pltpu.VMEM(piece.shape, piece.dtype) for piece in pieces],
            pltpu.SemaphoreType.DMA((len(pieces),)),
            pltpu.SemaphoreType.DMA((len(pieces) + count,)),
        ],
        compiler_params=pltpu.CompilerParams(vmem_limit_bytes=SMALL_VMEM),
        cost_estimate=COST,
    )(info, array, own, from_even, from_odd, *pieces)


def partner(tile, parity, count):
    other = tile + 1 if tile % 2 == parity else tile - 1
    return other if 0 <= other < count else tile


def far_partner(tile, base, count):
    other = ((tile - base) ^ 2) + base if tile >= base else tile
    return other if 0 <= other < count else tile


def paired(value, partners):
    width = lax.axis_size("dp")
    pairs = []
    for tile, other in enumerate(partners):
        for sample in range(width):
            moved = sample ^ 1 if other == tile and width % 2 == 0 else sample
            pairs.append((tile * width + sample, other * width + moved))
    return lax.ppermute(value, ("seq", "dp"), pairs)


def exchanged(value, parity):
    count = lax.axis_size("seq")
    return paired(value, [partner(tile, parity, count) for tile in range(count)])


def far_partners(count):
    both = [[far_partner(tile, base, count) for tile in range(count)] for base in (0, 2)]
    return [partners for partners in both if partners != list(range(count))]


def after(value, *others):
    return lax.optimization_barrier((value, *others))[0]


def turned(value, step):
    count = lax.axis_size("pipe")
    return lax.ppermute(value, "pipe", [(i, (i + step) % count) for i in range(count)])


def total_over(value, axis, *late):
    count = lax.axis_size(axis)
    step = 1
    while step < count:
        other = lax.ppermute(value, axis, [(i, i ^ step) for i in range(count)])
        step *= 2
        value = value + (other if step < count else after(other, *late))
    return value


def local(queries, keys, values, grad_out, norm_gains, kv_tiles):
    query, key, value, grad = (a[0, 0, 0] for a in (queries, keys, values, grad_out))
    rows = query.shape[0]
    seq_count = lax.axis_size("seq")
    key_first, key_count = KEY_GROUP
    away_first, away_count = AWAY_GROUP
    fars = far_partners(seq_count)
    arrays = (query, grad, key, value)
    asks = [pack_call(query, grad, *QUERY_GROUPS[0])]
    away_pair = pack_call(after(key, asks[0]), value, away_first, away_count)
    for first, count in QUERY_GROUPS[1:]:
        asks.append(pack_call(after(query, away_pair), grad, first, count))
    told_pairs = [(exchanged(ask, 0), exchanged(ask, 1)) for ask in asks]
    key_pair = pack_call(after(key, asks[-1]), value, key_first, key_count)
    key_pair = after(key_pair, *told_pairs[0])
    key_pairs = (exchanged(key_pair, 0), exchanged(key_pair, 1))
    info = info_call(kv_tiles[0, 0, 0], after(norm_gains[0], asks[-1]))
    away_pair = turned(away_pair, -1)
    sums = None
    for (first, count), told in zip(QUERY_GROUPS, told_pairs):
        sums = sums_call(info, arrays, *told, first, count, key_first, sums, len(fars))
    ready = [after(value, *key_pairs) for value in sums]
    received = [exchanged(ready[0], 0), exchanged(ready[1], 1)]
    received += [paired(value, partners) for value, partners in zip(ready[2:], fars)]
    all_sums = (*sums[:2], *received)
    asked = ask_call(info, after(query, away_pair, sums[0]), grad, away_first, away_count)
    asked = turned(asked, -1)
    away_sent = after(away_pair, *received)
    away_pairs = (exchanged(away_sent, 0), exchanged(away_sent, 1))
    gains, parts = [], None
    for (first, count), told in zip(QUERY_GROUPS, told_pairs):
        *parts, gain = grads_call(
            info, arrays, *told, all_sums, first, count, key_first, parts, len(fars)
        )
        gains.append(gain[:2])
    pair_low, own, to_even, to_odd = parts
    pieces = [turned(pair_low, -1)]
    places = [(slice(1, 3), 0)]
    answer = (own, exchanged(to_even, 0), exchanged(to_odd, 1))
    operands = [(array, key_first, None) for array in arrays]
    low, own, to_even, to_odd, gain = main_call(
        after(info, pair_low, asked), operands, *key_pairs, key_count, away_first, key_first
    )
    gains.append(gain[:2])
    key_answer = (own, exchanged(to_even, 0), exchanged(to_odd, 1))
    operands = [(asked, 0, 0), (asked, 0, 1), (away_pair, 0, 0), (away_pair, 0, 1)]
    query_low, own, to_even, to_odd, gain = main_call(
        after(asked, low), operands, *away_pairs, away_count, away_count, 0
    )
    returned = (exchanged(to_even, 0), exchanged(to_odd, 1))
    pieces.append(query_low)
    places.append((0, away_first * HEAD_DIM))
    low = answer_call(info, query, *answer, low)
    gains.append(turned(after(gain[:2], low, pieces[0]), 1))
    pieces.append(turned(after(low, gains[-1]), -1))
    places.append((0, 0))
    low = finish_call(after(info, pieces[0]), (key, key_first, None), *key_answer, key_count)
    pieces.append(turned(low, -1))
    places.append((slice(1, 3), key_first * HEAD_DIM))
    out = last_call(
        asked, operands[2], own, *returned, pieces, tuple(places), away_first, away_count
    )
    summed = total_over(total_over(sum(gains), "dp"), "seq", out)
    tokens = lax.axis_size("dp") * seq_count * rows * HEADS
    return (out[None, :, None, None], (summed / math.sqrt(tokens))[None])


def solution(mesh):
    placed = (
        P("pipe", "dp", "seq", None, None),
        P("pipe", "dp", "seq", None, None),
        P("pipe", "dp", "seq", None, None),
        P("pipe", "dp", "seq", None, None),
        P("pipe", None, None),
        P("pipe", "dp", "seq", None),
    )
    return jax.shard_map(
        local,
        mesh=mesh,
        in_specs=placed,
        out_specs=(P("pipe", None, "dp", "seq", None, None), P("pipe", None, None)),
        check_vma=False,
    )
```

```python
import functools
import math

import jax
import jax.numpy as jnp
from jax import lax
from jax.experimental import pallas as pl
from jax.experimental.pallas import tpu as pltpu
from jax.sharding import PartitionSpec as P

HEADS = 12
HEAD_DIM = 128
EPSILON = 1e-06
ROOT_SCALE = HEAD_DIM ** (-0.5)
EXP2_SCALE = ROOT_SCALE * math.log2(math.e)
QUERY_GROUPS = ((0, 3), (3, 2))
KEY_GROUP = (5, 2)
AWAY_GROUP = (7, 5)
MAIN_VMEM = 20 * 1024 * 1024
SMALL_VMEM = 12 * 1024 * 1024
PACK_VMEM = 4 * 1024 * 1024
COST = pl.CostEstimate(flops=1, bytes_accessed=1, transcendentals=0)
LONG_COST = pl.CostEstimate(flops=2 * 10**10, bytes_accessed=1, transcendentals=0)
GRAD_COST = pl.CostEstimate(flops=4000000000, bytes_accessed=1, transcendentals=0)
MAIN_COST = pl.CostEstimate(flops=6 * 10**9, bytes_accessed=1, transcendentals=0)


def dot_nt(left, right):
    return lax.dot_general(
        left, right, (((1,), (1,)), ((), ())), preferred_element_type=jnp.float32
    )


def dot_nn(left, right):
    return lax.dot_general(
        left, right, (((1,), (0,)), ((), ())), preferred_element_type=jnp.float32
    )


def dot_tn(left, right):
    return lax.dot_general(
        left, right, (((0,), (0,)), ((), ())), preferred_element_type=jnp.float32
    )


def normalize(source, gain):
    floats = source.astype(jnp.float32)
    scaled = lax.rsqrt(jnp.mean(floats * floats, axis=-1, keepdims=True) + EPSILON)
    normed = floats * scaled
    return floats, scaled, normed, (normed * gain).astype(jnp.bfloat16)


def norm_back(grad_hat, floats, scaled, gain):
    scaled_grad = gain * grad_hat
    projected = jnp.sum(scaled_grad * floats, axis=-1, keepdims=True)
    return scaled * scaled_grad - (scaled**3 * projected * (1.0 / HEAD_DIM)) * floats


def pack_kernel(first_in, second_in, out, sems, *, start, width):
    rows = first_in.shape[0]
    copies = [
        pltpu.make_async_copy(
            source.at[:, start : start + width], out.at[slot, :rows], sems.at[slot]
        )
        for slot, source in enumerate((first_in, second_in))
    ]
    for copy in copies:
        copy.start()
    for copy in copies:
        copy.wait()


def info_kernel(listed, gains, info):
    tile = lax.axis_index("seq")
    last = lax.axis_size("seq") - 1
    info[...] = jnp.zeros_like(info)
    info[0:2, :] = gains[...]
    for parity in range(2):
        other = jnp.where(lax.rem(tile, 2) == parity, tile + 1, tile - 1)
        found = listed[0] == other
        for slot in range(1, listed.shape[0]):
            found = found | (listed[slot] == other)
        found = found & (other >= 0) & (other <= last)
        live = jnp.where(found, 1.0, 0.0)
        info[2 + parity : 3 + parity, :] = jnp.full((1, HEAD_DIM), live, jnp.float32)


def ask_kernel(info, query, grad, out, sems, *, start, width):
    rows = query.shape[0]
    value = info[...]
    planes = []
    for _ in range(3):
        low = value.astype(jnp.bfloat16)
        planes.append(low)
        value = value - low.astype(jnp.float32)
    planes.append(jnp.zeros_like(planes[0]))
    out[0, rows : rows + 16, :HEAD_DIM] = jnp.concatenate(planes[:2], axis=0)
    out[1, rows : rows + 16, :HEAD_DIM] = jnp.concatenate(planes[2:], axis=0)
    pack_kernel(query, grad, out, sems, start=start, width=width)


def told_info(told):
    floats = told[...].astype(jnp.float32)
    return floats[0, 0:8] + floats[0, 8:16] + floats[1, 0:8]


def main_kernel(
    info, query, grad, key, value, pair_even, pair_odd, *rest
):
    query_out, own_out, even_out, odd_out, gain_out = rest[-5:]
    told = told_info(info) if len(info.shape) == 3 else info[...]
    query_gain = told[0:1]
    key_gain = told[1:2]
    rows = query.shape[0]
    lives = [jnp.concatenate([told[row : row + 1]] * (rows // HEAD_DIM), axis=1) for row in (2, 3)]
    query_floats, query_scale, query_normed, query_hat = normalize(query[...], query_gain)
    grad_in = grad[...]
    sides = (
        (key[...], value[...], None),
        (pair_even[0], pair_even[1], lives[0]),
        (pair_odd[0], pair_odd[1], lives[1]),
    )
    parts = []
    totals = None
    for key_in, value_in, live in sides:
        _, _, key_normed, key_hat = normalize(key_in, key_gain)
        weights = jnp.exp2(dot_nt(key_hat, query_hat) * EXP2_SCALE)
        grad_probs = dot_nt(value_in, grad_in)
        weight_sum = jnp.sum(weights, axis=0, keepdims=True)
        cross_sum = jnp.sum(weights * grad_probs, axis=0, keepdims=True)
        if live is not None:
            weight_sum = weight_sum * live
            cross_sum = cross_sum * live
        totals = weight_sum if totals is None else totals + weight_sum
        crosses = cross_sum if live is None else crosses + cross_sum
        parts.append((key_normed, key_hat, weights, grad_probs, live))
    inverse = 1.0 / totals
    deltas = crosses * inverse
    query_grad_t = None
    key_gain_sum = None
    for (key_normed, key_hat, weights, grad_probs, live), out in zip(
        parts, (own_out, even_out, odd_out)
    ):
        probs = weights * (inverse if live is None else inverse * live)
        dscores = (probs * (grad_probs - deltas)).astype(jnp.bfloat16)
        key_part = dot_nn(dscores, query_hat) * ROOT_SCALE
        value_part = dot_nn(probs.astype(jnp.bfloat16), grad_in)
        out[0] = key_part.astype(out.dtype)
        out[1] = value_part.astype(out.dtype)
        gain_part = jnp.sum(key_part * key_normed, axis=0, keepdims=True)
        key_gain_sum = gain_part if key_gain_sum is None else key_gain_sum + gain_part
        query_part = dot_tn(key_hat, dscores)
        query_grad_t = query_part if query_grad_t is None else query_grad_t + query_part
    query_grad = query_grad_t.T * ROOT_SCALE
    query_out[...] = norm_back(query_grad, query_floats, query_scale, query_gain).astype(
        query_out.dtype
    )
    query_gain_sum = jnp.sum(query_grad * query_normed, axis=0, keepdims=True)

    @pl.when(pl.program_id(0) == 0)
    def _():
        gain_out[...] = jnp.zeros_like(gain_out)

    gain_out[0:1, :] += query_gain_sum
    gain_out[1:2, :] += key_gain_sum


def tile_sums(key_hat, value_in, query_hat, grad_in):
    weights = jnp.exp2(dot_nt(key_hat, query_hat) * EXP2_SCALE)
    grad_probs = dot_nt(value_in, grad_in)
    return weights, grad_probs


def wide_lives(told, rows):
    return [jnp.concatenate([told[row : row + 1]] * (rows // HEAD_DIM), axis=1) for row in (2, 3)]


def near_is_even():
    place = lax.rem(lax.axis_index("seq"), 4)
    return (place == 0) | (place == 3)


def sums_kernel(info, query, grad, key, value, pair_even, pair_odd, *rest, far_count):
    outs = rest[-2 - far_count :]
    told = info[...]
    _, _, _, key_hat = normalize(key[...], told[1:2])
    value_in = value[...]
    rows = []
    for query_in, grad_in in (
        (query[...], grad[...]), (pair_even[0], pair_even[1]), (pair_odd[0], pair_odd[1])
    ):
        _, _, _, query_hat = normalize(query_in, told[0:1])
        weights, grad_probs = tile_sums(key_hat, value_in, query_hat, grad_in)
        rows.append(
            [
                jnp.sum(weights, axis=0, keepdims=True),
                jnp.sum(weights * grad_probs, axis=0, keepdims=True),
            ]
        )
    own, even, odd = rows
    tail = wide_lives(told, query.shape[0])
    blank = jnp.zeros_like(tail[0])
    outs[0][...] = jnp.concatenate([*own, *even, *tail, blank, blank], axis=0)
    outs[1][...] = jnp.concatenate([*own, *odd, *tail, blank, blank], axis=0)
    near = near_is_even()
    for index, out in enumerate(outs[2:]):
        first, second = (even, odd) if index == 0 else (odd, even)
        chosen = [jnp.where(near, one, two) for one, two in zip(first, second)]
        out[...] = jnp.concatenate([*chosen, *[blank] * 6], axis=0)


def grads_kernel(
    info, query, grad, key, value, pair_even, pair_odd,
    sent_even, sent_odd, from_even, from_odd, *rest, far_count,
):
    fars = [far[0:2, :] for far in rest[:far_count]]
    pair_out, own_out, even_out, odd_out, gain_out = rest[-5:]
    told = info[...]
    near = near_is_even()
    if far_count == 2:
        far_even = jnp.where(near, fars[0], fars[1])
        far_odd = jnp.where(near, fars[1], fars[0])
    elif far_count == 1:
        far_even = jnp.where(near, fars[0], jnp.zeros_like(fars[0]))
        far_odd = jnp.where(near, jnp.zeros_like(fars[0]), fars[0])
    else:
        far_even = far_odd = jnp.zeros_like(from_even[0:2, :])
    own_sums = (
        sent_even[0:2, :]
        + sent_even[4:5, :] * from_even[2:4, :]
        + sent_even[5:6, :] * from_odd[2:4, :]
    )
    even_sums = (
        from_even[0:2, :] + from_even[4:5, :] * sent_even[2:4, :] + from_even[5:6, :] * far_even
    )
    odd_sums = (
        from_odd[0:2, :] + from_odd[5:6, :] * sent_odd[2:4, :] + from_odd[4:5, :] * far_odd
    )
    key_floats, key_scale, key_normed, key_hat = normalize(key[...], told[1:2])
    value_in = value[...]
    key_grad = value_grad = query_gain_sum = None
    for query_in, grad_in, sums, live, out in (
        (query[...], grad[...], own_sums, None, own_out),
        (pair_even[0], pair_even[1], even_sums, from_even[4:5, :], even_out),
        (pair_odd[0], pair_odd[1], odd_sums, from_odd[5:6, :], odd_out),
    ):
        _, _, query_normed, query_hat = normalize(query_in, told[0:1])
        weights, grad_probs = tile_sums(key_hat, value_in, query_hat, grad_in)
        inverse = 1.0 / sums[0:1]
        deltas = sums[1:2] * inverse
        probs = weights * (inverse if live is None else inverse * live)
        dscores = (probs * (grad_probs - deltas)).astype(jnp.bfloat16)
        key_part = dot_nn(dscores, query_hat)
        value_part = dot_nn(probs.astype(jnp.bfloat16), grad_in)
        query_part = dot_tn(key_hat, dscores).T * ROOT_SCALE
        out[...] = query_part.astype(out.dtype)
        gain_part = jnp.sum(query_part * query_normed, axis=0, keepdims=True)
        key_grad = key_part if key_grad is None else key_grad + key_part
        value_grad = value_part if value_grad is None else value_grad + value_part
        query_gain_sum = gain_part if query_gain_sum is None else query_gain_sum + gain_part
    key_grad = key_grad * ROOT_SCALE
    key_back = norm_back(key_grad, key_floats, key_scale, told[1:2])
    pair_out[0] = key_back.astype(pair_out.dtype)
    pair_out[1] = value_grad.astype(pair_out.dtype)

    @pl.when(pl.program_id(0) == 0)
    def _():
        gain_out[...] = jnp.zeros_like(gain_out)

    gain_out[0:1, :] += query_gain_sum
    gain_out[1:2, :] += jnp.sum(key_grad * key_normed, axis=0, keepdims=True)


def answer_kernel(info, query, own, from_even, from_odd, _, out):
    gain = info[0:1, :]
    floats, scaled, _, _ = normalize(query[...], gain)
    total = own[...] + from_even[...].astype(jnp.float32) + from_odd[...].astype(jnp.float32)
    out[...] = norm_back(total, floats, scaled, gain).astype(out.dtype)


def finished(info, key, own, from_even, from_odd):
    told = told_info(info) if len(info.shape) == 3 else info[...]
    key_gain = told[1:2]
    key_floats, key_scale, _, _ = normalize(key[...], key_gain)
    key_grad = own[0] + from_even[0].astype(jnp.float32) + from_odd[0].astype(jnp.float32)
    value_grad = own[1] + from_even[1].astype(jnp.float32) + from_odd[1].astype(jnp.float32)
    return norm_back(key_grad, key_floats, key_scale, key_gain), value_grad


def finish_kernel(info, key, own, from_even, from_odd, out):
    key_grad, value_grad = finished(info, key, own, from_even, from_odd)
    out[0] = key_grad.astype(out.dtype)
    out[1] = value_grad.astype(out.dtype)


def last_kernel(info, key, own, from_even, from_odd, *rest, places, first, count):
    amount = len(places)
    pieces, (out, held) = rest[:amount], rest[amount : amount + 2]
    staged, (load_sems, store_sems) = rest[amount + 2 : -2], rest[-2:]
    head = pl.program_id(0)
    loads = [
        pltpu.make_async_copy(piece, stage, load_sems.at[slot])
        for slot, (piece, stage) in enumerate(zip(pieces, staged))
    ]
    stores = [
        pltpu.make_async_copy(
            stage, out.at[planes, :, start : start + stage.shape[-1]], store_sems.at[slot]
        )
        for slot, (stage, (planes, start)) in enumerate(zip(staged, places))
    ]

    def head_copy(index):
        start = pl.multiple_of((first + index) * HEAD_DIM, HEAD_DIM)
        return pltpu.make_async_copy(
            held.at[index],
            out.at[pl.ds(1, 2), :, pl.ds(start, HEAD_DIM)],
            store_sems.at[amount + index],
        )

    @pl.when(head == 0)
    def _():
        for load in loads:
            load.start()

    @pl.when(head == min(1, count - 1))
    def _():
        for load, store in zip(loads, stores):
            load.wait()
            store.start()

    key_grad, value_grad = finished(info, key, own, from_even, from_odd)
    held[head, 0] = key_grad.astype(held.dtype)
    held[head, 1] = value_grad.astype(held.dtype)
    head_copy(head).start()

    @pl.when(head == count - 1)
    def _():
        for store in stores:
            store.wait()
        for index in range(count):
            head_copy(index).wait()


def head_block(rows, first, slot=None):
    if slot is None:
        return pl.BlockSpec((rows, HEAD_DIM), lambda head: (0, first + head))
    return pl.BlockSpec((None, rows, HEAD_DIM), lambda head: (slot, 0, first + head))


def pair_block(rows, first=0):
    return pl.BlockSpec((2, rows, HEAD_DIM), lambda head: (0, 0, first + head))


def whole_block(shape):
    return pl.BlockSpec(shape, lambda head: (0,) * len(shape))


def pack_params(limit):
    return dict(
        scratch_shapes=[pltpu.SemaphoreType.DMA((2,))],
        compiler_params=pltpu.CompilerParams(vmem_limit_bytes=limit),
        cost_estimate=COST,
    )


def pack_call(first_in, second_in, first, count, limit=PACK_VMEM):
    rows = first_in.shape[0]
    width = count * HEAD_DIM
    return pl.pallas_call(
        functools.partial(pack_kernel, start=first * HEAD_DIM, width=width),
        grid=(1,),
        in_specs=[pl.BlockSpec(memory_space=pl.ANY)] * 2,
        out_specs=whole_block((2, rows, width)),
        out_shape=jax.ShapeDtypeStruct((2, rows, width), jnp.bfloat16),
        **pack_params(limit),
    )(first_in, second_in)


def ask_call(info, query, grad, first, count):
    rows = query.shape[0]
    width = count * HEAD_DIM
    return pl.pallas_call(
        functools.partial(ask_kernel, start=first * HEAD_DIM, width=width),
        grid=(1,),
        in_specs=[whole_block(info.shape)] + [pl.BlockSpec(memory_space=pl.ANY)] * 2,
        out_specs=whole_block((2, rows + 16, width)),
        out_shape=jax.ShapeDtypeStruct((2, rows + 16, width), jnp.bfloat16),
        **pack_params(PACK_VMEM),
    )(info, query, grad)


def info_call(listed, gains):
    return pl.pallas_call(
        info_kernel,
        in_specs=[pl.BlockSpec(memory_space=pltpu.SMEM), pl.BlockSpec(memory_space=pltpu.VMEM)],
        out_specs=pl.BlockSpec(memory_space=pltpu.VMEM),
        out_shape=jax.ShapeDtypeStruct((8, HEAD_DIM), jnp.float32),
        compiler_params=pltpu.CompilerParams(vmem_limit_bytes=PACK_VMEM),
        cost_estimate=LONG_COST,
    )(listed, gains)


def info_block(info):
    if info.ndim == 2:
        return whole_block(info.shape)
    below = info.shape[1] // 16 - 1
    return pl.BlockSpec((2, 16, HEAD_DIM), lambda head: (0, below, 0))


def main_call(info, operands, pair_even, pair_odd, count, heads, place):
    rows = pair_even.shape[1]
    lanes = count * HEAD_DIM
    return pl.pallas_call(
        main_kernel,
        grid=(count,),
        in_specs=[info_block(info)]
        + [head_block(rows, first, slot) for _, first, slot in operands]
        + [pair_block(rows)] * 2,
        out_specs=[head_block(rows, place)] + [pair_block(rows)] * 3 + [whole_block((8, HEAD_DIM))],
        out_shape=[
            jax.ShapeDtypeStruct((rows, heads * HEAD_DIM), jnp.bfloat16),
            jax.ShapeDtypeStruct((2, rows, lanes), jnp.float32),
            jax.ShapeDtypeStruct((2, rows, lanes), jnp.bfloat16),
            jax.ShapeDtypeStruct((2, rows, lanes), jnp.bfloat16),
            jax.ShapeDtypeStruct((8, HEAD_DIM), jnp.float32),
        ],
        compiler_params=pltpu.CompilerParams(vmem_limit_bytes=MAIN_VMEM),
        cost_estimate=MAIN_COST,
    )(info, *[array for array, _, _ in operands], pair_even, pair_odd)


def finish_call(info, key, own, from_even, from_odd, count):
    array, first, slot = key
    rows = own.shape[1]
    return pl.pallas_call(
        finish_kernel,
        grid=(count,),
        in_specs=[info_block(info), head_block(rows, first, slot)] + [pair_block(rows)] * 3,
        out_specs=pair_block(rows),
        out_shape=jax.ShapeDtypeStruct((2, rows, count * HEAD_DIM), jnp.bfloat16),
        compiler_params=pltpu.CompilerParams(vmem_limit_bytes=SMALL_VMEM),
        cost_estimate=COST,
    )(info, array, own, from_even, from_odd)


def row_block(rows, first):
    return pl.BlockSpec((8, rows), lambda head: (first + head, 0))


def sums_call(info, arrays, pair_even, pair_odd, first, count, heads, earlier, far_count):
    rows = pair_even.shape[1]
    amount = 2 + far_count
    earlier = [] if earlier is None else earlier
    return pl.pallas_call(
        functools.partial(sums_kernel, far_count=far_count),
        grid=(count,),
        in_specs=[info_block(info)]
        + [head_block(rows, first)] * 4
        + [pair_block(rows)] * 2
        + [pl.BlockSpec(memory_space=pl.ANY)] * len(earlier),
        out_specs=[row_block(rows, first)] * amount,
        out_shape=[jax.ShapeDtypeStruct((8 * heads, rows), jnp.float32)] * amount,
        input_output_aliases={7 + index: index for index in range(len(earlier))},
        compiler_params=pltpu.CompilerParams(vmem_limit_bytes=MAIN_VMEM),
        cost_estimate=MAIN_COST,
    )(info, *arrays, pair_even, pair_odd, *earlier)


def grads_call(info, arrays, pair_even, pair_odd, sums, first, count, heads, earlier, far_count):
    rows = pair_even.shape[1]
    lanes = heads * HEAD_DIM
    earlier = [] if earlier is None else earlier
    place = 7 + len(sums)
    return pl.pallas_call(
        functools.partial(grads_kernel, far_count=far_count),
        grid=(count,),
        in_specs=[info_block(info)]
        + [head_block(rows, first)] * 4
        + [pair_block(rows)] * 2
        + [row_block(rows, first)] * len(sums)
        + [pl.BlockSpec(memory_space=pl.ANY)] * len(earlier),
        out_specs=[pair_block(rows, first)]
        + [head_block(rows, first)] * 3
        + [whole_block((8, HEAD_DIM))],
        out_shape=[
            jax.ShapeDtypeStruct((2, rows, lanes), jnp.bfloat16),
            jax.ShapeDtypeStruct((rows, lanes), jnp.float32),
            jax.ShapeDtypeStruct((rows, lanes), jnp.bfloat16),
            jax.ShapeDtypeStruct((rows, lanes), jnp.bfloat16),
            jax.ShapeDtypeStruct((8, HEAD_DIM), jnp.float32),
        ],
        input_output_aliases={place + index: index for index in range(len(earlier))},
        compiler_params=pltpu.CompilerParams(vmem_limit_bytes=MAIN_VMEM),
        cost_estimate=GRAD_COST,
    )(info, *arrays, pair_even, pair_odd, *sums, *earlier)


def answer_call(info, query, own, from_even, from_odd, low):
    rows, lanes = own.shape
    return pl.pallas_call(
        answer_kernel,
        grid=(lanes // HEAD_DIM,),
        in_specs=[info_block(info)]
        + [head_block(rows, 0)] * 4
        + [pl.BlockSpec(memory_space=pl.ANY)],
        out_specs=head_block(rows, 0),
        out_shape=jax.ShapeDtypeStruct(low.shape, low.dtype),
        input_output_aliases={5: 0},
        compiler_params=pltpu.CompilerParams(vmem_limit_bytes=SMALL_VMEM),
        cost_estimate=LONG_COST,
    )(info, query, own, from_even, from_odd, low)


def last_call(info, key, own, from_even, from_odd, pieces, places, first, count):
    array, offset, slot = key
    rows = own.shape[1]
    anywhere = pl.BlockSpec(memory_space=pl.ANY)
    return pl.pallas_call(
        functools.partial(last_kernel, places=places, first=first, count=count),
        grid=(count,),
        in_specs=[info_block(info), head_block(rows, offset, slot)]
        + [pair_block(rows)] * 3
        + [anywhere] * len(pieces),
        out_specs=anywhere,
        out_shape=jax.ShapeDtypeStruct((3, rows, HEADS * HEAD_DIM), jnp.bfloat16),
        scratch_shapes=[
            pltpu.VMEM((count, 2, rows, HEAD_DIM), jnp.bfloat16),
            *[pltpu.VMEM(piece.shape, piece.dtype) for piece in pieces],
            pltpu.SemaphoreType.DMA((len(pieces),)),
            pltpu.SemaphoreType.DMA((len(pieces) + count,)),
        ],
        compiler_params=pltpu.CompilerParams(vmem_limit_bytes=SMALL_VMEM),
        cost_estimate=COST,
    )(info, array, own, from_even, from_odd, *pieces)


def partner(tile, parity, count):
    other = tile + 1 if tile % 2 == parity else tile - 1
    return other if 0 <= other < count else tile


def far_partner(tile, base, count):
    other = ((tile - base) ^ 2) + base if tile >= base else tile
    return other if 0 <= other < count else tile


def paired(value, partners):
    width = lax.axis_size("dp")
    pairs = []
    for tile, other in enumerate(partners):
        for sample in range(width):
            moved = sample ^ 1 if other == tile and width % 2 == 0 else sample
            pairs.append((tile * width + sample, other * width + moved))
    return lax.ppermute(value, ("seq", "dp"), pairs)


def exchanged(value, parity):
    count = lax.axis_size("seq")
    return paired(value, [partner(tile, parity, count) for tile in range(count)])


def far_partners(count):
    both = [[far_partner(tile, base, count) for tile in range(count)] for base in (0, 2)]
    return [partners for partners in both if partners != list(range(count))]


def after(value, *others):
    return lax.optimization_barrier((value, *others))[0]


def turned(value, step):
    count = lax.axis_size("pipe")
    return lax.ppermute(value, "pipe", [(i, (i + step) % count) for i in range(count)])


def total_over(value, axis, *late):
    count = lax.axis_size(axis)
    step = 1
    while step < count:
        other = lax.ppermute(value, axis, [(i, i ^ step) for i in range(count)])
        step *= 2
        value = value + (other if step < count else after(other, *late))
    return value


def local(queries, keys, values, grad_out, norm_gains, kv_tiles):
    query, key, value, grad = (a[0, 0, 0] for a in (queries, keys, values, grad_out))
    rows = query.shape[0]
    seq_count = lax.axis_size("seq")
    key_first, key_count = KEY_GROUP
    away_first, away_count = AWAY_GROUP
    fars = far_partners(seq_count)
    arrays = (query, grad, key, value)
    asks = [pack_call(query, grad, *QUERY_GROUPS[0])]
    away_pair = pack_call(after(key, asks[0]), value, away_first, away_count)
    for first, count in QUERY_GROUPS[1:]:
        asks.append(pack_call(after(query, away_pair), grad, first, count))
    told_pairs = [(exchanged(ask, 0), exchanged(ask, 1)) for ask in asks]
    key_pair = pack_call(after(key, asks[-1]), value, key_first, key_count)
    key_pair = after(key_pair, *told_pairs[0])
    key_pairs = (exchanged(key_pair, 0), exchanged(key_pair, 1))
    info = info_call(kv_tiles[0, 0, 0], after(norm_gains[0], asks[-1]))
    away_pair = turned(away_pair, -1)
    sums = None
    for (first, count), told in zip(QUERY_GROUPS, told_pairs):
        sums = sums_call(info, arrays, *told, first, count, key_first, sums, len(fars))
    ready = [*sums[:2], *[after(value, *key_pairs) for value in sums[2:]]]
    received = [exchanged(ready[0], 0), exchanged(ready[1], 1)]
    received += [paired(value, partners) for value, partners in zip(ready[2:], fars)]
    all_sums = (*sums[:2], *received)
    asked = ask_call(info, after(query, away_pair, sums[0]), grad, away_first, away_count)
    asked = turned(asked, -1)
    away_sent = after(away_pair, *received)
    away_pairs = (exchanged(away_sent, 0), exchanged(away_sent, 1))
    gains, parts = [], None
    for (first, count), told in zip(QUERY_GROUPS, told_pairs):
        *parts, gain = grads_call(
            info, arrays, *told, all_sums, first, count, key_first, parts, len(fars)
        )
        gains.append(gain[:2])
    pair_low, own, to_even, to_odd = parts
    pieces = [turned(pair_low, -1)]
    places = [(slice(1, 3), 0)]
    answer = (own, exchanged(to_even, 0), exchanged(to_odd, 1))
    operands = [(array, key_first, None) for array in arrays]
    low, own, to_even, to_odd, gain = main_call(
        after(info, pair_low, asked), operands, *key_pairs, key_count, away_first, key_first
    )
    gains.append(gain[:2])
    key_answer = (own, exchanged(to_even, 0), exchanged(to_odd, 1))
    operands = [(asked, 0, 0), (asked, 0, 1), (away_pair, 0, 0), (away_pair, 0, 1)]
    query_low, own, to_even, to_odd, gain = main_call(
        after(asked, low), operands, *away_pairs, away_count, away_count, 0
    )
    returned = (exchanged(to_even, 0), exchanged(to_odd, 1))
    pieces.append(query_low)
    places.append((0, away_first * HEAD_DIM))
    gains.append(turned(after(gain[:2], pieces[0]), 1))
    low = answer_call(info, query, *answer, low)
    pieces.append(turned(after(low, gains[-1]), -1))
    places.append((0, 0))
    low = finish_call(after(info, pieces[0]), (key, key_first, None), *key_answer, key_count)
    pieces.append(turned(low, -1))
    places.append((slice(1, 3), key_first * HEAD_DIM))
    out = last_call(
        asked, operands[2], own, *returned, pieces, tuple(places), away_first, away_count
    )
    summed = total_over(total_over(sum(gains), "dp"), "seq", out)
    tokens = lax.axis_size("dp") * seq_count * rows * HEADS
    return (out[None, :, None, None], (summed / math.sqrt(tokens))[None])


def solution(mesh):
    placed = (
        P("pipe", "dp", "seq", None, None),
        P("pipe", "dp", "seq", None, None),
        P("pipe", "dp", "seq", None, None),
        P("pipe", "dp", "seq", None, None),
        P("pipe", None, None),
        P("pipe", "dp", "seq", None),
    )
    return jax.shard_map(
        local,
        mesh=mesh,
        in_specs=placed,
        out_specs=(P("pipe", None, "dp", "seq", None, None), P("pipe", None, None)),
        check_vma=False,
    )
```

```python
import functools
import math

import jax
import jax.numpy as jnp
from jax import lax
from jax.experimental import pallas as pl
from jax.experimental.pallas import tpu as pltpu
from jax.sharding import PartitionSpec as P

HEADS = 12
HEAD_DIM = 128
EPSILON = 1e-06
ROOT_SCALE = HEAD_DIM ** (-0.5)
EXP2_SCALE = ROOT_SCALE * math.log2(math.e)
QUERY_GROUPS = ((0, 4), (4, 2))
KEY_GROUP = (6, 1)
AWAY_GROUP = (7, 5)
MAIN_VMEM = 20 * 1024 * 1024
SMALL_VMEM = 12 * 1024 * 1024
PACK_VMEM = 4 * 1024 * 1024
COST = pl.CostEstimate(flops=1, bytes_accessed=1, transcendentals=0)
LONG_COST = pl.CostEstimate(flops=2 * 10**10, bytes_accessed=1, transcendentals=0)
GRAD_COST = pl.CostEstimate(flops=4000000000, bytes_accessed=1, transcendentals=0)
MAIN_COST = pl.CostEstimate(flops=6 * 10**9, bytes_accessed=1, transcendentals=0)


def dot_nt(left, right):
    return lax.dot_general(
        left, right, (((1,), (1,)), ((), ())), preferred_element_type=jnp.float32
    )


def dot_nn(left, right):
    return lax.dot_general(
        left, right, (((1,), (0,)), ((), ())), preferred_element_type=jnp.float32
    )


def dot_tn(left, right):
    return lax.dot_general(
        left, right, (((0,), (0,)), ((), ())), preferred_element_type=jnp.float32
    )


def normalize(source, gain):
    floats = source.astype(jnp.float32)
    scaled = lax.rsqrt(jnp.mean(floats * floats, axis=-1, keepdims=True) + EPSILON)
    normed = floats * scaled
    return floats, scaled, normed, (normed * gain).astype(jnp.bfloat16)


def norm_back(grad_hat, floats, scaled, gain):
    scaled_grad = gain * grad_hat
    projected = jnp.sum(scaled_grad * floats, axis=-1, keepdims=True)
    return scaled * scaled_grad - (scaled**3 * projected * (1.0 / HEAD_DIM)) * floats


def pack_kernel(first_in, second_in, out, sems, *, start, width):
    rows = first_in.shape[0]
    copies = [
        pltpu.make_async_copy(
            source.at[:, start : start + width], out.at[slot, :rows], sems.at[slot]
        )
        for slot, source in enumerate((first_in, second_in))
    ]
    for copy in copies:
        copy.start()
    for copy in copies:
        copy.wait()


def info_kernel(listed, gains, info):
    tile = lax.axis_index("seq")
    last = lax.axis_size("seq") - 1
    info[...] = jnp.zeros_like(info)
    info[0:2, :] = gains[...]
    for parity in range(2):
        other = jnp.where(lax.rem(tile, 2) == parity, tile + 1, tile - 1)
        found = listed[0] == other
        for slot in range(1, listed.shape[0]):
            found = found | (listed[slot] == other)
        found = found & (other >= 0) & (other <= last)
        live = jnp.where(found, 1.0, 0.0)
        info[2 + parity : 3 + parity, :] = jnp.full((1, HEAD_DIM), live, jnp.float32)


def ask_kernel(info, query, grad, out, sems, *, start, width):
    rows = query.shape[0]
    value = info[...]
    planes = []
    for _ in range(3):
        low = value.astype(jnp.bfloat16)
        planes.append(low)
        value = value - low.astype(jnp.float32)
    planes.append(jnp.zeros_like(planes[0]))
    out[0, rows : rows + 16, :HEAD_DIM] = jnp.concatenate(planes[:2], axis=0)
    out[1, rows : rows + 16, :HEAD_DIM] = jnp.concatenate(planes[2:], axis=0)
    pack_kernel(query, grad, out, sems, start=start, width=width)


def told_info(told):
    floats = told[...].astype(jnp.float32)
    return floats[0, 0:8] + floats[0, 8:16] + floats[1, 0:8]


def main_kernel(
    info, query, grad, key, value, pair_even, pair_odd, *rest
):
    query_out, own_out, even_out, odd_out, gain_out = rest[-5:]
    told = told_info(info) if len(info.shape) == 3 else info[...]
    query_gain = told[0:1]
    key_gain = told[1:2]
    rows = query.shape[0]
    lives = [jnp.concatenate([told[row : row + 1]] * (rows // HEAD_DIM), axis=1) for row in (2, 3)]
    query_floats, query_scale, query_normed, query_hat = normalize(query[...], query_gain)
    grad_in = grad[...]
    sides = (
        (key[...], value[...], None),
        (pair_even[0], pair_even[1], lives[0]),
        (pair_odd[0], pair_odd[1], lives[1]),
    )
    parts = []
    totals = None
    for key_in, value_in, live in sides:
        _, _, key_normed, key_hat = normalize(key_in, key_gain)
        weights = jnp.exp2(dot_nt(key_hat, query_hat) * EXP2_SCALE)
        grad_probs = dot_nt(value_in, grad_in)
        weight_sum = jnp.sum(weights, axis=0, keepdims=True)
        cross_sum = jnp.sum(weights * grad_probs, axis=0, keepdims=True)
        if live is not None:
            weight_sum = weight_sum * live
            cross_sum = cross_sum * live
        totals = weight_sum if totals is None else totals + weight_sum
        crosses = cross_sum if live is None else crosses + cross_sum
        parts.append((key_normed, key_hat, weights, grad_probs, live))
    inverse = 1.0 / totals
    deltas = crosses * inverse
    query_grad_t = None
    key_gain_sum = None
    for (key_normed, key_hat, weights, grad_probs, live), out in zip(
        parts, (own_out, even_out, odd_out)
    ):
        probs = weights * (inverse if live is None else inverse * live)
        dscores = (probs * (grad_probs - deltas)).astype(jnp.bfloat16)
        key_part = dot_nn(dscores, query_hat) * ROOT_SCALE
        value_part = dot_nn(probs.astype(jnp.bfloat16), grad_in)
        out[0] = key_part.astype(out.dtype)
        out[1] = value_part.astype(out.dtype)
        gain_part = jnp.sum(key_part * key_normed, axis=0, keepdims=True)
        key_gain_sum = gain_part if key_gain_sum is None else key_gain_sum + gain_part
        query_part = dot_tn(key_hat, dscores)
        query_grad_t = query_part if query_grad_t is None else query_grad_t + query_part
    query_grad = query_grad_t.T * ROOT_SCALE
    query_out[...] = norm_back(query_grad, query_floats, query_scale, query_gain).astype(
        query_out.dtype
    )
    query_gain_sum = jnp.sum(query_grad * query_normed, axis=0, keepdims=True)

    @pl.when(pl.program_id(0) == 0)
    def _():
        gain_out[...] = jnp.zeros_like(gain_out)

    gain_out[0:1, :] += query_gain_sum
    gain_out[1:2, :] += key_gain_sum


def tile_sums(key_hat, value_in, query_hat, grad_in):
    weights = jnp.exp2(dot_nt(key_hat, query_hat) * EXP2_SCALE)
    grad_probs = dot_nt(value_in, grad_in)
    return weights, grad_probs


def wide_lives(told, rows):
    return [jnp.concatenate([told[row : row + 1]] * (rows // HEAD_DIM), axis=1) for row in (2, 3)]


def near_is_even():
    place = lax.rem(lax.axis_index("seq"), 4)
    return (place == 0) | (place == 3)


def sums_kernel(info, query, grad, key, value, pair_even, pair_odd, *rest, far_count):
    outs = rest[-2 - far_count :]
    told = info[...]
    _, _, _, key_hat = normalize(key[...], told[1:2])
    value_in = value[...]
    rows = []
    for query_in, grad_in in (
        (query[...], grad[...]), (pair_even[0], pair_even[1]), (pair_odd[0], pair_odd[1])
    ):
        _, _, _, query_hat = normalize(query_in, told[0:1])
        weights, grad_probs = tile_sums(key_hat, value_in, query_hat, grad_in)
        rows.append(
            [
                jnp.sum(weights, axis=0, keepdims=True),
                jnp.sum(weights * grad_probs, axis=0, keepdims=True),
            ]
        )
    own, even, odd = rows
    tail = wide_lives(told, query.shape[0])
    blank = jnp.zeros_like(tail[0])
    outs[0][...] = jnp.concatenate([*own, *even, *tail, blank, blank], axis=0)
    outs[1][...] = jnp.concatenate([*own, *odd, *tail, blank, blank], axis=0)
    near = near_is_even()
    for index, out in enumerate(outs[2:]):
        first, second = (even, odd) if index == 0 else (odd, even)
        chosen = [jnp.where(near, one, two) for one, two in zip(first, second)]
        out[...] = jnp.concatenate([*chosen, *[blank] * 6], axis=0)


def grads_kernel(
    info, query, grad, key, value, pair_even, pair_odd,
    sent_even, sent_odd, from_even, from_odd, *rest, far_count,
):
    fars = [far[0:2, :] for far in rest[:far_count]]
    pair_out, own_out, even_out, odd_out, gain_out = rest[-5:]
    told = info[...]
    near = near_is_even()
    if far_count == 2:
        far_even = jnp.where(near, fars[0], fars[1])
        far_odd = jnp.where(near, fars[1], fars[0])
    elif far_count == 1:
        far_even = jnp.where(near, fars[0], jnp.zeros_like(fars[0]))
        far_odd = jnp.where(near, jnp.zeros_like(fars[0]), fars[0])
    else:
        far_even = far_odd = jnp.zeros_like(from_even[0:2, :])
    own_sums = (
        sent_even[0:2, :]
        + sent_even[4:5, :] * from_even[2:4, :]
        + sent_even[5:6, :] * from_odd[2:4, :]
    )
    even_sums = (
        from_even[0:2, :] + from_even[4:5, :] * sent_even[2:4, :] + from_even[5:6, :] * far_even
    )
    odd_sums = (
        from_odd[0:2, :] + from_odd[5:6, :] * sent_odd[2:4, :] + from_odd[4:5, :] * far_odd
    )
    key_floats, key_scale, key_normed, key_hat = normalize(key[...], told[1:2])
    value_in = value[...]
    key_grad = value_grad = query_gain_sum = None
    for query_in, grad_in, sums, live, out in (
        (query[...], grad[...], own_sums, None, own_out),
        (pair_even[0], pair_even[1], even_sums, from_even[4:5, :], even_out),
        (pair_odd[0], pair_odd[1], odd_sums, from_odd[5:6, :], odd_out),
    ):
        _, _, query_normed, query_hat = normalize(query_in, told[0:1])
        weights, grad_probs = tile_sums(key_hat, value_in, query_hat, grad_in)
        inverse = 1.0 / sums[0:1]
        deltas = sums[1:2] * inverse
        probs = weights * (inverse if live is None else inverse * live)
        dscores = (probs * (grad_probs - deltas)).astype(jnp.bfloat16)
        key_part = dot_nn(dscores, query_hat)
        value_part = dot_nn(probs.astype(jnp.bfloat16), grad_in)
        query_part = dot_tn(key_hat, dscores).T * ROOT_SCALE
        out[...] = query_part.astype(out.dtype)
        gain_part = jnp.sum(query_part * query_normed, axis=0, keepdims=True)
        key_grad = key_part if key_grad is None else key_grad + key_part
        value_grad = value_part if value_grad is None else value_grad + value_part
        query_gain_sum = gain_part if query_gain_sum is None else query_gain_sum + gain_part
    key_grad = key_grad * ROOT_SCALE
    key_back = norm_back(key_grad, key_floats, key_scale, told[1:2])
    pair_out[0] = key_back.astype(pair_out.dtype)
    pair_out[1] = value_grad.astype(pair_out.dtype)

    @pl.when(pl.program_id(0) == 0)
    def _():
        gain_out[...] = jnp.zeros_like(gain_out)

    gain_out[0:1, :] += query_gain_sum
    gain_out[1:2, :] += jnp.sum(key_grad * key_normed, axis=0, keepdims=True)


def answer_kernel(info, query, own, from_even, from_odd, _, out):
    gain = info[0:1, :]
    floats, scaled, _, _ = normalize(query[...], gain)
    total = own[...] + from_even[...].astype(jnp.float32) + from_odd[...].astype(jnp.float32)
    out[...] = norm_back(total, floats, scaled, gain).astype(out.dtype)


def finished(info, key, own, from_even, from_odd):
    told = told_info(info) if len(info.shape) == 3 else info[...]
    key_gain = told[1:2]
    key_floats, key_scale, _, _ = normalize(key[...], key_gain)
    key_grad = own[0] + from_even[0].astype(jnp.float32) + from_odd[0].astype(jnp.float32)
    value_grad = own[1] + from_even[1].astype(jnp.float32) + from_odd[1].astype(jnp.float32)
    return norm_back(key_grad, key_floats, key_scale, key_gain), value_grad


def finish_kernel(info, key, own, from_even, from_odd, out):
    key_grad, value_grad = finished(info, key, own, from_even, from_odd)
    out[0] = key_grad.astype(out.dtype)
    out[1] = value_grad.astype(out.dtype)


def last_kernel(info, key, own, from_even, from_odd, *rest, places, first, count):
    amount = len(places)
    pieces, (out, held) = rest[:amount], rest[amount : amount + 2]
    staged, (load_sems, store_sems) = rest[amount + 2 : -2], rest[-2:]
    head = pl.program_id(0)
    loads = [
        pltpu.make_async_copy(piece, stage, load_sems.at[slot])
        for slot, (piece, stage) in enumerate(zip(pieces, staged))
    ]
    stores = [
        pltpu.make_async_copy(
            stage, out.at[planes, :, start : start + stage.shape[-1]], store_sems.at[slot]
        )
        for slot, (stage, (planes, start)) in enumerate(zip(staged, places))
    ]

    def head_copy(index):
        start = pl.multiple_of((first + index) * HEAD_DIM, HEAD_DIM)
        return pltpu.make_async_copy(
            held.at[index],
            out.at[pl.ds(1, 2), :, pl.ds(start, HEAD_DIM)],
            store_sems.at[amount + index],
        )

    @pl.when(head == 0)
    def _():
        for load in loads:
            load.start()

    @pl.when(head == min(1, count - 1))
    def _():
        for load, store in zip(loads, stores):
            load.wait()
            store.start()

    key_grad, value_grad = finished(info, key, own, from_even, from_odd)
    held[head, 0] = key_grad.astype(held.dtype)
    held[head, 1] = value_grad.astype(held.dtype)
    head_copy(head).start()

    @pl.when(head == count - 1)
    def _():
        for store in stores:
            store.wait()
        for index in range(count):
            head_copy(index).wait()


def head_block(rows, first, slot=None):
    if slot is None:
        return pl.BlockSpec((rows, HEAD_DIM), lambda head: (0, first + head))
    return pl.BlockSpec((None, rows, HEAD_DIM), lambda head: (slot, 0, first + head))


def pair_block(rows, first=0):
    return pl.BlockSpec((2, rows, HEAD_DIM), lambda head: (0, 0, first + head))


def whole_block(shape):
    return pl.BlockSpec(shape, lambda head: (0,) * len(shape))


def pack_params(limit):
    return dict(
        scratch_shapes=[pltpu.SemaphoreType.DMA((2,))],
        compiler_params=pltpu.CompilerParams(vmem_limit_bytes=limit),
        cost_estimate=COST,
    )


def pack_call(first_in, second_in, first, count, limit=PACK_VMEM):
    rows = first_in.shape[0]
    width = count * HEAD_DIM
    return pl.pallas_call(
        functools.partial(pack_kernel, start=first * HEAD_DIM, width=width),
        grid=(1,),
        in_specs=[pl.BlockSpec(memory_space=pl.ANY)] * 2,
        out_specs=whole_block((2, rows, width)),
        out_shape=jax.ShapeDtypeStruct((2, rows, width), jnp.bfloat16),
        **pack_params(limit),
    )(first_in, second_in)


def ask_call(info, query, grad, first, count):
    rows = query.shape[0]
    width = count * HEAD_DIM
    return pl.pallas_call(
        functools.partial(ask_kernel, start=first * HEAD_DIM, width=width),
        grid=(1,),
        in_specs=[whole_block(info.shape)] + [pl.BlockSpec(memory_space=pl.ANY)] * 2,
        out_specs=whole_block((2, rows + 16, width)),
        out_shape=jax.ShapeDtypeStruct((2, rows + 16, width), jnp.bfloat16),
        **pack_params(PACK_VMEM),
    )(info, query, grad)


def info_call(listed, gains):
    return pl.pallas_call(
        info_kernel,
        in_specs=[pl.BlockSpec(memory_space=pltpu.SMEM), pl.BlockSpec(memory_space=pltpu.VMEM)],
        out_specs=pl.BlockSpec(memory_space=pltpu.VMEM),
        out_shape=jax.ShapeDtypeStruct((8, HEAD_DIM), jnp.float32),
        compiler_params=pltpu.CompilerParams(vmem_limit_bytes=PACK_VMEM),
        cost_estimate=LONG_COST,
    )(listed, gains)


def info_block(info):
    if info.ndim == 2:
        return whole_block(info.shape)
    below = info.shape[1] // 16 - 1
    return pl.BlockSpec((2, 16, HEAD_DIM), lambda head: (0, below, 0))


def main_call(info, operands, pair_even, pair_odd, count, heads, place):
    rows = pair_even.shape[1]
    lanes = count * HEAD_DIM
    return pl.pallas_call(
        main_kernel,
        grid=(count,),
        in_specs=[info_block(info)]
        + [head_block(rows, first, slot) for _, first, slot in operands]
        + [pair_block(rows)] * 2,
        out_specs=[head_block(rows, place)] + [pair_block(rows)] * 3 + [whole_block((8, HEAD_DIM))],
        out_shape=[
            jax.ShapeDtypeStruct((rows, heads * HEAD_DIM), jnp.bfloat16),
            jax.ShapeDtypeStruct((2, rows, lanes), jnp.float32),
            jax.ShapeDtypeStruct((2, rows, lanes), jnp.bfloat16),
            jax.ShapeDtypeStruct((2, rows, lanes), jnp.bfloat16),
            jax.ShapeDtypeStruct((8, HEAD_DIM), jnp.float32),
        ],
        compiler_params=pltpu.CompilerParams(vmem_limit_bytes=MAIN_VMEM),
        cost_estimate=MAIN_COST,
    )(info, *[array for array, _, _ in operands], pair_even, pair_odd)


def finish_call(info, key, own, from_even, from_odd, count):
    array, first, slot = key
    rows = own.shape[1]
    return pl.pallas_call(
        finish_kernel,
        grid=(count,),
        in_specs=[info_block(info), head_block(rows, first, slot)] + [pair_block(rows)] * 3,
        out_specs=pair_block(rows),
        out_shape=jax.ShapeDtypeStruct((2, rows, count * HEAD_DIM), jnp.bfloat16),
        compiler_params=pltpu.CompilerParams(vmem_limit_bytes=SMALL_VMEM),
        cost_estimate=COST,
    )(info, array, own, from_even, from_odd)


def row_block(rows, first):
    return pl.BlockSpec((8, rows), lambda head: (first + head, 0))


def sums_call(info, arrays, pair_even, pair_odd, first, count, heads, earlier, far_count):
    rows = pair_even.shape[1]
    amount = 2 + far_count
    earlier = [] if earlier is None else earlier
    return pl.pallas_call(
        functools.partial(sums_kernel, far_count=far_count),
        grid=(count,),
        in_specs=[info_block(info)]
        + [head_block(rows, first)] * 4
        + [pair_block(rows)] * 2
        + [pl.BlockSpec(memory_space=pl.ANY)] * len(earlier),
        out_specs=[row_block(rows, first)] * amount,
        out_shape=[jax.ShapeDtypeStruct((8 * heads, rows), jnp.float32)] * amount,
        input_output_aliases={7 + index: index for index in range(len(earlier))},
        compiler_params=pltpu.CompilerParams(vmem_limit_bytes=MAIN_VMEM),
        cost_estimate=MAIN_COST,
    )(info, *arrays, pair_even, pair_odd, *earlier)


def grads_call(info, arrays, pair_even, pair_odd, sums, first, count, heads, earlier, far_count):
    rows = pair_even.shape[1]
    lanes = heads * HEAD_DIM
    earlier = [] if earlier is None else earlier
    place = 7 + len(sums)
    return pl.pallas_call(
        functools.partial(grads_kernel, far_count=far_count),
        grid=(count,),
        in_specs=[info_block(info)]
        + [head_block(rows, first)] * 4
        + [pair_block(rows)] * 2
        + [row_block(rows, first)] * len(sums)
        + [pl.BlockSpec(memory_space=pl.ANY)] * len(earlier),
        out_specs=[pair_block(rows, first)]
        + [head_block(rows, first)] * 3
        + [whole_block((8, HEAD_DIM))],
        out_shape=[
            jax.ShapeDtypeStruct((2, rows, lanes), jnp.bfloat16),
            jax.ShapeDtypeStruct((rows, lanes), jnp.float32),
            jax.ShapeDtypeStruct((rows, lanes), jnp.bfloat16),
            jax.ShapeDtypeStruct((rows, lanes), jnp.bfloat16),
            jax.ShapeDtypeStruct((8, HEAD_DIM), jnp.float32),
        ],
        input_output_aliases={place + index: index for index in range(len(earlier))},
        compiler_params=pltpu.CompilerParams(vmem_limit_bytes=MAIN_VMEM),
        cost_estimate=GRAD_COST,
    )(info, *arrays, pair_even, pair_odd, *sums, *earlier)


def answer_call(info, query, own, from_even, from_odd, low):
    rows, lanes = own.shape
    return pl.pallas_call(
        answer_kernel,
        grid=(lanes // HEAD_DIM,),
        in_specs=[info_block(info)]
        + [head_block(rows, 0)] * 4
        + [pl.BlockSpec(memory_space=pl.ANY)],
        out_specs=head_block(rows, 0),
        out_shape=jax.ShapeDtypeStruct(low.shape, low.dtype),
        input_output_aliases={5: 0},
        compiler_params=pltpu.CompilerParams(vmem_limit_bytes=SMALL_VMEM),
        cost_estimate=LONG_COST,
    )(info, query, own, from_even, from_odd, low)


def last_call(info, key, own, from_even, from_odd, pieces, places, first, count):
    array, offset, slot = key
    rows = own.shape[1]
    anywhere = pl.BlockSpec(memory_space=pl.ANY)
    return pl.pallas_call(
        functools.partial(last_kernel, places=places, first=first, count=count),
        grid=(count,),
        in_specs=[info_block(info), head_block(rows, offset, slot)]
        + [pair_block(rows)] * 3
        + [anywhere] * len(pieces),
        out_specs=anywhere,
        out_shape=jax.ShapeDtypeStruct((3, rows, HEADS * HEAD_DIM), jnp.bfloat16),
        scratch_shapes=[
            pltpu.VMEM((count, 2, rows, HEAD_DIM), jnp.bfloat16),
            *[pltpu.VMEM(piece.shape, piece.dtype) for piece in pieces],
            pltpu.SemaphoreType.DMA((len(pieces),)),
            pltpu.SemaphoreType.DMA((len(pieces) + count,)),
        ],
        compiler_params=pltpu.CompilerParams(vmem_limit_bytes=SMALL_VMEM),
        cost_estimate=COST,
    )(info, array, own, from_even, from_odd, *pieces)


def partner(tile, parity, count):
    other = tile + 1 if tile % 2 == parity else tile - 1
    return other if 0 <= other < count else tile


def far_partner(tile, base, count):
    other = ((tile - base) ^ 2) + base if tile >= base else tile
    return other if 0 <= other < count else tile


def paired(value, partners):
    width = lax.axis_size("dp")
    pairs = []
    for tile, other in enumerate(partners):
        for sample in range(width):
            moved = sample ^ 1 if other == tile and width % 2 == 0 else sample
            pairs.append((tile * width + sample, other * width + moved))
    return lax.ppermute(value, ("seq", "dp"), pairs)


def exchanged(value, parity):
    count = lax.axis_size("seq")
    return paired(value, [partner(tile, parity, count) for tile in range(count)])


def far_partners(count):
    both = [[far_partner(tile, base, count) for tile in range(count)] for base in (0, 2)]
    return [partners for partners in both if partners != list(range(count))]


def after(value, *others):
    return lax.optimization_barrier((value, *others))[0]


def turned(value, step):
    count = lax.axis_size("pipe")
    return lax.ppermute(value, "pipe", [(i, (i + step) % count) for i in range(count)])


def total_over(value, axis, *late):
    count = lax.axis_size(axis)
    step = 1
    while step < count:
        other = lax.ppermute(value, axis, [(i, i ^ step) for i in range(count)])
        step *= 2
        value = value + (other if step < count else after(other, *late))
    return value


def local(queries, keys, values, grad_out, norm_gains, kv_tiles):
    query, key, value, grad = (a[0, 0, 0] for a in (queries, keys, values, grad_out))
    rows = query.shape[0]
    seq_count = lax.axis_size("seq")
    key_first, key_count = KEY_GROUP
    away_first, away_count = AWAY_GROUP
    fars = far_partners(seq_count)
    arrays = (query, grad, key, value)
    asks = [pack_call(query, grad, *QUERY_GROUPS[0])]
    away_pair = pack_call(after(key, asks[0]), value, away_first, away_count)
    for first, count in QUERY_GROUPS[1:]:
        asks.append(pack_call(after(query, away_pair), grad, first, count))
    told_pairs = [(exchanged(ask, 0), exchanged(ask, 1)) for ask in asks]
    key_pair = pack_call(after(key, asks[-1]), value, key_first, key_count)
    key_pair = after(key_pair, *told_pairs[0])
    key_pairs = (exchanged(key_pair, 0), exchanged(key_pair, 1))
    info = info_call(kv_tiles[0, 0, 0], after(norm_gains[0], asks[-1]))
    away_pair = turned(away_pair, -1)
    sums = None
    for (first, count), told in zip(QUERY_GROUPS, told_pairs):
        sums = sums_call(info, arrays, *told, first, count, key_first, sums, len(fars))
    ready = [*sums[:2], *[after(value, *key_pairs) for value in sums[2:]]]
    received = [exchanged(ready[0], 0), exchanged(ready[1], 1)]
    received += [paired(value, partners) for value, partners in zip(ready[2:], fars)]
    all_sums = (*sums[:2], *received)
    asked = ask_call(info, after(query, away_pair, sums[0]), grad, away_first, away_count)
    asked = turned(asked, -1)
    away_sent = after(away_pair, *received)
    away_pairs = (exchanged(away_sent, 0), exchanged(away_sent, 1))
    gains, parts = [], None
    for (first, count), told in zip(QUERY_GROUPS, told_pairs):
        *parts, gain = grads_call(
            info, arrays, *told, all_sums, first, count, key_first, parts, len(fars)
        )
        gains.append(gain[:2])
    pair_low, own, to_even, to_odd = parts
    pieces = [turned(pair_low, -1)]
    places = [(slice(1, 3), 0)]
    answer = (own, exchanged(to_even, 0), exchanged(to_odd, 1))
    operands = [(array, key_first, None) for array in arrays]
    low, own, to_even, to_odd, gain = main_call(
        after(info, pair_low, asked), operands, *key_pairs, key_count, away_first, key_first
    )
    gains.append(gain[:2])
    key_answer = (own, exchanged(to_even, 0), exchanged(to_odd, 1))
    operands = [(asked, 0, 0), (asked, 0, 1), (away_pair, 0, 0), (away_pair, 0, 1)]
    query_low, own, to_even, to_odd, gain = main_call(
        after(asked, low), operands, *away_pairs, away_count, away_count, 0
    )
    returned = (exchanged(to_even, 0), exchanged(to_odd, 1))
    pieces.append(query_low)
    places.append((0, away_first * HEAD_DIM))
    gains.append(turned(after(gain[:2], pieces[0]), 1))
    key_low = finish_call(after(info, pieces[0]), (key, key_first, None), *key_answer, key_count)
    pieces.append(turned(key_low, -1))
    places.append((slice(1, 3), key_first * HEAD_DIM))
    low = answer_call(info, query, *answer, low)
    pieces.append(turned(after(low, gains[-1], key_low), -1))
    places.append((0, 0))
    out = last_call(
        asked, operands[2], own, *returned, pieces, tuple(places), away_first, away_count
    )
    summed = total_over(total_over(sum(gains), "dp"), "seq", out)
    tokens = lax.axis_size("dp") * seq_count * rows * HEADS
    return (out[None, :, None, None], (summed / math.sqrt(tokens))[None])


def solution(mesh):
    placed = (
        P("pipe", "dp", "seq", None, None),
        P("pipe", "dp", "seq", None, None),
        P("pipe", "dp", "seq", None, None),
        P("pipe", "dp", "seq", None, None),
        P("pipe", None, None),
        P("pipe", "dp", "seq", None),
    )
    return jax.shard_map(
        local,
        mesh=mesh,
        in_specs=placed,
        out_specs=(P("pipe", None, "dp", "seq", None, None), P("pipe", None, None)),
        check_vma=False,
    )
```

```python
import functools
import math

import jax
import jax.numpy as jnp
from jax import lax
from jax.experimental import pallas as pl
from jax.experimental.pallas import tpu as pltpu
from jax.sharding import PartitionSpec as P

HEADS = 12
HEAD_DIM = 128
EPSILON = 1e-06
ROOT_SCALE = HEAD_DIM ** (-0.5)
EXP2_SCALE = ROOT_SCALE * math.log2(math.e)
QUERY_GROUPS = ((0, 3), (3, 2))
KEY_GROUP = (5, 2)
AWAY_GROUP = (7, 5)
MAIN_VMEM = 20 * 1024 * 1024
SMALL_VMEM = 12 * 1024 * 1024
PACK_VMEM = 4 * 1024 * 1024
COST = pl.CostEstimate(flops=1, bytes_accessed=1, transcendentals=0)
LONG_COST = pl.CostEstimate(flops=2 * 10**10, bytes_accessed=1, transcendentals=0)
MAIN_COST = pl.CostEstimate(flops=6 * 10**9, bytes_accessed=1, transcendentals=0)


def dot_nt(left, right):
    return lax.dot_general(
        left, right, (((1,), (1,)), ((), ())), preferred_element_type=jnp.float32
    )


def dot_nn(left, right):
    return lax.dot_general(
        left, right, (((1,), (0,)), ((), ())), preferred_element_type=jnp.float32
    )


def dot_tn(left, right):
    return lax.dot_general(
        left, right, (((0,), (0,)), ((), ())), preferred_element_type=jnp.float32
    )


def normalize(source, gain):
    floats = source.astype(jnp.float32)
    scaled = lax.rsqrt(jnp.mean(floats * floats, axis=-1, keepdims=True) + EPSILON)
    normed = floats * scaled
    return floats, scaled, normed, (normed * gain).astype(jnp.bfloat16)


def norm_back(grad_hat, floats, scaled, gain):
    scaled_grad = gain * grad_hat
    projected = jnp.sum(scaled_grad * floats, axis=-1, keepdims=True)
    return scaled * scaled_grad - (scaled**3 * projected * (1.0 / HEAD_DIM)) * floats


def pack_kernel(first_in, second_in, out, sems, *, start, width):
    rows = first_in.shape[0]
    copies = [
        pltpu.make_async_copy(
            source.at[:, start : start + width], out.at[slot, :rows], sems.at[slot]
        )
        for slot, source in enumerate((first_in, second_in))
    ]
    for copy in copies:
        copy.start()
    for copy in copies:
        copy.wait()


def info_kernel(listed, gains, info):
    tile = lax.axis_index("seq")
    last = lax.axis_size("seq") - 1
    info[...] = jnp.zeros_like(info)
    info[0:2, :] = gains[...]
    for parity in range(2):
        other = jnp.where(lax.rem(tile, 2) == parity, tile + 1, tile - 1)
        found = listed[0] == other
        for slot in range(1, listed.shape[0]):
            found = found | (listed[slot] == other)
        found = found & (other >= 0) & (other <= last)
        live = jnp.where(found, 1.0, 0.0)
        info[2 + parity : 3 + parity, :] = jnp.full((1, HEAD_DIM), live, jnp.float32)


def ask_kernel(info, query, grad, out, sems, *, start, width):
    rows = query.shape[0]
    value = info[...]
    planes = []
    for _ in range(3):
        low = value.astype(jnp.bfloat16)
        planes.append(low)
        value = value - low.astype(jnp.float32)
    planes.append(jnp.zeros_like(planes[0]))
    out[0, rows : rows + 16, :HEAD_DIM] = jnp.concatenate(planes[:2], axis=0)
    out[1, rows : rows + 16, :HEAD_DIM] = jnp.concatenate(planes[2:], axis=0)
    pack_kernel(query, grad, out, sems, start=start, width=width)


def told_info(told):
    floats = told[...].astype(jnp.float32)
    return floats[0, 0:8] + floats[0, 8:16] + floats[1, 0:8]


def main_kernel(
    info, query, grad, key, value, pair_even, pair_odd, *rest
):
    query_out, own_out, even_out, odd_out, gain_out = rest[-5:]
    told = told_info(info) if len(info.shape) == 3 else info[...]
    query_gain = told[0:1]
    key_gain = told[1:2]
    rows = query.shape[0]
    lives = [jnp.concatenate([told[row : row + 1]] * (rows // HEAD_DIM), axis=1) for row in (2, 3)]
    query_floats, query_scale, query_normed, query_hat = normalize(query[...], query_gain)
    grad_in = grad[...]
    sides = (
        (key[...], value[...], None),
        (pair_even[0], pair_even[1], lives[0]),
        (pair_odd[0], pair_odd[1], lives[1]),
    )
    parts = []
    totals = None
    for key_in, value_in, live in sides:
        _, _, key_normed, key_hat = normalize(key_in, key_gain)
        weights = jnp.exp2(dot_nt(key_hat, query_hat) * EXP2_SCALE)
        grad_probs = dot_nt(value_in, grad_in)
        weight_sum = jnp.sum(weights, axis=0, keepdims=True)
        cross_sum = jnp.sum(weights * grad_probs, axis=0, keepdims=True)
        if live is not None:
            weight_sum = weight_sum * live
            cross_sum = cross_sum * live
        totals = weight_sum if totals is None else totals + weight_sum
        crosses = cross_sum if live is None else crosses + cross_sum
        parts.append((key_normed, key_hat, weights, grad_probs, live))
    inverse = 1.0 / totals
    deltas = crosses * inverse
    query_grad_t = None
    key_gain_sum = None
    for (key_normed, key_hat, weights, grad_probs, live), out in zip(
        parts, (own_out, even_out, odd_out)
    ):
        probs = weights * (inverse if live is None else inverse * live)
        dscores = (probs * (grad_probs - deltas)).astype(jnp.bfloat16)
        key_part = dot_nn(dscores, query_hat) * ROOT_SCALE
        value_part = dot_nn(probs.astype(jnp.bfloat16), grad_in)
        out[0] = key_part.astype(out.dtype)
        out[1] = value_part.astype(out.dtype)
        gain_part = jnp.sum(key_part * key_normed, axis=0, keepdims=True)
        key_gain_sum = gain_part if key_gain_sum is None else key_gain_sum + gain_part
        query_part = dot_tn(key_hat, dscores)
        query_grad_t = query_part if query_grad_t is None else query_grad_t + query_part
    query_grad = query_grad_t.T * ROOT_SCALE
    query_out[...] = norm_back(query_grad, query_floats, query_scale, query_gain).astype(
        query_out.dtype
    )
    query_gain_sum = jnp.sum(query_grad * query_normed, axis=0, keepdims=True)

    @pl.when(pl.program_id(0) == 0)
    def _():
        gain_out[...] = jnp.zeros_like(gain_out)

    gain_out[0:1, :] += query_gain_sum
    gain_out[1:2, :] += key_gain_sum


def tile_sums(key_hat, value_in, query_hat, grad_in):
    weights = jnp.exp2(dot_nt(key_hat, query_hat) * EXP2_SCALE)
    grad_probs = dot_nt(value_in, grad_in)
    return weights, grad_probs


def wide_lives(told, rows):
    return [jnp.concatenate([told[row : row + 1]] * (rows // HEAD_DIM), axis=1) for row in (2, 3)]


def near_is_even():
    place = lax.rem(lax.axis_index("seq"), 4)
    return (place == 0) | (place == 3)


def sums_kernel(info, query, grad, key, value, pair_even, pair_odd, *rest, far_count):
    outs = rest[-2 - far_count :]
    told = info[...]
    _, _, _, key_hat = normalize(key[...], told[1:2])
    value_in = value[...]
    rows = []
    for query_in, grad_in in (
        (query[...], grad[...]), (pair_even[0], pair_even[1]), (pair_odd[0], pair_odd[1])
    ):
        _, _, _, query_hat = normalize(query_in, told[0:1])
        weights, grad_probs = tile_sums(key_hat, value_in, query_hat, grad_in)
        rows.append(
            [
                jnp.sum(weights, axis=0, keepdims=True),
                jnp.sum(weights * grad_probs, axis=0, keepdims=True),
            ]
        )
    own, even, odd = rows
    tail = wide_lives(told, query.shape[0])
    blank = jnp.zeros_like(tail[0])
    outs[0][...] = jnp.concatenate([*own, *even, *tail, blank, blank], axis=0)
    outs[1][...] = jnp.concatenate([*own, *odd, *tail, blank, blank], axis=0)
    near = near_is_even()
    for index, out in enumerate(outs[2:]):
        first, second = (even, odd) if index == 0 else (odd, even)
        chosen = [jnp.where(near, one, two) for one, two in zip(first, second)]
        out[...] = jnp.concatenate([*chosen, *[blank] * 6], axis=0)


def grads_kernel(
    info, query, grad, key, value, pair_even, pair_odd,
    sent_even, sent_odd, from_even, from_odd, *rest, far_count,
):
    fars = [far[0:2, :] for far in rest[:far_count]]
    pair_out, own_out, even_out, odd_out, gain_out = rest[-5:]
    told = info[...]
    near = near_is_even()
    if far_count == 2:
        far_even = jnp.where(near, fars[0], fars[1])
        far_odd = jnp.where(near, fars[1], fars[0])
    elif far_count == 1:
        far_even = jnp.where(near, fars[0], jnp.zeros_like(fars[0]))
        far_odd = jnp.where(near, jnp.zeros_like(fars[0]), fars[0])
    else:
        far_even = far_odd = jnp.zeros_like(from_even[0:2, :])
    own_sums = (
        sent_even[0:2, :]
        + sent_even[4:5, :] * from_even[2:4, :]
        + sent_even[5:6, :] * from_odd[2:4, :]
    )
    even_sums = (
        from_even[0:2, :] + from_even[4:5, :] * sent_even[2:4, :] + from_even[5:6, :] * far_even
    )
    odd_sums = (
        from_odd[0:2, :] + from_odd[5:6, :] * sent_odd[2:4, :] + from_odd[4:5, :] * far_odd
    )
    key_floats, key_scale, key_normed, key_hat = normalize(key[...], told[1:2])
    value_in = value[...]
    key_grad = value_grad = query_gain_sum = None
    for query_in, grad_in, sums, live, out in (
        (query[...], grad[...], own_sums, None, own_out),
        (pair_even[0], pair_even[1], even_sums, from_even[4:5, :], even_out),
        (pair_odd[0], pair_odd[1], odd_sums, from_odd[5:6, :], odd_out),
    ):
        _, _, query_normed, query_hat = normalize(query_in, told[0:1])
        weights, grad_probs = tile_sums(key_hat, value_in, query_hat, grad_in)
        inverse = 1.0 / sums[0:1]
        deltas = sums[1:2] * inverse
        probs = weights * (inverse if live is None else inverse * live)
        dscores = (probs * (grad_probs - deltas)).astype(jnp.bfloat16)
        key_part = dot_nn(dscores, query_hat)
        value_part = dot_nn(probs.astype(jnp.bfloat16), grad_in)
        query_part = dot_tn(key_hat, dscores).T * ROOT_SCALE
        out[...] = query_part.astype(out.dtype)
        gain_part = jnp.sum(query_part * query_normed, axis=0, keepdims=True)
        key_grad = key_part if key_grad is None else key_grad + key_part
        value_grad = value_part if value_grad is None else value_grad + value_part
        query_gain_sum = gain_part if query_gain_sum is None else query_gain_sum + gain_part
    key_grad = key_grad * ROOT_SCALE
    key_back = norm_back(key_grad, key_floats, key_scale, told[1:2])
    pair_out[0] = key_back.astype(pair_out.dtype)
    pair_out[1] = value_grad.astype(pair_out.dtype)

    @pl.when(pl.program_id(0) == 0)
    def _():
        gain_out[...] = jnp.zeros_like(gain_out)

    gain_out[0:1, :] += query_gain_sum
    gain_out[1:2, :] += jnp.sum(key_grad * key_normed, axis=0, keepdims=True)


def answer_kernel(info, query, own, from_even, from_odd, _, out):
    gain = info[0:1, :]
    floats, scaled, _, _ = normalize(query[...], gain)
    total = own[...] + from_even[...].astype(jnp.float32) + from_odd[...].astype(jnp.float32)
    out[...] = norm_back(total, floats, scaled, gain).astype(out.dtype)


def finished(info, key, own, from_even, from_odd):
    told = told_info(info) if len(info.shape) == 3 else info[...]
    key_gain = told[1:2]
    key_floats, key_scale, _, _ = normalize(key[...], key_gain)
    key_grad = own[0] + from_even[0].astype(jnp.float32) + from_odd[0].astype(jnp.float32)
    value_grad = own[1] + from_even[1].astype(jnp.float32) + from_odd[1].astype(jnp.float32)
    return norm_back(key_grad, key_floats, key_scale, key_gain), value_grad


def finish_kernel(info, key, own, from_even, from_odd, out):
    key_grad, value_grad = finished(info, key, own, from_even, from_odd)
    out[0] = key_grad.astype(out.dtype)
    out[1] = value_grad.astype(out.dtype)


def place_kernel(*refs, places):
    amount = len(places)
    pieces, out, staged = refs[:amount], refs[amount], refs[amount + 1 : -2]
    load_sems, store_sems = refs[-2:]
    loads = [
        pltpu.make_async_copy(piece, stage, load_sems.at[slot])
        for slot, (piece, stage) in enumerate(zip(pieces, staged))
    ]
    stores = [
        pltpu.make_async_copy(
            stage, out.at[planes, :, start : start + stage.shape[-1]], store_sems.at[slot]
        )
        for slot, (stage, (planes, start)) in enumerate(zip(staged, places))
    ]
    for load in loads:
        load.start()
    for load, store in zip(loads, stores):
        load.wait()
        store.start()
    for store in stores:
        store.wait()


def last_kernel(info, key, own, from_even, from_odd, *rest, places, first, count):
    amount = len(places)
    pieces, (_, out, held) = rest[:amount], rest[amount : amount + 3]
    staged, (load_sems, store_sems) = rest[amount + 3 : -2], rest[-2:]
    head = pl.program_id(0)
    loads = [
        pltpu.make_async_copy(piece, stage, load_sems.at[slot])
        for slot, (piece, stage) in enumerate(zip(pieces, staged))
    ]
    stores = [
        pltpu.make_async_copy(
            stage, out.at[planes, :, start : start + stage.shape[-1]], store_sems.at[slot]
        )
        for slot, (stage, (planes, start)) in enumerate(zip(staged, places))
    ]

    def head_copy(index):
        start = pl.multiple_of((first + index) * HEAD_DIM, HEAD_DIM)
        return pltpu.make_async_copy(
            held.at[index],
            out.at[pl.ds(1, 2), :, pl.ds(start, HEAD_DIM)],
            store_sems.at[amount + index],
        )

    @pl.when(head == 0)
    def _():
        for load in loads:
            load.start()

    @pl.when(head == min(1, count - 1))
    def _():
        for load, store in zip(loads, stores):
            load.wait()
            store.start()

    key_grad, value_grad = finished(info, key, own, from_even, from_odd)
    held[head, 0] = key_grad.astype(held.dtype)
    held[head, 1] = value_grad.astype(held.dtype)
    head_copy(head).start()

    @pl.when(head == count - 1)
    def _():
        for store in stores:
            store.wait()
        for index in range(count):
            head_copy(index).wait()


def head_block(rows, first, slot=None):
    if slot is None:
        return pl.BlockSpec((rows, HEAD_DIM), lambda head: (0, first + head))
    return pl.BlockSpec((None, rows, HEAD_DIM), lambda head: (slot, 0, first + head))


def pair_block(rows, first=0):
    return pl.BlockSpec((2, rows, HEAD_DIM), lambda head: (0, 0, first + head))


def whole_block(shape):
    return pl.BlockSpec(shape, lambda head: (0,) * len(shape))


def pack_params(limit):
    return dict(
        scratch_shapes=[pltpu.SemaphoreType.DMA((2,))],
        compiler_params=pltpu.CompilerParams(vmem_limit_bytes=limit),
        cost_estimate=COST,
    )


def pack_call(first_in, second_in, first, count, limit=PACK_VMEM):
    rows = first_in.shape[0]
    width = count * HEAD_DIM
    return pl.pallas_call(
        functools.partial(pack_kernel, start=first * HEAD_DIM, width=width),
        grid=(1,),
        in_specs=[pl.BlockSpec(memory_space=pl.ANY)] * 2,
        out_specs=whole_block((2, rows, width)),
        out_shape=jax.ShapeDtypeStruct((2, rows, width), jnp.bfloat16),
        **pack_params(limit),
    )(first_in, second_in)


def ask_call(info, query, grad, first, count):
    rows = query.shape[0]
    width = count * HEAD_DIM
    return pl.pallas_call(
        functools.partial(ask_kernel, start=first * HEAD_DIM, width=width),
        grid=(1,),
        in_specs=[whole_block(info.shape)] + [pl.BlockSpec(memory_space=pl.ANY)] * 2,
        out_specs=whole_block((2, rows + 16, width)),
        out_shape=jax.ShapeDtypeStruct((2, rows + 16, width), jnp.bfloat16),
        **pack_params(PACK_VMEM),
    )(info, query, grad)


def info_call(listed, gains):
    return pl.pallas_call(
        info_kernel,
        in_specs=[pl.BlockSpec(memory_space=pltpu.SMEM), pl.BlockSpec(memory_space=pltpu.VMEM)],
        out_specs=pl.BlockSpec(memory_space=pltpu.VMEM),
        out_shape=jax.ShapeDtypeStruct((8, HEAD_DIM), jnp.float32),
        compiler_params=pltpu.CompilerParams(vmem_limit_bytes=PACK_VMEM),
        cost_estimate=LONG_COST,
    )(listed, gains)


def info_block(info):
    if info.ndim == 2:
        return whole_block(info.shape)
    below = info.shape[1] // 16 - 1
    return pl.BlockSpec((2, 16, HEAD_DIM), lambda head: (0, below, 0))


def main_call(info, operands, pair_even, pair_odd, count, heads, place):
    rows = pair_even.shape[1]
    lanes = count * HEAD_DIM
    return pl.pallas_call(
        main_kernel,
        grid=(count,),
        in_specs=[info_block(info)]
        + [head_block(rows, first, slot) for _, first, slot in operands]
        + [pair_block(rows)] * 2,
        out_specs=[head_block(rows, place)] + [pair_block(rows)] * 3 + [whole_block((8, HEAD_DIM))],
        out_shape=[
            jax.ShapeDtypeStruct((rows, heads * HEAD_DIM), jnp.bfloat16),
            jax.ShapeDtypeStruct((2, rows, lanes), jnp.float32),
            jax.ShapeDtypeStruct((2, rows, lanes), jnp.bfloat16),
            jax.ShapeDtypeStruct((2, rows, lanes), jnp.bfloat16),
            jax.ShapeDtypeStruct((8, HEAD_DIM), jnp.float32),
        ],
        compiler_params=pltpu.CompilerParams(vmem_limit_bytes=MAIN_VMEM),
        cost_estimate=MAIN_COST,
    )(info, *[array for array, _, _ in operands], pair_even, pair_odd)


def finish_call(info, key, own, from_even, from_odd, count):
    array, first, slot = key
    rows = own.shape[1]
    return pl.pallas_call(
        finish_kernel,
        grid=(count,),
        in_specs=[info_block(info), head_block(rows, first, slot)] + [pair_block(rows)] * 3,
        out_specs=pair_block(rows),
        out_shape=jax.ShapeDtypeStruct((2, rows, count * HEAD_DIM), jnp.bfloat16),
        compiler_params=pltpu.CompilerParams(vmem_limit_bytes=SMALL_VMEM),
        cost_estimate=COST,
    )(info, array, own, from_even, from_odd)


def row_block(rows, first):
    return pl.BlockSpec((8, rows), lambda head: (first + head, 0))


def sums_call(info, arrays, pair_even, pair_odd, first, count, heads, earlier, far_count):
    rows = pair_even.shape[1]
    amount = 2 + far_count
    earlier = [] if earlier is None else earlier
    return pl.pallas_call(
        functools.partial(sums_kernel, far_count=far_count),
        grid=(count,),
        in_specs=[info_block(info)]
        + [head_block(rows, first)] * 4
        + [pair_block(rows)] * 2
        + [pl.BlockSpec(memory_space=pl.ANY)] * len(earlier),
        out_specs=[row_block(rows, first)] * amount,
        out_shape=[jax.ShapeDtypeStruct((8 * heads, rows), jnp.float32)] * amount,
        input_output_aliases={7 + index: index for index in range(len(earlier))},
        compiler_params=pltpu.CompilerParams(vmem_limit_bytes=MAIN_VMEM),
        cost_estimate=MAIN_COST,
    )(info, *arrays, pair_even, pair_odd, *earlier)


def grads_call(info, arrays, pair_even, pair_odd, sums, first, count, heads, earlier, far_count):
    rows = pair_even.shape[1]
    lanes = heads * HEAD_DIM
    earlier = [] if earlier is None else earlier
    place = 7 + len(sums)
    return pl.pallas_call(
        functools.partial(grads_kernel, far_count=far_count),
        grid=(count,),
        in_specs=[info_block(info)]
        + [head_block(rows, first)] * 4
        + [pair_block(rows)] * 2
        + [row_block(rows, first)] * len(sums)
        + [pl.BlockSpec(memory_space=pl.ANY)] * len(earlier),
        out_specs=[pair_block(rows, first)]
        + [head_block(rows, first)] * 3
        + [whole_block((8, HEAD_DIM))],
        out_shape=[
            jax.ShapeDtypeStruct((2, rows, lanes), jnp.bfloat16),
            jax.ShapeDtypeStruct((rows, lanes), jnp.float32),
            jax.ShapeDtypeStruct((rows, lanes), jnp.bfloat16),
            jax.ShapeDtypeStruct((rows, lanes), jnp.bfloat16),
            jax.ShapeDtypeStruct((8, HEAD_DIM), jnp.float32),
        ],
        input_output_aliases={place + index: index for index in range(len(earlier))},
        compiler_params=pltpu.CompilerParams(vmem_limit_bytes=MAIN_VMEM),
        cost_estimate=COST,
    )(info, *arrays, pair_even, pair_odd, *sums, *earlier)


def answer_call(info, query, own, from_even, from_odd, low):
    rows, lanes = own.shape
    return pl.pallas_call(
        answer_kernel,
        grid=(lanes // HEAD_DIM,),
        in_specs=[info_block(info)]
        + [head_block(rows, 0)] * 4
        + [pl.BlockSpec(memory_space=pl.ANY)],
        out_specs=head_block(rows, 0),
        out_shape=jax.ShapeDtypeStruct(low.shape, low.dtype),
        input_output_aliases={5: 0},
        compiler_params=pltpu.CompilerParams(vmem_limit_bytes=SMALL_VMEM),
        cost_estimate=LONG_COST,
    )(info, query, own, from_even, from_odd, low)


def place_call(pieces, places):
    rows = pieces[0].shape[-2]
    anywhere = pl.BlockSpec(memory_space=pl.ANY)
    return pl.pallas_call(
        functools.partial(place_kernel, places=places),
        in_specs=[anywhere] * len(pieces),
        out_specs=anywhere,
        out_shape=jax.ShapeDtypeStruct((3, rows, HEADS * HEAD_DIM), jnp.bfloat16),
        scratch_shapes=[
            *[pltpu.VMEM(piece.shape, piece.dtype) for piece in pieces],
            pltpu.SemaphoreType.DMA((len(pieces),)),
            pltpu.SemaphoreType.DMA((len(pieces),)),
        ],
        compiler_params=pltpu.CompilerParams(vmem_limit_bytes=SMALL_VMEM),
        cost_estimate=COST,
    )(*pieces)


def last_call(info, key, own, from_even, from_odd, pieces, places, placed, first, count):
    array, offset, slot = key
    rows = own.shape[1]
    anywhere = pl.BlockSpec(memory_space=pl.ANY)
    return pl.pallas_call(
        functools.partial(last_kernel, places=places, first=first, count=count),
        grid=(count,),
        in_specs=[info_block(info), head_block(rows, offset, slot)]
        + [pair_block(rows)] * 3
        + [anywhere] * (len(pieces) + 1),
        out_specs=anywhere,
        out_shape=jax.ShapeDtypeStruct((3, rows, HEADS * HEAD_DIM), jnp.bfloat16),
        input_output_aliases={5 + len(pieces): 0},
        scratch_shapes=[
            pltpu.VMEM((count, 2, rows, HEAD_DIM), jnp.bfloat16),
            *[pltpu.VMEM(piece.shape, piece.dtype) for piece in pieces],
            pltpu.SemaphoreType.DMA((len(pieces),)),
            pltpu.SemaphoreType.DMA((len(pieces) + count,)),
        ],
        compiler_params=pltpu.CompilerParams(vmem_limit_bytes=SMALL_VMEM),
        cost_estimate=COST,
    )(info, array, own, from_even, from_odd, *pieces, placed)


def partner(tile, parity, count):
    other = tile + 1 if tile % 2 == parity else tile - 1
    return other if 0 <= other < count else tile


def far_partner(tile, base, count):
    other = ((tile - base) ^ 2) + base if tile >= base else tile
    return other if 0 <= other < count else tile


def paired(value, partners):
    width = lax.axis_size("dp")
    pairs = []
    for tile, other in enumerate(partners):
        for sample in range(width):
            moved = sample ^ 1 if other == tile and width % 2 == 0 else sample
            pairs.append((tile * width + sample, other * width + moved))
    return lax.ppermute(value, ("seq", "dp"), pairs)


def exchanged(value, parity):
    count = lax.axis_size("seq")
    return paired(value, [partner(tile, parity, count) for tile in range(count)])


def far_partners(count):
    both = [[far_partner(tile, base, count) for tile in range(count)] for base in (0, 2)]
    return [partners for partners in both if partners != list(range(count))]


def after(value, *others):
    return lax.optimization_barrier((value, *others))[0]


def turned(value, step):
    count = lax.axis_size("pipe")
    return lax.ppermute(value, "pipe", [(i, (i + step) % count) for i in range(count)])


def total_over(value, axis, *late):
    count = lax.axis_size(axis)
    step = 1
    while step < count:
        sent = after(value, *late) if 2 * step >= count else value
        value = value + lax.ppermute(sent, axis, [(i, i ^ step) for i in range(count)])
        step *= 2
    return value


def local(queries, keys, values, grad_out, norm_gains, kv_tiles):
    query, key, value, grad = (a[0, 0, 0] for a in (queries, keys, values, grad_out))
    rows = query.shape[0]
    seq_count = lax.axis_size("seq")
    key_first, key_count = KEY_GROUP
    away_first, away_count = AWAY_GROUP
    fars = far_partners(seq_count)
    arrays = (query, grad, key, value)
    asks = [pack_call(query, grad, *QUERY_GROUPS[0])]
    away_pair = pack_call(after(key, asks[0]), value, away_first, away_count)
    for first, count in QUERY_GROUPS[1:]:
        asks.append(pack_call(after(query, away_pair), grad, first, count))
    told_pairs = [(exchanged(ask, 0), exchanged(ask, 1)) for ask in asks]
    key_pair = pack_call(after(key, asks[-1]), value, key_first, key_count)
    key_pair = after(key_pair, *told_pairs[0])
    key_pairs = (exchanged(key_pair, 0), exchanged(key_pair, 1))
    info = info_call(kv_tiles[0, 0, 0], after(norm_gains[0], asks[-1]))
    away_pair = turned(away_pair, -1)
    sums = None
    for (first, count), told in zip(QUERY_GROUPS, told_pairs):
        sums = sums_call(info, arrays, *told, first, count, key_first, sums, len(fars))
    received = [exchanged(sums[0], 0), exchanged(sums[1], 1)]
    received += [
        paired(value, partners) for value, partners in zip(sums[2:], fars)
    ]
    all_sums = (*sums[:2], *received)
    asked = ask_call(info, after(query, away_pair, sums[0]), grad, away_first, away_count)
    asked = turned(asked, -1)
    away_sent = after(away_pair, *key_pairs, *received)
    away_pairs = (exchanged(away_sent, 0), exchanged(away_sent, 1))
    gains, parts = [], None
    for (first, count), told in zip(QUERY_GROUPS, told_pairs):
        *parts, gain = grads_call(
            info, arrays, *told, all_sums, first, count, key_first, parts, len(fars)
        )
        gains.append(gain[:2])
    pair_low, own, to_even, to_odd = parts
    pieces = [turned(pair_low, -1)]
    places = [(slice(1, 3), 0)]
    answer = (own, exchanged(to_even, 0), exchanged(to_odd, 1))
    operands = [(array, key_first, None) for array in arrays]
    low, own, to_even, to_odd, gain = main_call(
        after(info, pair_low), operands, *key_pairs, key_count, away_first, key_first
    )
    gains.append(gain[:2])
    key_answer = (own, exchanged(to_even, 0), exchanged(to_odd, 1))
    operands = [(asked, 0, 0), (asked, 0, 1), (away_pair, 0, 0), (away_pair, 0, 1)]
    query_low, own, to_even, to_odd, gain = main_call(
        after(asked, low), operands, *away_pairs, away_count, away_count, 0
    )
    returned = (exchanged(to_even, 0), exchanged(to_odd, 1))
    pieces.append(query_low)
    places.append((0, away_first * HEAD_DIM))
    low = answer_call(info, query, *answer, low)
    gains.append(turned(after(gain[:2], low, pieces[0]), 1))
    pieces.append(turned(after(low, gains[-1]), -1))
    places.append((0, 0))
    low = finish_call(after(info, pieces[0]), (key, key_first, None), *key_answer, key_count)
    pieces.append(turned(low, -1))
    places.append((slice(1, 3), key_first * HEAD_DIM))
    placed = place_call(pieces[:2], tuple(places[:2]))
    out = last_call(
        asked, operands[2], own, *returned, pieces[2:], tuple(places[2:]), placed,
        away_first, away_count,
    )
    summed = total_over(total_over(sum(gains), "dp"), "seq", placed)
    tokens = lax.axis_size("dp") * seq_count * rows * HEADS
    return (out[None, :, None, None], (summed / math.sqrt(tokens))[None])


def solution(mesh):
    placed = (
        P("pipe", "dp", "seq", None, None),
        P("pipe", "dp", "seq", None, None),
        P("pipe", "dp", "seq", None, None),
        P("pipe", "dp", "seq", None, None),
        P("pipe", None, None),
        P("pipe", "dp", "seq", None),
    )
    return jax.shard_map(
        local,
        mesh=mesh,
        in_specs=placed,
        out_specs=(P("pipe", None, "dp", "seq", None, None), P("pipe", None, None)),
        check_vma=False,
    )
```

```python
import functools
import math

import jax
import jax.numpy as jnp
from jax import lax
from jax.experimental import pallas as pl
from jax.experimental.pallas import tpu as pltpu
from jax.sharding import PartitionSpec as P

HEADS = 12
HEAD_DIM = 128
EPSILON = 1e-06
ROOT_SCALE = HEAD_DIM ** (-0.5)
EXP2_SCALE = ROOT_SCALE * math.log2(math.e)
QUERY_GROUPS = ((0, 3), (3, 2))
KEY_GROUP = (5, 2)
AWAY_GROUP = (7, 5)
MAIN_VMEM = 20 * 1024 * 1024
SMALL_VMEM = 12 * 1024 * 1024
PACK_VMEM = 4 * 1024 * 1024
COST = pl.CostEstimate(flops=1, bytes_accessed=1, transcendentals=0)
LONG_COST = pl.CostEstimate(flops=2 * 10**10, bytes_accessed=1, transcendentals=0)
GRAD_COST = pl.CostEstimate(flops=4000000000, bytes_accessed=1, transcendentals=0)
MAIN_COST = pl.CostEstimate(flops=6 * 10**9, bytes_accessed=1, transcendentals=0)


def dot_nt(left, right):
    return lax.dot_general(
        left, right, (((1,), (1,)), ((), ())), preferred_element_type=jnp.float32
    )


def dot_nn(left, right):
    return lax.dot_general(
        left, right, (((1,), (0,)), ((), ())), preferred_element_type=jnp.float32
    )


def dot_tn(left, right):
    return lax.dot_general(
        left, right, (((0,), (0,)), ((), ())), preferred_element_type=jnp.float32
    )


def normalize(source, gain):
    floats = source.astype(jnp.float32)
    scaled = lax.rsqrt(jnp.mean(floats * floats, axis=-1, keepdims=True) + EPSILON)
    normed = floats * scaled
    return floats, scaled, normed, (normed * gain).astype(jnp.bfloat16)


def norm_back(grad_hat, floats, scaled, gain):
    scaled_grad = gain * grad_hat
    projected = jnp.sum(scaled_grad * floats, axis=-1, keepdims=True)
    return scaled * scaled_grad - (scaled**3 * projected * (1.0 / HEAD_DIM)) * floats


def pack_kernel(first_in, second_in, out, sems, *, start, width):
    rows = first_in.shape[0]
    copies = [
        pltpu.make_async_copy(
            source.at[:, start : start + width], out.at[slot, :rows], sems.at[slot]
        )
        for slot, source in enumerate((first_in, second_in))
    ]
    for copy in copies:
        copy.start()
    for copy in copies:
        copy.wait()


def info_kernel(listed, gains, info):
    tile = lax.axis_index("seq")
    last = lax.axis_size("seq") - 1
    info[...] = jnp.zeros_like(info)
    info[0:2, :] = gains[...]
    for parity in range(2):
        other = jnp.where(lax.rem(tile, 2) == parity, tile + 1, tile - 1)
        found = listed[0] == other
        for slot in range(1, listed.shape[0]):
            found = found | (listed[slot] == other)
        found = found & (other >= 0) & (other <= last)
        live = jnp.where(found, 1.0, 0.0)
        info[2 + parity : 3 + parity, :] = jnp.full((1, HEAD_DIM), live, jnp.float32)


def ask_kernel(info, query, grad, out, sems, *, start, width):
    rows = query.shape[0]
    value = info[...]
    planes = []
    for _ in range(3):
        low = value.astype(jnp.bfloat16)
        planes.append(low)
        value = value - low.astype(jnp.float32)
    planes.append(jnp.zeros_like(planes[0]))
    out[0, rows : rows + 16, :HEAD_DIM] = jnp.concatenate(planes[:2], axis=0)
    out[1, rows : rows + 16, :HEAD_DIM] = jnp.concatenate(planes[2:], axis=0)
    pack_kernel(query, grad, out, sems, start=start, width=width)


def told_info(told):
    floats = told[...].astype(jnp.float32)
    return floats[0, 0:8] + floats[0, 8:16] + floats[1, 0:8]


def main_kernel(
    info, query, grad, key, value, pair_even, pair_odd, *rest
):
    query_out, own_out, even_out, odd_out, gain_out = rest[-5:]
    told = told_info(info) if len(info.shape) == 3 else info[...]
    query_gain = told[0:1]
    key_gain = told[1:2]
    rows = query.shape[0]
    lives = [jnp.concatenate([told[row : row + 1]] * (rows // HEAD_DIM), axis=1) for row in (2, 3)]
    query_floats, query_scale, query_normed, query_hat = normalize(query[...], query_gain)
    grad_in = grad[...]
    sides = (
        (key[...], value[...], None),
        (pair_even[0], pair_even[1], lives[0]),
        (pair_odd[0], pair_odd[1], lives[1]),
    )
    parts = []
    totals = None
    for key_in, value_in, live in sides:
        _, _, key_normed, key_hat = normalize(key_in, key_gain)
        weights = jnp.exp2(dot_nt(key_hat, query_hat) * EXP2_SCALE)
        grad_probs = dot_nt(value_in, grad_in)
        weight_sum = jnp.sum(weights, axis=0, keepdims=True)
        cross_sum = jnp.sum(weights * grad_probs, axis=0, keepdims=True)
        if live is not None:
            weight_sum = weight_sum * live
            cross_sum = cross_sum * live
        totals = weight_sum if totals is None else totals + weight_sum
        crosses = cross_sum if live is None else crosses + cross_sum
        parts.append((key_normed, key_hat, weights, grad_probs, live))
    inverse = 1.0 / totals
    deltas = crosses * inverse
    query_grad_t = None
    key_gain_sum = None
    for (key_normed, key_hat, weights, grad_probs, live), out in zip(
        parts, (own_out, even_out, odd_out)
    ):
        probs = weights * (inverse if live is None else inverse * live)
        dscores = (probs * (grad_probs - deltas)).astype(jnp.bfloat16)
        key_part = dot_nn(dscores, query_hat) * ROOT_SCALE
        value_part = dot_nn(probs.astype(jnp.bfloat16), grad_in)
        out[0] = key_part.astype(out.dtype)
        out[1] = value_part.astype(out.dtype)
        gain_part = jnp.sum(key_part * key_normed, axis=0, keepdims=True)
        key_gain_sum = gain_part if key_gain_sum is None else key_gain_sum + gain_part
        query_part = dot_tn(key_hat, dscores)
        query_grad_t = query_part if query_grad_t is None else query_grad_t + query_part
    query_grad = query_grad_t.T * ROOT_SCALE
    query_out[...] = norm_back(query_grad, query_floats, query_scale, query_gain).astype(
        query_out.dtype
    )
    query_gain_sum = jnp.sum(query_grad * query_normed, axis=0, keepdims=True)

    @pl.when(pl.program_id(0) == 0)
    def _():
        gain_out[...] = jnp.zeros_like(gain_out)

    gain_out[0:1, :] += query_gain_sum
    gain_out[1:2, :] += key_gain_sum


def tile_sums(key_hat, value_in, query_hat, grad_in):
    weights = jnp.exp2(dot_nt(key_hat, query_hat) * EXP2_SCALE)
    grad_probs = dot_nt(value_in, grad_in)
    return weights, grad_probs


def wide_lives(told, rows):
    return [jnp.concatenate([told[row : row + 1]] * (rows // HEAD_DIM), axis=1) for row in (2, 3)]


def near_is_even():
    place = lax.rem(lax.axis_index("seq"), 4)
    return (place == 0) | (place == 3)


def sums_kernel(info, query, grad, key, value, pair_even, pair_odd, *rest, far_count):
    outs = rest[-2 - far_count :]
    told = info[...]
    _, _, _, key_hat = normalize(key[...], told[1:2])
    value_in = value[...]
    rows = []
    for query_in, grad_in in (
        (query[...], grad[...]), (pair_even[0], pair_even[1]), (pair_odd[0], pair_odd[1])
    ):
        _, _, _, query_hat = normalize(query_in, told[0:1])
        weights, grad_probs = tile_sums(key_hat, value_in, query_hat, grad_in)
        rows.append(
            [
                jnp.sum(weights, axis=0, keepdims=True),
                jnp.sum(weights * grad_probs, axis=0, keepdims=True),
            ]
        )
    own, even, odd = rows
    tail = wide_lives(told, query.shape[0])
    blank = jnp.zeros_like(tail[0])
    outs[0][...] = jnp.concatenate([*own, *even, *tail, blank, blank], axis=0)
    outs[1][...] = jnp.concatenate([*own, *odd, *tail, blank, blank], axis=0)
    near = near_is_even()
    for index, out in enumerate(outs[2:]):
        first, second = (even, odd) if index == 0 else (odd, even)
        chosen = [jnp.where(near, one, two) for one, two in zip(first, second)]
        out[...] = jnp.concatenate([*chosen, *[blank] * 6], axis=0)


def grads_kernel(
    info, query, grad, key, value, pair_even, pair_odd,
    sent_even, sent_odd, from_even, from_odd, *rest, far_count,
):
    fars = [far[0:2, :] for far in rest[:far_count]]
    pair_out, own_out, even_out, odd_out, gain_out = rest[-5:]
    told = info[...]
    near = near_is_even()
    if far_count == 2:
        far_even = jnp.where(near, fars[0], fars[1])
        far_odd = jnp.where(near, fars[1], fars[0])
    elif far_count == 1:
        far_even = jnp.where(near, fars[0], jnp.zeros_like(fars[0]))
        far_odd = jnp.where(near, jnp.zeros_like(fars[0]), fars[0])
    else:
        far_even = far_odd = jnp.zeros_like(from_even[0:2, :])
    own_sums = (
        sent_even[0:2, :]
        + sent_even[4:5, :] * from_even[2:4, :]
        + sent_even[5:6, :] * from_odd[2:4, :]
    )
    even_sums = (
        from_even[0:2, :] + from_even[4:5, :] * sent_even[2:4, :] + from_even[5:6, :] * far_even
    )
    odd_sums = (
        from_odd[0:2, :] + from_odd[5:6, :] * sent_odd[2:4, :] + from_odd[4:5, :] * far_odd
    )
    key_floats, key_scale, key_normed, key_hat = normalize(key[...], told[1:2])
    value_in = value[...]
    key_grad = value_grad = query_gain_sum = None
    for query_in, grad_in, sums, live, out in (
        (query[...], grad[...], own_sums, None, own_out),
        (pair_even[0], pair_even[1], even_sums, from_even[4:5, :], even_out),
        (pair_odd[0], pair_odd[1], odd_sums, from_odd[5:6, :], odd_out),
    ):
        _, _, query_normed, query_hat = normalize(query_in, told[0:1])
        weights, grad_probs = tile_sums(key_hat, value_in, query_hat, grad_in)
        inverse = 1.0 / sums[0:1]
        deltas = sums[1:2] * inverse
        probs = weights * (inverse if live is None else inverse * live)
        dscores = (probs * (grad_probs - deltas)).astype(jnp.bfloat16)
        key_part = dot_nn(dscores, query_hat)
        value_part = dot_nn(probs.astype(jnp.bfloat16), grad_in)
        query_part = dot_tn(key_hat, dscores).T * ROOT_SCALE
        out[...] = query_part.astype(out.dtype)
        gain_part = jnp.sum(query_part * query_normed, axis=0, keepdims=True)
        key_grad = key_part if key_grad is None else key_grad + key_part
        value_grad = value_part if value_grad is None else value_grad + value_part
        query_gain_sum = gain_part if query_gain_sum is None else query_gain_sum + gain_part
    key_grad = key_grad * ROOT_SCALE
    key_back = norm_back(key_grad, key_floats, key_scale, told[1:2])
    pair_out[0] = key_back.astype(pair_out.dtype)
    pair_out[1] = value_grad.astype(pair_out.dtype)

    @pl.when(pl.program_id(0) == 0)
    def _():
        gain_out[...] = jnp.zeros_like(gain_out)

    gain_out[0:1, :] += query_gain_sum
    gain_out[1:2, :] += jnp.sum(key_grad * key_normed, axis=0, keepdims=True)


def answer_kernel(info, query, own, from_even, from_odd, _, out):
    gain = info[0:1, :]
    floats, scaled, _, _ = normalize(query[...], gain)
    total = own[...] + from_even[...].astype(jnp.float32) + from_odd[...].astype(jnp.float32)
    out[...] = norm_back(total, floats, scaled, gain).astype(out.dtype)


def finished(info, key, own, from_even, from_odd):
    told = told_info(info) if len(info.shape) == 3 else info[...]
    key_gain = told[1:2]
    key_floats, key_scale, _, _ = normalize(key[...], key_gain)
    key_grad = own[0] + from_even[0].astype(jnp.float32) + from_odd[0].astype(jnp.float32)
    value_grad = own[1] + from_even[1].astype(jnp.float32) + from_odd[1].astype(jnp.float32)
    return norm_back(key_grad, key_floats, key_scale, key_gain), value_grad


def finish_kernel(info, key, own, from_even, from_odd, out):
    key_grad, value_grad = finished(info, key, own, from_even, from_odd)
    out[0] = key_grad.astype(out.dtype)
    out[1] = value_grad.astype(out.dtype)


def place_kernel(*refs, places):
    amount = len(places)
    pieces, out, staged = refs[:amount], refs[amount], refs[amount + 1 : -2]
    load_sems, store_sems = refs[-2:]
    loads = [
        pltpu.make_async_copy(piece, stage, load_sems.at[slot])
        for slot, (piece, stage) in enumerate(zip(pieces, staged))
    ]
    stores = [
        pltpu.make_async_copy(
            stage, out.at[planes, :, start : start + stage.shape[-1]], store_sems.at[slot]
        )
        for slot, (stage, (planes, start)) in enumerate(zip(staged, places))
    ]
    for load in loads:
        load.start()
    for load, store in zip(loads, stores):
        load.wait()
        store.start()
    for store in stores:
        store.wait()


def last_kernel(info, key, own, from_even, from_odd, *rest, places, first, count):
    amount = len(places)
    pieces, (_, out, held) = rest[:amount], rest[amount : amount + 3]
    staged, (load_sems, store_sems) = rest[amount + 3 : -2], rest[-2:]
    head = pl.program_id(0)
    loads = [
        pltpu.make_async_copy(piece, stage, load_sems.at[slot])
        for slot, (piece, stage) in enumerate(zip(pieces, staged))
    ]
    stores = [
        pltpu.make_async_copy(
            stage, out.at[planes, :, start : start + stage.shape[-1]], store_sems.at[slot]
        )
        for slot, (stage, (planes, start)) in enumerate(zip(staged, places))
    ]

    def head_copy(index):
        start = pl.multiple_of((first + index) * HEAD_DIM, HEAD_DIM)
        return pltpu.make_async_copy(
            held.at[index],
            out.at[pl.ds(1, 2), :, pl.ds(start, HEAD_DIM)],
            store_sems.at[amount + index],
        )

    @pl.when(head == 0)
    def _():
        for load in loads:
            load.start()

    @pl.when(head == min(1, count - 1))
    def _():
        for load, store in zip(loads, stores):
            load.wait()
            store.start()

    key_grad, value_grad = finished(info, key, own, from_even, from_odd)
    held[head, 0] = key_grad.astype(held.dtype)
    held[head, 1] = value_grad.astype(held.dtype)
    head_copy(head).start()

    @pl.when(head == count - 1)
    def _():
        for store in stores:
            store.wait()
        for index in range(count):
            head_copy(index).wait()


def head_block(rows, first, slot=None):
    if slot is None:
        return pl.BlockSpec((rows, HEAD_DIM), lambda head: (0, first + head))
    return pl.BlockSpec((None, rows, HEAD_DIM), lambda head: (slot, 0, first + head))


def pair_block(rows, first=0):
    return pl.BlockSpec((2, rows, HEAD_DIM), lambda head: (0, 0, first + head))


def whole_block(shape):
    return pl.BlockSpec(shape, lambda head: (0,) * len(shape))


def pack_params(limit):
    return dict(
        scratch_shapes=[pltpu.SemaphoreType.DMA((2,))],
        compiler_params=pltpu.CompilerParams(vmem_limit_bytes=limit),
        cost_estimate=COST,
    )


def pack_call(first_in, second_in, first, count, limit=PACK_VMEM):
    rows = first_in.shape[0]
    width = count * HEAD_DIM
    return pl.pallas_call(
        functools.partial(pack_kernel, start=first * HEAD_DIM, width=width),
        grid=(1,),
        in_specs=[pl.BlockSpec(memory_space=pl.ANY)] * 2,
        out_specs=whole_block((2, rows, width)),
        out_shape=jax.ShapeDtypeStruct((2, rows, width), jnp.bfloat16),
        **pack_params(limit),
    )(first_in, second_in)


def ask_call(info, query, grad, first, count):
    rows = query.shape[0]
    width = count * HEAD_DIM
    return pl.pallas_call(
        functools.partial(ask_kernel, start=first * HEAD_DIM, width=width),
        grid=(1,),
        in_specs=[whole_block(info.shape)] + [pl.BlockSpec(memory_space=pl.ANY)] * 2,
        out_specs=whole_block((2, rows + 16, width)),
        out_shape=jax.ShapeDtypeStruct((2, rows + 16, width), jnp.bfloat16),
        **pack_params(PACK_VMEM),
    )(info, query, grad)


def info_call(listed, gains):
    return pl.pallas_call(
        info_kernel,
        in_specs=[pl.BlockSpec(memory_space=pltpu.SMEM), pl.BlockSpec(memory_space=pltpu.VMEM)],
        out_specs=pl.BlockSpec(memory_space=pltpu.VMEM),
        out_shape=jax.ShapeDtypeStruct((8, HEAD_DIM), jnp.float32),
        compiler_params=pltpu.CompilerParams(vmem_limit_bytes=PACK_VMEM),
        cost_estimate=LONG_COST,
    )(listed, gains)


def info_block(info):
    if info.ndim == 2:
        return whole_block(info.shape)
    below = info.shape[1] // 16 - 1
    return pl.BlockSpec((2, 16, HEAD_DIM), lambda head: (0, below, 0))


def main_call(info, operands, pair_even, pair_odd, count, heads, place):
    rows = pair_even.shape[1]
    lanes = count * HEAD_DIM
    return pl.pallas_call(
        main_kernel,
        grid=(count,),
        in_specs=[info_block(info)]
        + [head_block(rows, first, slot) for _, first, slot in operands]
        + [pair_block(rows)] * 2,
        out_specs=[head_block(rows, place)] + [pair_block(rows)] * 3 + [whole_block((8, HEAD_DIM))],
        out_shape=[
            jax.ShapeDtypeStruct((rows, heads * HEAD_DIM), jnp.bfloat16),
            jax.ShapeDtypeStruct((2, rows, lanes), jnp.float32),
            jax.ShapeDtypeStruct((2, rows, lanes), jnp.bfloat16),
            jax.ShapeDtypeStruct((2, rows, lanes), jnp.bfloat16),
            jax.ShapeDtypeStruct((8, HEAD_DIM), jnp.float32),
        ],
        compiler_params=pltpu.CompilerParams(vmem_limit_bytes=MAIN_VMEM),
        cost_estimate=MAIN_COST,
    )(info, *[array for array, _, _ in operands], pair_even, pair_odd)


def finish_call(info, key, own, from_even, from_odd, count):
    array, first, slot = key
    rows = own.shape[1]
    return pl.pallas_call(
        finish_kernel,
        grid=(count,),
        in_specs=[info_block(info), head_block(rows, first, slot)] + [pair_block(rows)] * 3,
        out_specs=pair_block(rows),
        out_shape=jax.ShapeDtypeStruct((2, rows, count * HEAD_DIM), jnp.bfloat16),
        compiler_params=pltpu.CompilerParams(vmem_limit_bytes=SMALL_VMEM),
        cost_estimate=COST,
    )(info, array, own, from_even, from_odd)


def row_block(rows, first):
    return pl.BlockSpec((8, rows), lambda head: (first + head, 0))


def sums_call(info, arrays, pair_even, pair_odd, first, count, heads, earlier, far_count):
    rows = pair_even.shape[1]
    amount = 2 + far_count
    earlier = [] if earlier is None else earlier
    return pl.pallas_call(
        functools.partial(sums_kernel, far_count=far_count),
        grid=(count,),
        in_specs=[info_block(info)]
        + [head_block(rows, first)] * 4
        + [pair_block(rows)] * 2
        + [pl.BlockSpec(memory_space=pl.ANY)] * len(earlier),
        out_specs=[row_block(rows, first)] * amount,
        out_shape=[jax.ShapeDtypeStruct((8 * heads, rows), jnp.float32)] * amount,
        input_output_aliases={7 + index: index for index in range(len(earlier))},
        compiler_params=pltpu.CompilerParams(vmem_limit_bytes=MAIN_VMEM),
        cost_estimate=MAIN_COST,
    )(info, *arrays, pair_even, pair_odd, *earlier)


def grads_call(info, arrays, pair_even, pair_odd, sums, first, count, heads, earlier, far_count):
    rows = pair_even.shape[1]
    lanes = heads * HEAD_DIM
    earlier = [] if earlier is None else earlier
    place = 7 + len(sums)
    return pl.pallas_call(
        functools.partial(grads_kernel, far_count=far_count),
        grid=(count,),
        in_specs=[info_block(info)]
        + [head_block(rows, first)] * 4
        + [pair_block(rows)] * 2
        + [row_block(rows, first)] * len(sums)
        + [pl.BlockSpec(memory_space=pl.ANY)] * len(earlier),
        out_specs=[pair_block(rows, first)]
        + [head_block(rows, first)] * 3
        + [whole_block((8, HEAD_DIM))],
        out_shape=[
            jax.ShapeDtypeStruct((2, rows, lanes), jnp.bfloat16),
            jax.ShapeDtypeStruct((rows, lanes), jnp.float32),
            jax.ShapeDtypeStruct((rows, lanes), jnp.bfloat16),
            jax.ShapeDtypeStruct((rows, lanes), jnp.bfloat16),
            jax.ShapeDtypeStruct((8, HEAD_DIM), jnp.float32),
        ],
        input_output_aliases={place + index: index for index in range(len(earlier))},
        compiler_params=pltpu.CompilerParams(vmem_limit_bytes=MAIN_VMEM),
        cost_estimate=GRAD_COST,
    )(info, *arrays, pair_even, pair_odd, *sums, *earlier)


def answer_call(info, query, own, from_even, from_odd, low):
    rows, lanes = own.shape
    return pl.pallas_call(
        answer_kernel,
        grid=(lanes // HEAD_DIM,),
        in_specs=[info_block(info)]
        + [head_block(rows, 0)] * 4
        + [pl.BlockSpec(memory_space=pl.ANY)],
        out_specs=head_block(rows, 0),
        out_shape=jax.ShapeDtypeStruct(low.shape, low.dtype),
        input_output_aliases={5: 0},
        compiler_params=pltpu.CompilerParams(vmem_limit_bytes=SMALL_VMEM),
        cost_estimate=LONG_COST,
    )(info, query, own, from_even, from_odd, low)


def place_call(pieces, places):
    rows = pieces[0].shape[-2]
    anywhere = pl.BlockSpec(memory_space=pl.ANY)
    return pl.pallas_call(
        functools.partial(place_kernel, places=places),
        in_specs=[anywhere] * len(pieces),
        out_specs=anywhere,
        out_shape=jax.ShapeDtypeStruct((3, rows, HEADS * HEAD_DIM), jnp.bfloat16),
        scratch_shapes=[
            *[pltpu.VMEM(piece.shape, piece.dtype) for piece in pieces],
            pltpu.SemaphoreType.DMA((len(pieces),)),
            pltpu.SemaphoreType.DMA((len(pieces),)),
        ],
        compiler_params=pltpu.CompilerParams(vmem_limit_bytes=SMALL_VMEM),
        cost_estimate=COST,
    )(*pieces)


def last_call(info, key, own, from_even, from_odd, pieces, places, placed, first, count):
    array, offset, slot = key
    rows = own.shape[1]
    anywhere = pl.BlockSpec(memory_space=pl.ANY)
    return pl.pallas_call(
        functools.partial(last_kernel, places=places, first=first, count=count),
        grid=(count,),
        in_specs=[info_block(info), head_block(rows, offset, slot)]
        + [pair_block(rows)] * 3
        + [anywhere] * (len(pieces) + 1),
        out_specs=anywhere,
        out_shape=jax.ShapeDtypeStruct((3, rows, HEADS * HEAD_DIM), jnp.bfloat16),
        input_output_aliases={5 + len(pieces): 0},
        scratch_shapes=[
            pltpu.VMEM((count, 2, rows, HEAD_DIM), jnp.bfloat16),
            *[pltpu.VMEM(piece.shape, piece.dtype) for piece in pieces],
            pltpu.SemaphoreType.DMA((len(pieces),)),
            pltpu.SemaphoreType.DMA((len(pieces) + count,)),
        ],
        compiler_params=pltpu.CompilerParams(vmem_limit_bytes=SMALL_VMEM),
        cost_estimate=COST,
    )(info, array, own, from_even, from_odd, *pieces, placed)


def partner(tile, parity, count):
    other = tile + 1 if tile % 2 == parity else tile - 1
    return other if 0 <= other < count else tile


def far_partner(tile, base, count):
    other = ((tile - base) ^ 2) + base if tile >= base else tile
    return other if 0 <= other < count else tile


def paired(value, partners):
    width = lax.axis_size("dp")
    pairs = []
    for tile, other in enumerate(partners):
        for sample in range(width):
            moved = sample ^ 1 if other == tile and width % 2 == 0 else sample
            pairs.append((tile * width + sample, other * width + moved))
    return lax.ppermute(value, ("seq", "dp"), pairs)


def exchanged(value, parity):
    count = lax.axis_size("seq")
    return paired(value, [partner(tile, parity, count) for tile in range(count)])


def far_partners(count):
    both = [[far_partner(tile, base, count) for tile in range(count)] for base in (0, 2)]
    return [partners for partners in both if partners != list(range(count))]


def after(value, *others):
    return lax.optimization_barrier((value, *others))[0]


def turned(value, step):
    count = lax.axis_size("pipe")
    return lax.ppermute(value, "pipe", [(i, (i + step) % count) for i in range(count)])


def total_over(value, axis, *late):
    count = lax.axis_size(axis)
    step = 1
    while step < count:
        sent = after(value, *late) if 2 * step >= count else value
        value = value + lax.ppermute(sent, axis, [(i, i ^ step) for i in range(count)])
        step *= 2
    return value


def local(queries, keys, values, grad_out, norm_gains, kv_tiles):
    query, key, value, grad = (a[0, 0, 0] for a in (queries, keys, values, grad_out))
    rows = query.shape[0]
    seq_count = lax.axis_size("seq")
    key_first, key_count = KEY_GROUP
    away_first, away_count = AWAY_GROUP
    fars = far_partners(seq_count)
    arrays = (query, grad, key, value)
    asks = [pack_call(query, grad, *QUERY_GROUPS[0])]
    away_pair = pack_call(after(key, asks[0]), value, away_first, away_count)
    for first, count in QUERY_GROUPS[1:]:
        asks.append(pack_call(after(query, away_pair), grad, first, count))
    told_pairs = [(exchanged(ask, 0), exchanged(ask, 1)) for ask in asks]
    key_pair = pack_call(after(key, asks[-1]), value, key_first, key_count)
    key_pair = after(key_pair, *told_pairs[0])
    key_pairs = (exchanged(key_pair, 0), exchanged(key_pair, 1))
    info = info_call(kv_tiles[0, 0, 0], after(norm_gains[0], asks[-1]))
    away_pair = turned(away_pair, -1)
    sums = None
    for (first, count), told in zip(QUERY_GROUPS, told_pairs):
        sums = sums_call(info, arrays, *told, first, count, key_first, sums, len(fars))
    ready = [*sums[:2], *[after(value, *key_pairs) for value in sums[2:]]]
    received = [exchanged(ready[0], 0), exchanged(ready[1], 1)]
    received += [paired(value, partners) for value, partners in zip(ready[2:], fars)]
    all_sums = (*sums[:2], *received)
    asked = ask_call(info, after(query, away_pair, sums[0]), grad, away_first, away_count)
    asked = turned(asked, -1)
    away_sent = after(away_pair, *received)
    away_pairs = (exchanged(away_sent, 0), exchanged(away_sent, 1))
    gains, parts = [], None
    for (first, count), told in zip(QUERY_GROUPS, told_pairs):
        *parts, gain = grads_call(
            info, arrays, *told, all_sums, first, count, key_first, parts, len(fars)
        )
        gains.append(gain[:2])
    pair_low, own, to_even, to_odd = parts
    pieces = [turned(pair_low, -1)]
    places = [(slice(1, 3), 0)]
    answer = (own, exchanged(to_even, 0), exchanged(to_odd, 1))
    operands = [(array, key_first, None) for array in arrays]
    low, own, to_even, to_odd, gain = main_call(
        after(info, pair_low, asked), operands, *key_pairs, key_count, away_first, key_first
    )
    gains.append(gain[:2])
    key_answer = (own, exchanged(to_even, 0), exchanged(to_odd, 1))
    operands = [(asked, 0, 0), (asked, 0, 1), (away_pair, 0, 0), (away_pair, 0, 1)]
    query_low, own, to_even, to_odd, gain = main_call(
        after(asked, low), operands, *away_pairs, away_count, away_count, 0
    )
    returned = (exchanged(to_even, 0), exchanged(to_odd, 1))
    pieces.append(query_low)
    places.append((0, away_first * HEAD_DIM))
    gains.append(turned(after(gain[:2], pieces[0]), 1))
    low = answer_call(info, query, *answer, low)
    pieces.append(turned(after(low, gains[-1]), -1))
    places.append((0, 0))
    low = finish_call(after(info, pieces[0]), (key, key_first, None), *key_answer, key_count)
    pieces.append(turned(low, -1))
    places.append((slice(1, 3), key_first * HEAD_DIM))
    placed = place_call(pieces[:2], tuple(places[:2]))
    out = last_call(
        asked, operands[2], own, *returned, pieces[2:], tuple(places[2:]), placed,
        away_first, away_count,
    )
    summed = total_over(total_over(sum(gains), "dp"), "seq", placed)
    tokens = lax.axis_size("dp") * seq_count * rows * HEADS
    return (out[None, :, None, None], (summed / math.sqrt(tokens))[None])


def solution(mesh):
    placed = (
        P("pipe", "dp", "seq", None, None),
        P("pipe", "dp", "seq", None, None),
        P("pipe", "dp", "seq", None, None),
        P("pipe", "dp", "seq", None, None),
        P("pipe", None, None),
        P("pipe", "dp", "seq", None),
    )
    return jax.shard_map(
        local,
        mesh=mesh,
        in_specs=placed,
        out_specs=(P("pipe", None, "dp", "seq", None, None), P("pipe", None, None)),
        check_vma=False,
    )
```

```python
import functools
import math

import jax
import jax.numpy as jnp
from jax import lax
from jax.experimental import pallas as pl
from jax.experimental.pallas import tpu as pltpu
from jax.sharding import PartitionSpec as P

HEADS = 12
HEAD_DIM = 128
EPSILON = 1e-06
ROOT_SCALE = HEAD_DIM ** (-0.5)
EXP2_SCALE = ROOT_SCALE * math.log2(math.e)
QUERY_GROUPS = ((0, 3), (3, 2))
KEY_GROUP = (5, 2)
AWAY_GROUP = (7, 5)
MAIN_VMEM = 20 * 1024 * 1024
SMALL_VMEM = 12 * 1024 * 1024
PACK_VMEM = 4 * 1024 * 1024
COST = pl.CostEstimate(flops=1, bytes_accessed=1, transcendentals=0)
LONG_COST = pl.CostEstimate(flops=2 * 10**10, bytes_accessed=1, transcendentals=0)
MAIN_COST = pl.CostEstimate(flops=6 * 10**9, bytes_accessed=1, transcendentals=0)


def dot_nt(left, right):
    return lax.dot_general(
        left, right, (((1,), (1,)), ((), ())), preferred_element_type=jnp.float32
    )


def dot_nn(left, right):
    return lax.dot_general(
        left, right, (((1,), (0,)), ((), ())), preferred_element_type=jnp.float32
    )


def dot_tn(left, right):
    return lax.dot_general(
        left, right, (((0,), (0,)), ((), ())), preferred_element_type=jnp.float32
    )


def normalize(source, gain):
    floats = source.astype(jnp.float32)
    scaled = lax.rsqrt(jnp.mean(floats * floats, axis=-1, keepdims=True) + EPSILON)
    normed = floats * scaled
    return floats, scaled, normed, (normed * gain).astype(jnp.bfloat16)


def norm_back(grad_hat, floats, scaled, gain):
    scaled_grad = gain * grad_hat
    projected = jnp.sum(scaled_grad * floats, axis=-1, keepdims=True)
    return scaled * scaled_grad - (scaled**3 * projected * (1.0 / HEAD_DIM)) * floats


def pack_kernel(first_in, second_in, out, sems, *, start, width):
    rows = first_in.shape[0]
    copies = [
        pltpu.make_async_copy(
            source.at[:, start : start + width], out.at[slot, :rows], sems.at[slot]
        )
        for slot, source in enumerate((first_in, second_in))
    ]
    for copy in copies:
        copy.start()
    for copy in copies:
        copy.wait()


def info_kernel(listed, gains, info):
    tile = lax.axis_index("seq")
    last = lax.axis_size("seq") - 1
    info[...] = jnp.zeros_like(info)
    info[0:2, :] = gains[...]
    for parity in range(2):
        other = jnp.where(lax.rem(tile, 2) == parity, tile + 1, tile - 1)
        found = listed[0] == other
        for slot in range(1, listed.shape[0]):
            found = found | (listed[slot] == other)
        found = found & (other >= 0) & (other <= last)
        live = jnp.where(found, 1.0, 0.0)
        info[2 + parity : 3 + parity, :] = jnp.full((1, HEAD_DIM), live, jnp.float32)


def ask_kernel(info, query, grad, out, sems, *, start, width):
    rows = query.shape[0]
    value = info[...]
    planes = []
    for _ in range(3):
        low = value.astype(jnp.bfloat16)
        planes.append(low)
        value = value - low.astype(jnp.float32)
    planes.append(jnp.zeros_like(planes[0]))
    out[0, rows : rows + 16, :HEAD_DIM] = jnp.concatenate(planes[:2], axis=0)
    out[1, rows : rows + 16, :HEAD_DIM] = jnp.concatenate(planes[2:], axis=0)
    pack_kernel(query, grad, out, sems, start=start, width=width)


def told_info(told):
    floats = told[...].astype(jnp.float32)
    return floats[0, 0:8] + floats[0, 8:16] + floats[1, 0:8]


def main_kernel(
    info, query, grad, key, value, pair_even, pair_odd, *rest
):
    query_out, own_out, even_out, odd_out, gain_out = rest[-5:]
    told = told_info(info) if len(info.shape) == 3 else info[...]
    query_gain = told[0:1]
    key_gain = told[1:2]
    rows = query.shape[0]
    lives = [jnp.concatenate([told[row : row + 1]] * (rows // HEAD_DIM), axis=1) for row in (2, 3)]
    query_floats, query_scale, query_normed, query_hat = normalize(query[...], query_gain)
    grad_in = grad[...]
    sides = (
        (key[...], value[...], None),
        (pair_even[0], pair_even[1], lives[0]),
        (pair_odd[0], pair_odd[1], lives[1]),
    )
    parts = []
    totals = None
    for key_in, value_in, live in sides:
        _, _, key_normed, key_hat = normalize(key_in, key_gain)
        weights = jnp.exp2(dot_nt(key_hat, query_hat) * EXP2_SCALE)
        grad_probs = dot_nt(value_in, grad_in)
        weight_sum = jnp.sum(weights, axis=0, keepdims=True)
        cross_sum = jnp.sum(weights * grad_probs, axis=0, keepdims=True)
        if live is not None:
            weight_sum = weight_sum * live
            cross_sum = cross_sum * live
        totals = weight_sum if totals is None else totals + weight_sum
        crosses = cross_sum if live is None else crosses + cross_sum
        parts.append((key_normed, key_hat, weights, grad_probs, live))
    inverse = 1.0 / totals
    deltas = crosses * inverse
    query_grad_t = None
    key_gain_sum = None
    for (key_normed, key_hat, weights, grad_probs, live), out in zip(
        parts, (own_out, even_out, odd_out)
    ):
        probs = weights * (inverse if live is None else inverse * live)
        dscores = (probs * (grad_probs - deltas)).astype(jnp.bfloat16)
        key_part = dot_nn(dscores, query_hat) * ROOT_SCALE
        value_part = dot_nn(probs.astype(jnp.bfloat16), grad_in)
        out[0] = key_part.astype(out.dtype)
        out[1] = value_part.astype(out.dtype)
        gain_part = jnp.sum(key_part * key_normed, axis=0, keepdims=True)
        key_gain_sum = gain_part if key_gain_sum is None else key_gain_sum + gain_part
        query_part = dot_tn(key_hat, dscores)
        query_grad_t = query_part if query_grad_t is None else query_grad_t + query_part
    query_grad = query_grad_t.T * ROOT_SCALE
    query_out[...] = norm_back(query_grad, query_floats, query_scale, query_gain).astype(
        query_out.dtype
    )
    query_gain_sum = jnp.sum(query_grad * query_normed, axis=0, keepdims=True)

    @pl.when(pl.program_id(0) == 0)
    def _():
        gain_out[...] = jnp.zeros_like(gain_out)

    gain_out[0:1, :] += query_gain_sum
    gain_out[1:2, :] += key_gain_sum


def tile_sums(key_hat, value_in, query_hat, grad_in):
    weights = jnp.exp2(dot_nt(key_hat, query_hat) * EXP2_SCALE)
    grad_probs = dot_nt(value_in, grad_in)
    return weights, grad_probs


def wide_lives(told, rows):
    return [jnp.concatenate([told[row : row + 1]] * (rows // HEAD_DIM), axis=1) for row in (2, 3)]


def near_is_even():
    place = lax.rem(lax.axis_index("seq"), 4)
    return (place == 0) | (place == 3)


def sums_kernel(info, query, grad, key, value, pair_even, pair_odd, *rest, far_count):
    outs = rest[-2 - far_count :]
    told = info[...]
    _, _, _, key_hat = normalize(key[...], told[1:2])
    value_in = value[...]
    rows = []
    for query_in, grad_in in (
        (query[...], grad[...]), (pair_even[0], pair_even[1]), (pair_odd[0], pair_odd[1])
    ):
        _, _, _, query_hat = normalize(query_in, told[0:1])
        weights, grad_probs = tile_sums(key_hat, value_in, query_hat, grad_in)
        rows.append(
            [
                jnp.sum(weights, axis=0, keepdims=True),
                jnp.sum(weights * grad_probs, axis=0, keepdims=True),
            ]
        )
    own, even, odd = rows
    tail = wide_lives(told, query.shape[0])
    blank = jnp.zeros_like(tail[0])
    outs[0][...] = jnp.concatenate([*own, *even, *tail, blank, blank], axis=0)
    outs[1][...] = jnp.concatenate([*own, *odd, *tail, blank, blank], axis=0)
    near = near_is_even()
    for index, out in enumerate(outs[2:]):
        first, second = (even, odd) if index == 0 else (odd, even)
        chosen = [jnp.where(near, one, two) for one, two in zip(first, second)]
        out[...] = jnp.concatenate([*chosen, *[blank] * 6], axis=0)


def grads_kernel(
    info, query, grad, key, value, pair_even, pair_odd,
    sent_even, sent_odd, from_even, from_odd, *rest, far_count,
):
    fars = [far[0:2, :] for far in rest[:far_count]]
    pair_out, own_out, even_out, odd_out, gain_out = rest[-5:]
    told = info[...]
    near = near_is_even()
    if far_count == 2:
        far_even = jnp.where(near, fars[0], fars[1])
        far_odd = jnp.where(near, fars[1], fars[0])
    elif far_count == 1:
        far_even = jnp.where(near, fars[0], jnp.zeros_like(fars[0]))
        far_odd = jnp.where(near, jnp.zeros_like(fars[0]), fars[0])
    else:
        far_even = far_odd = jnp.zeros_like(from_even[0:2, :])
    own_sums = (
        sent_even[0:2, :]
        + sent_even[4:5, :] * from_even[2:4, :]
        + sent_even[5:6, :] * from_odd[2:4, :]
    )
    even_sums = (
        from_even[0:2, :] + from_even[4:5, :] * sent_even[2:4, :] + from_even[5:6, :] * far_even
    )
    odd_sums = (
        from_odd[0:2, :] + from_odd[5:6, :] * sent_odd[2:4, :] + from_odd[4:5, :] * far_odd
    )
    key_floats, key_scale, key_normed, key_hat = normalize(key[...], told[1:2])
    value_in = value[...]
    key_grad = value_grad = query_gain_sum = None
    for query_in, grad_in, sums, live, out in (
        (query[...], grad[...], own_sums, None, own_out),
        (pair_even[0], pair_even[1], even_sums, from_even[4:5, :], even_out),
        (pair_odd[0], pair_odd[1], odd_sums, from_odd[5:6, :], odd_out),
    ):
        _, _, query_normed, query_hat = normalize(query_in, told[0:1])
        weights, grad_probs = tile_sums(key_hat, value_in, query_hat, grad_in)
        inverse = 1.0 / sums[0:1]
        deltas = sums[1:2] * inverse
        probs = weights * (inverse if live is None else inverse * live)
        dscores = (probs * (grad_probs - deltas)).astype(jnp.bfloat16)
        key_part = dot_nn(dscores, query_hat)
        value_part = dot_nn(probs.astype(jnp.bfloat16), grad_in)
        query_part = dot_tn(key_hat, dscores).T * ROOT_SCALE
        out[...] = query_part.astype(out.dtype)
        gain_part = jnp.sum(query_part * query_normed, axis=0, keepdims=True)
        key_grad = key_part if key_grad is None else key_grad + key_part
        value_grad = value_part if value_grad is None else value_grad + value_part
        query_gain_sum = gain_part if query_gain_sum is None else query_gain_sum + gain_part
    key_grad = key_grad * ROOT_SCALE
    key_back = norm_back(key_grad, key_floats, key_scale, told[1:2])
    pair_out[0] = key_back.astype(pair_out.dtype)
    pair_out[1] = value_grad.astype(pair_out.dtype)

    @pl.when(pl.program_id(0) == 0)
    def _():
        gain_out[...] = jnp.zeros_like(gain_out)

    gain_out[0:1, :] += query_gain_sum
    gain_out[1:2, :] += jnp.sum(key_grad * key_normed, axis=0, keepdims=True)


def answer_kernel(info, query, own, from_even, from_odd, _, out):
    gain = info[0:1, :]
    floats, scaled, _, _ = normalize(query[...], gain)
    total = own[...] + from_even[...].astype(jnp.float32) + from_odd[...].astype(jnp.float32)
    out[...] = norm_back(total, floats, scaled, gain).astype(out.dtype)


def finished(info, key, own, from_even, from_odd):
    told = told_info(info) if len(info.shape) == 3 else info[...]
    key_gain = told[1:2]
    key_floats, key_scale, _, _ = normalize(key[...], key_gain)
    key_grad = own[0].astype(jnp.float32) + from_even[0].astype(jnp.float32) + from_odd[0].astype(jnp.float32)
    value_grad = own[1].astype(jnp.float32) + from_even[1].astype(jnp.float32) + from_odd[1].astype(jnp.float32)
    return norm_back(key_grad, key_floats, key_scale, key_gain), value_grad


def finish_kernel(info, key, own, from_even, from_odd, out):
    key_grad, value_grad = finished(info, key, own, from_even, from_odd)
    out[0] = key_grad.astype(out.dtype)
    out[1] = value_grad.astype(out.dtype)


def place_kernel(*refs, places):
    amount = len(places)
    pieces, out, staged = refs[:amount], refs[amount], refs[amount + 1 : -2]
    load_sems, store_sems = refs[-2:]
    loads = [
        pltpu.make_async_copy(piece, stage, load_sems.at[slot])
        for slot, (piece, stage) in enumerate(zip(pieces, staged))
    ]
    stores = [
        pltpu.make_async_copy(
            stage, out.at[planes, :, start : start + stage.shape[-1]], store_sems.at[slot]
        )
        for slot, (stage, (planes, start)) in enumerate(zip(staged, places))
    ]
    for load in loads:
        load.start()
    for load, store in zip(loads, stores):
        load.wait()
        store.start()
    for store in stores:
        store.wait()


def last_kernel(info, key, own, from_even, from_odd, *rest, places, first, count):
    amount = len(places)
    pieces, (_, out, held) = rest[:amount], rest[amount : amount + 3]
    staged, (load_sems, store_sems) = rest[amount + 3 : -2], rest[-2:]
    head = pl.program_id(0)
    loads = [
        pltpu.make_async_copy(piece, stage, load_sems.at[slot])
        for slot, (piece, stage) in enumerate(zip(pieces, staged))
    ]
    stores = [
        pltpu.make_async_copy(
            stage, out.at[planes, :, start : start + stage.shape[-1]], store_sems.at[slot]
        )
        for slot, (stage, (planes, start)) in enumerate(zip(staged, places))
    ]

    def head_copy(index):
        start = pl.multiple_of((first + index) * HEAD_DIM, HEAD_DIM)
        return pltpu.make_async_copy(
            held.at[index],
            out.at[pl.ds(1, 2), :, pl.ds(start, HEAD_DIM)],
            store_sems.at[amount + index],
        )

    @pl.when(head == 0)
    def _():
        for load in loads:
            load.start()

    @pl.when(head == min(1, count - 1))
    def _():
        for load, store in zip(loads, stores):
            load.wait()
            store.start()

    key_grad, value_grad = finished(info, key, own, from_even, from_odd)
    held[head, 0] = key_grad.astype(held.dtype)
    held[head, 1] = value_grad.astype(held.dtype)
    head_copy(head).start()

    @pl.when(head == count - 1)
    def _():
        for store in stores:
            store.wait()
        for index in range(count):
            head_copy(index).wait()


def head_block(rows, first, slot=None):
    if slot is None:
        return pl.BlockSpec((rows, HEAD_DIM), lambda head: (0, first + head))
    return pl.BlockSpec((None, rows, HEAD_DIM), lambda head: (slot, 0, first + head))


def pair_block(rows, first=0):
    return pl.BlockSpec((2, rows, HEAD_DIM), lambda head: (0, 0, first + head))


def whole_block(shape):
    return pl.BlockSpec(shape, lambda head: (0,) * len(shape))


def pack_params(limit):
    return dict(
        scratch_shapes=[pltpu.SemaphoreType.DMA((2,))],
        compiler_params=pltpu.CompilerParams(vmem_limit_bytes=limit),
        cost_estimate=COST,
    )


def pack_call(first_in, second_in, first, count, limit=PACK_VMEM):
    rows = first_in.shape[0]
    width = count * HEAD_DIM
    return pl.pallas_call(
        functools.partial(pack_kernel, start=first * HEAD_DIM, width=width),
        grid=(1,),
        in_specs=[pl.BlockSpec(memory_space=pl.ANY)] * 2,
        out_specs=whole_block((2, rows, width)),
        out_shape=jax.ShapeDtypeStruct((2, rows, width), jnp.bfloat16),
        **pack_params(limit),
    )(first_in, second_in)


def ask_call(info, query, grad, first, count):
    rows = query.shape[0]
    width = count * HEAD_DIM
    return pl.pallas_call(
        functools.partial(ask_kernel, start=first * HEAD_DIM, width=width),
        grid=(1,),
        in_specs=[whole_block(info.shape)] + [pl.BlockSpec(memory_space=pl.ANY)] * 2,
        out_specs=whole_block((2, rows + 16, width)),
        out_shape=jax.ShapeDtypeStruct((2, rows + 16, width), jnp.bfloat16),
        **pack_params(PACK_VMEM),
    )(info, query, grad)


def info_call(listed, gains):
    return pl.pallas_call(
        info_kernel,
        in_specs=[pl.BlockSpec(memory_space=pltpu.SMEM), pl.BlockSpec(memory_space=pltpu.VMEM)],
        out_specs=pl.BlockSpec(memory_space=pltpu.VMEM),
        out_shape=jax.ShapeDtypeStruct((8, HEAD_DIM), jnp.float32),
        compiler_params=pltpu.CompilerParams(vmem_limit_bytes=PACK_VMEM),
        cost_estimate=LONG_COST,
    )(listed, gains)


def info_block(info):
    if info.ndim == 2:
        return whole_block(info.shape)
    below = info.shape[1] // 16 - 1
    return pl.BlockSpec((2, 16, HEAD_DIM), lambda head: (0, below, 0))


def main_call(info, operands, pair_even, pair_odd, count, heads, place):
    rows = pair_even.shape[1]
    lanes = count * HEAD_DIM
    return pl.pallas_call(
        main_kernel,
        grid=(count,),
        in_specs=[info_block(info)]
        + [head_block(rows, first, slot) for _, first, slot in operands]
        + [pair_block(rows)] * 2,
        out_specs=[head_block(rows, place)] + [pair_block(rows)] * 3 + [whole_block((8, HEAD_DIM))],
        out_shape=[
            jax.ShapeDtypeStruct((rows, heads * HEAD_DIM), jnp.bfloat16),
            jax.ShapeDtypeStruct((2, rows, lanes), jnp.bfloat16),
            jax.ShapeDtypeStruct((2, rows, lanes), jnp.bfloat16),
            jax.ShapeDtypeStruct((2, rows, lanes), jnp.bfloat16),
            jax.ShapeDtypeStruct((8, HEAD_DIM), jnp.float32),
        ],
        compiler_params=pltpu.CompilerParams(vmem_limit_bytes=MAIN_VMEM),
        cost_estimate=MAIN_COST,
    )(info, *[array for array, _, _ in operands], pair_even, pair_odd)


def finish_call(info, key, own, from_even, from_odd, count):
    array, first, slot = key
    rows = own.shape[1]
    return pl.pallas_call(
        finish_kernel,
        grid=(count,),
        in_specs=[info_block(info), head_block(rows, first, slot)] + [pair_block(rows)] * 3,
        out_specs=pair_block(rows),
        out_shape=jax.ShapeDtypeStruct((2, rows, count * HEAD_DIM), jnp.bfloat16),
        compiler_params=pltpu.CompilerParams(vmem_limit_bytes=SMALL_VMEM),
        cost_estimate=COST,
    )(info, array, own, from_even, from_odd)


def row_block(rows, first):
    return pl.BlockSpec((8, rows), lambda head: (first + head, 0))


def sums_call(info, arrays, pair_even, pair_odd, first, count, heads, earlier, far_count):
    rows = pair_even.shape[1]
    amount = 2 + far_count
    earlier = [] if earlier is None else earlier
    return pl.pallas_call(
        functools.partial(sums_kernel, far_count=far_count),
        grid=(count,),
        in_specs=[info_block(info)]
        + [head_block(rows, first)] * 4
        + [pair_block(rows)] * 2
        + [pl.BlockSpec(memory_space=pl.ANY)] * len(earlier),
        out_specs=[row_block(rows, first)] * amount,
        out_shape=[jax.ShapeDtypeStruct((8 * heads, rows), jnp.float32)] * amount,
        input_output_aliases={7 + index: index for index in range(len(earlier))},
        compiler_params=pltpu.CompilerParams(vmem_limit_bytes=MAIN_VMEM),
        cost_estimate=MAIN_COST,
    )(info, *arrays, pair_even, pair_odd, *earlier)


def grads_call(info, arrays, pair_even, pair_odd, sums, first, count, heads, earlier, far_count):
    rows = pair_even.shape[1]
    lanes = heads * HEAD_DIM
    earlier = [] if earlier is None else earlier
    place = 7 + len(sums)
    return pl.pallas_call(
        functools.partial(grads_kernel, far_count=far_count),
        grid=(count,),
        in_specs=[info_block(info)]
        + [head_block(rows, first)] * 4
        + [pair_block(rows)] * 2
        + [row_block(rows, first)] * len(sums)
        + [pl.BlockSpec(memory_space=pl.ANY)] * len(earlier),
        out_specs=[pair_block(rows, first)]
        + [head_block(rows, first)] * 3
        + [whole_block((8, HEAD_DIM))],
        out_shape=[
            jax.ShapeDtypeStruct((2, rows, lanes), jnp.bfloat16),
            jax.ShapeDtypeStruct((rows, lanes), jnp.float32),
            jax.ShapeDtypeStruct((rows, lanes), jnp.bfloat16),
            jax.ShapeDtypeStruct((rows, lanes), jnp.bfloat16),
            jax.ShapeDtypeStruct((8, HEAD_DIM), jnp.float32),
        ],
        input_output_aliases={place + index: index for index in range(len(earlier))},
        compiler_params=pltpu.CompilerParams(vmem_limit_bytes=MAIN_VMEM),
        cost_estimate=COST,
    )(info, *arrays, pair_even, pair_odd, *sums, *earlier)


def answer_call(info, query, own, from_even, from_odd, low):
    rows, lanes = own.shape
    return pl.pallas_call(
        answer_kernel,
        grid=(lanes // HEAD_DIM,),
        in_specs=[info_block(info)]
        + [head_block(rows, 0)] * 4
        + [pl.BlockSpec(memory_space=pl.ANY)],
        out_specs=head_block(rows, 0),
        out_shape=jax.ShapeDtypeStruct(low.shape, low.dtype),
        input_output_aliases={5: 0},
        compiler_params=pltpu.CompilerParams(vmem_limit_bytes=SMALL_VMEM),
        cost_estimate=LONG_COST,
    )(info, query, own, from_even, from_odd, low)


def place_call(pieces, places):
    rows = pieces[0].shape[-2]
    anywhere = pl.BlockSpec(memory_space=pl.ANY)
    return pl.pallas_call(
        functools.partial(place_kernel, places=places),
        in_specs=[anywhere] * len(pieces),
        out_specs=anywhere,
        out_shape=jax.ShapeDtypeStruct((3, rows, HEADS * HEAD_DIM), jnp.bfloat16),
        scratch_shapes=[
            *[pltpu.VMEM(piece.shape, piece.dtype) for piece in pieces],
            pltpu.SemaphoreType.DMA((len(pieces),)),
            pltpu.SemaphoreType.DMA((len(pieces),)),
        ],
        compiler_params=pltpu.CompilerParams(vmem_limit_bytes=SMALL_VMEM),
        cost_estimate=COST,
    )(*pieces)


def last_call(info, key, own, from_even, from_odd, pieces, places, placed, first, count):
    array, offset, slot = key
    rows = own.shape[1]
    anywhere = pl.BlockSpec(memory_space=pl.ANY)
    return pl.pallas_call(
        functools.partial(last_kernel, places=places, first=first, count=count),
        grid=(count,),
        in_specs=[info_block(info), head_block(rows, offset, slot)]
        + [pair_block(rows)] * 3
        + [anywhere] * (len(pieces) + 1),
        out_specs=anywhere,
        out_shape=jax.ShapeDtypeStruct((3, rows, HEADS * HEAD_DIM), jnp.bfloat16),
        input_output_aliases={5 + len(pieces): 0},
        scratch_shapes=[
            pltpu.VMEM((count, 2, rows, HEAD_DIM), jnp.bfloat16),
            *[pltpu.VMEM(piece.shape, piece.dtype) for piece in pieces],
            pltpu.SemaphoreType.DMA((len(pieces),)),
            pltpu.SemaphoreType.DMA((len(pieces) + count,)),
        ],
        compiler_params=pltpu.CompilerParams(vmem_limit_bytes=SMALL_VMEM),
        cost_estimate=COST,
    )(info, array, own, from_even, from_odd, *pieces, placed)


def partner(tile, parity, count):
    other = tile + 1 if tile % 2 == parity else tile - 1
    return other if 0 <= other < count else tile


def far_partner(tile, base, count):
    other = ((tile - base) ^ 2) + base if tile >= base else tile
    return other if 0 <= other < count else tile


def paired(value, partners):
    width = lax.axis_size("dp")
    pairs = []
    for tile, other in enumerate(partners):
        for sample in range(width):
            moved = sample ^ 1 if other == tile and width % 2 == 0 else sample
            pairs.append((tile * width + sample, other * width + moved))
    return lax.ppermute(value, ("seq", "dp"), pairs)


def exchanged(value, parity):
    count = lax.axis_size("seq")
    return paired(value, [partner(tile, parity, count) for tile in range(count)])


def far_partners(count):
    both = [[far_partner(tile, base, count) for tile in range(count)] for base in (0, 2)]
    return [partners for partners in both if partners != list(range(count))]


def after(value, *others):
    return lax.optimization_barrier((value, *others))[0]


def turned(value, step):
    count = lax.axis_size("pipe")
    return lax.ppermute(value, "pipe", [(i, (i + step) % count) for i in range(count)])


def total_over(value, axis, *late):
    count = lax.axis_size(axis)
    step = 1
    while step < count:
        sent = after(value, *late) if 2 * step >= count else value
        value = value + lax.ppermute(sent, axis, [(i, i ^ step) for i in range(count)])
        step *= 2
    return value


def local(queries, keys, values, grad_out, norm_gains, kv_tiles):
    query, key, value, grad = (a[0, 0, 0] for a in (queries, keys, values, grad_out))
    rows = query.shape[0]
    seq_count = lax.axis_size("seq")
    key_first, key_count = KEY_GROUP
    away_first, away_count = AWAY_GROUP
    fars = far_partners(seq_count)
    arrays = (query, grad, key, value)
    asks = [pack_call(query, grad, *QUERY_GROUPS[0])]
    away_pair = pack_call(after(key, asks[0]), value, away_first, away_count)
    for first, count in QUERY_GROUPS[1:]:
        asks.append(pack_call(after(query, away_pair), grad, first, count))
    told_pairs = [(exchanged(ask, 0), exchanged(ask, 1)) for ask in asks]
    key_pair = pack_call(after(key, asks[-1]), value, key_first, key_count)
    key_pair = after(key_pair, *told_pairs[0])
    key_pairs = (exchanged(key_pair, 0), exchanged(key_pair, 1))
    info = info_call(kv_tiles[0, 0, 0], after(norm_gains[0], asks[-1]))
    away_pair = turned(away_pair, -1)
    sums = None
    for (first, count), told in zip(QUERY_GROUPS, told_pairs):
        sums = sums_call(info, arrays, *told, first, count, key_first, sums, len(fars))
    received = [exchanged(sums[0], 0), exchanged(sums[1], 1)]
    received += [
        paired(value, partners) for value, partners in zip(sums[2:], fars)
    ]
    all_sums = (*sums[:2], *received)
    asked = ask_call(info, after(query, away_pair, sums[0]), grad, away_first, away_count)
    asked = turned(asked, -1)
    away_sent = after(away_pair, *key_pairs, *received)
    away_pairs = (exchanged(away_sent, 0), exchanged(away_sent, 1))
    gains, parts = [], None
    for (first, count), told in zip(QUERY_GROUPS, told_pairs):
        *parts, gain = grads_call(
            info, arrays, *told, all_sums, first, count, key_first, parts, len(fars)
        )
        gains.append(gain[:2])
    pair_low, own, to_even, to_odd = parts
    pieces = [turned(pair_low, -1)]
    places = [(slice(1, 3), 0)]
    answer = (own, exchanged(to_even, 0), exchanged(to_odd, 1))
    operands = [(array, key_first, None) for array in arrays]
    low, own, to_even, to_odd, gain = main_call(
        after(info, pair_low), operands, *key_pairs, key_count, away_first, key_first
    )
    gains.append(gain[:2])
    key_answer = (own, exchanged(to_even, 0), exchanged(to_odd, 1))
    operands = [(asked, 0, 0), (asked, 0, 1), (away_pair, 0, 0), (away_pair, 0, 1)]
    query_low, own, to_even, to_odd, gain = main_call(
        after(asked, low), operands, *away_pairs, away_count, away_count, 0
    )
    returned = (exchanged(to_even, 0), exchanged(to_odd, 1))
    pieces.append(query_low)
    places.append((0, away_first * HEAD_DIM))
    low = answer_call(info, query, *answer, low)
    gains.append(turned(after(gain[:2], low, pieces[0]), 1))
    pieces.append(turned(after(low, gains[-1]), -1))
    places.append((0, 0))
    low = finish_call(after(info, pieces[0]), (key, key_first, None), *key_answer, key_count)
    pieces.append(turned(low, -1))
    places.append((slice(1, 3), key_first * HEAD_DIM))
    placed = place_call(pieces[:2], tuple(places[:2]))
    out = last_call(
        asked, operands[2], own, *returned, pieces[2:], tuple(places[2:]), placed,
        away_first, away_count,
    )
    summed = total_over(total_over(sum(gains), "dp"), "seq", placed)
    tokens = lax.axis_size("dp") * seq_count * rows * HEADS
    return (out[None, :, None, None], (summed / math.sqrt(tokens))[None])


def solution(mesh):
    placed = (
        P("pipe", "dp", "seq", None, None),
        P("pipe", "dp", "seq", None, None),
        P("pipe", "dp", "seq", None, None),
        P("pipe", "dp", "seq", None, None),
        P("pipe", None, None),
        P("pipe", "dp", "seq", None),
    )
    return jax.shard_map(
        local,
        mesh=mesh,
        in_specs=placed,
        out_specs=(P("pipe", None, "dp", "seq", None, None), P("pipe", None, None)),
        check_vma=False,
    )
```
